32 devices in a mesh: dp: 8 (over z, core), mp: 2 (over x), pre: 2 (over y).
Axes of the slice: x: 2, y: 2, z: 4, core: 2. Of those that a mesh axis runs over, the one named last changes fastest.
Arguments:
- activations: bfloat16 [12288, 1024], P('dp'), may hold values from -6 to 6
- grad_output: bfloat16 [12288, 4096], P('dp', ('mp', 'pre')), may hold values from -0.0546875 to 0.0546875
- left_old: float32 [1024, 1024], P(('mp', 'pre'), 'dp'), may hold values from -1 to 9, as said below
- right_old: float32 [4096, 4096], P(('mp', 'pre'), 'dp'), may hold values from -1 to 9, as said below
- probe_left: float32 [1024], replicated, may hold values from -6 to 6
- probe_right: float32 [4096], replicated, may hold values from -6 to 6
Outputs:
- left_new: float32 [1024, 1024], P(('mp', 'pre'), 'dp')
- right_new: float32 [4096, 4096], P(('mp', 'pre'), 'dp')
- update: float32 [1024, 4096], P('dp', ('mp', 'pre'))
The draws below stay inside these ranges and needn't reach their ends.
Inputs may be any that keep to these rules, and one draw needn't show every extreme that they name: `left_old`: symmetric and positive definite. `right_old`: symmetric and positive definite.
All inputs are finite; a program needn't handle non-finite values.
Results may differ from the reference program's by a relative error of at most 0.0003.
Values sent between devices are 32-bit elements; how exact they have to be, the bound alone decides.
No kernel may reach another device: no remote copies, remote signals or barrier semaphores. Data moves between devices by JAX's collectives and lax.ppermute only.
A program may use at most 64 MiB of HBM per device.

```python
import math
import jax
import jax.numpy as jnp
from jax import lax

D = 1024
FF = 4096
TOKENS = 12288


def symmetric_draw(key, order):
    first_key, second_key = jax.random.split(jax.random.fold_in(key, 7))
    random_part = jax.random.normal(first_key, (order, order), jnp.float32) * (0.5 / math.sqrt(order))
    off_part = (random_part + random_part.T) * 0.5
    diagonal = jax.random.uniform(second_key, (order,), jnp.float32, 1.0, 2.0)
    return off_part + jnp.diag(diagonal)


def draw_left_old(key, part):
    return symmetric_draw(key, D)


def draw_right_old(key, part):
    return symmetric_draw(key, FF)


def level_of(own_key, shape, pieces, low, top_value):
    def one(dim, parts):
        heights = jax.random.uniform(jax.random.fold_in(jax.random.fold_in(own_key, 6), dim), (parts,), jnp.float32, low / len(pieces), top_value / len(pieces))
        return jnp.repeat(jnp.exp(heights), shape[dim] // parts).reshape((-1,) + (1,) * (len(shape) - dim - 1))

    level = one(*pieces[0])
    for cut in pieces[1:]:
        level = level * one(*cut)
    return level


def normal_values(key, extent, spread, reach, cuts=(), held_as=jnp.bfloat16):
    drawn = spread * jax.random.normal(key, extent, jnp.float32)
    if cuts:
        drawn = drawn * level_of(key, extent, cuts, -0.22, 0.18)
    return jnp.clip(drawn, -reach, reach).astype(held_as)


def setup_inputs(seed: int = 0) -> dict:
    splits = jax.random.split(jax.random.key(seed), 7)
    return {
        "activations": normal_values(splits[0], (TOKENS, D), 1.0, 6.0, ((0, 8),)),
        "grad_output": normal_values(splits[1], (TOKENS, FF), TOKENS ** -0.5, 0.0546875, ((0, 8), (1, 4))),
        "left_old": draw_left_old(jax.random.fold_in(splits[6], 71), 0),
        "right_old": draw_right_old(jax.random.fold_in(splits[6], 71), 0),
        "probe_left": normal_values(splits[4], (D,), 1.0, 6.0, (), jnp.float32),
        "probe_right": normal_values(splits[5], (FF,), 1.0, 6.0, (), jnp.float32),
    }


beta_decay = 0.9
norm_floor = 1e-06

def length_of(vector):
    return jnp.sqrt(jnp.sum(vector * vector) + norm_floor)

def largest(matrix, probe):
    highest = lax.Precision.HIGHEST
    first_image = jnp.dot(matrix, probe, precision=highest, preferred_element_type=jnp.float32)
    unit_vector = first_image / length_of(first_image)
    second_image = jnp.dot(matrix, unit_vector, precision=highest, preferred_element_type=jnp.float32)
    return length_of(second_image)

def reference(activations, grad_output, left_old, right_old, probe_left, probe_right):
    highest = lax.Precision.HIGHEST
    gradient = jnp.dot(activations.T, grad_output, preferred_element_type=jnp.float32)
    left_new = beta_decay * left_old + jnp.dot(gradient, gradient.T, precision=highest, preferred_element_type=jnp.float32) / FF
    right_new = beta_decay * right_old + jnp.dot(gradient.T, gradient, precision=highest, preferred_element_type=jnp.float32) / D
    top_left = largest(left_new, probe_left)
    top_right = largest(right_new, probe_right)
    half_step = (5.0 * gradient - jnp.dot(left_new, gradient, precision=highest, preferred_element_type=jnp.float32) / top_left) * 0.25
    update = (5.0 * half_step - jnp.dot(half_step, right_new, precision=highest, preferred_element_type=jnp.float32) / top_right) * 0.25
    update = update * (top_left * top_right) ** (-0.25)
    return (left_new, right_new, update)
```

```python
import jax
import jax.numpy as jnp
from jax import lax
from jax.sharding import PartitionSpec as P

beta_decay = 0.9
norm_floor = 1e-06
chunk_count = 4


def length_of(vector):
    return jnp.sqrt(jnp.sum(vector * vector) + norm_floor)


def product(a, b, a_dim, b_dim):
    return lax.dot_general(
        a,
        b,
        (((a_dim,), (b_dim,)), ((), ())),
        precision=lax.Precision.HIGH,
        preferred_element_type=jnp.float32,
    )


def select_by(index, options):
    result = None
    for value, array in options.items():
        result = array if result is None else jnp.where(index == value, array, result)
    return result


def make_step(mesh):
    dp, mp, pre = (mesh.shape[name] for name in ("dp", "mp", "pre"))
    models = mp * pre
    cores = dp // models
    line = dp // cores
    axes = ("dp", "mp", "pre")

    def number(d, x, y):
        return (d * mp + x) * pre + y

    everyone = [(d, x, y) for d in range(dp) for x in range(mp) for y in range(pre)]

    def send(array, target):
        pairs = []
        for place in everyone:
            goal = target(*place)
            if goal is not None:
                pairs.append((number(*place), number(*goal)))
        return lax.ppermute(array, axes, pairs)

    def to_core(array, shift):
        return send(array, lambda d, x, y: (d // cores * cores + (d + shift) % cores, x, y))

    def up(array):
        return send(array, lambda d, x, y: (d + cores, x, y) if d + cores < dp else None)

    def down(array):
        return send(array, lambda d, x, y: (d - cores, x, y) if d >= cores else None)

    def chain(pieces, place, consume):
        count = len(pieces)
        steps = count + line - 2

        def mine(t, skew):
            return select_by(
                skew, {k: pieces[min(max(t - k, 0), count - 1)] for k in range(line)}
            )

        back = line - 1 - place
        sent_up, got_down = [], []
        from_below = from_above = None
        results = []
        for t in range(steps + 1):
            going_up, going_down = mine(t, place), mine(t, back)
            if t:
                going_up = going_up + from_below
                going_down = going_down + from_above
            sent_up.append(going_up)
            if t < steps:
                from_below = up(going_up)
                from_above = down(going_down)
                got_down.append(from_above)
            j = t - (line - 1)
            if j >= 0:
                whole = select_by(
                    place,
                    {
                        k: sent_up[j + k] + got_down[j + line - 2 - k]
                        if k < line - 1
                        else sent_up[j + k]
                        for k in range(line)
                    },
                )
                results.append(consume(j, whole))
        return results

    def shards(activations, grad_output, left_old, right_old, probe_left, probe_right):
        data_index = lax.axis_index("dp")
        model_index = lax.axis_index(("mp", "pre"))
        core = data_index % cores
        place = data_index // cores
        width = activations.shape[1]
        block = grad_output.shape[1]
        hidden = block * models
        panel = block // cores
        own_rows = width // dp
        piece = panel // chunk_count
        is_owner = model_index == place

        def half_of(array, which, axis):
            return lax.dynamic_slice_in_dim(array, which * panel, panel, axis)

        def local(which):
            return lax.dot_general(
                half_of(grad_output, which, 1),
                activations,
                (((0,), (0,)), ((), ())),
                preferred_element_type=jnp.float32,
            )

        arrived = [to_core(local((core + s) % cores), s) for s in range(1, cores)]
        summed = local(core)
        for other in arrived:
            summed = summed + other
        pieces = [summed[j * piece : (j + 1) * piece] for j in range(chunk_count)]

        def owner_of(d):
            return (d // cores) // pre, (d // cores) % pre

        def spread_first(array, along_pre):
            result = None
            for s in range(1, pre if along_pre else mp):
                def target(d, x, y, s=s):
                    if (x, y) != owner_of(d):
                        return None
                    return (d, x, (y + s) % pre) if along_pre else (d, (x + s) % mp, y)

                got = send(array, target)
                result = got if result is None else result + got
            return result

        def spread_second(array, along_pre):
            result = None
            for s in range(1, pre if along_pre else mp):
                def target(d, x, y, s=s):
                    ox, oy = owner_of(d)
                    if along_pre:
                        return (d, x, (y + s) % pre) if y == oy else None
                    return (d, (x + s) % mp, y) if x == ox else None

                got = send(array, target)
                result = got if result is None else result + got
            return result

        def spread(array, along_pre):
            first = spread_first(array, along_pre)
            held = jnp.where(is_owner, array, first)
            second = spread_second(held, not along_pre)
            owner_x, owner_y = place // pre, place % pre
            same = (
                lax.axis_index("mp") == owner_x if along_pre else lax.axis_index("pre") == owner_y
            )
            return jnp.where(same, held, second)

        def after_gradient(j, whole):
            others = [to_core(whole, s) for s in range(1, cores)]
            panel_part = spread(whole, j % 2 == 0)
            return whole, others, panel_part

        done = chain(pieces, place, after_gradient)
        own = [d[0] for d in done]
        others = [[d[1][s] for d in done] for s in range(cores - 1)]
        panel_t = jnp.concatenate([d[2] for d in done], axis=0)

        def old_rows(which, j):
            return lax.dynamic_slice_in_dim(right_old, which * panel + j * piece, piece, 0)

        def right_piece(rows, which, j):
            gram = product(rows, panel_t, 1, 1)
            return beta_decay * old_rows(which, j) + gram / width

        right_own, right_other, mixed = [], [[] for _ in range(cores - 1)], []
        for j in range(chunk_count):
            total = None
            got = []
            for s in range(cores - 1):
                block_rows = right_piece(others[s][j], (core - s - 1) % cores, j)
                right_other[s].append(block_rows)
                got.append(to_core(product(block_rows, panel_t, 1, 0), -(s + 1)))
            block_rows = right_piece(own[j], core, j)
            right_own.append(block_rows)
            total = product(block_rows, panel_t, 1, 0)
            for g in got:
                total = total + g
            mixed.append(total)

        def by_core(own_part, other_parts, axis):
            return select_by(
                core,
                {
                    c: jnp.concatenate(
                        [
                            own_part if h == c else other_parts[(c - h) % cores - 1]
                            for h in range(cores)
                        ],
                        axis=axis,
                    )
                    for c in range(cores)
                },
            )

        right_new = by_core(
            jnp.concatenate(right_own, axis=0),
            [jnp.concatenate(r, axis=0) for r in right_other],
            0,
        )

        grad_t = by_core(
            jnp.concatenate(own, axis=0), [jnp.concatenate(o, axis=0) for o in others], 0
        )
        old_columns = lax.all_gather(left_old, ("mp", "pre"), axis=0, tiled=True)
        grad_rows = lax.dynamic_slice_in_dim(grad_t, data_index * own_rows, own_rows, 1)
        left_gram = lax.psum(product(grad_t, grad_rows, 0, 0), ("mp", "pre"))
        left_columns = beta_decay * old_columns + left_gram / hidden
        left_new = lax.dynamic_slice_in_dim(
            left_columns, model_index * (width // models), width // models, 0
        )

        def sum_dp(vector):
            total = vector
            for s in range(1, dp):
                total = total + send(vector, lambda d, x, y, s=s: ((d + s) % dp, x, y))
            return total

        def sum_models(vector):
            total = vector
            for s in range(1, models):

                def target(d, x, y, s=s):
                    m = (x * pre + y + s) % models
                    return d, m // pre, m % pre

                total = total + send(vector, target)
            return total

        def matvec(matrix, vector, dim):
            if dim:
                return jnp.sum(matrix * vector[None, :], axis=1)
            return jnp.sum(matrix * vector[:, None], axis=0)

        right_part = matvec(
            right_new, lax.dynamic_slice_in_dim(probe_right, data_index * panel, panel, 0), 1
        )
        left_part = matvec(left_columns, probe_left, 0)
        left_part = lax.dynamic_update_slice_in_dim(
            jnp.zeros((width,), jnp.float32), left_part, data_index * own_rows, 0
        )
        first = sum_dp(jnp.concatenate([right_part, left_part]))
        first_right, first_left = first[:block], first[block:]
        second_left = matvec(left_columns, first_left / length_of(first_left), 0)
        second = sum_models(
            jnp.concatenate(
                [matvec(right_new, first_right, 0), jnp.sum(first_right * first_right)[None]]
            )
        )
        second_right = second[:panel] / jnp.sqrt(second[panel] + norm_floor)
        squares = sum_dp(
            jnp.stack([jnp.sum(second_left * second_left), jnp.sum(second_right * second_right)])
        )
        tops = jnp.sqrt(squares + norm_floor)
        top_left, top_right = tops[0], tops[1]
        scale = (top_left * top_right) ** (-0.25) / 16.0

        def left_mix(columns, which):
            row = lax.broadcasted_iota(jnp.int32, columns.shape, 0)
            col = lax.broadcasted_iota(jnp.int32, columns.shape, 1) + (
                (place * cores + which) * own_rows
            )
            return 5.0 * (row == col).astype(jnp.float32) - columns / top_left

        mixes = [left_mix(left_columns, core)] + [
            left_mix(to_core(left_columns, s), (core - s) % cores) for s in range(1, cores)
        ]

        def finish(j, whole):
            inner = (5.0 * own[j] - whole / top_right) * scale
            mine = product(mixes[0], inner, 0, 1)
            theirs = [
                to_core(product(mixes[s], inner, 0, 1), -s) for s in range(1, cores)
            ]
            return mine, theirs

        out = chain(mixed, place, finish)
        mine = jnp.concatenate([o[0] for o in out], axis=1)
        theirs = [jnp.concatenate([o[1][s] for o in out], axis=1) for s in range(cores - 1)]
        update = by_core(mine, theirs[::-1], 1)
        return left_new, right_new, update

    return shards


def solution(mesh):
    in_specs = (
        P("dp", None),
        P("dp", ("mp", "pre")),
        P(("mp", "pre"), "dp"),
        P(("mp", "pre"), "dp"),
        P(),
        P(),
    )
    out_specs = (P(("mp", "pre"), "dp"), P(("mp", "pre"), "dp"), P("dp", ("mp", "pre")))
    return jax.shard_map(
        make_step(mesh), mesh=mesh, in_specs=in_specs, out_specs=out_specs, check_vma=False
    )
```

```python
import jax
import jax.numpy as jnp
from jax import lax
from jax.sharding import Mesh, PartitionSpec as P

beta_decay = 0.9
norm_floor = 1e-06
chunk_count = 4

LINE, CORE, MP, PRE = "line", "core", "mp", "pre"
AXES = (LINE, CORE, MP, PRE)


def halves(x):
    high = lax.reduce_precision(x, 8, 7)
    return high.astype(jnp.bfloat16), (x - high).astype(jnp.bfloat16)


def product(a, b, a_dim, b_dim):
    def one(x, y):
        return lax.dot_general(
            x, y, (((a_dim,), (b_dim,)), ((), ())), preferred_element_type=jnp.float32
        )

    return one(a[0], b[0]) + (one(a[0], b[1]) + one(a[1], b[0]))


def rows_of(pair, start, count):
    return tuple(x[start : start + count] for x in pair)


def select_by(index, options):
    result = None
    for value, array in options.items():
        result = array if result is None else jnp.where(index == value, array, result)
    return result


def tie(*values):
    return lax.optimization_barrier(values)


def make_step(sizes):
    line, cores, mp, pre = (sizes[name] for name in AXES)
    models = mp * pre

    def along(array, axis, pairs):
        return lax.ppermute(array, axis, pairs)

    def swap(array, axis, bit):
        return along(array, axis, [(i, i ^ bit) for i in range(sizes[axis])])

    def total_over(array, axes):
        for axis in axes:
            bit = 1
            while bit < sizes[axis]:
                array = array + swap(array, axis, bit)
                bit *= 2
        return array

    def snake(array, outward):
        pairs = []
        for z in range(line):
            for c in range(cores):
                step = 1 if (c == 0) == outward else -1
                goal = z + step
                if 0 <= goal < line:
                    pairs.append((z * cores + c, goal * cores + c))
                else:
                    pairs.append((z * cores + c, z * cores + 1 - c))
        return along(array, (LINE, CORE), pairs)

    def shards(activations, grad_output, left_old, right_old, probe_left, probe_right):
        z, core = lax.axis_index(LINE), lax.axis_index(CORE)
        x, y = lax.axis_index(MP), lax.axis_index(PRE)
        model = x * pre + y
        width = activations.shape[1]
        block = grad_output.shape[1]
        hidden = block * models
        panel = block // cores
        own_rows = width // (line * cores)
        line_rows = own_rows * cores
        piece = panel // chunk_count
        owner_x, owner_y = z // pre, z % pre

        def to_partner(array):
            return swap(array, CORE, 1)

        def by_core(mine, theirs, axis):
            return jnp.where(
                core == 0,
                jnp.concatenate([mine, theirs], axis),
                jnp.concatenate([theirs, mine], axis),
            )

        def half_of(array, which, axis):
            return lax.dynamic_slice_in_dim(array, which * panel, panel, axis)

        def chain(summed, beside):
            steps = chunk_count + line - 2
            back = line - 1 - z
            first, last = z == 0, z == line - 1

            def mine(index):
                return lax.dynamic_slice_in_dim(summed, index * piece, piece, 0)

            sent_up, got_down = [], []
            below = above = None
            for t in range(steps + 1):
                going_up, going_down = mine(t - z), mine(t - back)
                if t:
                    going_up = going_up + jnp.where(first, 0.0, below)
                    going_down = going_down + jnp.where(last, 0.0, above)
                sent_up.append(going_up)
                j = t - (line - 1)
                whole = None
                if j >= 0:
                    whole = select_by(
                        z,
                        {
                            k: sent_up[j + k] + got_down[j + line - 2 - k]
                            if k < line - 1
                            else sent_up[j + k]
                            for k in range(line)
                        },
                    )
                if t < steps:
                    out = snake(jnp.where(core == 0, going_up, going_down), True)
                    home = snake(jnp.where(core == 0, going_down, going_up), False)
                    extra = beside(t, whole)
                    out, home, *extra = tie(out, home, *extra)
                    below = jnp.where(core == 0, out, home)
                    above = jnp.where(core == 0, home, out)
                    got_down.append(above)
                else:
                    beside(t, whole)

        def local(which):
            return lax.dot_general(
                half_of(grad_output, which, 1),
                activations,
                (((0,), (0,)), ((), ())),
                preferred_element_type=jnp.float32,
            )

        arrived = to_partner(local(1 - core))
        kept, arrived = tie(local(core), arrived)
        summed = kept + arrived

        own, wide, panel_t = [], [], []
        old_theirs = [None]

        def spread_pre(array):
            result = array
            for s in range(1, pre):
                got = along(array, PRE, [(i, (i + s) % pre) for i in range(pre)])
                result = jnp.where((y - s) % pre == owner_y, got, result)
            return result

        def spread_mp(array):
            result = array
            for s in range(1, mp):
                got = along(array, MP, [(i, (i + s) % mp) for i in range(mp)])
                result = jnp.where((x - s) % mp == owner_x, got, result)
            return result

        crossing = {}

        def beside_gradient(t, whole):
            waits = []
            j = t - (line - 1)
            if t == 1:
                old_theirs[0] = to_partner(half_of(right_old, 1 - core, 0))
                waits.append(old_theirs[0])
            if whole is not None:
                own.append(whole)
                crossing["pre", j] = spread_pre(whole)
                waits.append(crossing["pre", j])
            if 0 <= j - 1:
                crossing["mp", j - 1] = spread_mp(crossing["pre", j - 1])
                waits.append(crossing["mp", j - 1])
            if 0 <= j - 2:
                crossing["core", j - 2] = to_partner(crossing["mp", j - 2])
                waits.append(crossing["core", j - 2])
            return waits

        chain(summed, beside_gradient)
        last = chunk_count - 1
        if ("mp", last - 1) not in crossing:
            crossing["mp", last - 1] = spread_mp(crossing["pre", last - 1])
        crossing["mp", last] = spread_mp(crossing["pre", last])
        for j in range(chunk_count):
            if ("core", j) not in crossing:
                crossing["core", j] = to_partner(crossing["mp", j])
        grad_t = jnp.concatenate(own, axis=0)
        grad_pair = halves(grad_t)

        old_mine = half_of(right_old, core, 0)
        right_mine, right_theirs = [], []
        mixed = None
        for j in range(chunk_count):
            pair = halves(jnp.concatenate([crossing["mp", j], crossing["core", j]], axis=0))
            old = jnp.concatenate(
                [
                    old_mine[:, j * piece : (j + 1) * piece],
                    old_theirs[0][:, j * piece : (j + 1) * piece],
                ],
                axis=1,
            )
            right = beta_decay * old + product(grad_pair, pair, 1, 1) / width
            right_mine.append(right[:, :piece])
            right_theirs.append(right[:, piece:])
            term = product(halves(right), pair, 1, 0)
            mixed = term if mixed is None else mixed + term
        right_mine = jnp.concatenate(right_mine, axis=1)
        right_theirs = jnp.concatenate(right_theirs, axis=1)

        columns = lax.dynamic_slice_in_dim(grad_t, z * line_rows, line_rows, 1)
        left_part = product(grad_pair, halves(columns), 0, 0) / hidden
        at = (model * left_old.shape[0], core * own_rows)
        left_part = lax.dynamic_update_slice(
            left_part,
            lax.dynamic_slice(left_part, at, left_old.shape) + beta_decay * left_old,
            at,
        )
        left_columns = lax.psum(left_part, (CORE, MP, PRE))
        left_new = lax.dynamic_slice(left_columns, at, left_old.shape)

        wholes = {}

        def beside_mixed(t, whole):
            if whole is not None:
                wholes[t - (line - 1)] = whole
            if t == 0:
                crossing["right"] = to_partner(right_theirs)
                return [crossing["right"]]
            return []

        chain(mixed, beside_mixed)
        right_new = by_core(right_mine, crossing["right"], 0)

        def matvec(matrix, vector):
            return jnp.sum(matrix * vector[None, :], axis=1)

        def matvec_t(matrix, vector):
            return jnp.sum(matrix * vector[:, None], axis=0)

        def probe_panel(which):
            return lax.dynamic_slice_in_dim(probe_right, (z * cores + which) * panel, panel, 0)

        first_right = total_over(
            matvec(right_mine, probe_panel(core)) + matvec(right_theirs, probe_panel(1 - core)),
            (LINE,),
        )
        second_right = total_over(
            jnp.concatenate(
                [
                    by_core(
                        matvec_t(right_mine, first_right), matvec_t(right_theirs, first_right), 0
                    ),
                    jnp.sum(first_right * first_right)[None],
                ]
            ),
            (CORE, MP, PRE),
        )
        second_right = second_right[:block] / jnp.sqrt(second_right[block] + norm_floor)
        first_left = total_over(
            lax.dynamic_update_slice_in_dim(
                jnp.zeros((width,), jnp.float32),
                matvec_t(left_columns, probe_left),
                z * line_rows,
                0,
            ),
            (LINE,),
        )
        unit_left = first_left / jnp.sqrt(jnp.sum(first_left * first_left) + norm_floor)
        second_left = matvec_t(left_columns, unit_left)
        squares = total_over(
            jnp.stack([jnp.sum(second_left * second_left), jnp.sum(second_right * second_right)]),
            (LINE,),
        )
        tops = jnp.sqrt(squares + norm_floor)
        top_left, top_right = tops[0], tops[1]
        scale = (top_left * top_right) ** (-0.25) / 16.0

        row = lax.broadcasted_iota(jnp.int32, left_columns.shape, 0)
        col = lax.broadcasted_iota(jnp.int32, left_columns.shape, 1) + z * line_rows
        left_mix = 5.0 * (row == col).astype(jnp.float32) - left_columns / top_left
        mixed = jnp.concatenate([wholes[j] for j in range(chunk_count)], axis=0)
        inner = (5.0 * grad_t - mixed / top_right) * scale
        rows = product(halves(left_mix), halves(inner), 0, 1)
        mine = lax.dynamic_slice_in_dim(rows, core * own_rows, own_rows, 0)
        theirs = to_partner(
            lax.dynamic_slice_in_dim(rows, (1 - core) * own_rows, own_rows, 0)
        )
        return left_new, right_new, by_core(mine, theirs, 1)

    return shards


def solution(mesh):
    dp, mp, pre = (mesh.shape[name] for name in ("dp", "mp", "pre"))
    cores = dp // (mp * pre)
    assert cores == 2
    split = Mesh(mesh.devices.reshape(dp // cores, cores, mp, pre), AXES)
    factor = P((MP, PRE), (LINE, CORE))
    in_specs = (
        P((LINE, CORE), None),
        P((LINE, CORE), (MP, PRE)),
        factor,
        factor,
        P(),
        P(),
    )
    out_specs = (factor, factor, P((LINE, CORE), (MP, PRE)))
    return jax.shard_map(
        make_step(dict(split.shape)),
        mesh=split,
        in_specs=in_specs,
        out_specs=out_specs,
        check_vma=False,
    )
```

```python
import jax
import jax.numpy as jnp
from jax import lax
from jax.sharding import Mesh, PartitionSpec as P

beta_decay = 0.9
norm_floor = 1e-06
chunk_count = 4

LINE, CORE, MP, PRE = "line", "core", "mp", "pre"
AXES = (LINE, CORE, MP, PRE)


def halves(x):
    high = lax.reduce_precision(x, 8, 7)
    return high.astype(jnp.bfloat16), (x - high).astype(jnp.bfloat16)


def product(a, b, a_dim, b_dim):
    def one(x, y):
        return lax.dot_general(
            x, y, (((a_dim,), (b_dim,)), ((), ())), preferred_element_type=jnp.float32
        )

    return one(a[0], b[0]) + (one(a[0], b[1]) + one(a[1], b[0]))


def rows_of(pair, start, count):
    return tuple(x[start : start + count] for x in pair)


def select_by(index, options):
    result = None
    for value, array in options.items():
        result = array if result is None else jnp.where(index == value, array, result)
    return result


def tie(*values):
    return lax.optimization_barrier(values)


def make_step(sizes):
    line, cores, mp, pre = (sizes[name] for name in AXES)
    models = mp * pre

    def along(array, axis, pairs):
        return lax.ppermute(array, axis, pairs)

    def swap(array, axis, bit):
        return along(array, axis, [(i, i ^ bit) for i in range(sizes[axis])])

    def total_over(array, axes):
        for axis in axes:
            bit = 1
            while bit < sizes[axis]:
                array = array + swap(array, axis, bit)
                bit *= 2
        return array

    def snake(array, outward):
        pairs = []
        for z in range(line):
            for c in range(cores):
                step = 1 if (c == 0) == outward else -1
                goal = z + step
                if 0 <= goal < line:
                    pairs.append((z * cores + c, goal * cores + c))
                else:
                    pairs.append((z * cores + c, z * cores + 1 - c))
        return along(array, (LINE, CORE), pairs)

    def shards(activations, grad_output, left_old, right_old, probe_left, probe_right):
        z, core = lax.axis_index(LINE), lax.axis_index(CORE)
        x, y = lax.axis_index(MP), lax.axis_index(PRE)
        model = x * pre + y
        width = activations.shape[1]
        block = grad_output.shape[1]
        hidden = block * models
        panel = block // cores
        own_rows = width // (line * cores)
        line_rows = own_rows * cores
        piece = panel // chunk_count
        owner_x, owner_y = z // pre, z % pre

        def to_partner(array):
            return swap(array, CORE, 1)

        def by_core(mine, theirs, axis):
            return jnp.where(
                core == 0,
                jnp.concatenate([mine, theirs], axis),
                jnp.concatenate([theirs, mine], axis),
            )

        def half_of(array, which, axis):
            return lax.dynamic_slice_in_dim(array, which * panel, panel, axis)

        def chain(summed, beside):
            steps = chunk_count + line - 2
            there = jnp.where(core == 0, z, line - 1 - z)
            back = line - 1 - there

            def mine(index):
                return lax.dynamic_slice_in_dim(summed, index * piece, piece, 0)

            sent, got = [], []
            out = home = None
            for t in range(steps + 1):
                going_out = mine(t - there)
                if t:
                    going_out = going_out + jnp.where(there == 0, 0.0, out)
                sent.append(going_out)
                j = t - (line - 1)
                whole = None
                if j >= 0:
                    whole = select_by(
                        there,
                        {
                            k: sent[j + k] + got[j + line - 2 - k]
                            if k < line - 1
                            else sent[j + k]
                            for k in range(line)
                        },
                    )
                if t < steps:
                    going_home = mine(t - back)
                    if t:
                        going_home = going_home + jnp.where(back == 0, 0.0, home)
                    out, home = snake(going_out, True), snake(going_home, False)
                    extra = beside(t, whole)
                    out, home, *values = tie(out, home, *extra.values())
                    state.update(zip(extra, values))
                    got.append(home)
                else:
                    return whole

        def local(which):
            return lax.dot_general(
                half_of(grad_output, which, 1),
                activations,
                (((0,), (0,)), ((), ())),
                preferred_element_type=jnp.float32,
            )

        arrived = to_partner(local(1 - core))
        kept, arrived = tie(local(core), arrived)
        summed = kept + arrived

        state = {}

        def spread_pre(array):
            result = array
            for s in range(1, pre):
                got = along(array, PRE, [(i, (i + s) % pre) for i in range(pre)])
                result = jnp.where((y - s) % pre == owner_y, got, result)
            return result

        def spread_mp(array):
            result = array
            for s in range(1, mp):
                got = along(array, MP, [(i, (i + s) % mp) for i in range(mp)])
                result = jnp.where((x - s) % mp == owner_x, got, result)
            return result

        def first_way(array):
            half = array.shape[0] // 2
            return spread_pre(array[:half]), spread_mp(array[half:])

        def second_way(pair):
            return jnp.concatenate([spread_mp(pair[0]), spread_pre(pair[1])], axis=0)

        own = []

        def spread_steps(j):
            extra = {}
            if 0 <= j <= last:
                extra["a", j], extra["b", j] = first_way(own[j])
            if 0 <= j - 1 <= last:
                extra["panel", j - 1] = second_way((state["a", j - 1], state["b", j - 1]))
            if 0 <= j - 2 <= last:
                extra["across", j - 2] = to_partner(state["panel", j - 2])
            return extra

        def beside_gradient(t, whole):
            if whole is not None:
                own.append(whole)
            extra = spread_steps(t - (line - 1))
            if t == 1:
                extra["old"] = to_partner(half_of(right_old, 1 - core, 0))
            return extra

        last = chunk_count - 1
        own.append(chain(summed, beside_gradient))
        grad_t = jnp.concatenate(own, axis=0)

        old_mine = half_of(right_old, core, 0)

        def right_piece(j, grad_pair, panel_mine, panel_theirs, mixed):
            pair = halves(jnp.concatenate([panel_mine, panel_theirs], axis=0))
            old = jnp.concatenate(
                [
                    old_mine[:, j * piece : (j + 1) * piece],
                    state["old"][:, j * piece : (j + 1) * piece],
                ],
                axis=1,
            )
            right = beta_decay * old + product(grad_pair, pair, 1, 1) / width
            term = product(halves(right), pair, 1, 0)
            return right, term if mixed is None else mixed + term

        def keep(extra):
            state.update(zip(extra, tie(*extra.values())))

        extra = spread_steps(last)
        grad_pair = halves(grad_t)
        mixed, rights, done = None, [], 0
        for j in range(last + 1, last + 3):
            extra["pair", 0], extra["pair", 1] = grad_pair
            if mixed is not None:
                extra["mixed"] = mixed
            keep(extra)
            grad_pair = state["pair", 0], state["pair", 1]
            mixed = state.get("mixed")
            extra = spread_steps(j)
            if j == last + 1:
                left_part = product(
                    grad_pair,
                    [lax.dynamic_slice_in_dim(h, z * line_rows, line_rows, 1) for h in grad_pair],
                    0,
                    0,
                ) / hidden
                at = (model * left_old.shape[0], core * own_rows)
                left_part = lax.dynamic_update_slice(
                    left_part,
                    lax.dynamic_slice(left_part, at, left_old.shape) + beta_decay * left_old,
                    at,
                )
                extra["left"] = left_part
            while ("across", done) in state:
                right, mixed = right_piece(
                    done, grad_pair, state["panel", done], state["across", done], mixed
                )
                rights.append(right)
                done += 1
        extra["mixed"] = mixed
        keep(extra)
        mixed = state["mixed"]
        for j in range(done, last + 1):
            right, mixed = right_piece(
                j, grad_pair, state["panel", j], state["across", j], mixed
            )
            rights.append(right)
        right_mine = jnp.concatenate([r[:, :piece] for r in rights], axis=1)
        right_theirs = jnp.concatenate([r[:, piece:] for r in rights], axis=1)

        def matvec(matrix, vector):
            return jnp.sum(matrix * vector[None, :], axis=1)

        def matvec_t(matrix, vector):
            return jnp.sum(matrix * vector[:, None], axis=0)

        def probe_panel(which):
            return lax.dynamic_slice_in_dim(probe_right, (z * cores + which) * panel, panel, 0)

        wholes = []

        def left_times(left_pair, array):
            return product(halves(array), left_pair, 1, 0)

        def beside_mixed(t, whole):
            extra = {}
            if whole is not None:
                wholes.append(whole)
            if t < 2:
                left = state["left"]
                half = width // 2
                ways = ((MP,), (PRE,)) if t == 0 else ((PRE,), (MP,))
                extra["left"] = jnp.concatenate(
                    [total_over(left[:half], ways[0]), total_over(left[half:], ways[1])], axis=0
                )
            if t == 2:
                extra["left"] = total_over(state["left"], (CORE,))
            if t == 0:
                extra["right"] = to_partner(right_theirs)
                extra["first"] = total_over(
                    matvec(right_mine, probe_panel(core))
                    + matvec(right_theirs, probe_panel(1 - core)),
                    (LINE,),
                )
            if t == 1:
                first = state["first"]
                extra["right_new"] = by_core(right_mine, state["right"], 0)
                extra["second"] = total_over(
                    jnp.concatenate(
                        [
                            by_core(
                                matvec_t(right_mine, first), matvec_t(right_theirs, first), 0
                            ),
                            jnp.sum(first * first)[None],
                        ]
                    ),
                    (CORE, MP),
                )
            if t == 2:
                extra["second"] = total_over(state["second"], (PRE,))
            if t == steps - 2:
                left = state["left"]
                extra["first_left"] = total_over(
                    lax.dynamic_update_slice_in_dim(
                        jnp.zeros((width,), jnp.float32),
                        matvec_t(left, probe_left),
                        z * line_rows,
                        0,
                    ),
                    (LINE,),
                )
                pair = halves(left)
                extra["pair", 0], extra["pair", 1] = pair
                extra["left_grad"] = left_times(pair, grad_t)
            if t == steps - 1:
                first = state["first_left"]
                second_left = matvec_t(
                    state["left"], first / jnp.sqrt(jnp.sum(first * first) + norm_floor)
                )
                second = state["second"]
                second_right = second[:block] / jnp.sqrt(second[block] + norm_floor)
                extra["squares"] = total_over(
                    jnp.stack(
                        [
                            jnp.sum(second_left * second_left),
                            jnp.sum(second_right * second_right),
                        ]
                    ),
                    (LINE,),
                )
            return extra

        steps = chunk_count + line - 2
        wholes.append(chain(mixed, beside_mixed))
        tops = jnp.sqrt(state["squares"] + norm_floor)
        top_left, top_right = tops[0], tops[1]
        scale = (top_left * top_right) ** (-0.25) / 16.0
        pair = state["pair", 0], state["pair", 1]

        def line_columns(array):
            return lax.dynamic_slice_in_dim(array, z * line_rows, line_rows, 1)

        finished = []
        for j, whole in enumerate(wholes):
            span = slice(j * piece, (j + 1) * piece)
            finished.append(
                (
                    25.0 * line_columns(own[j])
                    - state["left_grad"][span] * (5.0 / top_left)
                    - (5.0 * line_columns(whole) - left_times(pair, whole) / top_left)
                    / top_right
                )
                * scale
            )
        finished = jnp.concatenate(finished, axis=0)
        mine = lax.dynamic_slice_in_dim(finished, core * own_rows, own_rows, 1)
        theirs = to_partner(
            lax.dynamic_slice_in_dim(finished, (1 - core) * own_rows, own_rows, 1)
        )
        update = by_core(mine, theirs, 0).T
        left_new = lax.dynamic_slice(state["left"], at, left_old.shape)
        return left_new, state["right_new"], update

    return shards


def solution(mesh):
    dp, mp, pre = (mesh.shape[name] for name in ("dp", "mp", "pre"))
    cores = dp // (mp * pre)
    assert cores == 2
    split = Mesh(mesh.devices.reshape(dp // cores, cores, mp, pre), AXES)
    factor = P((MP, PRE), (LINE, CORE))
    in_specs = (
        P((LINE, CORE), None),
        P((LINE, CORE), (MP, PRE)),
        factor,
        factor,
        P(),
        P(),
    )
    out_specs = (factor, factor, P((LINE, CORE), (MP, PRE)))
    return jax.shard_map(
        make_step(dict(split.shape)),
        mesh=split,
        in_specs=in_specs,
        out_specs=out_specs,
        check_vma=False,
    )
```

```python
import jax
import jax.numpy as jnp
from jax import lax
from jax.sharding import Mesh, PartitionSpec as P

beta_decay = 0.9
norm_floor = 1e-06
chunk_count = 8
lag = 2

LINE, CORE, MP, PRE = "line", "core", "mp", "pre"
AXES = (LINE, CORE, MP, PRE)


def halves(x):
    high = lax.reduce_precision(x, 8, 7)
    return high.astype(jnp.bfloat16), (x - high).astype(jnp.bfloat16)


def product(a, b, a_dim, b_dim):
    def one(x, y):
        return lax.dot_general(
            x, y, (((a_dim,), (b_dim,)), ((), ())), preferred_element_type=jnp.float32
        )

    return one(a[0], b[0]) + (one(a[0], b[1]) + one(a[1], b[0]))


def select_by(index, options):
    result = None
    for value, array in options.items():
        result = array if result is None else jnp.where(index == value, array, result)
    return result


def tie(values):
    return lax.optimization_barrier(tuple(values))


class Windows:
    def __init__(self):
        self.now = 0
        self.processes = []

    def add(self, process):
        self.processes.append([process, None, None])

    def open(self):
        for entry in list(self.processes):
            process, due, values = entry
            if due is not None and due >= self.now:
                continue
            try:
                count, entry[2] = process.send(values)
                entry[1] = self.now + count - 1
            except StopIteration:
                self.processes.remove(entry)

    def close(self, *others):
        due = [entry for entry in self.processes if entry[1] == self.now and entry[2]]
        flat = list(others)
        for entry in due:
            flat.extend(entry[2])
        if flat:
            flat = list(tie(flat))
        at = len(others)
        for entry in due:
            count = len(entry[2])
            entry[2] = flat[at : at + count]
            at += count
        self.now += 1
        return flat[: len(others)]


def make_step(sizes):
    line, cores, mp, pre = (sizes[name] for name in AXES)
    models = mp * pre
    count = chunk_count
    last = count - 1

    def swap(array, axis, bit):
        return lax.ppermute(array, axis, [(i, i ^ bit) for i in range(sizes[axis])])

    def total_over(array, axes):
        for axis in axes:
            bit = 1
            while bit < sizes[axis]:
                (array,) = yield 1, (array + swap(array, axis, bit),)
                bit *= 2
        return array

    def snake(array, outward):
        pairs = []
        for z in range(line):
            for c in range(cores):
                goal = z + (1 if (c == 0) == outward else -1)
                if 0 <= goal < line:
                    pairs.append((z * cores + c, goal * cores + c))
                else:
                    pairs.append((z * cores + c, z * cores + 1 - c))
        return lax.ppermute(array, (LINE, CORE), pairs)

    def shards(activations, grad_output, left_old, right_old, probe_left, probe_right):
        z, core = lax.axis_index(LINE), lax.axis_index(CORE)
        x, y = lax.axis_index(MP), lax.axis_index(PRE)
        model = x * pre + y
        width = activations.shape[1]
        block = grad_output.shape[1]
        hidden = block * models
        panel = block // cores
        own_rows = width // (line * cores)
        line_rows = own_rows * cores
        piece = panel // count
        owner_x, owner_y = z // pre, z % pre
        windows = Windows()
        state = {}

        def to_partner(array):
            return swap(array, CORE, 1)

        def pick(which, first, second):
            return jnp.where(which == 0, first, second)

        def by_core(mine, theirs, axis):
            return pick(
                core,
                jnp.concatenate([mine, theirs], axis),
                jnp.concatenate([theirs, mine], axis),
            )

        def line_columns(array):
            return select_by(
                z, {k: array[:, k * line_rows : (k + 1) * line_rows] for k in range(line)}
            )

        there = jnp.where(core == 0, z, line - 1 - z)
        back = line - 1 - there

        def chain(mine, wholes):
            final = count - 1 + lag * (line - 1)
            sent, out, home = [], [], []
            for t in range(final + 1):
                sending = t <= final - lag
                if sending:
                    going_out, going_home = mine(t - lag * there), mine(t - lag * back)
                    if t >= lag:
                        going_out = going_out + jnp.where(there == 0, 0.0, out[t - lag])
                        going_home = going_home + jnp.where(back == 0, 0.0, home[t - lag])
                    out.append(snake(going_out, True))
                    home.append(snake(going_home, False))
                else:
                    going_out = mine(t - lag * there) + jnp.where(there == 0, 0.0, out[t - lag])
                sent.append(going_out)
                j = t - lag * (line - 1)
                if j >= 0:
                    wholes.append(
                        select_by(
                            there,
                            {
                                k: sent[j + lag * k] + home[j + lag * (line - 2 - k)]
                                if k < line - 1
                                else sent[j + lag * k]
                                for k in range(line)
                            },
                        )
                    )
                if t == final:
                    return
                windows.open()
                due = t - lag + 1
                if 0 <= due < len(out):
                    out[due], home[due] = windows.close(out[due], home[due])
                else:
                    windows.close()

        def half_of(array, which, axis):
            return lax.dynamic_slice_in_dim(array, which * panel, panel, axis)

        def local(which):
            return lax.dot_general(
                half_of(grad_output, which, 1),
                activations,
                (((0,), (0,)), ((), ())),
                preferred_element_type=jnp.float32,
            )

        arrived = to_partner(local(1 - core))
        kept, arrived = tie((local(core), arrived))

        def rows_at(array, index):
            return lax.dynamic_slice_in_dim(array, index * piece, piece, 0)

        def spread_pre(array):
            result = array
            for s in range(1, pre):
                got = lax.ppermute(array, PRE, [(i, (i + s) % pre) for i in range(pre)])
                result = jnp.where((y - s) % pre == owner_y, got, result)
            return result

        def spread_mp(array):
            result = array
            for s in range(1, mp):
                got = lax.ppermute(array, MP, [(i, (i + s) % mp) for i in range(mp)])
                result = jnp.where((x - s) % mp == owner_x, got, result)
            return result

        own = []
        chain_end = count - 1 + lag * (line - 1)

        def hold():
            return 2 if windows.now < chain_end else 1

        def set_out(group):
            while len(own) <= group[-1]:
                yield 1, ()
            array = jnp.concatenate([own[j] for j in group], axis=0)
            half = array.shape[0] // 2
            state["way", group] = yield hold(), (
                spread_pre(array[:half]),
                spread_mp(array[half:]),
            )

        def arrive(unit, groups):
            while any(("way", group) not in state for group in groups):
                yield 1, ()
            a, b = zip(*(state["way", group] for group in groups))
            mine = jnp.concatenate(
                [
                    spread_mp(jnp.concatenate(a, axis=0)),
                    spread_pre(jnp.concatenate(b, axis=0)),
                ],
                axis=0,
            )
            (mine,) = yield hold(), (mine,)
            (theirs,) = yield 1, (to_partner(mine),)
            state["unit", unit] = jnp.concatenate([mine, theirs], axis=0)

        units = [(j, j + 1) for j in range(0, count, 2)]

        def unit_rows(array, unit):
            if unit < len(units) - 1:
                return array[2 * unit * piece : 2 * (unit + 1) * piece]
            parts = [array[j * piece : (j + 1) * piece] for j in units[unit]]
            half = piece // 2
            return jnp.concatenate([p[:half] for p in parts] + [p[half:] for p in parts], axis=0)

        def unit_columns(array, unit):
            if unit < len(units) - 1:
                return array[:, 2 * unit * piece : 2 * (unit + 1) * piece]
            parts = [array[:, j * piece : (j + 1) * piece] for j in units[unit]]
            half = piece // 2
            return jnp.concatenate(
                [p[:, :half] for p in parts] + [p[:, half:] for p in parts], axis=1
            )

        def old_right():
            (theirs,) = yield 2, (to_partner(half_of(right_old, 1 - core, 0)),)
            mine = half_of(right_old, core, 0)
            state["old"] = yield 1, [
                beta_decay
                * jnp.concatenate([unit_columns(mine, u), unit_columns(theirs, u)], axis=1)
                for u in range(len(units))
            ]

        for u, group in enumerate(units):
            if u < len(units) - 1:
                groups = [group]
            else:
                groups = [(j,) for j in group]
            for g in groups:
                windows.add(set_out(g))
            windows.add(arrive(u, groups))
        windows.add(old_right())

        rights = []

        def right_factor():
            while "pair" not in state:
                yield 1, ()
            mixed = None
            for u in range(len(units)):
                while ("unit", u) not in state:
                    yield 1, ()
                pair = halves(state["unit", u])
                right = state["old"][u] + product(state["pair"], pair, 1, 1) / width
                term = product(halves(right), pair, 1, 0)
                mixed = term if mixed is None else mixed + term
                if u < len(units) - 1:
                    right, mixed = yield 1, (right, mixed)
                rights.append(right)
            state["mixed"] = mixed

        at = (model * left_old.shape[0], core * own_rows)

        def left_factor():
            while "pair" not in state:
                yield 1, ()
            pair = state["pair"]
            part = product(pair, [line_columns(h) for h in pair], 0, 0) / hidden
            row = lax.broadcasted_iota(jnp.int32, part.shape, 0) // left_old.shape[0]
            old = jnp.tile(left_old, (models, cores))
            col = lax.broadcasted_iota(jnp.int32, part.shape, 1) // own_rows
            part = part + jnp.where((row == model) & (col == core), beta_decay * old, 0.0)
            (part,) = yield 1, (part,)
            while ("way", units[-1][-1:]) not in state or ("unit", len(units) - 2) not in state:
                yield 1, ()
            for ways in ((MP, PRE), (PRE, MP)):
                parts = []
                for h, axis in enumerate(ways):
                    half = part[h * width // 2 : (h + 1) * width // 2]
                    bit = 1
                    while bit < sizes[axis]:
                        half = half + swap(half, axis, bit)
                        bit *= 2
                    parts.append(half)
                (part,) = yield 3, (jnp.concatenate(parts, axis=0),)
            (part,) = yield 2, (part + to_partner(part),)
            state["left"] = part
            rows = lax.dynamic_slice_in_dim(part, at[0], left_old.shape[0], 0)
            (state["left_new"],) = yield 1, (
                pick(core, rows[:, :own_rows], rows[:, own_rows:]),
            )

        windows.add(right_factor())
        windows.add(left_factor())
        chain(lambda i: rows_at(kept, i) + rows_at(arrived, i), own)
        grad_t = jnp.concatenate(own, axis=0)
        state["pair"] = halves(grad_t)
        while "mixed" not in state:
            windows.open()
            if "mixed" not in state:
                windows.close()
        mixed = state["mixed"]

        def matvec(matrix, vector):
            return jnp.sum(matrix * vector[None, :], axis=1)

        def matvec_t(matrix, vector):
            return jnp.sum(matrix * vector[:, None], axis=0)

        def probe_panel(which):
            return lax.dynamic_slice_in_dim(probe_right, (z * cores + which) * panel, panel, 0)

        unit_width = 2 * piece
        half_piece = piece // 2

        def in_order(array):
            quarters = [array[:, i * half_piece : (i + 1) * half_piece] for i in range(4)]
            return [quarters[i] for i in (0, 2, 1, 3)]

        right_mine = jnp.concatenate(
            [r[:, :unit_width] for r in rights[:-1]] + in_order(rights[-1][:, :unit_width]),
            axis=1,
        )
        right_theirs = jnp.concatenate(
            [r[:, unit_width:] for r in rights[:-1]] + in_order(rights[-1][:, unit_width:]),
            axis=1,
        )

        def right_out():
            (theirs,) = yield 2, (to_partner(right_theirs),)
            (state["right_new"],) = yield 1, (by_core(right_mine, theirs, 0),)

        def right_power():
            first = matvec(right_mine, probe_panel(core)) + matvec(
                right_theirs, probe_panel(1 - core)
            )
            first = yield from total_over(first, (LINE,))
            second = jnp.concatenate(
                [
                    by_core(matvec_t(right_mine, first), matvec_t(right_theirs, first), 0),
                    jnp.sum(first * first)[None],
                ]
            )
            second = yield from total_over(second, (CORE, MP, PRE))
            state["second_right"] = second[:block] / jnp.sqrt(second[block] + norm_floor)

        def left_power():
            while "left" not in state:
                yield 1, ()
            left = state["left"]
            first = matvec_t(left, probe_left)
            spot = lax.broadcasted_iota(jnp.int32, (width,), 0) // line_rows
            first = yield from total_over(
                jnp.where(spot == z, jnp.tile(first, line), 0.0), (LINE,)
            )
            second_left = matvec_t(
                left, first / jnp.sqrt(jnp.sum(first * first) + norm_floor)
            )
            while "second_right" not in state:
                yield 1, ()
            second_right = state["second_right"]
            squares = jnp.stack(
                [jnp.sum(second_left * second_left), jnp.sum(second_right * second_right)]
            )
            squares = yield from total_over(squares, (LINE,))
            tops = jnp.sqrt(squares + norm_floor)
            top_left, top_right = tops[0], tops[1]
            scale = (top_left * top_right) ** (-0.25) / 16.0
            row = lax.broadcasted_iota(jnp.int32, left.shape, 0)
            col = lax.broadcasted_iota(jnp.int32, left.shape, 1) + z * line_rows
            mix = (5.0 * (row == col).astype(jnp.float32) - left / top_left) * scale
            state["mix"] = yield 1, halves(mix)
            state["top_right"] = top_right

        wholes = []

        def finish(first, end):
            inner = 5.0 * grad_t[first * piece : end * piece] - (
                jnp.concatenate(wholes[first:end], axis=0) / state["top_right"]
            )
            rows = product(state["mix"], halves(inner), 0, 1)
            upper, lower = rows[:own_rows], rows[own_rows:]
            return pick(core, upper, lower), to_partner(pick(core, lower, upper))

        def early():
            while "mix" not in state or len(wholes) < count - 2:
                yield 1, ()
            state["early"] = yield 1, finish(0, count - 2)

        windows.add(right_out())
        windows.add(right_power())
        windows.add(left_power())
        windows.add(early())
        chain(lambda i: rows_at(mixed, i), wholes)
        while windows.processes:
            windows.open()
            if windows.processes:
                windows.close()
        mine, theirs = (
            jnp.concatenate(parts, axis=1)
            for parts in zip(state["early"], finish(count - 2, count))
        )
        return state["left_new"], state["right_new"], by_core(mine, theirs, 1)

    return shards


def solution(mesh):
    dp, mp, pre = (mesh.shape[name] for name in ("dp", "mp", "pre"))
    cores = dp // (mp * pre)
    assert cores == 2
    split = Mesh(mesh.devices.reshape(dp // cores, cores, mp, pre), AXES)
    factor = P((MP, PRE), (LINE, CORE))
    in_specs = (
        P((LINE, CORE), None),
        P((LINE, CORE), (MP, PRE)),
        factor,
        factor,
        P(),
        P(),
    )
    out_specs = (factor, factor, P((LINE, CORE), (MP, PRE)))
    return jax.shard_map(
        make_step(dict(split.shape)),
        mesh=split,
        in_specs=in_specs,
        out_specs=out_specs,
        check_vma=False,
    )
```

```python
import jax
import jax.numpy as jnp
from jax import lax
from jax.sharding import Mesh, PartitionSpec as P

beta_decay = 0.9
norm_floor = 1e-06
chunk_count = 4

LINE, CORE, MP, PRE = "line", "core", "mp", "pre"
AXES = (LINE, CORE, MP, PRE)


def halves(x):
    high = lax.reduce_precision(x, 8, 7)
    return high.astype(jnp.bfloat16), (x - high).astype(jnp.bfloat16)


def product(a, b, a_dim, b_dim):
    def one(x, y):
        return lax.dot_general(
            x, y, (((a_dim,), (b_dim,)), ((), ())), preferred_element_type=jnp.float32
        )

    return one(a[0], b[0]) + (one(a[0], b[1]) + one(a[1], b[0]))


def select_by(index, options):
    result = None
    for value, array in options.items():
        result = array if result is None else jnp.where(index == value, array, result)
    return result


def tie(values):
    return lax.optimization_barrier(tuple(values))


class Windows:
    def __init__(self):
        self.now = 0
        self.processes = []

    def add(self, process):
        self.processes.append([process, None, None])

    def open(self):
        for entry in list(self.processes):
            process, due, values = entry
            if values and due >= self.now:
                continue
            try:
                count, entry[2] = process.send(values)
                entry[1] = self.now + count - 1
            except StopIteration:
                self.processes.remove(entry)

    def close(self, *others):
        due = [entry for entry in self.processes if entry[1] == self.now and entry[2]]
        flat = list(others)
        for entry in due:
            flat.extend(entry[2])
        if flat:
            flat = list(tie(flat))
        at = len(others)
        for entry in due:
            count = len(entry[2])
            entry[2] = flat[at : at + count]
            at += count
        self.now += 1
        return flat[: len(others)]


def make_step(sizes):
    line, cores, mp, pre = (sizes[name] for name in AXES)
    models = mp * pre
    count = chunk_count
    last = count - 1

    def swap(array, axis, bit):
        return lax.ppermute(array, axis, [(i, i ^ bit) for i in range(sizes[axis])])

    def total_over(array, axis):
        bit = 1
        while bit < sizes[axis]:
            array = array + swap(array, axis, bit)
            bit *= 2
        return array

    def total_line(array):
        total = array
        for s in range(1, line):
            total = total + lax.ppermute(array, LINE, [(i, (i + s) % line) for i in range(line)])
        return total

    def snake(array, outward):
        pairs = []
        for z in range(line):
            for c in range(cores):
                goal = z + (1 if (c == 0) == outward else -1)
                if 0 <= goal < line:
                    pairs.append((z * cores + c, goal * cores + c))
                else:
                    pairs.append((z * cores + c, z * cores + 1 - c))
        return lax.ppermute(array, (LINE, CORE), pairs)

    def shards(activations, grad_output, left_old, right_old, probe_left, probe_right):
        z, core = lax.axis_index(LINE), lax.axis_index(CORE)
        x, y = lax.axis_index(MP), lax.axis_index(PRE)
        model = x * pre + y
        width = activations.shape[1]
        block = grad_output.shape[1]
        hidden = block * models
        panel = block // cores
        own_rows = width // (line * cores)
        line_rows = own_rows * cores
        piece = width // count
        owner_x, owner_y = z // pre, z % pre
        windows = Windows()
        state = {}

        def to_partner(array):
            return swap(array, CORE, 1)

        def pick(which, first, second):
            return jnp.where(which == 0, first, second)

        def by_core(mine, theirs, axis):
            return pick(
                core,
                jnp.concatenate([mine, theirs], axis),
                jnp.concatenate([theirs, mine], axis),
            )

        def line_part(array):
            return lax.dynamic_slice_in_dim(array, z * line_rows, line_rows, 0)

        def line_part_of(pieces):
            options = {}
            for k in range(line):
                j, start = divmod(k * line_rows, piece)
                options[k] = pieces[j][start : start + line_rows]
            return select_by(z, options)

        there = jnp.where(core == 0, z, line - 1 - z)
        back = line - 1 - there

        def chain(mine, wholes, early):
            final = count - 1 + line - 1
            sent, out, home = [], [], []
            for t in range(final + 1):
                if early:
                    windows.open()
                going_out = mine(t, there)
                if t:
                    going_out = going_out + jnp.where(there == 0, 0.0, out[-1])
                sent.append(going_out)
                if t < final:
                    going_home = mine(t, back)
                    if t:
                        going_home = going_home + jnp.where(back == 0, 0.0, home[-1])
                    out.append(snake(going_out, True))
                    home.append(snake(going_home, False))
                j = t - (line - 1)
                if j >= 0:
                    wholes.append(
                        select_by(
                            there,
                            {
                                k: sent[j + k] + home[j + line - 2 - k]
                                if k < line - 1
                                else sent[j + k]
                                for k in range(line)
                            },
                        )
                    )
                if t < final:
                    windows.open()
                    out[-1], home[-1] = windows.close(out[-1], home[-1])

        def local(which):
            return lax.dot_general(
                activations,
                lax.dynamic_slice_in_dim(grad_output, which * panel, panel, 1),
                (((0,), (0,)), ((), ())),
                preferred_element_type=jnp.float32,
            )

        arrived = to_partner(local(1 - core))
        kept, arrived = tie((local(core), arrived))

        def rows_at(array, index):
            return lax.dynamic_slice_in_dim(array, index * piece, piece, 0)

        def matvec(matrix, vector):
            return jnp.sum(matrix * vector[None, :], axis=1)

        def matvec_t(matrix, vector):
            return jnp.sum(matrix * vector[:, None], axis=0)

        own = []

        def old_right():
            def half_of(which):
                return lax.dynamic_slice_in_dim(right_old, which * panel, panel, 0)

            (theirs,) = yield 2, (to_partner(half_of(1 - core)),)
            old = beta_decay * jnp.concatenate([half_of(core), theirs], axis=1)

            def probe_panel(which):
                return lax.dynamic_slice_in_dim(
                    probe_right, (z * cores + which) * panel, panel, 0
                )

            vector = jnp.concatenate([probe_panel(core), probe_panel(1 - core)])
            pair = halves(old)
            image = matvec(old, vector)
            old, image, *pair = yield 1, (old, image, *pair)
            state["old"], state["old_pair"] = old, pair
            (state["old_image"],) = yield 2, (total_line(image),)

        def spread(array, axis, place, owner):
            result = array
            size = sizes[axis]
            for s in range(1, size):
                got = lax.ppermute(array, axis, [(i, (i + s) % size) for i in range(size)])
                result = jnp.where((place - s) % size == owner, got, result)
            return result

        def panel_piece(j):
            while len(own) <= j:
                yield 1, ()
            (mine,) = yield 1, (spread(own[j], PRE, y, owner_y),)
            (mine,) = yield 1, (spread(mine, MP, x, owner_x),)
            (theirs,) = yield 1, (to_partner(mine),)
            pair = halves(jnp.concatenate([mine, theirs], axis=1))
            state["mixed", j] = product(pair, state["old_pair"], 1, 1)
            state["panel", j] = pair
            state["panel_full", j] = (mine, theirs)

        def over_models(array, first):
            half = array.shape[0] // 2
            ways = (MP, PRE) if first else (PRE, MP)
            return jnp.concatenate(
                [total_over(array[:half], ways[0]), total_over(array[half:], ways[1])], axis=0
            )

        def over_hidden(array):
            half = array.shape[0] // 2
            upper, lower = array[:half], array[half:]
            kept_half, sent_half = pick(core, upper, lower), pick(core, lower, upper)
            (part,) = yield 1, (kept_half + to_partner(sent_half),)
            (part,) = yield 1, (over_models(part, True),)
            (part,) = yield 1, (by_core_late(over_models(part, False)),)
            return part

        def by_core_late(part):
            return by_core(part, to_partner(part), 0)

        at = (model * left_old.shape[0], core * own_rows)

        def left_old_columns():
            shape = (width, line_rows)
            row = lax.broadcasted_iota(jnp.int32, shape, 0) // left_old.shape[0]
            col = lax.broadcasted_iota(jnp.int32, shape, 1) // own_rows
            old = jnp.tile(left_old, (models, cores))
            placed = jnp.where((row == model) & (col == core), beta_decay * old, 0.0)
            state["left_old"] = yield from over_hidden(placed)

        windows.add(old_right())
        for j in range(count):
            windows.add(panel_piece(j))
        windows.add(left_old_columns())
        chain(lambda t, place: rows_at(kept, t - place) + rows_at(arrived, t - place), own, False)
        grad = jnp.concatenate(own, axis=0)
        grad_pair = halves(grad)

        mixed_wholes = []

        def left_side():
            part = product(grad_pair, [line_part(h) for h in grad_pair], 1, 1) / hidden
            gram = yield from over_hidden(part)
            left = state["left_old"] + gram
            pair = halves(left)
            state["left_pair"] = pair
            state["left_grad"] = product(pair, grad_pair, 0, 0)
            first = matvec_t(left, probe_left)
            spot = lax.broadcasted_iota(jnp.int32, (width,), 0) // line_rows
            first = jnp.where(spot == z, jnp.tile(first, line), 0.0)
            own_left = lax.dynamic_slice_in_dim(left, at[0], left_old.shape[0], 0)
            own_left = pick(core, own_left[:, :own_rows], own_left[:, own_rows:])
            state["left"] = left
            state["first_left"], state["left_new"] = yield 1, (total_line(first), own_left)
            (state["gram_grad"],) = yield 1, (
                product(halves(gram), grad_pair, 0, 0) * (hidden / width),
            )

        def crossed():
            while "left_grad" not in state:
                yield 1, ()
            part = product(halves(state["left_grad"]), grad_pair, 1, 1) / width
            total = yield from over_hidden(part)
            total_pair = halves(total)
            (state["crossed"],) = yield 1, (product(total_pair, grad_pair, 1, 0),)

        own_probe = lax.dynamic_slice_in_dim(probe_right, (model * cores + core) * panel, panel, 0)

        def right_power():
            vector = matvec(grad, own_probe)
            (vector,) = yield 1, (total_over(total_over(vector, CORE), MP),)
            (vector,) = yield 1, (total_over(vector, PRE),)
            image = state["old_image"] + matvec_t(grad, vector) / width
            back_image = matvec_t(state["old"], image)
            joined = jnp.concatenate(
                [
                    matvec(grad, image),
                    by_core(back_image[:panel], back_image[panel:], 0),
                    jnp.sum(image * image)[None],
                ]
            )
            (joined,) = yield 1, (total_over(total_over(joined, CORE), MP),)
            (joined,) = yield 1, (total_over(joined, PRE),)
            while ("panel_full", last) not in state:
                yield 1, ()
            mine, theirs = (
                jnp.concatenate([state["panel_full", j][i] for j in range(count)], axis=0)
                for i in range(2)
            )
            vector = joined[:width]
            second = joined[width : width + block] + (
                by_core(matvec_t(mine, vector), matvec_t(theirs, vector), 0) / width
            )
            state["second_right"] = second / jnp.sqrt(joined[width + block] + norm_floor)

        def tops():
            while "first_left" not in state or "second_right" not in state:
                yield 1, ()
            first, second_right = state["first_left"], state["second_right"]
            unit = first / jnp.sqrt(jnp.sum(first * first) + norm_floor)
            second_left = matvec_t(state["left"], unit)
            squares = jnp.stack(
                [jnp.sum(second_left * second_left), jnp.sum(second_right * second_right)]
            )
            (squares,) = yield 1, (total_line(squares),)
            state["tops"] = jnp.sqrt(squares + norm_floor)

        def right_factor():
            while ("panel", last) not in state:
                yield 1, ()
            panels = [
                jnp.concatenate([state["panel", j][i] for j in range(count)], axis=0)
                for i in range(2)
            ]
            right = state["old"] + product(grad_pair, panels, 0, 0) / width
            (right,) = yield 1, (right,)
            (theirs,) = yield 1, (to_partner(right[:, panel:]),)
            (state["right_new"],) = yield 1, (by_core(right[:, :panel], theirs, 0),)

        def left_times(first, end):
            pair = [h[first * piece : end * piece] for h in state["left_pair"]]
            array = jnp.concatenate(mixed_wholes[first:end], axis=0)
            return product(pair, halves(array), 0, 0)

        def early():
            while "left_pair" not in state or len(mixed_wholes) < last:
                yield 1, ()
            (state["early"],) = yield 1, (left_times(0, last),)

        for process in (left_side, right_power, crossed, right_factor, tops, early):
            windows.add(process())

        def mixed_piece(t, place):
            return select_by(
                place,
                {k: state["mixed", min(max(t - k, 0), last)] for k in range(line) if k <= t},
            )

        chain(mixed_piece, mixed_wholes, True)
        while windows.processes:
            windows.open()
            if windows.processes:
                windows.close()
        top_left, top_right = state["tops"][0], state["tops"][1]
        scale = (top_left * top_right) ** (-0.25) / 16.0
        rows = state["early"] + left_times(last, count) + state["crossed"]
        mixed = line_part_of(mixed_wholes) + state["gram_grad"]
        rows = (
            25.0 * line_part_of(own)
            - state["left_grad"] * (5.0 / top_left)
            - (5.0 * mixed - rows / top_left) / top_right
        ) * scale
        upper, lower = rows[:own_rows], rows[own_rows:]
        mine, theirs = pick(core, upper, lower), to_partner(pick(core, lower, upper))
        return state["left_new"], state["right_new"], by_core(mine, theirs, 1)

    return shards


def solution(mesh):
    dp, mp, pre = (mesh.shape[name] for name in ("dp", "mp", "pre"))
    cores = dp // (mp * pre)
    assert cores == 2
    split = Mesh(mesh.devices.reshape(dp // cores, cores, mp, pre), AXES)
    factor = P((MP, PRE), (LINE, CORE))
    in_specs = (
        P((LINE, CORE), None),
        P((LINE, CORE), (MP, PRE)),
        factor,
        factor,
        P(),
        P(),
    )
    out_specs = (factor, factor, P((LINE, CORE), (MP, PRE)))
    return jax.shard_map(
        make_step(dict(split.shape)),
        mesh=split,
        in_specs=in_specs,
        out_specs=out_specs,
        check_vma=False,
    )
```

```python
import jax
import jax.numpy as jnp
from jax import lax
from jax.experimental import pallas as pl
from jax.experimental.pallas import tpu as pltpu
from jax.sharding import Mesh, PartitionSpec as P

beta_decay = 0.9
norm_floor = 1e-06
count = 4

LINE, CORE, MP, PRE = "line", "core", "mp", "pre"
AXES = (LINE, CORE, MP, PRE)
f32, bf16 = jnp.float32, jnp.bfloat16


def halves(x):
    high = x.astype(bf16)
    return high, (x - high.astype(f32)).astype(bf16)


def whole_of(high, low):
    return high.astype(f32) + low.astype(f32)


def product(a, b, a_dim, b_dim):
    def one(x, y):
        return lax.dot_general(
            x, y, (((a_dim,), (b_dim,)), ((), ())), preferred_element_type=f32
        )

    return one(a[0], b[0]) + (one(a[0], b[1]) + one(a[1], b[0]))


def select_by(index, options):
    result = None
    for value, array in options.items():
        result = array if result is None else jnp.where(index == value, array, result)
    return result


def tie(values):
    return lax.optimization_barrier(tuple(values))


def call(body, outputs, numbers, arrays, space=pltpu.VMEM, scratch=(), mebibytes=32):
    inputs, results = len(arrays), len(outputs)

    def kernel(*refs):
        body(
            refs[0],
            refs[1 : 1 + inputs],
            refs[1 + inputs : 1 + inputs + results],
            *refs[1 + inputs + results :],
        )

    return pl.pallas_call(
        kernel,
        out_shape=[jax.ShapeDtypeStruct(shape, dtype) for shape, dtype in outputs],
        in_specs=[pl.BlockSpec(memory_space=pltpu.SMEM)]
        + [pl.BlockSpec(memory_space=space)] * inputs,
        out_specs=[pl.BlockSpec(memory_space=pltpu.VMEM)] * results,
        scratch_shapes=scratch,
        compiler_params=pltpu.CompilerParams(vmem_limit_bytes=mebibytes << 20),
        cost_estimate=pl.CostEstimate(flops=1, bytes_accessed=1, transcendentals=0),
    )(numbers, *arrays)


def chosen_sums(numbers, wanted, shape):
    arrays = []

    def place(array):
        for i, known in enumerate(arrays):
            if known is array:
                return i
        arrays.append(array)
        return len(arrays) - 1

    wanted = [
        (which, {k: [(place(a), r) for a, r in terms] for k, terms in options.items()})
        for which, options in wanted
    ]
    most = max(len(terms) for _, options in wanted for terms in options.values())

    def body(number, inputs, outputs, held, sems):
        def copies(o, terms):
            return [
                pltpu.make_async_copy(
                    inputs[a].at[pl.ds(r, shape[0])], held.at[o, i], sems.at[o, i]
                )
                for i, (a, r) in enumerate(terms)
            ]

        for o, (which, options) in enumerate(wanted):
            for k, terms in options.items():

                @pl.when(number[which] == k)
                def _():
                    for copy in copies(o, terms):
                        copy.start()

        for o, (which, options) in enumerate(wanted):
            for k, terms in options.items():

                @pl.when(number[which] == k)
                def _():
                    for copy in copies(o, terms):
                        copy.wait()
                    total = jnp.zeros(shape, f32)
                    for i in range(len(terms)):
                        total = held[o, i] if i == 0 else total + held[o, i]
                    outputs[o][...] = total

    return call(
        body,
        [(shape, f32)] * len(wanted),
        numbers,
        arrays,
        pl.ANY,
        [
            pltpu.VMEM((len(wanted), most) + shape, f32),
            pltpu.SemaphoreType.DMA((len(wanted), most)),
        ],
        24,
    )


class Windows:
    def __init__(self):
        self.now = 0
        self.processes = []

    def add(self, process):
        self.processes.append([process, None, None])

    def open(self):
        for entry in list(self.processes):
            process, due, values = entry
            if values and due >= self.now:
                continue
            try:
                windows, entry[2] = process.send(values)
                entry[1] = self.now + windows - 1
            except StopIteration:
                self.processes.remove(entry)

    def close(self, *others):
        due = [entry for entry in self.processes if entry[1] == self.now and entry[2]]
        flat = list(others)
        for entry in due:
            flat.extend(entry[2])
        if flat:
            flat = list(tie(flat))
        at = len(others)
        for entry in due:
            size = len(entry[2])
            entry[2] = flat[at : at + size]
            at += size
        self.now += 1
        return flat[: len(others)]


def make_step(sizes):
    line, cores, mp, pre = (sizes[name] for name in AXES)
    models = mp * pre
    last = count - 1

    def swap(array, axis, bit):
        return lax.ppermute(array, axis, [(i, i ^ bit) for i in range(sizes[axis])])

    def total_over(array, axis):
        bit = 1
        while bit < sizes[axis]:
            array = array + swap(array, axis, bit)
            bit *= 2
        return array

    def total_line(array):
        total = array
        for s in range(1, line):
            total = total + lax.ppermute(array, LINE, [(i, (i + s) % line) for i in range(line)])
        return total

    def snake(array, outward):
        pairs = []
        for z in range(line):
            for c in range(cores):
                goal = z + (1 if (c == 0) == outward else -1)
                if 0 <= goal < line:
                    pairs.append((z * cores + c, goal * cores + c))
                else:
                    pairs.append((z * cores + c, z * cores + 1 - c))
        return lax.ppermute(array, (LINE, CORE), pairs)

    def shards(activations, grad_output, left_old, right_old, probe_left, probe_right):
        z, core = lax.axis_index(LINE), lax.axis_index(CORE)
        x, y = lax.axis_index(MP), lax.axis_index(PRE)
        model = x * pre + y
        width = activations.shape[1]
        block = grad_output.shape[1]
        hidden = block * models
        panel = block // cores
        own_rows = width // (line * cores)
        model_rows = width // models
        piece = width // count
        owner_x, owner_y = z // pre, z % pre
        there = jnp.where(core == 0, z, line - 1 - z)
        numbers = jnp.stack(
            [z, core, there, line - 1 - there, x == owner_x, y == owner_y]
        ).astype(jnp.int32)
        Z, C, THERE, BACK, IN_X, IN_Y = range(6)
        shape = (piece, panel)
        windows = Windows()
        state = {}

        def to_partner(array):
            return swap(array, CORE, 1)

        def device(number):
            return number[Z] * cores + number[C]

        def local(which):
            return lax.dot_general(
                activations,
                lax.dynamic_slice_in_dim(grad_output, which * panel, panel, 1),
                (((0,), (0,)), ((), ())),
                preferred_element_type=f32,
            )

        arrived = to_partner(local(1 - core))
        kept, arrived = tie((local(core), arrived))

        class Chain:
            def __init__(self, terms):
                self.terms = terms
                self.sent, self.out, self.home, self.wholes = [], [], [], []

            def combine(self, t):
                wanted = []
                for which, got in ((THERE, self.out), (BACK, self.home)):
                    options = {}
                    for k in range(line):
                        options[k] = []
                        if 0 <= t - k < count:
                            options[k] = self.terms(t - k)
                            if k:
                                options[k] = options[k] + [(got[t - 1], 0)]
                    wanted.append((which, options))
                return chosen_sums(numbers, wanted, shape)

            def send(self, going_out, going_home):
                self.sent.append(going_out)
                self.out.append(snake(going_out, True))
                self.home.append(snake(going_home, False))

            def finish(self, t):
                j = t - (line - 1)
                if not 0 <= j < count:
                    return
                options = {
                    k: [(self.sent[j + k], 0), (self.home[j + line - 2 - k], 0)]
                    for k in range(line - 1)
                }
                options[line - 1] = self.terms(j) + [(self.out[j + line - 2], 0)]
                self.wholes += chosen_sums(numbers, [(THERE, options)], shape)

        gradient = Chain(lambda j: [(kept, j * piece), (arrived, j * piece)])
        mixed = Chain(lambda j: [(state["kept", j], 0), (state["swapped", j], 0)])
        own = gradient.wholes

        def row(array):
            return array.reshape(1, -1)

        def panel_of(which):
            return row(lax.dynamic_slice_in_dim(probe_right, which * panel, panel, 0))

        def old_right():
            def body(number, inputs, outputs):
                old = beta_decay * inputs[0][...]
                outputs[0][...], outputs[1][...] = halves(old)
                outputs[2][...] = jnp.sum(old * inputs[1][...], axis=1, keepdims=True).T

            high, low, image = call(
                body,
                [((block, panel), bf16), ((block, panel), bf16), ((1, block), f32)],
                numbers,
                [right_old, panel_of(z * cores + core)],
            )
            image = image + to_partner(image)
            high, low, image = yield 1, (high, low, image)
            state["old"] = high, low
            (state["old_image"],) = yield 1, (total_line(image),)

        def old_left():
            spot = lax.broadcasted_iota(jnp.int32, (own_rows, width), 1) // model_rows
            rows = jnp.where(spot == model, jnp.tile(beta_decay * left_old.T, (1, models)), 0.0)
            (rows,) = yield 1, (total_over(rows, MP),)
            (state["old_left"],) = yield 1, (total_over(rows, PRE),)

        def choose(number, first, second):
            return chosen_sums(
                numbers, [(number, {1: [(first, 0)], 0: [(second, 0)]})], first.shape
            )[0]

        def spread(array, axis, place, owner):
            result = None
            size = sizes[axis]
            for s in range(1, size):
                got = lax.ppermute(array, axis, [(i, (i + s) % size) for i in range(size)])
                if result is None:
                    result = got
                else:
                    result = jnp.where((place - s) % size == owner, got, result)
            return result

        def panel_piece(j):
            while len(own) <= j:
                yield 1, ()
            whole = own[j]
            got, state["other", j] = yield 1, (
                spread(whole, PRE, y, owner_y),
                to_partner(whole),
            )
            held = choose(IN_Y, whole, got)
            held, got = yield 1, (held, spread(held, MP, x, owner_x))

            def body(number, inputs, outputs):
                here = jnp.full(shape, number[IN_X], jnp.int32) == 1
                pair = halves(jnp.where(here, inputs[0][...], inputs[1][...]))
                outputs[0][...], outputs[1][...] = pair
                both = product(pair, (inputs[2][...], inputs[3][...]), 1, 1)
                first, second = both[:, :panel], both[:, panel:]
                zeroth = jnp.full(shape, number[C], jnp.int32) == 0
                outputs[2][...] = jnp.where(zeroth, first, second)
                outputs[3][...] = jnp.where(zeroth, second, first)

            high, low, state["kept", j], away = call(
                body,
                [(shape, bf16), (shape, bf16), (shape, f32), (shape, f32)],
                numbers,
                [held, got, *state["old"]],
            )
            state["swapped", j] = to_partner(away)
            state["panel", j] = yield 1, (high, low)

        def over_models(array, first):
            ways = (MP, PRE) if first else (PRE, MP)
            return tuple(total_over(half, way) for half, way in zip(array, ways))

        def left_side():
            while ("other", last) not in state:
                yield 1, ()

            def body(number, inputs, outputs):
                zeroth = jnp.full(shape, number[C], jnp.int32) == 0
                for j in range(count):
                    mine, other = inputs[j][...], inputs[count + j][...]
                    rows = pl.ds(j * piece, piece)
                    for i, part in enumerate(
                        (jnp.where(zeroth, mine, other), jnp.where(zeroth, other, mine))
                    ):
                        columns = pl.ds(i * panel, panel)
                        outputs[0][rows, columns], outputs[1][rows, columns] = halves(part)
                rows = pl.ds(pl.multiple_of(device(number) * own_rows, own_rows), own_rows)
                gram = product(
                    (outputs[0][rows, :], outputs[1][rows, :]),
                    (outputs[0][...], outputs[1][...]),
                    1,
                    1,
                )
                outputs[2][...] = gram[: own_rows // 2] / hidden
                outputs[3][...] = gram[own_rows // 2 :] / hidden

            half = (own_rows // 2, width)
            high, low, *gram = call(
                body,
                [((width, block), bf16)] * 2 + [(half, f32)] * 2,
                numbers,
                [*own, *(state["other", j] for j in range(count))],
            )
            state["block"] = high, low
            gram = yield 1, over_models(gram, True)
            gram = yield 1, over_models(gram, False)

            def body(number, inputs, outputs):
                gram = jnp.concatenate([inputs[0][...], inputs[1][...]], axis=0)
                left = inputs[2][...] + gram
                outputs[0][...] = left
                image = jnp.sum(left * inputs[3][...], axis=1, keepdims=True)
                at = lax.broadcasted_iota(jnp.int32, left.shape, 0) + device(number) * own_rows
                here = lax.broadcasted_iota(jnp.int32, left.shape, 1) == at
                outputs[1][...] = jnp.sum(jnp.where(here, image, 0.0), axis=0, keepdims=True)
                grad = inputs[4][...], inputs[5][...]
                left_grad = product(halves(left), grad, 1, 0)
                outputs[2][...] = left_grad
                outputs[3][...] = product(halves(gram), grad, 1, 0) * (hidden / width)
                crossed = product(halves(left_grad), grad, 1, 1) / width
                outputs[4][...] = crossed[: own_rows // 2]
                outputs[5][...] = crossed[own_rows // 2 :]

            rows = (own_rows, width)
            left, first, left_grad, gram_grad, *crossed = call(
                body,
                [(rows, f32), ((1, width), f32), ((own_rows, block), f32)]
                + [((own_rows, block), f32)]
                + [(half, f32)] * 2,
                numbers,
                [*gram, state["old_left"], row(probe_left), *state["block"]],
            )
            state["left_parts"] = left_grad, gram_grad
            state["left"] = left
            first = total_line(first + to_partner(first))
            state["first"], state["partner_left"], *crossed = yield 1, (
                first,
                to_partner(left),
                *over_models(crossed, True),
            )
            state["crossed"] = yield 1, over_models(crossed, False)
            options = {
                m: left[:, m * model_rows : (m + 1) * model_rows] for m in range(models)
            }
            (state["left_new"],) = yield 1, (select_by(model, options).T,)

        def right_power():
            while len(own) < count:
                yield 1, ()

            def body(number, inputs, outputs):
                probe = inputs[count][...]
                for j in range(count):
                    image = jnp.sum(inputs[j][...] * probe, axis=1, keepdims=True)
                    outputs[0][:, j * piece : (j + 1) * piece] = image.T

            (image,) = call(
                body, [((1, width), f32)], numbers, [*own, panel_of(model * cores + core)]
            )
            (image,) = yield 1, (total_over(total_over(image, CORE), MP),)
            (image,) = yield 1, (total_over(image, PRE),)

            def body(number, inputs, outputs):
                grad = whole_of(inputs[2][...], inputs[3][...])
                first = inputs[0][...] + (
                    jnp.sum(grad * inputs[1][...].T, axis=0, keepdims=True) / width
                )
                outputs[0][:, :width] = jnp.sum(grad * first, axis=1, keepdims=True).T
                old = whole_of(inputs[4][...], inputs[5][...])
                outputs[0][:, width : width + panel] = jnp.sum(
                    old * first.T, axis=0, keepdims=True
                )
                square = jnp.sum(first * first, axis=1, keepdims=True)
                outputs[0][:, width + panel :] = jnp.broadcast_to(square, (1, 128))

            (joined,) = call(
                body,
                [((1, width + panel + 128), f32)],
                numbers,
                [state["old_image"], image, *state["block"], *state["old"]],
            )
            (joined,) = yield 1, (total_over(total_over(joined, MP), PRE),)
            state["joined"] = joined

        def tops():
            while not ("first" in state and "joined" in state and ("panel", last) in state):
                yield 1, ()

            def body(number, inputs, outputs):
                joined = inputs[0][...]
                vector = joined[:, :width].T
                second = joined[:, width : width + panel]
                for j in range(count):
                    part = whole_of(inputs[3 + 2 * j][...], inputs[4 + 2 * j][...])
                    rows = vector[j * piece : (j + 1) * piece]
                    second = second + jnp.sum(part * rows, axis=0, keepdims=True) / width
                square = joined[:, width + panel : width + panel + 1]
                second = second / jnp.sqrt(square + norm_floor)
                right = jnp.sum(second * second, axis=1, keepdims=True)
                first = inputs[1][...]
                unit = first / jnp.sqrt(
                    jnp.sum(first * first, axis=1, keepdims=True) + norm_floor
                )
                second = jnp.sum(inputs[2][...] * unit, axis=1, keepdims=True)
                left = jnp.sum(second * second, axis=0, keepdims=True)
                spot = lax.broadcasted_iota(jnp.int32, (1, 128), 1)
                outputs[0][...] = jnp.where(spot == 0, left, right)

            panels = [half for j in range(count) for half in state["panel", j]]
            (squares,) = call(
                body,
                [((1, 128), f32)],
                numbers,
                [state["joined"], state["first"], state["left"], *panels],
            )
            (state["squares"],) = yield 1, (total_line(squares + to_partner(squares)),)

        def scales(squares):
            top = jnp.sqrt(squares + norm_floor)
            top_left, top_right = top[:, 0:1], top[:, 1:2]
            return top_left, top_right, 1.0 / (16.0 * jnp.sqrt(jnp.sqrt(top_left * top_right)))

        def first_part():
            while "squares" not in state or "crossed" not in state:
                yield 1, ()

            def body(number, inputs, outputs):
                top_left, top_right, scale = scales(inputs[0][...])
                crossed = halves(jnp.concatenate([inputs[3][...], inputs[4][...]], axis=0))
                rows = pl.ds(pl.multiple_of(device(number) * own_rows, own_rows), own_rows)
                own = whole_of(inputs[5][rows, :], inputs[6][rows, :])
                crossed = product(crossed, (inputs[5][...], inputs[6][...]), 1, 0)
                outputs[0][...] = (
                    25.0 * own
                    - inputs[1][...] * (5.0 / top_left)
                    - (5.0 * inputs[2][...] - crossed / top_left) / top_right
                ) * scale

            (state["first_part"],) = yield 1, call(
                body,
                [((own_rows, block), f32)],
                numbers,
                [state["squares"], *state["left_parts"], *state["crossed"], *state["block"]],
            )

        def right_factor():
            while ("panel", last) not in state or "block" not in state or windows.now < 10:
                yield 1, ()

            def body(number, inputs, outputs):
                pair = [
                    jnp.concatenate([inputs[3 + 2 * j + i][...] for j in range(count)], axis=0)
                    for i in range(2)
                ]
                gram = product((inputs[1][...], inputs[2][...]), pair, 0, 0)
                outputs[0][...] = beta_decay * inputs[0][...] + gram / width

            panels = [half for j in range(count) for half in state["panel", j]]
            (state["right_new"],) = yield 1, call(
                body,
                [((block, panel), f32)],
                numbers,
                [right_old, *state["block"], *panels],
                mebibytes=40,
            )

        windows.add(old_right())
        windows.add(old_left())
        for j in range(count):
            windows.add(panel_piece(j))
        for process in (left_side, right_power, tops, first_part, right_factor):
            windows.add(process())

        steps = count + line - 2
        going = gradient.combine(0)
        for t in range(2 * steps):
            current = gradient if t < steps else mixed
            current.send(*going)
            gradient.finish(t)
            mixed.finish(t - steps)
            windows.open()
            if t + 1 < steps:
                going = gradient.combine(t + 1)
            elif t + 1 < 2 * steps:
                going = mixed.combine(t + 1 - steps)
            else:
                going = mixed.out[-1], mixed.home[-1]
            going = windows.close(*going)
        mixed.out[-1], mixed.home[-1] = going
        mixed.finish(steps)
        while windows.processes:
            windows.open()
            if windows.processes:
                windows.close()

        def body(number, inputs, outputs):
            top_left, top_right, scale = scales(inputs[0][...])
            sums = jnp.concatenate([inputs[3 + j][...] for j in range(count)], axis=0)
            pair = halves(sums)
            for i in range(2):
                other = number[C] if i == 0 else 1 - number[C]
                at = number[Z] * cores + other
                rows = inputs[3][:own_rows]
                for k in range(1, line * cores):
                    j, start = divmod(k * own_rows, piece)
                    here = jnp.full((own_rows, panel), at, jnp.int32) == k
                    rows = jnp.where(here, inputs[3 + j][start : start + own_rows], rows)
                left = product(halves(inputs[1 + i][...]), pair, 1, 0)
                outputs[i][...] = (left / top_left - 5.0 * rows) * (scale / top_right)

        mine, theirs = call(
            body,
            [((own_rows, panel), f32)] * 2,
            numbers,
            [state["squares"], state["left"], state["partner_left"], *mixed.wholes],
        )
        theirs = to_partner(theirs)

        def body(number, inputs, outputs):
            zeroth = jnp.full((own_rows, panel), number[C], jnp.int32) == 0
            mine, theirs = inputs[1][...], inputs[2][...]
            low, high = jnp.where(zeroth, mine, theirs), jnp.where(zeroth, theirs, mine)
            outputs[0][:, :panel] = inputs[0][:, :panel] + low
            outputs[0][:, panel:] = inputs[0][:, panel:] + high

        (update,) = call(
            body,
            [((own_rows, block), f32)],
            numbers,
            [state["first_part"], mine, theirs],
        )
        return state["left_new"], state["right_new"], update

    return shards


def solution(mesh):
    dp, mp, pre = (mesh.shape[name] for name in ("dp", "mp", "pre"))
    cores = dp // (mp * pre)
    assert cores == 2
    split = Mesh(mesh.devices.reshape(dp // cores, cores, mp, pre), AXES)
    factor = P((MP, PRE), (LINE, CORE))
    in_specs = (
        P((LINE, CORE), None),
        P((LINE, CORE), (MP, PRE)),
        factor,
        factor,
        P(),
        P(),
    )
    out_specs = (factor, factor, P((LINE, CORE), (MP, PRE)))
    return jax.shard_map(
        make_step(dict(split.shape)),
        mesh=split,
        in_specs=in_specs,
        out_specs=out_specs,
        check_vma=False,
    )
```

```python
import jax
import jax.numpy as jnp
from jax import lax
from jax.experimental import pallas as pl
from jax.experimental.pallas import tpu as pltpu
from jax.sharding import Mesh, PartitionSpec as P

beta_decay = 0.9
norm_floor = 1e-06
count = 4

LINE, CORE, MP, PRE = "line", "core", "mp", "pre"
AXES = (LINE, CORE, MP, PRE)
f32, bf16 = jnp.float32, jnp.bfloat16


def halves(x):
    high = x.astype(bf16)
    return high, (x - high.astype(f32)).astype(bf16)


def whole_of(high, low):
    return high.astype(f32) + low.astype(f32)


def product(a, b, a_dim, b_dim):
    def one(x, y):
        return lax.dot_general(
            x, y, (((a_dim,), (b_dim,)), ((), ())), preferred_element_type=f32
        )

    return one(a[0], b[0]) + (one(a[0], b[1]) + one(a[1], b[0]))


def select_by(index, options):
    result = None
    for value, array in options.items():
        result = array if result is None else jnp.where(index == value, array, result)
    return result


def tie(values):
    return lax.optimization_barrier(tuple(values))


def call(body, outputs, numbers, arrays, space=pltpu.VMEM, scratch=(), mebibytes=32):
    inputs, results = len(arrays), len(outputs)

    def kernel(*refs):
        body(
            refs[0],
            refs[1 : 1 + inputs],
            refs[1 + inputs : 1 + inputs + results],
            *refs[1 + inputs + results :],
        )

    return pl.pallas_call(
        kernel,
        out_shape=[jax.ShapeDtypeStruct(shape, dtype) for shape, dtype in outputs],
        in_specs=[pl.BlockSpec(memory_space=pltpu.SMEM)]
        + [pl.BlockSpec(memory_space=space)] * inputs,
        out_specs=[pl.BlockSpec(memory_space=pltpu.VMEM)] * results,
        scratch_shapes=scratch,
        compiler_params=pltpu.CompilerParams(vmem_limit_bytes=mebibytes << 20),
        cost_estimate=pl.CostEstimate(flops=1, bytes_accessed=1, transcendentals=0),
    )(numbers, *arrays)


def plus(numbers, a, b):
    def body(number, inputs, outputs):
        outputs[0][...] = inputs[0][...] + inputs[1][...]

    return call(body, [(a.shape, f32)], numbers, [a, b])[0]


def chosen_sums(numbers, wanted, shape, more=0):
    arrays = []

    def place(array):
        for i, known in enumerate(arrays):
            if known is array:
                return i
        arrays.append(array)
        return len(arrays) - 1

    wanted = [
        (which, {k: [(place(a), r) for a, r in terms] for k, terms in options.items()})
        for which, options in wanted
    ]
    most = max(len(terms) for _, options in wanted for terms in options.values())

    def body(number, inputs, outputs, held, sems):
        def copies(o, terms):
            return [
                pltpu.make_async_copy(
                    inputs[a].at[pl.ds(r, shape[0])], held.at[o, i], sems.at[o, i]
                )
                for i, (a, r) in enumerate(terms)
            ]

        for o, (which, options) in enumerate(wanted):
            for k, terms in options.items():

                @pl.when(number[which] == k)
                def _():
                    for copy in copies(o, terms):
                        copy.start()

        for o, (which, options) in enumerate(wanted):
            for k, terms in options.items():

                @pl.when(number[which] == k)
                def _():
                    for copy in copies(o, terms):
                        copy.wait()
                    total = jnp.zeros(shape, f32)
                    for i in range(len(terms)):
                        total = held[o, i] if i == 0 else total + held[o, i]
                    outputs[o][: shape[0]] = total
            if more:
                outputs[o][shape[0] :] = jnp.zeros((more,) + shape[1:], f32)

    return call(
        body,
        [((shape[0] + more,) + shape[1:], f32)] * len(wanted),
        numbers,
        arrays,
        pl.ANY,
        [
            pltpu.VMEM((len(wanted), most) + shape, f32),
            pltpu.SemaphoreType.DMA((len(wanted), most)),
        ],
        24,
    )


class Windows:
    def __init__(self):
        self.now = 0
        self.processes = []

    def add(self, process):
        self.processes.append([process, None, None])

    def open(self):
        ended = []
        for entry in self.processes:
            process, due, values = entry
            if values and due >= self.now:
                continue
            try:
                windows, entry[2] = process.send(values)
                entry[1] = self.now + windows - 1
            except StopIteration:
                ended.append(entry)
        for entry in ended:
            self.processes.remove(entry)

    def close(self, *others):
        due = [entry for entry in self.processes if entry[1] == self.now and entry[2]]
        flat = list(others)
        for entry in due:
            flat.extend(entry[2])
        if flat:
            flat = list(tie(flat))
        at = len(others)
        for entry in due:
            size = len(entry[2])
            entry[2] = flat[at : at + size]
            at += size
        self.now += 1
        return flat[: len(others)]


def make_step(sizes):
    line, cores, mp, pre = (sizes[name] for name in AXES)
    models = mp * pre
    last = count - 1

    def swap(array, axis, bit):
        return lax.ppermute(array, axis, [(i, i ^ bit) for i in range(sizes[axis])])

    def bits(axis):
        return [1 << i for i in range(sizes[axis].bit_length() - 1)]

    def total(numbers, array, axes):
        for axis in axes:
            for bit in bits(axis):
                array, got = yield 1, (array, swap(array, axis, bit))
                array = plus(numbers, array, got)
        return array

    def snake(array, outward):
        pairs = []
        for z in range(line):
            for c in range(cores):
                goal = z + (1 if (c == 0) == outward else -1)
                if 0 <= goal < line:
                    pairs.append((z * cores + c, goal * cores + c))
                else:
                    pairs.append((z * cores + c, z * cores + 1 - c))
        return lax.ppermute(array, (LINE, CORE), pairs)

    def shards(activations, grad_output, left_old, right_old, probe_left, probe_right):
        z, core = lax.axis_index(LINE), lax.axis_index(CORE)
        x, y = lax.axis_index(MP), lax.axis_index(PRE)
        model = x * pre + y
        width = activations.shape[1]
        block = grad_output.shape[1]
        hidden = block * models
        panel = block // cores
        own_rows = width // (line * cores)
        model_rows = width // models
        piece = width // count
        owner_x, owner_y = z // pre, z % pre
        there = jnp.where(core == 0, z, line - 1 - z)
        numbers = jnp.stack(
            [z, core, there, line - 1 - there, x == owner_x, y == owner_y]
        ).astype(jnp.int32)
        Z, C, THERE, BACK, IN_X, IN_Y = range(6)
        shape = (piece, panel)
        windows = Windows()
        state = {}

        def to_partner(array):
            return swap(array, CORE, 1)

        def device(number):
            return number[Z] * cores + number[C]

        def local(which):
            return lax.dot_general(
                activations,
                lax.dynamic_slice_in_dim(grad_output, which * panel, panel, 1),
                (((0,), (0,)), ((), ())),
                preferred_element_type=f32,
            )

        arrived = to_partner(local(1 - core))
        kept, arrived, left_old, right_old = tie((local(core), arrived, left_old, right_old))

        class Chain:
            def __init__(self, terms):
                self.terms = terms
                self.sent, self.out, self.home, self.wholes = [], [], [], []

            def combine(self, t):
                wanted = []
                for which, got in ((THERE, self.out), (BACK, self.home)):
                    options = {}
                    for k in range(line):
                        options[k] = []
                        if 0 <= t - k < count:
                            options[k] = self.terms(t - k)
                            if k:
                                options[k] = options[k] + [(got[t - 1], 0)]
                    wanted.append((which, options))
                return chosen_sums(numbers, wanted, shape, 8)

            def send(self, going_out, going_home):
                self.sent.append(going_out)
                self.out.append(snake(going_out, True))
                self.home.append(snake(going_home, False))

            def finish(self, t):
                j = t - (line - 1)
                if not 0 <= j < count:
                    return
                options = {
                    k: [(self.sent[j + k], 0), (self.home[j + line - 2 - k], 0)]
                    for k in range(line - 1)
                }
                options[line - 1] = self.terms(j) + [(self.out[j + line - 2], 0)]
                self.wholes += chosen_sums(numbers, [(THERE, options)], shape)

        gradient = Chain(lambda j: [(kept, j * piece), (arrived, j * piece)])
        mixed = Chain(lambda j: [(state["kept", j], 0), (state["swapped", j], 0)])
        own = gradient.wholes

        def row(array):
            return array.reshape(1, -1)

        def exchange(array, axis):
            return total(numbers, array, (axis,))

        def placed(number, column):
            wide = (own_rows, width)
            at = lax.broadcasted_iota(jnp.int32, wide, 0) + device(number) * own_rows
            here = lax.broadcasted_iota(jnp.int32, wide, 1) == at
            return jnp.sum(jnp.where(here, column, 0.0), axis=0, keepdims=True)

        def panel_of(which):
            return row(lax.dynamic_slice_in_dim(probe_right, which * panel, panel, 0))

        def old_right():
            def body(number, inputs, outputs):
                old = beta_decay * inputs[0][...]
                outputs[0][...], outputs[1][...] = halves(old)
                outputs[2][...] = jnp.sum(old * inputs[1][...], axis=1, keepdims=True).T

            high, low, image = call(
                body,
                [((block, panel), bf16), ((block, panel), bf16), ((1, block), f32)],
                numbers,
                [right_old, panel_of(z * cores + core)],
            )
            *state["old"], state["old_image"] = yield 1, (high, low, image)

        def old_left():
            spot = lax.broadcasted_iota(jnp.int32, (own_rows, width), 1) // model_rows
            rows = jnp.where(spot == model, jnp.tile(beta_decay * left_old.T, (1, models)), 0.0)
            (rows,) = yield 1, (rows,)
            rows = yield from exchange(rows, MP)
            rows = yield from exchange(rows, PRE)
            state["old_left"] = rows

            def body(number, inputs, outputs):
                outputs[0][:, :block] = inputs[1][...]
                image = jnp.sum(inputs[0][...] * inputs[2][...], axis=1, keepdims=True)
                outputs[0][:, block:] = placed(number, image)

            (images,) = call(
                body,
                [((1, block + width), f32)],
                numbers,
                [rows, state["old_image"], row(probe_left)],
            )
            state["old_images"] = yield from total(numbers, images, (CORE, LINE))

        def choose(number, first, second):
            return chosen_sums(
                numbers, [(number, {1: [(first, 0)], 0: [(second, 0)]})], first.shape
            )[0]

        def spread(array, axis, place, owner):
            result = None
            size = sizes[axis]
            for s in range(1, size):
                got = lax.ppermute(array, axis, [(i, (i + s) % size) for i in range(size)])
                if result is None:
                    result = got
                else:
                    result = jnp.where((place - s) % size == owner, got, result)
            return result

        def panel_piece(j):
            while len(own) <= j:
                yield 1, ()
            whole = own[j]
            got, state["other", j] = yield 1, (
                spread(whole, PRE, y, owner_y),
                to_partner(whole),
            )
            held = choose(IN_Y, whole, got)
            held, got = yield 1, (held, spread(held, MP, x, owner_x))

            def body(number, inputs, outputs):
                here = jnp.full(shape, number[IN_X], jnp.int32) == 1
                pair = halves(jnp.where(here, inputs[0][...], inputs[1][...]))
                outputs[0][...], outputs[1][...] = pair
                both = product(pair, (inputs[2][...], inputs[3][...]), 1, 1)
                first, second = both[:, :panel], both[:, panel:]
                zeroth = jnp.full(shape, number[C], jnp.int32) == 0
                outputs[2][...] = jnp.where(zeroth, first, second)
                outputs[3][...] = jnp.where(zeroth, second, first)

            high, low, state["kept", j], away = call(
                body,
                [(shape, bf16), (shape, bf16), (shape, f32), (shape, f32)],
                numbers,
                [held, got, *state["old"]],
            )
            state["swapped", j] = to_partner(away)
            state["panel", j] = yield 1, (high, low)

        def over_models(array):
            for ways in ((MP, PRE), (PRE, MP)):
                for level in range(max(len(bits(MP)), len(bits(PRE)))):
                    got = []
                    for half, way in zip(array, ways):
                        if level < len(bits(way)):
                            got.append(swap(half, way, bits(way)[level]))
                        else:
                            got.append(jnp.zeros_like(half))
                    *array, one, other = yield 1, (*array, *got)
                    array = [plus(numbers, array[0], one), plus(numbers, array[1], other)]
            return array

        def crossing(crossed):
            crossed = yield from over_models(crossed)

            def body(number, inputs, outputs):
                pair = halves(jnp.concatenate([inputs[0][...], inputs[1][...]], axis=0))
                outputs[0][...] = product(pair, (inputs[2][...], inputs[3][...]), 1, 0)

            (state["crossed"],) = yield 1, call(
                body, [((own_rows, block), f32)], numbers, [*crossed, *state["block"]]
            )

        def left_side():
            while ("other", last) not in state:
                yield 1, ()

            def body(number, inputs, outputs):
                zeroth = jnp.full(shape, number[C], jnp.int32) == 0
                for j in range(count):
                    mine, other = inputs[j][...], inputs[count + j][...]
                    rows = pl.ds(j * piece, piece)
                    for i, part in enumerate(
                        (jnp.where(zeroth, mine, other), jnp.where(zeroth, other, mine))
                    ):
                        columns = pl.ds(i * panel, panel)
                        outputs[0][rows, columns], outputs[1][rows, columns] = halves(part)
                rows = pl.ds(pl.multiple_of(device(number) * own_rows, own_rows), own_rows)
                gram = product(
                    (outputs[0][rows, :], outputs[1][rows, :]),
                    (outputs[0][...], outputs[1][...]),
                    1,
                    1,
                )
                outputs[2][...] = gram[: own_rows // 2] / hidden
                outputs[3][...] = gram[own_rows // 2 :] / hidden

            half = (own_rows // 2, width)
            high, low, *gram = call(
                body,
                [((width, block), bf16)] * 2 + [(half, f32)] * 2,
                numbers,
                [*own, *(state["other", j] for j in range(count))],
            )
            state["block"] = high, low
            gram = yield from over_models(gram)

            def body(number, inputs, outputs):
                gram = jnp.concatenate([inputs[0][...], inputs[1][...]], axis=0)
                left = inputs[2][...] + gram
                outputs[0][...] = left
                grad = inputs[3][...], inputs[4][...]
                left_grad = product(halves(left), grad, 1, 0)
                outputs[1][...] = left_grad
                outputs[2][...] = product(halves(gram), grad, 1, 0) * (hidden / width)
                crossed = product(halves(left_grad), grad, 1, 1) / width
                outputs[3][...] = crossed[: own_rows // 2]
                outputs[4][...] = crossed[own_rows // 2 :]

            rows = (own_rows, width)
            left, left_grad, gram_grad, *crossed = call(
                body,
                [(rows, f32), ((own_rows, block), f32), ((own_rows, block), f32)]
                + [(half, f32)] * 2,
                numbers,
                [*gram, state["old_left"], *state["block"]],
            )
            state["left_parts"] = left_grad, gram_grad
            state["left"] = left
            windows.add(crossing(crossed))
            (state["partner_left"],) = yield 1, (to_partner(left),)
            options = {
                m: left[:, m * model_rows : (m + 1) * model_rows] for m in range(models)
            }
            (state["left_new"],) = yield 1, (select_by(model, options).T,)

        def powers():
            while len(own) < count:
                yield 1, ()

            def body(number, inputs, outputs):
                right, left = inputs[count][...], inputs[count + 1][...].T
                across = jnp.zeros((1, panel), f32)
                for j in range(count):
                    rows = slice(j * piece, (j + 1) * piece)
                    across += jnp.sum(inputs[j][...] * left[rows], axis=0, keepdims=True)
                for i, vector in enumerate((right, across)):
                    for j in range(count):
                        image = jnp.sum(inputs[j][...] * vector, axis=1, keepdims=True)
                        at = i * width + j * piece
                        outputs[0][:, at : at + piece] = image.T

            (images,) = call(
                body,
                [((1, 2 * width), f32)],
                numbers,
                [*own, panel_of(model * cores + core), row(probe_left)],
            )
            images = yield from total(numbers, images, (CORE, MP, PRE))
            while "block" not in state or "old_images" not in state:
                yield 1, ()

            def body(number, inputs, outputs):
                grad = whole_of(inputs[2][...], inputs[3][...])
                first = inputs[0][:, :block] + (
                    jnp.sum(grad * inputs[1][:, :width].T, axis=0, keepdims=True) / width
                )
                outputs[0][:, :width] = jnp.sum(grad * first, axis=1, keepdims=True).T
                old = whole_of(inputs[4][...], inputs[5][...])
                outputs[0][:, width : width + panel] = jnp.sum(
                    old * first.T, axis=0, keepdims=True
                )
                square = jnp.sum(first * first, axis=1, keepdims=True)
                outputs[0][:, width + panel :] = jnp.broadcast_to(square, (1, 128))

            (joined,) = call(
                body,
                [((1, width + panel + 128), f32)],
                numbers,
                [state["old_images"], images, *state["block"], *state["old"]],
            )
            joined = yield from total(numbers, joined, (MP, PRE))
            while "left" not in state or ("panel", last) not in state:
                yield 1, ()

            def body(number, inputs, outputs):
                joined = inputs[0][...]
                vector = joined[:, :width].T
                second = joined[:, width : width + panel]
                for j in range(count):
                    part = whole_of(inputs[4 + 2 * j][...], inputs[5 + 2 * j][...])
                    rows = vector[j * piece : (j + 1) * piece]
                    second = second + jnp.sum(part * rows, axis=0, keepdims=True) / width
                square = joined[:, width + panel : width + panel + 1]
                second = second / jnp.sqrt(square + norm_floor)
                right = jnp.sum(second * second, axis=1, keepdims=True)
                first = inputs[1][:, block:] + inputs[2][:, width:] / hidden
                unit = first / jnp.sqrt(
                    jnp.sum(first * first, axis=1, keepdims=True) + norm_floor
                )
                second = jnp.sum(inputs[3][...] * unit, axis=1, keepdims=True)
                left = jnp.sum(second * second, axis=0, keepdims=True)
                spot = lax.broadcasted_iota(jnp.int32, (1, 128), 1)
                outputs[0][...] = jnp.where(spot == 0, left, right)

            panels = [half for j in range(count) for half in state["panel", j]]
            (squares,) = call(
                body,
                [((1, 128), f32)],
                numbers,
                [joined, state["old_images"], images, state["left"], *panels],
            )
            for axis in (CORE, LINE):
                for bit in bits(axis):
                    squares = plus(numbers, squares, swap(squares, axis, bit))
            (state["squares"],) = yield 1, (squares,)

        def scales(squares):
            top = jnp.sqrt(squares + norm_floor)
            top_left, top_right = top[:, 0:1], top[:, 1:2]
            return top_left, top_right, 1.0 / (16.0 * jnp.sqrt(jnp.sqrt(top_left * top_right)))

        def right_factor():
            while ("panel", last) not in state or "block" not in state or windows.now < 10:
                yield 1, ()

            def body(number, inputs, outputs):
                pair = [
                    jnp.concatenate([inputs[3 + 2 * j + i][...] for j in range(count)], axis=0)
                    for i in range(2)
                ]
                gram = product((inputs[1][...], inputs[2][...]), pair, 0, 0)
                outputs[0][...] = beta_decay * inputs[0][...] + gram / width

            panels = [half for j in range(count) for half in state["panel", j]]
            (state["right_new"],) = yield 1, call(
                body,
                [((block, panel), f32)],
                numbers,
                [right_old, *state["block"], *panels],
                mebibytes=40,
            )

        windows.add(old_right())
        windows.add(old_left())
        for j in range(count):
            windows.add(panel_piece(j))
        for process in (left_side, powers, right_factor):
            windows.add(process())

        steps = count + line - 2
        going = gradient.combine(0)
        for t in range(2 * steps):
            current = gradient if t < steps else mixed
            current.send(*going)
            gradient.finish(t)
            mixed.finish(t - steps)
            windows.open()
            if t + 1 < steps:
                going = gradient.combine(t + 1)
            elif t + 1 < 2 * steps:
                going = mixed.combine(t + 1 - steps)
            else:
                going = ()
            *going, current.out[-1], current.home[-1] = windows.close(
                *going, current.out[-1], current.home[-1]
            )
        mixed.finish(steps)
        while windows.processes:
            windows.open()
            if windows.processes:
                windows.close()

        def body(number, inputs, outputs):
            top_left, top_right, scale = scales(inputs[0][...])
            sums = jnp.concatenate([inputs[3 + j][...] for j in range(count)], axis=0)
            pair = halves(sums)
            for i in range(2):
                other = number[C] if i == 0 else 1 - number[C]
                at = number[Z] * cores + other
                rows = inputs[3][:own_rows]
                for k in range(1, line * cores):
                    j, start = divmod(k * own_rows, piece)
                    here = jnp.full((own_rows, panel), at, jnp.int32) == k
                    rows = jnp.where(here, inputs[3 + j][start : start + own_rows], rows)
                left = product(halves(inputs[1 + i][...]), pair, 1, 0)
                outputs[i][...] = (left / top_left - 5.0 * rows) * (scale / top_right)

        mine, theirs = call(
            body,
            [((own_rows, panel), f32)] * 2,
            numbers,
            [state["squares"], state["left"], state["partner_left"], *mixed.wholes],
        )
        theirs = to_partner(theirs)

        def body(number, inputs, outputs):
            zeroth = jnp.full((own_rows, panel), number[C], jnp.int32) == 0
            mine, theirs = inputs[1][...], inputs[2][...]
            parts = jnp.where(zeroth, mine, theirs), jnp.where(zeroth, theirs, mine)
            top_left, top_right, scale = scales(inputs[0][...])
            rows = pl.ds(pl.multiple_of(device(number) * own_rows, own_rows), own_rows)
            for i, part in enumerate(parts):
                span = pl.ds(i * panel, panel)
                own = whole_of(inputs[6][rows, span], inputs[7][rows, span])
                outputs[0][:, span] = part + scale * (
                    25.0 * own
                    - inputs[3][:, span] * (5.0 / top_left)
                    - (5.0 * inputs[4][:, span] - inputs[5][:, span] / top_left) / top_right
                )

        (update,) = call(
            body,
            [((own_rows, block), f32)],
            numbers,
            [
                state["squares"],
                mine,
                theirs,
                *state["left_parts"],
                state["crossed"],
                *state["block"],
            ],
        )
        return state["left_new"], state["right_new"], update

    return shards


def solution(mesh):
    dp, mp, pre = (mesh.shape[name] for name in ("dp", "mp", "pre"))
    cores = dp // (mp * pre)
    assert cores == 2
    split = Mesh(mesh.devices.reshape(dp // cores, cores, mp, pre), AXES)
    factor = P((MP, PRE), (LINE, CORE))
    in_specs = (
        P((LINE, CORE), None),
        P((LINE, CORE), (MP, PRE)),
        factor,
        factor,
        P(),
        P(),
    )
    out_specs = (factor, factor, P((LINE, CORE), (MP, PRE)))
    return jax.shard_map(
        make_step(dict(split.shape)),
        mesh=split,
        in_specs=in_specs,
        out_specs=out_specs,
        check_vma=False,
    )
```

```python
import jax
import jax.numpy as jnp
from jax import lax
from jax.experimental import pallas as pl
from jax.experimental.pallas import tpu as pltpu
from jax.sharding import Mesh, PartitionSpec as P

beta_decay = 0.9
norm_floor = 1e-06
count = 4

LINE, CORE, MP, PRE = "line", "core", "mp", "pre"
AXES = (LINE, CORE, MP, PRE)
f32, bf16 = jnp.float32, jnp.bfloat16


def halves(x):
    high = x.astype(bf16)
    return high, (x - high.astype(f32)).astype(bf16)


def whole_of(high, low):
    return high.astype(f32) + low.astype(f32)


def product(a, b, a_dim, b_dim):
    def one(x, y):
        return lax.dot_general(
            x, y, (((a_dim,), (b_dim,)), ((), ())), preferred_element_type=f32
        )

    return one(a[0], b[0]) + (one(a[0], b[1]) + one(a[1], b[0]))


def select_by(index, options):
    result = None
    for value, array in options.items():
        result = array if result is None else jnp.where(index == value, array, result)
    return result


def tie(values):
    return lax.optimization_barrier(tuple(values))


def call(body, outputs, numbers, arrays, space=pltpu.VMEM, scratch=(), mebibytes=32):
    inputs, results = len(arrays), len(outputs)

    def kernel(*refs):
        body(
            refs[0],
            refs[1 : 1 + inputs],
            refs[1 + inputs : 1 + inputs + results],
            *refs[1 + inputs + results :],
        )

    return pl.pallas_call(
        kernel,
        out_shape=[jax.ShapeDtypeStruct(shape, dtype) for shape, dtype in outputs],
        in_specs=[pl.BlockSpec(memory_space=pltpu.SMEM)]
        + [pl.BlockSpec(memory_space=space)] * inputs,
        out_specs=[pl.BlockSpec(memory_space=pltpu.VMEM)] * results,
        scratch_shapes=scratch,
        compiler_params=pltpu.CompilerParams(vmem_limit_bytes=mebibytes << 20),
        cost_estimate=pl.CostEstimate(flops=1, bytes_accessed=1, transcendentals=0),
    )(numbers, *arrays)


def added(numbers, arrays):
    def body(number, inputs, outputs):
        total = inputs[0][...]
        for array in inputs[1:]:
            total = total + array[...]
        outputs[0][...] = total

    return call(body, [(arrays[0].shape, f32)], numbers, arrays)[0]


def fetching(body, outputs, numbers, choices, shape, arrays=(), mebibytes=24):
    sources = []

    def place(array):
        for i, known in enumerate(sources):
            if known is array:
                return i
        sources.append(array)
        return len(sources) - 1

    choices = [
        (which, {k: [(place(a), r) for a, r in terms] for k, terms in options.items()})
        for which, options in choices
    ]
    wholes = [place(array) for array in arrays]
    most = max([len(t) for _, options in choices for t in options.values()] + [1])
    many = max(len(choices), 1)

    def inner(number, inputs, results, held, sems, *kept):
        kept, kept_sems = kept[:-1], kept[-1]

        def copies(o, terms):
            return [
                pltpu.make_async_copy(
                    inputs[a].at[pl.ds(r, shape[0])], held.at[o, i], sems.at[o, i]
                )
                for i, (a, r) in enumerate(terms)
            ]

        loads = [
            pltpu.make_async_copy(inputs[a], kept[i], kept_sems.at[i])
            for i, a in enumerate(wholes)
        ]
        for o, (which, options) in enumerate(choices):
            for k, terms in options.items():

                @pl.when(number[which] == k)
                def _():
                    for copy in copies(o, terms):
                        copy.start()

        for copy in loads:
            copy.start()
        for o, (which, options) in enumerate(choices):
            for k, terms in options.items():

                @pl.when(number[which] == k)
                def _():
                    for copy in copies(o, terms):
                        copy.wait()
                    if not terms:
                        held[o, 0] = jnp.zeros(shape, f32)
                    if len(terms) > 1:
                        total = held[o, 0]
                        for i in range(1, len(terms)):
                            total = total + held[o, i]
                        held[o, 0] = total

        for copy in loads:
            copy.wait()
        body(number, [held.at[o, 0] for o in range(len(choices))], kept, results)

    return call(
        inner,
        outputs,
        numbers,
        sources,
        pl.ANY,
        [
            pltpu.VMEM((many, most) + tuple(shape), f32),
            pltpu.SemaphoreType.DMA((many, most)),
            *[pltpu.VMEM(array.shape, array.dtype) for array in arrays],
            pltpu.SemaphoreType.DMA((max(len(arrays), 1),)),
        ],
        mebibytes,
    )


def chosen_sums(numbers, choices, shape, more=0):
    def body(number, sums, inputs, outputs):
        for result, total in zip(outputs, sums):
            result[: shape[0]] = total[...]
            if more:
                result[shape[0] :] = jnp.zeros((more,) + shape[1:], f32)

    out = [((shape[0] + more,) + shape[1:], f32)] * len(choices)
    return fetching(body, out, numbers, choices, shape)


class Windows:
    def __init__(self):
        self.now = 0
        self.processes = []

    def add(self, process):
        self.processes.append([process, None, None])

    def open(self):
        ended = []
        for entry in self.processes:
            process, due, values = entry
            if values and due >= self.now:
                continue
            try:
                windows, entry[2] = process.send(values)
                entry[1] = self.now + windows - 1
            except StopIteration:
                ended.append(entry)
        for entry in ended:
            self.processes.remove(entry)

    def close(self, *others):
        due = [entry for entry in self.processes if entry[1] == self.now and entry[2]]
        flat = list(others)
        for entry in due:
            flat.extend(entry[2])
        if flat:
            flat = list(tie(flat))
        at = len(others)
        for entry in due:
            size = len(entry[2])
            entry[2] = flat[at : at + size]
            at += size
        self.now += 1
        return flat[: len(others)]


def make_step(sizes):
    line, cores, mp, pre = (sizes[name] for name in AXES)
    models = mp * pre
    last = count - 1

    def swap(array, axis, bit):
        return lax.ppermute(array, axis, [(i, i ^ bit) for i in range(sizes[axis])])

    def bits(axis):
        return [1 << i for i in range(sizes[axis].bit_length() - 1)]

    def total(numbers, array, axes):
        for axis in axes:
            for bit in bits(axis):
                pair = yield 1, (array, swap(array, axis, bit))
                array = added(numbers, pair)
        return array

    def from_all(array, axes):
        size = 1
        for axis in axes:
            size *= sizes[axis]
        return [array] + [
            lax.ppermute(array, axes, [(i, (i + s) % size) for i in range(size)])
            for s in range(1, size)
        ]

    def snake(array, outward):
        pairs = []
        for z in range(line):
            for c in range(cores):
                goal = z + (1 if (c == 0) == outward else -1)
                if 0 <= goal < line:
                    pairs.append((z * cores + c, goal * cores + c))
                else:
                    pairs.append((z * cores + c, z * cores + 1 - c))
        return lax.ppermute(array, (LINE, CORE), pairs)

    def shards(activations, grad_output, left_old, right_old, probe_left, probe_right):
        z, core = lax.axis_index(LINE), lax.axis_index(CORE)
        x, y = lax.axis_index(MP), lax.axis_index(PRE)
        model = x * pre + y
        width = activations.shape[1]
        block = grad_output.shape[1]
        hidden = block * models
        panel = block // cores
        own_rows = width // (line * cores)
        model_rows = width // models
        piece = width // count
        owner_x, owner_y = z // pre, z % pre
        there = jnp.where(core == 0, z, line - 1 - z)
        numbers = jnp.stack(
            [z, core, there, line - 1 - there, x == owner_x, y == owner_y]
        ).astype(jnp.int32)
        Z, C, THERE, BACK, IN_X, IN_Y = range(6)
        shape = (piece, panel)
        windows = Windows()
        state = {}

        def to_partner(array):
            return swap(array, CORE, 1)

        def device(number):
            return number[Z] * cores + number[C]

        def local(first, end):
            rows = (end - first) * piece
            tokens = activations.shape[0]

            def body(number, inputs, outputs, left, right, sems):
                copies = (
                    pltpu.make_async_copy(
                        inputs[0].at[:, pl.ds(first * piece, rows)], left, sems.at[0]
                    ),
                    pltpu.make_async_copy(inputs[1], right, sems.at[1]),
                )
                for copy in copies:
                    copy.start()
                for copy in copies:
                    copy.wait()
                zeroth = jnp.full(shape, number[C], jnp.int32) == 0
                for j in range(end - first):
                    both = lax.dot_general(
                        left[:, j * piece : (j + 1) * piece],
                        right[...],
                        (((0,), (0,)), ((), ())),
                        preferred_element_type=f32,
                    )
                    low, high = both[:, :panel], both[:, panel:]
                    outputs[0][j * piece : (j + 1) * piece] = jnp.where(zeroth, low, high)
                    outputs[1 + j][...] = jnp.where(zeroth, high, low)

            return call(
                body,
                [((rows, panel), f32)] + [(shape, f32)] * (end - first),
                numbers,
                [activations, grad_output],
                pl.ANY,
                [
                    pltpu.VMEM((tokens, rows), bf16),
                    pltpu.VMEM(grad_output.shape, bf16),
                    pltpu.SemaphoreType.DMA((2,)),
                ],
            )

        kept_first, away = local(0, 1)
        arrived = [to_partner(away)]
        kept_first, first_arrived, left_old, right_old = tie(
            (kept_first, arrived[0], left_old, right_old)
        )
        kept_rest, *away = local(1, count)
        arrived = [first_arrived] + [to_partner(a) for a in away]

        class Chain:
            def __init__(self, terms, halved=False):
                self.terms, self.halved = terms, halved
                self.sent, self.out, self.home = [], [], []
                self.options, self.wholes, self.parts = [], [], []

            def combine(self, t):
                wanted = []
                for which, got in ((THERE, self.out), (BACK, self.home)):
                    options = {}
                    for k in range(line):
                        options[k] = []
                        if 0 <= t - k < count:
                            options[k] = self.terms(t - k)
                            if k:
                                options[k] = options[k] + [(got[t - 1], 0)]
                    wanted.append((which, options))
                return chosen_sums(numbers, wanted, shape, 8)

            def send(self, going_out, going_home):
                self.sent.append(going_out)
                self.out.append(snake(going_out, True))
                self.home.append(snake(going_home, False))

            def finish(self, t):
                j = t - (line - 1)
                if not 0 <= j < count:
                    return
                options = {
                    k: [(self.sent[j + k], 0), (self.home[j + line - 2 - k], 0)]
                    for k in range(line - 1)
                }
                options[line - 1] = self.terms(j) + [(self.out[j + line - 2], 0)]
                self.options.append((THERE, options))
                if self.halved:
                    half = shape[0] // 2

                    def body(number, sums, inputs, outputs):
                        outputs[0][...] = sums[0][...]
                        outputs[1][...] = sums[0][:half]
                        outputs[2][...] = sums[0][half:]

                    whole, *parts = fetching(
                        body,
                        [(shape, f32)] + [((half, panel), f32)] * 2,
                        numbers,
                        self.options[-1:],
                        shape,
                    )
                    self.wholes.append(whole)
                    self.parts.append(parts)

        gradient = Chain(
            lambda j: [
                (kept_rest, (j - 1) * piece) if j else (kept_first, 0),
                (arrived[j], 0),
            ],
            True,
        )
        mixed = Chain(lambda j: [(state["kept", j], 0), (state["swapped", j], 0)])
        own = gradient.wholes

        def row(array):
            return array.reshape(1, -1)

        def exchange(array, axis):
            return total(numbers, array, (axis,))

        def placed(number, column):
            wide = (own_rows, width)
            at = lax.broadcasted_iota(jnp.int32, wide, 0) + device(number) * own_rows
            here = lax.broadcasted_iota(jnp.int32, wide, 1) == at
            return jnp.sum(jnp.where(here, column, 0.0), axis=0, keepdims=True)

        def panel_of(which):
            return row(lax.dynamic_slice_in_dim(probe_right, which * panel, panel, 0))

        left_turned = (beta_decay * left_old).T

        def old_factors():
            def body(number, inputs, outputs):
                old = beta_decay * inputs[0][...]
                outputs[0][...], outputs[1][...] = halves(old)
                image = jnp.sum(old * inputs[1][...], axis=1, keepdims=True)
                outputs[2][:, :block] = image.T
                image = jnp.sum(inputs[2][...] * inputs[3][...], axis=1, keepdims=True)
                outputs[2][:, block:] = placed(number, image)

            own_probe = lax.dynamic_slice_in_dim(probe_left, model * model_rows, model_rows, 0)
            high, low, images = call(
                body,
                [((block, panel), bf16), ((block, panel), bf16), ((1, block + width), f32)],
                numbers,
                [right_old, panel_of(z * cores + core), left_turned, row(own_probe)],
            )
            *state["old"], images = yield 1, (high, low, images)
            state["old_images"] = yield from total(numbers, images, (LINE, CORE))

        def old_left():
            spot = lax.broadcasted_iota(jnp.int32, (own_rows, width), 1) // model_rows
            rows = jnp.where(spot == model, jnp.tile(left_turned, (1, models)), 0.0)
            (rows,) = yield 1, (rows,)
            state["old_left"] = yield from total(numbers, rows, (MP, PRE))

        def spread(array, axis, place, owner):
            result = None
            size = sizes[axis]
            for s in range(1, size):
                got = lax.ppermute(array, axis, [(i, (i + s) % size) for i in range(size)])
                if result is None:
                    result = got
                else:
                    result = jnp.where((place - s) % size == owner, got, result)
            return result

        def panel_piece(j):
            while len(own) <= j:
                yield 1, ()
            half = shape[0] // 2, panel
            upper, lower = gradient.parts[j]
            state["other", j], *got = yield 1, (
                to_partner(own[j]),
                spread(upper, PRE, y, owner_y),
                spread(lower, MP, x, owner_x),
            )
            held = chosen_sums(
                numbers,
                [
                    (number, {1: [(first, 0)], 0: [(second, 0)]})
                    for number, first, second in ((IN_Y, upper, got[0]), (IN_X, lower, got[1]))
                ],
                half,
            )
            *held, first, second = yield 1, (
                *held,
                spread(held[0], MP, x, owner_x),
                spread(held[1], PRE, y, owner_y),
            )

            def body(number, inputs, outputs):
                parts = []
                for i, which in enumerate((IN_X, IN_Y)):
                    here = jnp.full(half, number[which], jnp.int32) == 1
                    parts.append(jnp.where(here, inputs[i][...], inputs[2 + i][...]))
                pair = halves(jnp.concatenate(parts, axis=0))
                outputs[0][...], outputs[1][...] = pair
                both = product(pair, (inputs[4][...], inputs[5][...]), 1, 1)
                low, high = both[:, :panel], both[:, panel:]
                zeroth = jnp.full(shape, number[C], jnp.int32) == 0
                outputs[2][...] = jnp.where(zeroth, low, high)
                outputs[3][...] = jnp.where(zeroth, high, low)

            high, low, state["kept", j], away = call(
                body,
                [(shape, bf16), (shape, bf16), (shape, f32), (shape, f32)],
                numbers,
                [*held, first, second, *state["old"]],
            )
            state["swapped", j] = to_partner(away)
            state["panel", j] = yield 1, (high, low)

        def over_models(array):
            levels = max(len(bits(MP)), len(bits(PRE)))
            for step, ways in enumerate(((MP, PRE), (PRE, MP))):
                for level in range(levels):
                    got = []
                    for half, way in zip(array, ways):
                        if level < len(bits(way)):
                            got.append(swap(half, way, bits(way)[level]))
                        else:
                            got.append(jnp.zeros_like(half))
                    terms = yield 1, (*array, *got)
                    if step == 0 or level < levels - 1:
                        array = [added(numbers, terms[i::2]) for i in range(2)]
            return terms

        def joined_halves(inputs):
            return jnp.concatenate(
                [inputs[0][...] + inputs[2][...], inputs[1][...] + inputs[3][...]], axis=0
            )

        def first_part(crossed):
            crossed = yield from over_models(crossed)
            while "squares" not in state:
                yield 1, ()

            def body(number, sums, inputs, outputs):
                squares = jnp.concatenate([array[...] for array in inputs[8:]], axis=0)
                squares = jnp.sum(squares, axis=0, keepdims=True)
                outputs[1][...] = squares
                top_left, top_right, scale = scales(squares)
                grad = inputs[6][...], inputs[7][...]
                rows = pl.ds(pl.multiple_of(device(number) * own_rows, own_rows), own_rows)
                own = whole_of(inputs[6][rows, :], inputs[7][rows, :])
                crossed = product(halves(joined_halves(inputs)), grad, 1, 0)
                outputs[0][...] = scale * (
                    25.0 * own
                    - inputs[4][...] * (5.0 / top_left)
                    - (5.0 * inputs[5][...] - crossed / top_left) / top_right
                )

            state["first_part"], state["total"] = yield 1, fetching(
                body,
                [((own_rows, block), f32), ((1, 128), f32)],
                numbers,
                [],
                shape,
                [*crossed, *state["left_parts"], *state["block"], *state["squares"]],
            )

        def left_side():
            while ("other", last) not in state:
                yield 1, ()

            def body(number, inputs, outputs):
                zeroth = jnp.full(shape, number[C], jnp.int32) == 0
                for j in range(count):
                    mine, other = inputs[j][...], inputs[count + j][...]
                    rows = pl.ds(j * piece, piece)
                    for i, part in enumerate(
                        (jnp.where(zeroth, mine, other), jnp.where(zeroth, other, mine))
                    ):
                        columns = pl.ds(i * panel, panel)
                        outputs[0][rows, columns], outputs[1][rows, columns] = halves(part)
                rows = pl.ds(pl.multiple_of(device(number) * own_rows, own_rows), own_rows)
                gram = product(
                    (outputs[0][rows, :], outputs[1][rows, :]),
                    (outputs[0][...], outputs[1][...]),
                    1,
                    1,
                )
                outputs[2][...] = gram[: own_rows // 2] / hidden
                outputs[3][...] = gram[own_rows // 2 :] / hidden

            half = (own_rows // 2, width)
            high, low, *gram = call(
                body,
                [((width, block), bf16)] * 2 + [(half, f32)] * 2,
                numbers,
                [*own, *(state["other", j] for j in range(count))],
            )
            state["block"] = high, low
            gram = yield from over_models(gram)

            def body(number, sums, inputs, outputs):
                gram = joined_halves(inputs)
                left = inputs[4][...] + gram
                outputs[0][...] = left
                grad = inputs[5][...], inputs[6][...]
                left_grad = product(halves(left), grad, 1, 0)
                outputs[1][...] = left_grad
                outputs[2][...] = product(halves(gram), grad, 1, 0) * (hidden / width)
                crossed = product(halves(left_grad), grad, 1, 1) / width
                outputs[3][...] = crossed[: own_rows // 2]
                outputs[4][...] = crossed[own_rows // 2 :]

            rows = (own_rows, width)
            left, left_grad, gram_grad, *crossed = fetching(
                body,
                [(rows, f32), ((own_rows, block), f32), ((own_rows, block), f32)]
                + [(half, f32)] * 2,
                numbers,
                [],
                shape,
                [*gram, state["old_left"], *state["block"]],
            )
            state["left_parts"] = left_grad, gram_grad
            state["left"] = left
            windows.add(first_part(crossed))
            (state["partner_left"],) = yield 1, (to_partner(left),)
            options = {
                m: left[:, m * model_rows : (m + 1) * model_rows] for m in range(models)
            }
            (state["left_new"],) = yield 1, (select_by(model, options).T,)

        def powers():
            while len(own) < count:
                yield 1, ()

            def body(number, inputs, outputs):
                right, left = inputs[count][...], inputs[count + 1][...].T
                across = jnp.zeros((1, panel), f32)
                for j in range(count):
                    rows = slice(j * piece, (j + 1) * piece)
                    across += jnp.sum(inputs[j][...] * left[rows], axis=0, keepdims=True)
                for i, vector in enumerate((right, across)):
                    for j in range(count):
                        image = jnp.sum(inputs[j][...] * vector, axis=1, keepdims=True)
                        at = i * width + j * piece
                        outputs[0][:, at : at + piece] = image.T
                outputs[0][:, width:] += (hidden / cores) * inputs[count + 2][:, block:]

            (images,) = call(
                body,
                [((1, 2 * width), f32)],
                numbers,
                [
                    *own,
                    panel_of(model * cores + core),
                    row(probe_left),
                    state["old_images"],
                ],
            )
            images = yield from total(numbers, images, (CORE,))
            images = yield 1, from_all(images, (MP, PRE))
            while "block" not in state:
                yield 1, ()

            def body(number, inputs, outputs):
                images = inputs[5][...]
                for array in inputs[6:]:
                    images = images + array[...]
                outputs[1][...] = images[:, width:] / hidden
                grad = whole_of(inputs[1][...], inputs[2][...])
                first = inputs[0][:, :block] + (
                    jnp.sum(grad * images[:, :width].T, axis=0, keepdims=True) / width
                )
                outputs[0][:, :width] = jnp.sum(grad * first, axis=1, keepdims=True).T
                old = whole_of(inputs[3][...], inputs[4][...])
                outputs[0][:, width : width + panel] = jnp.sum(
                    old * first.T, axis=0, keepdims=True
                )
                square = jnp.sum(first * first, axis=1, keepdims=True)
                outputs[0][:, width + panel :] = jnp.broadcast_to(square, (1, 128))

            joined, first = call(
                body,
                [((1, width + panel + 128), f32), ((1, width), f32)],
                numbers,
                [state["old_images"], *state["block"], *state["old"], *images],
            )
            first, *joined = yield 1, (first, *from_all(joined, (MP, PRE)))
            while "left" not in state or ("panel", last) not in state:
                yield 1, ()

            def body(number, inputs, outputs):
                joined = inputs[2 + 2 * count][...]
                for array in inputs[3 + 2 * count :]:
                    joined = joined + array[...]
                vector = joined[:, :width].T
                second = joined[:, width : width + panel]
                for j in range(count):
                    part = whole_of(inputs[2 + 2 * j][...], inputs[3 + 2 * j][...])
                    rows = vector[j * piece : (j + 1) * piece]
                    second = second + jnp.sum(part * rows, axis=0, keepdims=True) / width
                square = joined[:, width + panel : width + panel + 1]
                second = second / jnp.sqrt(square + norm_floor)
                right = jnp.sum(second * second, axis=1, keepdims=True)
                first = inputs[0][...]
                unit = first / jnp.sqrt(
                    jnp.sum(first * first, axis=1, keepdims=True) + norm_floor
                )
                second = jnp.sum(inputs[1][...] * unit, axis=1, keepdims=True)
                left = jnp.sum(second * second, axis=0, keepdims=True)
                spot = lax.broadcasted_iota(jnp.int32, (1, 128), 1)
                outputs[0][...] = jnp.where(spot == 0, left, right)

            panels = [half for j in range(count) for half in state["panel", j]]
            (squares,) = call(
                body,
                [((1, 128), f32)],
                numbers,
                [first, state["left"], *panels, *joined],
            )
            (squares,) = yield 1, (squares,)
            state["squares"] = yield 1, from_all(squares, (LINE, CORE))

        def scales(squares):
            top = jnp.sqrt(squares + norm_floor)
            top_left, top_right = top[:, 0:1], top[:, 1:2]
            return top_left, top_right, 1.0 / (16.0 * jnp.sqrt(jnp.sqrt(top_left * top_right)))

        def right_factor():
            while ("panel", last) not in state or "block" not in state or windows.now < 2 * steps - 1:
                yield 1, ()

            def body(number, sums, inputs, outputs):
                pair = [
                    jnp.concatenate([inputs[3 + 2 * j + i][...] for j in range(count)], axis=0)
                    for i in range(2)
                ]
                gram = product((inputs[1][...], inputs[2][...]), pair, 0, 0)
                outputs[0][...] = beta_decay * inputs[0][...] + gram / width

            panels = [half for j in range(count) for half in state["panel", j]]
            (state["right_new"],) = yield 1, fetching(
                body,
                [((block, panel), f32)],
                numbers,
                [],
                shape,
                [right_old, *state["block"], *panels],
                44,
            )

        windows.add(old_factors())
        windows.add(old_left())
        for j in range(count):
            windows.add(panel_piece(j))
        steps = count + line - 2
        for process in (left_side, powers, right_factor):
            windows.add(process())

        going = gradient.combine(0)
        for t in range(2 * steps):
            current = gradient if t < steps else mixed
            current.send(*going)
            gradient.finish(t)
            mixed.finish(t - steps)
            windows.open()
            if t + 1 < steps:
                going = gradient.combine(t + 1)
            elif t + 1 < 2 * steps:
                going = mixed.combine(t + 1 - steps)
            else:
                going = ()
            *going, current.out[-1], current.home[-1] = windows.close(
                *going, current.out[-1], current.home[-1]
            )
        mixed.finish(steps)
        while windows.processes:
            windows.open()
            if windows.processes:
                windows.close()

        def body(number, sums, inputs, outputs):
            top_left, top_right, scale = scales(inputs[0][...])
            pair = halves(jnp.concatenate([array[...] for array in sums], axis=0))
            for i in range(2):
                other = number[C] if i == 0 else 1 - number[C]
                at = number[Z] * cores + other
                rows = sums[0][:own_rows]
                for k in range(1, line * cores):
                    j, start = divmod(k * own_rows, piece)
                    here = jnp.full((own_rows, panel), at, jnp.int32) == k
                    rows = jnp.where(here, sums[j][start : start + own_rows], rows)
                left = product(halves(inputs[1 + i][...]), pair, 1, 0)
                outputs[i][...] = (left / top_left - 5.0 * rows) * (scale / top_right)

        mine, theirs = fetching(
            body,
            [((own_rows, panel), f32)] * 2,
            numbers,
            mixed.options,
            shape,
            [state["total"], state["left"], state["partner_left"]],
            32,
        )
        theirs = to_partner(theirs)

        def body(number, inputs, outputs):
            zeroth = jnp.full((own_rows, panel), number[C], jnp.int32) == 0
            mine, theirs = inputs[1][...], inputs[2][...]
            parts = jnp.where(zeroth, mine, theirs), jnp.where(zeroth, theirs, mine)
            for i, part in enumerate(parts):
                span = pl.ds(i * panel, panel)
                outputs[0][:, span] = inputs[0][:, span] + part

        (update,) = call(
            body, [((own_rows, block), f32)], numbers, [state["first_part"], mine, theirs]
        )
        return state["left_new"], state["right_new"], update

    return shards


def solution(mesh):
    dp, mp, pre = (mesh.shape[name] for name in ("dp", "mp", "pre"))
    cores = dp // (mp * pre)
    assert cores == 2
    split = Mesh(mesh.devices.reshape(dp // cores, cores, mp, pre), AXES)
    factor = P((MP, PRE), (LINE, CORE))
    in_specs = (
        P((LINE, CORE), None),
        P((LINE, CORE), (MP, PRE)),
        factor,
        factor,
        P(),
        P(),
    )
    out_specs = (factor, factor, P((LINE, CORE), (MP, PRE)))
    return jax.shard_map(
        make_step(dict(split.shape)),
        mesh=split,
        in_specs=in_specs,
        out_specs=out_specs,
        check_vma=False,
    )
```

```python
import jax
import jax.numpy as jnp
from jax import lax
from jax.experimental import pallas as pl
from jax.experimental.pallas import tpu as pltpu
from jax.sharding import Mesh, PartitionSpec as P

beta_decay = 0.9
norm_floor = 1e-06
count = 4

LINE, CORE, MP, PRE = "line", "core", "mp", "pre"
AXES = (LINE, CORE, MP, PRE)
f32, bf16 = jnp.float32, jnp.bfloat16


def halves(x):
    high = x.astype(bf16)
    return high, (x - high.astype(f32)).astype(bf16)


def whole_of(high, low):
    return high.astype(f32) + low.astype(f32)


def product(a, b, a_dim, b_dim):
    def one(x, y):
        return lax.dot_general(
            x, y, (((a_dim,), (b_dim,)), ((), ())), preferred_element_type=f32
        )

    return one(a[0], b[0]) + (one(a[0], b[1]) + one(a[1], b[0]))


def select_by(index, options):
    result = None
    for value, array in options.items():
        result = array if result is None else jnp.where(index == value, array, result)
    return result


def tie(values):
    return lax.optimization_barrier(tuple(values))


def call(body, outputs, numbers, arrays, space=pltpu.VMEM, scratch=(), mebibytes=32):
    inputs, results = len(arrays), len(outputs)

    def kernel(*refs):
        body(
            refs[0],
            refs[1 : 1 + inputs],
            refs[1 + inputs : 1 + inputs + results],
            *refs[1 + inputs + results :],
        )

    return pl.pallas_call(
        kernel,
        out_shape=[jax.ShapeDtypeStruct(shape, dtype) for shape, dtype in outputs],
        in_specs=[pl.BlockSpec(memory_space=pltpu.SMEM)]
        + [pl.BlockSpec(memory_space=space)] * inputs,
        out_specs=[pl.BlockSpec(memory_space=pltpu.VMEM)] * results,
        scratch_shapes=scratch,
        compiler_params=pltpu.CompilerParams(vmem_limit_bytes=mebibytes << 20),
        cost_estimate=pl.CostEstimate(flops=1, bytes_accessed=1, transcendentals=0),
    )(numbers, *arrays)


def added(numbers, arrays):
    def body(number, inputs, outputs):
        total = inputs[0][...]
        for array in inputs[1:]:
            total = total + array[...]
        outputs[0][...] = total

    return call(body, [(arrays[0].shape, f32)], numbers, arrays)[0]


def fetching(body, outputs, numbers, choices, shape, arrays=(), mebibytes=24):
    sources = []

    def place(array):
        for i, known in enumerate(sources):
            if known is array:
                return i
        sources.append(array)
        return len(sources) - 1

    choices = [
        (which, {k: [(place(a), r) for a, r in terms] for k, terms in options.items()})
        for which, options in choices
    ]
    wholes = [place(array) for array in arrays]
    most = max([len(t) for _, options in choices for t in options.values()] + [1])
    many = max(len(choices), 1)

    def inner(number, inputs, results, held, sems, *kept):
        kept, kept_sems = kept[:-1], kept[-1]

        def copies(o, terms):
            return [
                pltpu.make_async_copy(
                    inputs[a].at[pl.ds(r, shape[0])], held.at[o, i], sems.at[o, i]
                )
                for i, (a, r) in enumerate(terms)
            ]

        loads = [
            pltpu.make_async_copy(inputs[a], kept[i], kept_sems.at[i])
            for i, a in enumerate(wholes)
        ]
        for o, (which, options) in enumerate(choices):
            for k, terms in options.items():

                @pl.when(number[which] == k)
                def _():
                    for copy in copies(o, terms):
                        copy.start()

        for copy in loads:
            copy.start()
        for o, (which, options) in enumerate(choices):
            for k, terms in options.items():

                @pl.when(number[which] == k)
                def _():
                    for copy in copies(o, terms):
                        copy.wait()
                    if not terms:
                        held[o, 0] = jnp.zeros(shape, f32)
                    if len(terms) > 1:
                        total = held[o, 0]
                        for i in range(1, len(terms)):
                            total = total + held[o, i]
                        held[o, 0] = total

        for copy in loads:
            copy.wait()
        body(number, [held.at[o, 0] for o in range(len(choices))], kept, results)

    return call(
        inner,
        outputs,
        numbers,
        sources,
        pl.ANY,
        [
            pltpu.VMEM((many, most) + tuple(shape), f32),
            pltpu.SemaphoreType.DMA((many, most)),
            *[pltpu.VMEM(array.shape, array.dtype) for array in arrays],
            pltpu.SemaphoreType.DMA((max(len(arrays), 1),)),
        ],
        mebibytes,
    )


def chosen_sums(numbers, choices, shape, more=0):
    def body(number, sums, inputs, outputs):
        for result, total in zip(outputs, sums):
            result[: shape[0]] = total[...]
            if more:
                result[shape[0] :] = jnp.zeros((more,) + shape[1:], f32)

    out = [((shape[0] + more,) + shape[1:], f32)] * len(choices)
    return fetching(body, out, numbers, choices, shape)


class Windows:
    def __init__(self):
        self.now = 0
        self.processes = []

    def add(self, process):
        self.processes.append([process, None, None])

    def open(self):
        ended = []
        for entry in self.processes:
            process, due, values = entry
            if values and due >= self.now:
                continue
            try:
                windows, entry[2] = process.send(values)
                entry[1] = self.now + windows - 1
            except StopIteration:
                ended.append(entry)
        for entry in ended:
            self.processes.remove(entry)

    def close(self, *others):
        due = [entry for entry in self.processes if entry[1] == self.now and entry[2]]
        flat = list(others)
        for entry in due:
            flat.extend(entry[2])
        if flat:
            flat = list(tie(flat))
        at = len(others)
        for entry in due:
            size = len(entry[2])
            entry[2] = flat[at : at + size]
            at += size
        self.now += 1
        return flat[: len(others)]


def make_step(sizes):
    line, cores, mp, pre = (sizes[name] for name in AXES)
    models = mp * pre
    last = count - 1

    def swap(array, axis, bit):
        return lax.ppermute(array, axis, [(i, i ^ bit) for i in range(sizes[axis])])

    def bits(axis):
        return [1 << i for i in range(sizes[axis].bit_length() - 1)]

    def total(numbers, array, axes):
        for axis in axes:
            for bit in bits(axis):
                pair = yield 1, (array, swap(array, axis, bit))
                array = added(numbers, pair)
        return array

    def from_all(array, axes):
        size = 1
        for axis in axes:
            size *= sizes[axis]
        return [array] + [
            lax.ppermute(array, axes, [(i, (i + s) % size) for i in range(size)])
            for s in range(1, size)
        ]

    def snake(array, outward):
        pairs = []
        for z in range(line):
            for c in range(cores):
                goal = z + (1 if (c == 0) == outward else -1)
                if 0 <= goal < line:
                    pairs.append((z * cores + c, goal * cores + c))
                else:
                    pairs.append((z * cores + c, z * cores + 1 - c))
        return lax.ppermute(array, (LINE, CORE), pairs)

    def shards(activations, grad_output, left_old, right_old, probe_left, probe_right):
        z, core = lax.axis_index(LINE), lax.axis_index(CORE)
        x, y = lax.axis_index(MP), lax.axis_index(PRE)
        model = x * pre + y
        width = activations.shape[1]
        block = grad_output.shape[1]
        hidden = block * models
        panel = block // cores
        own_rows = width // (line * cores)
        model_rows = width // models
        piece = width // count
        owner_x, owner_y = z // pre, z % pre
        there = jnp.where(core == 0, z, line - 1 - z)
        numbers = jnp.stack(
            [z, core, there, line - 1 - there, x == owner_x, y == owner_y]
        ).astype(jnp.int32)
        Z, C, THERE, BACK, IN_X, IN_Y = range(6)
        shape = (piece, panel)
        windows = Windows()
        state = {}

        def to_partner(array):
            return swap(array, CORE, 1)

        def device(number):
            return number[Z] * cores + number[C]

        def local(first, end):
            rows = (end - first) * piece
            tokens = activations.shape[0]

            def body(number, inputs, outputs, left, right, sems):
                copies = (
                    pltpu.make_async_copy(
                        inputs[0].at[:, pl.ds(first * piece, rows)], left, sems.at[0]
                    ),
                    pltpu.make_async_copy(inputs[1], right, sems.at[1]),
                )
                for copy in copies:
                    copy.start()
                for copy in copies:
                    copy.wait()
                zeroth = jnp.full(shape, number[C], jnp.int32) == 0
                for j in range(end - first):
                    both = lax.dot_general(
                        left[:, j * piece : (j + 1) * piece],
                        right[...],
                        (((0,), (0,)), ((), ())),
                        preferred_element_type=f32,
                    )
                    low, high = both[:, :panel], both[:, panel:]
                    outputs[0][j * piece : (j + 1) * piece] = jnp.where(zeroth, low, high)
                    outputs[1 + j][...] = jnp.where(zeroth, high, low)

            return call(
                body,
                [((rows, panel), f32)] + [(shape, f32)] * (end - first),
                numbers,
                [activations, grad_output],
                pl.ANY,
                [
                    pltpu.VMEM((tokens, rows), bf16),
                    pltpu.VMEM(grad_output.shape, bf16),
                    pltpu.SemaphoreType.DMA((2,)),
                ],
            )

        kept_first, away = local(0, 1)
        arrived = [to_partner(away)]
        kept_first, first_arrived, left_old, right_old = tie(
            (kept_first, arrived[0], left_old, right_old)
        )
        kept_rest, *away = local(1, count)
        arrived = [first_arrived] + [to_partner(a) for a in away]

        class Chain:
            def __init__(self, terms, halved=False):
                self.terms, self.halved = terms, halved
                self.sent, self.out, self.home = [], [], []
                self.options, self.wholes, self.parts = [], [], []

            def combine(self, t):
                wanted = []
                for which, got in ((THERE, self.out), (BACK, self.home)):
                    options = {}
                    for k in range(line):
                        options[k] = []
                        if 0 <= t - k < count:
                            options[k] = self.terms(t - k)
                            if k:
                                options[k] = options[k] + [(got[t - 1], 0)]
                    wanted.append((which, options))
                return chosen_sums(numbers, wanted, shape, 8)

            def send(self, going_out, going_home):
                self.sent.append(going_out)
                self.out.append(snake(going_out, True))
                self.home.append(snake(going_home, False))

            def finish(self, t):
                j = t - (line - 1)
                if not 0 <= j < count:
                    return
                options = {
                    k: [(self.sent[j + k], 0), (self.home[j + line - 2 - k], 0)]
                    for k in range(line - 1)
                }
                options[line - 1] = self.terms(j) + [(self.out[j + line - 2], 0)]
                self.options.append((THERE, options))
                if self.halved:
                    half = shape[0] // 2

                    def body(number, sums, inputs, outputs):
                        outputs[0][...] = sums[0][...]
                        outputs[1][...] = sums[0][:half]
                        outputs[2][...] = sums[0][half:]

                    whole, *parts = fetching(
                        body,
                        [(shape, f32)] + [((half, panel), f32)] * 2,
                        numbers,
                        self.options[-1:],
                        shape,
                    )
                    self.wholes.append(whole)
                    self.parts.append(parts)

        gradient = Chain(
            lambda j: [
                (kept_rest, (j - 1) * piece) if j else (kept_first, 0),
                (arrived[j], 0),
            ],
            True,
        )
        mixed = Chain(lambda j: [(state["kept", j], 0), (state["swapped", j], 0)])
        own = gradient.wholes

        def row(array):
            return array.reshape(1, -1)

        def exchange(array, axis):
            return total(numbers, array, (axis,))

        def placed(number, column):
            wide = (own_rows, width)
            at = lax.broadcasted_iota(jnp.int32, wide, 0) + device(number) * own_rows
            here = lax.broadcasted_iota(jnp.int32, wide, 1) == at
            return jnp.sum(jnp.where(here, column, 0.0), axis=0, keepdims=True)

        def panel_of(which):
            return row(lax.dynamic_slice_in_dim(probe_right, which * panel, panel, 0))

        left_turned = (beta_decay * left_old).T

        def old_factors():
            def body(number, inputs, outputs):
                old = beta_decay * inputs[0][...]
                outputs[0][...], outputs[1][...] = halves(old)
                image = jnp.sum(old * inputs[1][...], axis=1, keepdims=True)
                outputs[2][:, :block] = image.T
                image = jnp.sum(inputs[2][...] * inputs[3][...], axis=1, keepdims=True)
                outputs[2][:, block:] = placed(number, image)

            own_probe = lax.dynamic_slice_in_dim(probe_left, model * model_rows, model_rows, 0)
            high, low, images = call(
                body,
                [((block, panel), bf16), ((block, panel), bf16), ((1, block + width), f32)],
                numbers,
                [right_old, panel_of(z * cores + core), left_turned, row(own_probe)],
            )
            *state["old"], images = yield 1, (high, low, images)
            state["old_images"] = yield from total(numbers, images, (LINE, CORE))

        def old_left():
            spot = lax.broadcasted_iota(jnp.int32, (own_rows, width), 1) // model_rows
            rows = jnp.where(spot == model, jnp.tile(left_turned, (1, models)), 0.0)
            (rows,) = yield 1, (rows,)
            state["old_left"] = yield from total(numbers, rows, (MP, PRE))

        def spread(array, axis, place, owner):
            result = None
            size = sizes[axis]
            for s in range(1, size):
                got = lax.ppermute(array, axis, [(i, (i + s) % size) for i in range(size)])
                if result is None:
                    result = got
                else:
                    result = jnp.where((place - s) % size == owner, got, result)
            return result

        def panel_piece(j):
            while len(own) <= j:
                yield 1, ()
            half = shape[0] // 2, panel
            upper, lower = gradient.parts[j]
            state["other", j], *got = yield 1, (
                to_partner(own[j]),
                spread(upper, PRE, y, owner_y),
                spread(lower, MP, x, owner_x),
            )
            held = chosen_sums(
                numbers,
                [
                    (number, {1: [(first, 0)], 0: [(second, 0)]})
                    for number, first, second in ((IN_Y, upper, got[0]), (IN_X, lower, got[1]))
                ],
                half,
            )
            *held, first, second = yield 1, (
                *held,
                spread(held[0], MP, x, owner_x),
                spread(held[1], PRE, y, owner_y),
            )

            def body(number, inputs, outputs):
                parts = []
                for i, which in enumerate((IN_X, IN_Y)):
                    here = jnp.full(half, number[which], jnp.int32) == 1
                    parts.append(jnp.where(here, inputs[i][...], inputs[2 + i][...]))
                pair = halves(jnp.concatenate(parts, axis=0))
                outputs[0][...], outputs[1][...] = pair
                both = product(pair, (inputs[4][...], inputs[5][...]), 1, 1)
                low, high = both[:, :panel], both[:, panel:]
                zeroth = jnp.full(shape, number[C], jnp.int32) == 0
                outputs[2][...] = jnp.where(zeroth, low, high)
                outputs[3][...] = jnp.where(zeroth, high, low)

            high, low, state["kept", j], away = call(
                body,
                [(shape, bf16), (shape, bf16), (shape, f32), (shape, f32)],
                numbers,
                [*held, first, second, *state["old"]],
            )
            *state["panel", j], state["swapped", j] = yield 1, (high, low, to_partner(away))

        def over_models(array):
            levels = max(len(bits(MP)), len(bits(PRE)))
            for step, ways in enumerate(((MP, PRE), (PRE, MP))):
                for level in range(levels):
                    got = []
                    for half, way in zip(array, ways):
                        if level < len(bits(way)):
                            got.append(swap(half, way, bits(way)[level]))
                        else:
                            got.append(jnp.zeros_like(half))
                    terms = yield 1, (*array, *got)
                    if step == 0 or level < levels - 1:
                        array = [added(numbers, terms[i::2]) for i in range(2)]
            return terms

        def joined_halves(inputs):
            return jnp.concatenate(
                [inputs[0][...] + inputs[2][...], inputs[1][...] + inputs[3][...]], axis=0
            )

        def first_part(crossed):
            crossed = yield from over_models(crossed)
            while "squares" not in state:
                yield 1, ()

            def body(number, sums, inputs, outputs):
                squares = jnp.concatenate([array[...] for array in inputs[8:]], axis=0)
                squares = jnp.sum(squares, axis=0, keepdims=True)
                outputs[1][...] = squares
                top_left, top_right, scale = scales(squares)
                grad = inputs[6][...], inputs[7][...]
                rows = pl.ds(pl.multiple_of(device(number) * own_rows, own_rows), own_rows)
                own = whole_of(inputs[6][rows, :], inputs[7][rows, :])
                crossed = product(halves(joined_halves(inputs)), grad, 1, 0)
                outputs[0][...] = scale * (
                    25.0 * own
                    - inputs[4][...] * (5.0 / top_left)
                    - (5.0 * inputs[5][...] - crossed / top_left) / top_right
                )

            state["first_part"], state["total"] = yield 1, fetching(
                body,
                [((own_rows, block), f32), ((1, 128), f32)],
                numbers,
                [],
                shape,
                [*crossed, *state["left_parts"], *state["block"], *state["squares"]],
            )

        def left_side():
            while ("other", last) not in state:
                yield 1, ()

            def body(number, inputs, outputs):
                zeroth = jnp.full(shape, number[C], jnp.int32) == 0
                for j in range(count):
                    mine, other = inputs[j][...], inputs[count + j][...]
                    rows = pl.ds(j * piece, piece)
                    for i, part in enumerate(
                        (jnp.where(zeroth, mine, other), jnp.where(zeroth, other, mine))
                    ):
                        columns = pl.ds(i * panel, panel)
                        outputs[0][rows, columns], outputs[1][rows, columns] = halves(part)
                rows = pl.ds(pl.multiple_of(device(number) * own_rows, own_rows), own_rows)
                gram = product(
                    (outputs[0][rows, :], outputs[1][rows, :]),
                    (outputs[0][...], outputs[1][...]),
                    1,
                    1,
                )
                outputs[2][...] = gram[: own_rows // 2] / hidden
                outputs[3][...] = gram[own_rows // 2 :] / hidden

            half = (own_rows // 2, width)
            high, low, *gram = call(
                body,
                [((width, block), bf16)] * 2 + [(half, f32)] * 2,
                numbers,
                [*own, *(state["other", j] for j in range(count))],
            )
            state["block"] = high, low
            gram = yield from over_models(gram)

            def body(number, sums, inputs, outputs):
                gram = joined_halves(inputs)
                left = inputs[4][...] + gram
                outputs[0][...] = left
                grad = inputs[5][...], inputs[6][...]
                left_grad = product(halves(left), grad, 1, 0)
                outputs[1][...] = left_grad
                outputs[2][...] = product(halves(gram), grad, 1, 0) * (hidden / width)
                crossed = product(halves(left_grad), grad, 1, 1) / width
                outputs[3][...] = crossed[: own_rows // 2]
                outputs[4][...] = crossed[own_rows // 2 :]

            rows = (own_rows, width)
            left, left_grad, gram_grad, *crossed = fetching(
                body,
                [(rows, f32), ((own_rows, block), f32), ((own_rows, block), f32)]
                + [(half, f32)] * 2,
                numbers,
                [],
                shape,
                [*gram, state["old_left"], *state["block"]],
            )
            state["left_parts"] = left_grad, gram_grad
            state["left"] = left
            windows.add(first_part(crossed))
            (state["partner_left"],) = yield 1, (to_partner(left),)
            options = {
                m: left[:, m * model_rows : (m + 1) * model_rows] for m in range(models)
            }
            (state["left_new"],) = yield 1, (select_by(model, options).T,)

        def powers():
            while len(own) < count:
                yield 1, ()

            def body(number, inputs, outputs):
                right, left = inputs[count][...], inputs[count + 1][...].T
                across = jnp.zeros((1, panel), f32)
                for j in range(count):
                    rows = slice(j * piece, (j + 1) * piece)
                    across += jnp.sum(inputs[j][...] * left[rows], axis=0, keepdims=True)
                for i, vector in enumerate((right, across)):
                    for j in range(count):
                        image = jnp.sum(inputs[j][...] * vector, axis=1, keepdims=True)
                        at = i * width + j * piece
                        outputs[0][:, at : at + piece] = image.T
                outputs[0][:, width:] += (hidden / cores) * inputs[count + 2][:, block:]

            (images,) = call(
                body,
                [((1, 2 * width), f32)],
                numbers,
                [
                    *own,
                    panel_of(model * cores + core),
                    row(probe_left),
                    state["old_images"],
                ],
            )
            images = yield from total(numbers, images, (CORE,))
            images = yield 1, from_all(images, (MP, PRE))
            while "block" not in state:
                yield 1, ()

            def body(number, inputs, outputs):
                images = inputs[5][...]
                for array in inputs[6:]:
                    images = images + array[...]
                outputs[1][...] = images[:, width:] / hidden
                grad = whole_of(inputs[1][...], inputs[2][...])
                first = inputs[0][:, :block] + (
                    jnp.sum(grad * images[:, :width].T, axis=0, keepdims=True) / width
                )
                outputs[0][:, :width] = jnp.sum(grad * first, axis=1, keepdims=True).T
                old = whole_of(inputs[3][...], inputs[4][...])
                outputs[0][:, width : width + panel] = jnp.sum(
                    old * first.T, axis=0, keepdims=True
                )
                square = jnp.sum(first * first, axis=1, keepdims=True)
                outputs[0][:, width + panel :] = jnp.broadcast_to(square, (1, 128))

            joined, first = call(
                body,
                [((1, width + panel + 128), f32), ((1, width), f32)],
                numbers,
                [state["old_images"], *state["block"], *state["old"], *images],
            )
            first, *joined = yield 1, (first, *from_all(joined, (MP, PRE)))
            while "left" not in state or ("panel", last) not in state:
                yield 1, ()

            def body(number, inputs, outputs):
                joined = inputs[2 + 2 * count][...]
                for array in inputs[3 + 2 * count :]:
                    joined = joined + array[...]
                vector = joined[:, :width].T
                second = joined[:, width : width + panel]
                for j in range(count):
                    part = whole_of(inputs[2 + 2 * j][...], inputs[3 + 2 * j][...])
                    rows = vector[j * piece : (j + 1) * piece]
                    second = second + jnp.sum(part * rows, axis=0, keepdims=True) / width
                square = joined[:, width + panel : width + panel + 1]
                second = second / jnp.sqrt(square + norm_floor)
                right = jnp.sum(second * second, axis=1, keepdims=True)
                first = inputs[0][...]
                unit = first / jnp.sqrt(
                    jnp.sum(first * first, axis=1, keepdims=True) + norm_floor
                )
                second = jnp.sum(inputs[1][...] * unit, axis=1, keepdims=True)
                left = jnp.sum(second * second, axis=0, keepdims=True)
                spot = lax.broadcasted_iota(jnp.int32, (1, 128), 1)
                outputs[0][...] = jnp.where(spot == 0, left, right)

            panels = [half for j in range(count) for half in state["panel", j]]
            (squares,) = call(
                body,
                [((1, 128), f32)],
                numbers,
                [first, state["left"], *panels, *joined],
            )
            squares = added(numbers, (yield 1, (squares, to_partner(squares))))
            for bit in bits(LINE)[:-1]:
                squares = added(numbers, [squares, swap(squares, LINE, bit)])
            state["squares"] = yield 1, (squares, swap(squares, LINE, bits(LINE)[-1]))

        def scales(squares):
            top = jnp.sqrt(squares + norm_floor)
            top_left, top_right = top[:, 0:1], top[:, 1:2]
            return top_left, top_right, 1.0 / (16.0 * jnp.sqrt(jnp.sqrt(top_left * top_right)))

        def right_factor():
            while ("panel", last) not in state or "block" not in state or windows.now < 2 * steps - 1:
                yield 1, ()

            def body(number, sums, inputs, outputs):
                pair = [
                    jnp.concatenate([inputs[3 + 2 * j + i][...] for j in range(count)], axis=0)
                    for i in range(2)
                ]
                gram = product((inputs[1][...], inputs[2][...]), pair, 0, 0)
                outputs[0][...] = beta_decay * inputs[0][...] + gram / width

            panels = [half for j in range(count) for half in state["panel", j]]
            (state["right_new"],) = yield 1, fetching(
                body,
                [((block, panel), f32)],
                numbers,
                [],
                shape,
                [right_old, *state["block"], *panels],
                44,
            )

        windows.add(old_factors())
        windows.add(old_left())
        for j in range(count):
            windows.add(panel_piece(j))
        steps = count + line - 2
        for process in (left_side, powers, right_factor):
            windows.add(process())

        for t in range(2 * steps):
            windows.open()
            current = gradient if t < steps else mixed
            current.send(*current.combine(t % steps))
            gradient.finish(t)
            mixed.finish(t - steps)
            windows.open()
            current.out[-1], current.home[-1] = windows.close(current.out[-1], current.home[-1])
        mixed.finish(steps)
        while windows.processes:
            windows.open()
            if windows.processes:
                windows.close()

        def body(number, sums, inputs, outputs):
            top_left, top_right, scale = scales(inputs[0][...])
            pair = halves(jnp.concatenate([array[...] for array in sums], axis=0))
            for i in range(2):
                other = number[C] if i == 0 else 1 - number[C]
                at = number[Z] * cores + other
                rows = sums[0][:own_rows]
                for k in range(1, line * cores):
                    j, start = divmod(k * own_rows, piece)
                    here = jnp.full((own_rows, panel), at, jnp.int32) == k
                    rows = jnp.where(here, sums[j][start : start + own_rows], rows)
                left = product(halves(inputs[1 + i][...]), pair, 1, 0)
                outputs[i][...] = (left / top_left - 5.0 * rows) * (scale / top_right)

        mine, theirs = fetching(
            body,
            [((own_rows, panel), f32)] * 2,
            numbers,
            mixed.options,
            shape,
            [state["total"], state["left"], state["partner_left"]],
            32,
        )
        theirs = to_partner(theirs)

        def body(number, inputs, outputs):
            zeroth = jnp.full((own_rows, panel), number[C], jnp.int32) == 0
            mine, theirs = inputs[1][...], inputs[2][...]
            parts = jnp.where(zeroth, mine, theirs), jnp.where(zeroth, theirs, mine)
            for i, part in enumerate(parts):
                span = pl.ds(i * panel, panel)
                outputs[0][:, span] = inputs[0][:, span] + part

        (update,) = call(
            body, [((own_rows, block), f32)], numbers, [state["first_part"], mine, theirs]
        )
        return state["left_new"], state["right_new"], update

    return shards


def solution(mesh):
    dp, mp, pre = (mesh.shape[name] for name in ("dp", "mp", "pre"))
    cores = dp // (mp * pre)
    assert cores == 2
    split = Mesh(mesh.devices.reshape(dp // cores, cores, mp, pre), AXES)
    factor = P((MP, PRE), (LINE, CORE))
    in_specs = (
        P((LINE, CORE), None),
        P((LINE, CORE), (MP, PRE)),
        factor,
        factor,
        P(),
        P(),
    )
    out_specs = (factor, factor, P((LINE, CORE), (MP, PRE)))
    return jax.shard_map(
        make_step(dict(split.shape)),
        mesh=split,
        in_specs=in_specs,
        out_specs=out_specs,
        check_vma=False,
    )
```

```python
import jax
import jax.numpy as jnp
from jax import lax
from jax.experimental import pallas as pl
from jax.experimental.pallas import tpu as pltpu
from jax.sharding import Mesh, PartitionSpec as P

beta_decay = 0.9
norm_floor = 1e-06
count = 4

LINE, CORE, MP, PRE = "line", "core", "mp", "pre"
AXES = (LINE, CORE, MP, PRE)
f32, bf16 = jnp.float32, jnp.bfloat16


def halves(x):
    high = x.astype(bf16)
    return high, (x - high.astype(f32)).astype(bf16)


def whole_of(high, low):
    return high.astype(f32) + low.astype(f32)


def product(a, b, a_dim, b_dim):
    def one(x, y):
        return lax.dot_general(
            x, y, (((a_dim,), (b_dim,)), ((), ())), preferred_element_type=f32
        )

    return one(a[0], b[0]) + (one(a[0], b[1]) + one(a[1], b[0]))


def select_by(index, options):
    result = None
    for value, array in options.items():
        result = array if result is None else jnp.where(index == value, array, result)
    return result


def tie(values):
    return lax.optimization_barrier(tuple(values))


def call(body, outputs, numbers, arrays, space=pltpu.VMEM, scratch=(), mebibytes=32):
    inputs, results = len(arrays), len(outputs)

    def kernel(*refs):
        body(
            refs[0],
            refs[1 : 1 + inputs],
            refs[1 + inputs : 1 + inputs + results],
            *refs[1 + inputs + results :],
        )

    return pl.pallas_call(
        kernel,
        out_shape=[jax.ShapeDtypeStruct(shape, dtype) for shape, dtype in outputs],
        in_specs=[pl.BlockSpec(memory_space=pltpu.SMEM)]
        + [pl.BlockSpec(memory_space=space)] * inputs,
        out_specs=[pl.BlockSpec(memory_space=pltpu.VMEM)] * results,
        scratch_shapes=scratch,
        compiler_params=pltpu.CompilerParams(vmem_limit_bytes=mebibytes << 20),
        cost_estimate=pl.CostEstimate(flops=1, bytes_accessed=1, transcendentals=0),
    )(numbers, *arrays)


def added(numbers, arrays):
    def body(number, inputs, outputs):
        total = inputs[0][...]
        for array in inputs[1:]:
            total = total + array[...]
        outputs[0][...] = total

    return call(body, [(arrays[0].shape, f32)], numbers, arrays)[0]


def fetching(body, outputs, numbers, choices, shape, arrays=(), mebibytes=24):
    sources = []

    def place(array):
        for i, known in enumerate(sources):
            if known is array:
                return i
        sources.append(array)
        return len(sources) - 1

    choices = [
        (which, {k: [(place(a), r) for a, r in terms] for k, terms in options.items()})
        for which, options in choices
    ]
    wholes = [place(array) for array in arrays]
    most = max([len(t) for _, options in choices for t in options.values()] + [1])
    many = max(len(choices), 1)

    def inner(number, inputs, results, held, sems, *kept):
        kept, kept_sems = kept[:-1], kept[-1]

        def copies(o, terms):
            return [
                pltpu.make_async_copy(
                    inputs[a].at[pl.ds(r, shape[0])], held.at[o, i], sems.at[o, i]
                )
                for i, (a, r) in enumerate(terms)
            ]

        loads = [
            pltpu.make_async_copy(inputs[a], kept[i], kept_sems.at[i])
            for i, a in enumerate(wholes)
        ]
        for o, (which, options) in enumerate(choices):
            for k, terms in options.items():

                @pl.when(number[which] == k)
                def _():
                    for copy in copies(o, terms):
                        copy.start()

        for copy in loads:
            copy.start()
        for o, (which, options) in enumerate(choices):
            for k, terms in options.items():

                @pl.when(number[which] == k)
                def _():
                    for copy in copies(o, terms):
                        copy.wait()
                    if not terms:
                        held[o, 0] = jnp.zeros(shape, f32)
                    if len(terms) > 1:
                        total = held[o, 0]
                        for i in range(1, len(terms)):
                            total = total + held[o, i]
                        held[o, 0] = total

        for copy in loads:
            copy.wait()
        body(number, [held.at[o, 0] for o in range(len(choices))], kept, results)

    return call(
        inner,
        outputs,
        numbers,
        sources,
        pl.ANY,
        [
            pltpu.VMEM((many, most) + tuple(shape), f32),
            pltpu.SemaphoreType.DMA((many, most)),
            *[pltpu.VMEM(array.shape, array.dtype) for array in arrays],
            pltpu.SemaphoreType.DMA((max(len(arrays), 1),)),
        ],
        mebibytes,
    )


def chosen_sums(numbers, choices, shape, more=()):
    more = list(more) + [0] * (len(choices) - len(more))

    def body(number, sums, inputs, outputs):
        for result, total, rows in zip(outputs, sums, more):
            result[: shape[0]] = total[...]
            if rows:
                result[shape[0] :] = jnp.zeros((rows,) + shape[1:], f32)

    out = [((shape[0] + rows,) + shape[1:], f32) for rows in more]
    return fetching(body, out, numbers, choices, shape)


class Windows:
    def __init__(self):
        self.now = 0
        self.processes = []

    def add(self, process):
        self.processes.append([process, None, None])

    def open(self):
        ended = []
        for entry in self.processes:
            process, due, values = entry
            if values and due >= self.now:
                continue
            try:
                windows, entry[2] = process.send(values)
                entry[1] = self.now + windows - 1
            except StopIteration:
                ended.append(entry)
        for entry in ended:
            self.processes.remove(entry)

    def close(self, *others):
        due = [entry for entry in self.processes if entry[1] == self.now and entry[2]]
        flat = list(others)
        for entry in due:
            flat.extend(entry[2])
        if flat:
            flat = list(tie(flat))
        at = len(others)
        for entry in due:
            size = len(entry[2])
            entry[2] = flat[at : at + size]
            at += size
        self.now += 1
        return flat[: len(others)]


def make_step(sizes):
    line, cores, mp, pre = (sizes[name] for name in AXES)
    models = mp * pre
    last = count - 1

    def swap(array, axis, bit):
        return lax.ppermute(array, axis, [(i, i ^ bit) for i in range(sizes[axis])])

    def bits(axis):
        return [1 << i for i in range(sizes[axis].bit_length() - 1)]

    def total(numbers, array, axes):
        for axis in axes:
            for bit in bits(axis):
                pair = yield 1, (array, swap(array, axis, bit))
                array = added(numbers, pair)
        return array

    def snake(array, outward):
        pairs = []
        for z in range(line):
            for c in range(cores):
                goal = z + (1 if (c == 0) == outward else -1)
                if 0 <= goal < line:
                    pairs.append((z * cores + c, goal * cores + c))
                else:
                    pairs.append((z * cores + c, z * cores + 1 - c))
        return lax.ppermute(array, (LINE, CORE), pairs)

    def shards(activations, grad_output, left_old, right_old, probe_left, probe_right):
        z, core = lax.axis_index(LINE), lax.axis_index(CORE)
        x, y = lax.axis_index(MP), lax.axis_index(PRE)
        model = x * pre + y
        width = activations.shape[1]
        block = grad_output.shape[1]
        hidden = block * models
        panel = block // cores
        own_rows = width // (line * cores)
        model_rows = width // models
        piece = width // count
        owner_x, owner_y = z // pre, z % pre
        there = jnp.where(core == 0, z, line - 1 - z)
        numbers = jnp.stack(
            [z, core, there, line - 1 - there, x == owner_x, y == owner_y]
        ).astype(jnp.int32)
        Z, C, THERE, BACK, IN_X, IN_Y = range(6)
        shape = (piece, panel)
        windows = Windows()
        state = {}

        def to_partner(array):
            return swap(array, CORE, 1)

        def device(number):
            return number[Z] * cores + number[C]

        def local(first, end):
            rows = (end - first) * piece
            tokens = activations.shape[0]

            def body(number, inputs, outputs, left, right, sems):
                copies = (
                    pltpu.make_async_copy(
                        inputs[0].at[:, pl.ds(first * piece, rows)], left, sems.at[0]
                    ),
                    pltpu.make_async_copy(inputs[1], right, sems.at[1]),
                )
                for copy in copies:
                    copy.start()
                for copy in copies:
                    copy.wait()
                zeroth = jnp.full(shape, number[C], jnp.int32) == 0
                for j in range(end - first):
                    both = lax.dot_general(
                        left[:, j * piece : (j + 1) * piece],
                        right[...],
                        (((0,), (0,)), ((), ())),
                        preferred_element_type=f32,
                    )
                    low, high = both[:, :panel], both[:, panel:]
                    outputs[0][j * piece : (j + 1) * piece] = jnp.where(zeroth, low, high)
                    outputs[1 + j][...] = jnp.where(zeroth, high, low)

            return call(
                body,
                [((rows, panel), f32)] + [(shape, f32)] * (end - first),
                numbers,
                [activations, grad_output],
                pl.ANY,
                [
                    pltpu.VMEM((tokens, rows), bf16),
                    pltpu.VMEM(grad_output.shape, bf16),
                    pltpu.SemaphoreType.DMA((2,)),
                ],
                60,
            )

        kept_first, away = local(0, 1)
        arrived = [to_partner(away)]

        class Chain:
            def __init__(self, terms):
                self.terms = terms
                self.sent, self.out, self.home, self.options = [], [], [], []

            def next_sums(self, t):
                choices = []
                for which, got in ((THERE, self.out), (BACK, self.home)):
                    options = {}
                    for k in range(line):
                        options[k] = []
                        if 0 <= t - k < count:
                            options[k] = self.terms(t - k)
                            if k:
                                options[k] = options[k] + [(got[t - 1], 0)]
                    choices.append((which, options))
                return choices

            def send(self, going_out, going_home):
                self.sent.append(going_out)
                self.out.append(snake(going_out, True))
                self.home.append(snake(going_home, False))

            def finished(self, t):
                j = t - (line - 1)
                if not 0 <= j < count:
                    return []
                options = {
                    k: [(self.sent[j + k], 0), (self.home[j + line - 2 - k], 0)]
                    for k in range(line - 1)
                }
                options[line - 1] = self.terms(j) + [(self.out[j + line - 2], 0)]
                self.options.append((THERE, options))
                return self.options[-1:]

        gradient = Chain(
            lambda j: [
                (kept_rest[0], (j - 1) * piece) if j else (kept_first, 0),
                (arrived[j], 0),
            ]
        )
        mixed = Chain(lambda j: [(state["kept", j], 0), (state["swapped", j], 0)])
        own, wishes, kept_rest = [], [], []

        def row(array):
            return array.reshape(1, -1)

        def exchange(array, axis):
            return total(numbers, array, (axis,))

        def placed(number, column):
            wide = (own_rows, width)
            at = lax.broadcasted_iota(jnp.int32, wide, 0) + device(number) * own_rows
            here = lax.broadcasted_iota(jnp.int32, wide, 1) == at
            return jnp.sum(jnp.where(here, column, 0.0), axis=0, keepdims=True)

        def panel_of(which):
            return row(lax.dynamic_slice_in_dim(probe_right, which * panel, panel, 0))

        def left_turned():
            return (beta_decay * left_old).T

        def old_factors():
            def body(number, inputs, outputs):
                old = beta_decay * inputs[0][...]
                outputs[0][...], outputs[1][...] = halves(old)
                image = jnp.sum(old * inputs[1][...], axis=1, keepdims=True)
                outputs[2][:, :block] = image.T
                image = jnp.sum(inputs[2][...] * inputs[3][...], axis=1, keepdims=True)
                outputs[2][:, block:] = placed(number, image)

            own_probe = lax.dynamic_slice_in_dim(probe_left, model * model_rows, model_rows, 0)
            high, low, images = call(
                body,
                [((block, panel), bf16), ((block, panel), bf16), ((1, block + width), f32)],
                numbers,
                [right_old, panel_of(z * cores + core), left_turned(), row(own_probe)],
            )
            *state["old"], images = yield 1, (high, low, images)
            state["old_images"] = yield from total(numbers, images, (LINE, CORE))

        def old_left():
            spot = lax.broadcasted_iota(jnp.int32, (own_rows, width), 1) // model_rows
            rows = jnp.where(spot == model, jnp.tile(left_turned(), (1, models)), 0.0)
            (rows,) = yield 1, (rows,)
            state["old_left"] = yield from total(numbers, rows, (MP, PRE))

        def spread(array, axis, place, owner):
            result = None
            size = sizes[axis]
            for s in range(1, size):
                got = lax.ppermute(array, axis, [(i, (i + s) % size) for i in range(size)])
                if result is None:
                    result = got
                else:
                    result = jnp.where((place - s) % size == owner, got, result)
            return result

        def panel_piece(j):
            while len(own) <= j:
                yield 1, ()
            if j < depth:
                other, got = yield 1, (to_partner(own[j]), spread(own[j], PRE, y, owner_y))
                state["other", j] = other, 0
            else:
                (got,) = yield 1, (spread(own[j], PRE, y, owner_y),)
            wishes.append((("held", j), (IN_Y, {1: [(own[j], 0)], 0: [(got, 0)]})))
            while ("held", j) not in state:
                yield 1, ()
            held = state["held", j]
            held, got = yield 1, (held, spread(held, MP, x, owner_x))
            riders = []
            if j + depth < count:
                while len(own) <= j + depth:
                    yield 1, ()
                riders.append(own[j + depth])
            if j + depth == last:
                riders.append(first_images())

            def body(number, inputs, outputs):
                here = jnp.full(shape, number[IN_X], jnp.int32) == 1
                pair = halves(jnp.where(here, inputs[0][...], inputs[1][...]))
                outputs[0][...], outputs[1][...] = pair
                both = product(pair, (inputs[2][...], inputs[3][...]), 1, 1)
                low, high = both[:, :panel], both[:, panel:]
                zeroth = jnp.full(shape, number[C], jnp.int32) == 0
                outputs[2][...] = jnp.where(zeroth, low, high)
                outputs[3][:piece] = jnp.where(zeroth, high, low)
                at = piece
                for rider in inputs[4:]:
                    outputs[3][at : at + rider.shape[0]] = rider[...]
                    at += rider.shape[0]

            away_rows = piece + sum(rider.shape[0] for rider in riders)
            high, low, state["kept", j], away = call(
                body,
                [(shape, bf16), (shape, bf16), (shape, f32), ((away_rows, panel), f32)],
                numbers,
                [held, got, *state["old"], *riders],
            )
            *state["panel", j], got = yield 1, (high, low, to_partner(away))
            state["swapped", j] = got
            if j + depth < count:
                state["other", j + depth] = got, piece
            if j + depth == last:
                state["images"] = riders[-1], got, 2 * piece

        depth = 2
        image_rows = width // panel
        rider_rows = -(-2 * image_rows // 8) * 8

        def first_images():
            def body(number, inputs, outputs):
                right, left = inputs[count][...], inputs[count + 1][...].T
                across = jnp.zeros((1, panel), f32)
                for j in range(count):
                    rows = slice(j * piece, (j + 1) * piece)
                    across += jnp.sum(inputs[j][...] * left[rows], axis=0, keepdims=True)
                old = (hidden / cores) * inputs[count + 2][:, block:]
                outputs[0][...] = jnp.zeros((rider_rows, panel), f32)
                for i, vector in enumerate((right, across)):
                    image = jnp.concatenate(
                        [
                            jnp.sum(inputs[j][...] * vector, axis=1, keepdims=True).T
                            for j in range(count)
                        ],
                        axis=1,
                    )
                    if i:
                        image = image + old
                    for r in range(image_rows):
                        at = i * image_rows + r
                        outputs[0][at : at + 1] = image[:, r * panel : (r + 1) * panel]

            return call(
                body,
                [((rider_rows, panel), f32)],
                numbers,
                [
                    *own,
                    panel_of(model * cores + core),
                    row(probe_left),
                    state["old_images"],
                ],
            )[0]

        def over_models(array):
            steps = [(axis, bit) for axis in (PRE, MP) for bit in bits(axis)]
            for i, (axis, bit) in enumerate(steps):
                terms = yield 1, (array, swap(array, axis, bit))
                if i < len(steps) - 1:
                    array = added(numbers, terms)
            return terms

        def first_part(crossed):
            crossed = yield from over_models(crossed)
            while "squares" not in state:
                yield 1, ()

            def body(number, sums, inputs, outputs):
                squares = jnp.concatenate([array[...] for array in inputs[6:]], axis=0)
                squares = jnp.sum(squares, axis=0, keepdims=True)
                outputs[1][...] = squares
                top_left, top_right, scale = scales(squares)
                grad = inputs[4][...], inputs[5][...]
                rows = pl.ds(pl.multiple_of(device(number) * own_rows, own_rows), own_rows)
                own = whole_of(inputs[4][rows, :], inputs[5][rows, :])
                crossed = product(halves(inputs[0][...] + inputs[1][...]), grad, 1, 0)
                outputs[0][...] = scale * (
                    25.0 * own
                    - inputs[2][...] * (5.0 / top_left)
                    - (5.0 * inputs[3][...] - crossed / top_left) / top_right
                )

            state["first_part"], state["total"] = yield 1, fetching(
                body,
                [((own_rows, block), f32), ((1, 128), f32)],
                numbers,
                [],
                shape,
                [*crossed, *state["left_parts"], *state["block"], *state["squares"]],
            )

        def left_side():
            while ("other", last) not in state or "images" not in state:
                yield 1, ()
            other = [state["other", j] for j in range(count)]
            images, got, start = state["images"]

            def body(number, inputs, outputs):
                zeroth = jnp.full(shape, number[C], jnp.int32) == 0
                for j in range(count):
                    at = other[j][1]
                    mine, theirs = inputs[j][...], inputs[count + j][at : at + piece]
                    rows = pl.ds(j * piece, piece)
                    for i, part in enumerate(
                        (jnp.where(zeroth, mine, theirs), jnp.where(zeroth, theirs, mine))
                    ):
                        columns = pl.ds(i * panel, panel)
                        outputs[0][rows, columns], outputs[1][rows, columns] = halves(part)
                rows = pl.ds(pl.multiple_of(device(number) * own_rows, own_rows), own_rows)
                gram = product(
                    (outputs[0][rows, :], outputs[1][rows, :]),
                    (outputs[0][...], outputs[1][...]),
                    1,
                    1,
                )
                outputs[2][:own_rows] = gram / hidden
                outputs[2][own_rows:] = jnp.zeros((8, width), f32)
                images = inputs[2 * count][...] + inputs[2 * count + 1][start:]
                for i in range(2):
                    for r in range(image_rows):
                        at = i * image_rows + r
                        outputs[2][own_rows + i : own_rows + i + 1, pl.ds(r * panel, panel)] = (
                            images[at : at + 1]
                        )

            rows = (own_rows, width)
            high, low, gram = call(
                body,
                [((width, block), bf16)] * 2 + [((own_rows + 8, width), f32)],
                numbers,
                [*own, *(array for array, _ in other), images, got],
            )
            state["block"] = high, low
            gram = yield from over_models(gram)
            state["left_terms"] = gram

            def body(number, sums, inputs, outputs):
                gram = inputs[0][:own_rows] + inputs[1][:own_rows]
                left = inputs[2][...] + gram
                outputs[0][...] = left
                grad = inputs[3][...], inputs[4][...]
                left_grad = product(halves(left), grad, 1, 0)
                outputs[1][...] = left_grad
                outputs[2][...] = product(halves(gram), grad, 1, 0) * (hidden / width)
                outputs[3][...] = product(halves(left_grad), grad, 1, 1) / width

            left, left_grad, gram_grad, crossed = fetching(
                body,
                [(rows, f32), ((own_rows, block), f32), ((own_rows, block), f32), (rows, f32)],
                numbers,
                [],
                shape,
                [*gram, state["old_left"], *state["block"]],
            )
            state["left_parts"] = left_grad, gram_grad
            state["left"] = left
            windows.add(first_part(crossed))
            (state["partner_left"],) = yield 1, (to_partner(left),)
            options = {
                m: left[:, m * model_rows : (m + 1) * model_rows] for m in range(models)
            }
            (state["left_new"],) = yield 1, (select_by(model, options).T,)

        def powers():
            while "left_terms" not in state:
                yield 1, ()

            def body(number, inputs, outputs):
                images = inputs[5][own_rows:] + inputs[6][own_rows:]
                outputs[1][...] = images[1:2] / hidden
                grad = whole_of(inputs[1][...], inputs[2][...])
                first = inputs[0][:, :block] + (
                    jnp.sum(grad * images[0:1].T, axis=0, keepdims=True) / width
                )
                outputs[0][:, :width] = jnp.sum(grad * first, axis=1, keepdims=True).T
                old = whole_of(inputs[3][...], inputs[4][...])
                outputs[0][:, width : width + panel] = jnp.sum(
                    old * first.T, axis=0, keepdims=True
                )
                square = jnp.sum(first * first, axis=1, keepdims=True)
                outputs[0][:, width + panel :] = jnp.broadcast_to(square, (1, 128))

            joined, first = call(
                body,
                [((1, width + panel + 128), f32), ((1, width), f32)],
                numbers,
                [
                    state["old_images"],
                    *state["block"],
                    *state["old"],
                    *state["left_terms"],
                ],
            )
            for axis in (PRE, MP):
                for bit in bits(axis):
                    joined = added(numbers, [joined, swap(joined, axis, bit)])
            first, joined = yield 1, (first, joined)
            while "left" not in state or ("panel", last) not in state:
                yield 1, ()

            def body(number, inputs, outputs):
                joined = inputs[2 + 2 * count][...]
                for array in inputs[3 + 2 * count :]:
                    joined = joined + array[...]
                vector = joined[:, :width].T
                second = joined[:, width : width + panel]
                for j in range(count):
                    part = whole_of(inputs[2 + 2 * j][...], inputs[3 + 2 * j][...])
                    rows = vector[j * piece : (j + 1) * piece]
                    second = second + jnp.sum(part * rows, axis=0, keepdims=True) / width
                square = joined[:, width + panel : width + panel + 1]
                second = second / jnp.sqrt(square + norm_floor)
                right = jnp.sum(second * second, axis=1, keepdims=True)
                first = inputs[0][...]
                unit = first / jnp.sqrt(
                    jnp.sum(first * first, axis=1, keepdims=True) + norm_floor
                )
                second = jnp.sum(inputs[1][...] * unit, axis=1, keepdims=True)
                left = jnp.sum(second * second, axis=0, keepdims=True)
                spot = lax.broadcasted_iota(jnp.int32, (1, 128), 1)
                outputs[0][...] = jnp.where(spot == 0, left, right)

            panels = [half for j in range(count) for half in state["panel", j]]
            (squares,) = call(
                body,
                [((1, 128), f32)],
                numbers,
                [first, state["left"], *panels, joined],
            )
            squares = added(numbers, [squares, to_partner(squares)])
            for bit in bits(LINE)[:-1]:
                squares = added(numbers, [squares, swap(squares, LINE, bit)])
            state["squares"] = yield 1, (squares, swap(squares, LINE, bits(LINE)[-1]))

        def scales(squares):
            top = jnp.sqrt(squares + norm_floor)
            top_left, top_right = top[:, 0:1], top[:, 1:2]
            return top_left, top_right, 1.0 / (16.0 * jnp.sqrt(jnp.sqrt(top_left * top_right)))

        def right_factor():
            while ("panel", last) not in state or "block" not in state or windows.now < 2 * steps - 2:
                yield 1, ()

            def body(number, sums, inputs, outputs):
                pair = [
                    jnp.concatenate([inputs[3 + 2 * j + i][...] for j in range(count)], axis=0)
                    for i in range(2)
                ]
                gram = product((inputs[1][...], inputs[2][...]), pair, 0, 0)
                outputs[0][...] = beta_decay * inputs[0][...] + gram / width

            panels = [half for j in range(count) for half in state["panel", j]]
            (state["right_new"],) = yield 1, fetching(
                body,
                [((block, panel), f32)],
                numbers,
                [],
                shape,
                [right_old, *state["block"], *panels],
                44,
            )

        for j in range(count):
            windows.add(panel_piece(j))
        steps = count + line - 2
        for process in (left_side, powers, right_factor):
            windows.add(process())

        for t in range(2 * steps):
            windows.open()
            current = gradient if t < steps else mixed
            choices = current.next_sums(t % steps) + gradient.finished(t)
            mixed.finished(t - steps)
            names = [name for name, _ in wishes]
            choices += [choice for _, choice in wishes]
            wishes.clear()
            longer = 24 if steps < t < steps + 3 else 8
            results = list(chosen_sums(numbers, choices, shape, (longer, longer)))
            if t == 0:
                results[0], results[1], activations, grad_output, left_old, right_old = tie(
                    (*results, activations, grad_output, left_old, right_old)
                )
                windows.add(old_factors())
                windows.add(old_left())
                kept, *away = local(1, count)
                kept_rest.append(kept)
                arrived += [to_partner(a) for a in away]
            current.send(*results[:2])
            for name in reversed(names):
                state[name] = results.pop()
            own += results[2:]
            windows.open()
            current.out[-1], current.home[-1] = windows.close(current.out[-1], current.home[-1])
        mixed.finished(steps)
        while windows.processes:
            windows.open()
            if windows.processes:
                windows.close()

        def body(number, sums, inputs, outputs):
            top_left, top_right, scale = scales(inputs[0][...])
            pair = halves(jnp.concatenate([array[...] for array in sums], axis=0))
            for i in range(2):
                other = number[C] if i == 0 else 1 - number[C]
                at = number[Z] * cores + other
                rows = sums[0][:own_rows]
                for k in range(1, line * cores):
                    j, start = divmod(k * own_rows, piece)
                    here = jnp.full((own_rows, panel), at, jnp.int32) == k
                    rows = jnp.where(here, sums[j][start : start + own_rows], rows)
                left = product(halves(inputs[1 + i][...]), pair, 1, 0)
                outputs[i][...] = (left / top_left - 5.0 * rows) * (scale / top_right)

        mine, theirs = fetching(
            body,
            [((own_rows, panel), f32)] * 2,
            numbers,
            mixed.options,
            shape,
            [state["total"], state["left"], state["partner_left"]],
            32,
        )
        theirs = to_partner(theirs)

        def body(number, inputs, outputs):
            zeroth = jnp.full((own_rows, panel), number[C], jnp.int32) == 0
            mine, theirs = inputs[1][...], inputs[2][...]
            parts = jnp.where(zeroth, mine, theirs), jnp.where(zeroth, theirs, mine)
            for i, part in enumerate(parts):
                span = pl.ds(i * panel, panel)
                outputs[0][:, span] = inputs[0][:, span] + part

        (update,) = call(
            body, [((own_rows, block), f32)], numbers, [state["first_part"], mine, theirs]
        )
        return state["left_new"], state["right_new"], update

    return shards


def solution(mesh):
    dp, mp, pre = (mesh.shape[name] for name in ("dp", "mp", "pre"))
    cores = dp // (mp * pre)
    assert cores == 2
    split = Mesh(mesh.devices.reshape(dp // cores, cores, mp, pre), AXES)
    factor = P((MP, PRE), (LINE, CORE))
    in_specs = (
        P((LINE, CORE), None),
        P((LINE, CORE), (MP, PRE)),
        factor,
        factor,
        P(),
        P(),
    )
    out_specs = (factor, factor, P((LINE, CORE), (MP, PRE)))
    return jax.shard_map(
        make_step(dict(split.shape)),
        mesh=split,
        in_specs=in_specs,
        out_specs=out_specs,
        check_vma=False,
    )
```

```python
import jax
import jax.numpy as jnp
from jax import lax
from jax.experimental import pallas as pl
from jax.experimental.pallas import tpu as pltpu
from jax.sharding import Mesh, PartitionSpec as P

beta_decay = 0.9
norm_floor = 1e-06
count = 4

LINE, CORE, MP, PRE = "line", "core", "mp", "pre"
AXES = (LINE, CORE, MP, PRE)
f32, bf16 = jnp.float32, jnp.bfloat16


def halves(x):
    high = x.astype(bf16)
    return high, (x - high.astype(f32)).astype(bf16)


def whole_of(high, low):
    return high.astype(f32) + low.astype(f32)


def product(a, b, a_dim, b_dim):
    def one(x, y):
        return lax.dot_general(
            x, y, (((a_dim,), (b_dim,)), ((), ())), preferred_element_type=f32
        )

    return one(a[0], b[0]) + (one(a[0], b[1]) + one(a[1], b[0]))


def select_by(index, options):
    result = None
    for value, array in options.items():
        result = array if result is None else jnp.where(index == value, array, result)
    return result


def tie(values):
    return lax.optimization_barrier(tuple(values))


def call(body, outputs, numbers, arrays, space=pltpu.VMEM, scratch=(), mebibytes=32):
    inputs, results = len(arrays), len(outputs)

    def kernel(*refs):
        body(
            refs[0],
            refs[1 : 1 + inputs],
            refs[1 + inputs : 1 + inputs + results],
            *refs[1 + inputs + results :],
        )

    return pl.pallas_call(
        kernel,
        out_shape=[jax.ShapeDtypeStruct(shape, dtype) for shape, dtype in outputs],
        in_specs=[pl.BlockSpec(memory_space=pltpu.SMEM)]
        + [pl.BlockSpec(memory_space=space)] * inputs,
        out_specs=[pl.BlockSpec(memory_space=pltpu.VMEM)] * results,
        scratch_shapes=scratch,
        compiler_params=pltpu.CompilerParams(vmem_limit_bytes=mebibytes << 20),
        cost_estimate=pl.CostEstimate(flops=1, bytes_accessed=1, transcendentals=0),
    )(numbers, *arrays)


def added(numbers, arrays):
    def body(number, inputs, outputs):
        total = inputs[0][...]
        for array in inputs[1:]:
            total = total + array[...]
        outputs[0][...] = total

    return call(body, [(arrays[0].shape, f32)], numbers, arrays)[0]


def fetching(body, outputs, numbers, choices, shape, arrays=(), mebibytes=24):
    sources = []

    def place(array):
        for i, known in enumerate(sources):
            if known is array:
                return i
        sources.append(array)
        return len(sources) - 1

    choices = [
        (which, {k: [(place(a), r) for a, r in terms] for k, terms in options.items()})
        for which, options in choices
    ]
    wholes = [place(array) for array in arrays]
    most = max([len(t) for _, options in choices for t in options.values()] + [1])
    many = max(len(choices), 1)

    def inner(number, inputs, results, held, sems, *kept):
        kept, kept_sems = kept[:-1], kept[-1]

        def copies(o, terms):
            return [
                pltpu.make_async_copy(
                    inputs[a].at[pl.ds(r, shape[0])], held.at[o, i], sems.at[o, i]
                )
                for i, (a, r) in enumerate(terms)
            ]

        loads = [
            pltpu.make_async_copy(inputs[a], kept[i], kept_sems.at[i])
            for i, a in enumerate(wholes)
        ]
        for o, (which, options) in enumerate(choices):
            for k, terms in options.items():

                @pl.when(number[which] == k)
                def _():
                    for copy in copies(o, terms):
                        copy.start()

        for copy in loads:
            copy.start()
        for o, (which, options) in enumerate(choices):
            for k, terms in options.items():

                @pl.when(number[which] == k)
                def _():
                    for copy in copies(o, terms):
                        copy.wait()
                    if not terms:
                        held[o, 0] = jnp.zeros(shape, f32)
                    if len(terms) > 1:
                        total = held[o, 0]
                        for i in range(1, len(terms)):
                            total = total + held[o, i]
                        held[o, 0] = total

        for copy in loads:
            copy.wait()
        body(number, [held.at[o, 0] for o in range(len(choices))], kept, results)

    return call(
        inner,
        outputs,
        numbers,
        sources,
        pl.ANY,
        [
            pltpu.VMEM((many, most) + tuple(shape), f32),
            pltpu.SemaphoreType.DMA((many, most)),
            *[pltpu.VMEM(array.shape, array.dtype) for array in arrays],
            pltpu.SemaphoreType.DMA((max(len(arrays), 1),)),
        ],
        mebibytes,
    )


def chosen_sums(numbers, choices, shape, more=()):
    more = list(more) or [0] * len(choices)

    def body(number, sums, inputs, outputs):
        for result, total, rows in zip(outputs, sums, more):
            result[: shape[0]] = total[...]
            if rows:
                result[shape[0] :] = jnp.zeros((rows,) + shape[1:], f32)

    out = [((shape[0] + rows,) + shape[1:], f32) for rows in more]
    return fetching(body, out, numbers, choices, shape)


class Windows:
    def __init__(self):
        self.now = 0
        self.processes = []

    def add(self, process):
        self.processes.append([process, None, None])

    def open(self):
        ended = []
        for entry in self.processes:
            process, due, values = entry
            if values and due >= self.now:
                continue
            try:
                windows, entry[2] = process.send(values)
                entry[1] = self.now + windows - 1
            except StopIteration:
                ended.append(entry)
        for entry in ended:
            self.processes.remove(entry)

    def close(self, *others):
        due = [entry for entry in self.processes if entry[1] == self.now and entry[2]]
        flat = list(others)
        for entry in due:
            flat.extend(entry[2])
        if flat:
            flat = list(tie(flat))
        at = len(others)
        for entry in due:
            size = len(entry[2])
            entry[2] = flat[at : at + size]
            at += size
        self.now += 1
        return flat[: len(others)]


def make_step(sizes):
    line, cores, mp, pre = (sizes[name] for name in AXES)
    models = mp * pre
    last = count - 1

    def swap(array, axis, bit):
        return lax.ppermute(array, axis, [(i, i ^ bit) for i in range(sizes[axis])])

    def bits(axis):
        return [1 << i for i in range(sizes[axis].bit_length() - 1)]

    def total(numbers, array, axes):
        for axis in axes:
            for bit in bits(axis):
                pair = yield 1, (array, swap(array, axis, bit))
                array = added(numbers, pair)
        return array

    def snake(array, outward):
        pairs = []
        for z in range(line):
            for c in range(cores):
                goal = z + (1 if (c == 0) == outward else -1)
                if 0 <= goal < line:
                    pairs.append((z * cores + c, goal * cores + c))
                else:
                    pairs.append((z * cores + c, z * cores + 1 - c))
        return lax.ppermute(array, (LINE, CORE), pairs)

    def shards(activations, grad_output, left_old, right_old, probe_left, probe_right):
        z, core = lax.axis_index(LINE), lax.axis_index(CORE)
        x, y = lax.axis_index(MP), lax.axis_index(PRE)
        model = x * pre + y
        width = activations.shape[1]
        block = grad_output.shape[1]
        hidden = block * models
        panel = block // cores
        own_rows = width // (line * cores)
        model_rows = width // models
        piece = width // count
        owner_x, owner_y = z // pre, z % pre
        there = jnp.where(core == 0, z, line - 1 - z)
        numbers = jnp.stack(
            [z, core, there, line - 1 - there, x == owner_x, y == owner_y, model]
        ).astype(jnp.int32)
        Z, C, THERE, BACK, IN_X, IN_Y, MODEL = range(7)
        shape = (piece, panel)
        windows = Windows()
        state = {}

        def to_partner(array):
            return swap(array, CORE, 1)

        def device(number):
            return number[Z] * cores + number[C]

        def local(first, end):
            rows = (end - first) * piece
            tokens = activations.shape[0]

            parts = 4
            span = tokens // parts

            def body(number, inputs, outputs, left, right, sems):
                copies = []
                for i in range(parts):
                    at = pl.ds(i * span, span)
                    copies.append(
                        (
                            pltpu.make_async_copy(
                                inputs[0].at[at, pl.ds(first * piece, rows)],
                                left.at[at],
                                sems.at[0, i],
                            ),
                            pltpu.make_async_copy(
                                inputs[1].at[at], right.at[at], sems.at[1, i]
                            ),
                        )
                    )
                    for copy in copies[-1]:
                        copy.start()
                sums = [None] * (end - first)
                for i in range(parts):
                    for copy in copies[i]:
                        copy.wait()
                    at = slice(i * span, (i + 1) * span)
                    for j in range(end - first):
                        term = lax.dot_general(
                            left[at, j * piece : (j + 1) * piece],
                            right[at],
                            (((0,), (0,)), ((), ())),
                            preferred_element_type=f32,
                        )
                        sums[j] = term if i == 0 else sums[j] + term
                zeroth = jnp.full(shape, number[C], jnp.int32) == 0
                for j, both in enumerate(sums):
                    low, high = both[:, :panel], both[:, panel:]
                    outputs[0][j * piece : (j + 1) * piece] = jnp.where(zeroth, low, high)
                    outputs[1 + j][...] = jnp.where(zeroth, high, low)

            return call(
                body,
                [((rows, panel), f32)] + [(shape, f32)] * (end - first),
                numbers,
                [activations, grad_output],
                pl.ANY,
                [
                    pltpu.VMEM((tokens, rows), bf16),
                    pltpu.VMEM(grad_output.shape, bf16),
                    pltpu.SemaphoreType.DMA((2, parts)),
                ],
                60,
            )

        kept_first, away = local(0, 1)
        arrived = [to_partner(away)]

        class Chain:
            def __init__(self, terms):
                self.terms = terms
                self.sent, self.out, self.home, self.options = [], [], [], []

            def next_sums(self, t):
                choices = []
                for which, got in ((THERE, self.out), (BACK, self.home)):
                    options = {}
                    for k in range(line):
                        options[k] = []
                        if 0 <= t - k < count:
                            options[k] = self.terms(t - k)
                            if k:
                                options[k] = options[k] + [(got[t - 1], 0)]
                    choices.append((which, options))
                return choices

            def send(self, going_out, going_home):
                self.sent.append(going_out)
                self.out.append(snake(going_out, True))
                self.home.append(snake(going_home, False))

            def finished(self, t):
                j = t - (line - 1)
                if not 0 <= j < count:
                    return []
                options = {
                    k: [(self.sent[j + k], 0), (self.home[j + line - 2 - k], 0)]
                    for k in range(line - 1)
                }
                options[line - 1] = self.terms(j) + [(self.out[j + line - 2], 0)]
                self.options.append((THERE, options))
                return self.options[-1:]

        gradient = Chain(
            lambda j: [
                (kept_rest[0], (j - 1) * piece) if j else (kept_first, 0),
                (arrived[j], 0),
            ]
        )
        mixed = Chain(lambda j: [(state["kept", j], 0), (state["swapped", j], 0)])
        own, wishes, kept_rest = [], [], []

        def row(array):
            return array.reshape(1, -1)

        def exchange(array, axis):
            return total(numbers, array, (axis,))

        def placed(number, column):
            wide = (own_rows, width)
            at = lax.broadcasted_iota(jnp.int32, wide, 0) + device(number) * own_rows
            here = lax.broadcasted_iota(jnp.int32, wide, 1) == at
            return jnp.sum(jnp.where(here, column, 0.0), axis=0, keepdims=True)

        def panel_of(which):
            return row(lax.dynamic_slice_in_dim(probe_right, which * panel, panel, 0))

        def beside(first, second):
            def body(number, inputs, outputs):
                size = inputs[0].shape[1]
                outputs[0][:, :size] = inputs[0][...]
                outputs[0][:, size:] = inputs[1][...]

            shape = first.shape[0], first.shape[1] + second.shape[1]
            return call(body, [(shape, f32)], numbers, [first, second])[0]

        def left_turned():
            return (beta_decay * left_old).T

        def old_factors():
            def body(number, inputs, outputs):
                old = beta_decay * inputs[0][...]
                outputs[0][...], outputs[1][...] = halves(old)
                image = jnp.sum(old * inputs[1][...], axis=1, keepdims=True)
                outputs[2][:, :block] = image.T
                image = jnp.sum(inputs[2][...] * inputs[3][...], axis=1, keepdims=True)
                outputs[2][:, block:] = placed(number, image)

            own_probe = lax.dynamic_slice_in_dim(probe_left, model * model_rows, model_rows, 0)
            high, low, images = call(
                body,
                [((block, panel), bf16), ((block, panel), bf16), ((1, block + width), f32)],
                numbers,
                [right_old, panel_of(z * cores + core), left_turned(), row(own_probe)],
            )
            *state["old"], images = yield 1, (high, low, images)
            state["old_images"] = yield from total(numbers, images, (LINE, CORE))

        def old_left():
            rows = left_turned()
            for axis in (PRE, MP):
                for bit in bits(axis):
                    rows, got = yield 1, (rows, swap(rows, axis, bit))
                    rows = beside(rows, got)
            state["old_left"] = rows

        def spread(array, axis, place, owner):
            result = None
            size = sizes[axis]
            for s in range(1, size):
                got = lax.ppermute(array, axis, [(i, (i + s) % size) for i in range(size)])
                if result is None:
                    result = got
                else:
                    result = jnp.where((place - s) % size == owner, got, result)
            return result

        def panel_piece(j):
            while len(own) <= j:
                yield 1, ()
            if j < depth:
                other, got = yield 1, (to_partner(own[j]), spread(own[j], PRE, y, owner_y))
                state["other", j] = other, 0
            else:
                (got,) = yield 1, (spread(own[j], PRE, y, owner_y),)
            wishes.append((("held", j), (IN_Y, {1: [(own[j], 0)], 0: [(got, 0)]})))
            while ("held", j) not in state:
                yield 1, ()
            held = state["held", j]
            held, got = yield 1, (held, spread(held, MP, x, owner_x))
            riders = []
            if j + depth == last:
                while len(own) < count:
                    yield 1, ()
                riders = [*own[depth:], first_images()]

            def body(number, inputs, outputs):
                here = jnp.full(shape, number[IN_X], jnp.int32) == 1
                pair = halves(jnp.where(here, inputs[0][:piece], inputs[1][:piece]))
                outputs[0][...], outputs[1][...] = pair
                both = product(pair, (inputs[2][...], inputs[3][...]), 1, 1)
                low, high = both[:, :panel], both[:, panel:]
                zeroth = jnp.full(shape, number[C], jnp.int32) == 0
                outputs[2][...] = jnp.where(zeroth, low, high)
                outputs[3][:piece] = jnp.where(zeroth, high, low)
                at = piece
                for rider in inputs[4:]:
                    outputs[3][at : at + rider.shape[0]] = rider[...]
                    at += rider.shape[0]

            away_rows = piece + sum(rider.shape[0] for rider in riders)
            high, low, state["kept", j], away = call(
                body,
                [(shape, bf16), (shape, bf16), (shape, f32), ((away_rows, panel), f32)],
                numbers,
                [held, got, *state["old"], *riders],
            )
            *state["panel", j], got = yield 1, (high, low, to_partner(away))
            state["swapped", j] = got
            if riders:
                for i in range(depth, count):
                    state["other", i] = got, (i - depth + 1) * piece
                state["images"] = riders[-1], got, (count - depth + 1) * piece

        depth = 2
        image_rows = width // panel
        rider_rows = -(-2 * image_rows // 8) * 8

        def first_images():
            def body(number, inputs, outputs):
                right, left = inputs[count][...], inputs[count + 1][...].T
                across = jnp.zeros((1, panel), f32)
                for j in range(count):
                    rows = slice(j * piece, (j + 1) * piece)
                    across += jnp.sum(inputs[j][...] * left[rows], axis=0, keepdims=True)
                old = (hidden / cores) * inputs[count + 2][:, block:]
                outputs[0][...] = jnp.zeros((rider_rows, panel), f32)
                for i, vector in enumerate((right, across)):
                    image = jnp.concatenate(
                        [
                            jnp.sum(inputs[j][...] * vector, axis=1, keepdims=True).T
                            for j in range(count)
                        ],
                        axis=1,
                    )
                    if i:
                        image = image + old
                    for r in range(image_rows):
                        at = i * image_rows + r
                        outputs[0][at : at + 1] = image[:, r * panel : (r + 1) * panel]

            return call(
                body,
                [((rider_rows, panel), f32)],
                numbers,
                [
                    *own,
                    panel_of(model * cores + core),
                    row(probe_left),
                    state["old_images"],
                ],
            )[0]

        def over_models(array):
            steps = [(axis, bit) for axis in (PRE, MP) for bit in bits(axis)]
            for i, (axis, bit) in enumerate(steps):
                terms = yield 1, (array, swap(array, axis, bit))
                if i < len(steps) - 1:
                    array = added(numbers, terms)
            return terms

        def first_part(crossed):
            (crossed,) = yield 1, (crossed,)
            crossed = yield from over_models(crossed)
            while "squares" not in state:
                yield 1, ()

            def body(number, sums, inputs, outputs):
                top_left, top_right, scale = scales(inputs[6][...] + inputs[7][...])
                grad = inputs[4][...], inputs[5][...]
                rows = pl.ds(pl.multiple_of(device(number) * own_rows, own_rows), own_rows)
                own = whole_of(inputs[4][rows, :], inputs[5][rows, :])
                crossed = product(halves(inputs[0][...] + inputs[1][...]), grad, 1, 0)
                outputs[0][...] = scale * (
                    25.0 * own
                    - inputs[2][...] * (5.0 / top_left)
                    - (5.0 * inputs[3][...] - crossed / top_left) / top_right
                )

            (state["first_part"],) = fetching(
                body,
                [((own_rows, block), f32)],
                numbers,
                [],
                shape,
                [*crossed, *state["left_parts"], *state["block"], *state["squares"]],
            )

        def left_side():
            while ("other", last) not in state or "images" not in state:
                yield 1, ()
            other = [state["other", j] for j in range(count)]
            images, got, start = state["images"]

            def body(number, inputs, outputs):
                zeroth = jnp.full(shape, number[C], jnp.int32) == 0
                for j in range(count):
                    at = other[j][1]
                    mine, theirs = inputs[j][...], inputs[count + j][at : at + piece]
                    rows = pl.ds(j * piece, piece)
                    for i, part in enumerate(
                        (jnp.where(zeroth, mine, theirs), jnp.where(zeroth, theirs, mine))
                    ):
                        columns = pl.ds(i * panel, panel)
                        outputs[0][rows, columns], outputs[1][rows, columns] = halves(part)
                rows = pl.ds(pl.multiple_of(device(number) * own_rows, own_rows), own_rows)
                gram = product(
                    (outputs[0][rows, :], outputs[1][rows, :]),
                    (outputs[0][...], outputs[1][...]),
                    1,
                    1,
                )
                outputs[2][:own_rows] = gram / hidden
                outputs[2][own_rows:] = jnp.zeros((8, width), f32)
                images = inputs[2 * count][...] + inputs[2 * count + 1][start:]
                for i in range(2):
                    for r in range(image_rows):
                        at = i * image_rows + r
                        outputs[2][own_rows + i : own_rows + i + 1, pl.ds(r * panel, panel)] = (
                            images[at : at + 1]
                        )

            rows = (own_rows, width)
            high, low, gram = call(
                body,
                [((width, block), bf16)] * 2 + [((own_rows + 8, width), f32)],
                numbers,
                [*own, *(array for array, _ in other), images, got],
            )
            state["block"] = high, low
            gram = yield from over_models(gram)
            state["left_terms"] = gram

            def body(number, sums, inputs, outputs):
                gram = inputs[0][:own_rows] + inputs[1][:own_rows]
                old = []
                for m in range(models):
                    part = jnp.zeros((own_rows, model_rows), f32)
                    for k in range(models):
                        at = jnp.full(part.shape, number[MODEL], jnp.int32)
                        block_k = inputs[2][:, k * model_rows : (k + 1) * model_rows]
                        part = jnp.where(at == m ^ k, block_k, part)
                    old.append(part)
                left = jnp.concatenate(old, axis=1) + gram
                outputs[0][...] = left
                new = left[:, :model_rows]
                for m in range(1, models):
                    at = jnp.full(new.shape, number[MODEL], jnp.int32)
                    new = jnp.where(at == m, left[:, m * model_rows : (m + 1) * model_rows], new)
                outputs[4][...] = new.T
                grad = inputs[3][...], inputs[4][...]
                left_grad = product(halves(left), grad, 1, 0)
                outputs[1][...] = left_grad
                outputs[2][...] = product(halves(gram), grad, 1, 0) * (hidden / width)
                outputs[3][...] = product(halves(left_grad), grad, 1, 1) / width

            left, left_grad, gram_grad, crossed, new = fetching(
                body,
                [(rows, f32), ((own_rows, block), f32), ((own_rows, block), f32), (rows, f32)]
                + [((model_rows, own_rows), f32)],
                numbers,
                [],
                shape,
                [*gram, state["old_left"], *state["block"]],
            )
            state["left_parts"] = left_grad, gram_grad
            state["left"] = left
            windows.add(first_part(crossed))
            (state["partner_left"],) = yield 1, (to_partner(left),)
            state["left_new"] = new

        def powers():
            while "left_terms" not in state:
                yield 1, ()

            def body(number, inputs, outputs):
                images = inputs[5][own_rows:] + inputs[6][own_rows:]
                outputs[1][...] = images[1:2] / hidden
                grad = whole_of(inputs[1][...], inputs[2][...])
                first = inputs[0][:, :block] + (
                    jnp.sum(grad * images[0:1].T, axis=0, keepdims=True) / width
                )
                outputs[0][:, :width] = jnp.sum(grad * first, axis=1, keepdims=True).T
                old = whole_of(inputs[3][...], inputs[4][...])
                outputs[0][:, width : width + panel] = jnp.sum(
                    old * first.T, axis=0, keepdims=True
                )
                square = jnp.sum(first * first, axis=1, keepdims=True)
                outputs[0][:, width + panel :] = jnp.broadcast_to(square, (1, 128))

            joined, first = call(
                body,
                [((1, width + panel + 128), f32), ((1, width), f32)],
                numbers,
                [
                    state["old_images"],
                    *state["block"],
                    *state["old"],
                    *state["left_terms"],
                ],
            )
            for axis in (PRE, MP):
                for bit in bits(axis):
                    joined = added(numbers, [joined, swap(joined, axis, bit)])
            first, joined = yield 1, (first, joined)
            while "left" not in state or ("panel", last) not in state:
                yield 1, ()

            def body(number, inputs, outputs):
                joined = inputs[2 + 2 * count][...]
                for array in inputs[3 + 2 * count :]:
                    joined = joined + array[...]
                vector = joined[:, :width].T
                second = joined[:, width : width + panel]
                for j in range(count):
                    part = whole_of(inputs[2 + 2 * j][...], inputs[3 + 2 * j][...])
                    rows = vector[j * piece : (j + 1) * piece]
                    second = second + jnp.sum(part * rows, axis=0, keepdims=True) / width
                square = joined[:, width + panel : width + panel + 1]
                second = second / jnp.sqrt(square + norm_floor)
                right = jnp.sum(second * second, axis=1, keepdims=True)
                first = inputs[0][...]
                unit = first / jnp.sqrt(
                    jnp.sum(first * first, axis=1, keepdims=True) + norm_floor
                )
                second = jnp.sum(inputs[1][...] * unit, axis=1, keepdims=True)
                left = jnp.sum(second * second, axis=0, keepdims=True)
                spot = lax.broadcasted_iota(jnp.int32, (1, 128), 1)
                outputs[0][...] = jnp.where(spot == 0, left, right)

            panels = [half for j in range(count) for half in state["panel", j]]
            (squares,) = call(
                body,
                [((1, 128), f32)],
                numbers,
                [first, state["left"], *panels, joined],
            )
            squares = added(numbers, [squares, to_partner(squares)])
            for bit in bits(LINE)[:-1]:
                squares = added(numbers, [squares, swap(squares, LINE, bit)])
            state["squares"] = yield 1, (squares, swap(squares, LINE, bits(LINE)[-1]))

        def scales(squares):
            top = jnp.sqrt(squares + norm_floor)
            top_left, top_right = top[:, 0:1], top[:, 1:2]
            return top_left, top_right, 1.0 / (16.0 * jnp.sqrt(jnp.sqrt(top_left * top_right)))

        def right_factor():
            while ("panel", last) not in state or "block" not in state or windows.now < steps + 2:
                yield 1, ()

            def body(number, sums, inputs, outputs):
                pair = [
                    jnp.concatenate([inputs[3 + 2 * j + i][...] for j in range(count)], axis=0)
                    for i in range(2)
                ]
                gram = product((inputs[1][...], inputs[2][...]), pair, 0, 0)
                outputs[0][...] = beta_decay * inputs[0][...] + gram / width

            panels = [half for j in range(count) for half in state["panel", j]]
            (state["right_new"],) = yield 1, fetching(
                body,
                [((block, panel), f32)],
                numbers,
                [],
                shape,
                [right_old, *state["block"], *panels],
                44,
            )

        for j in range(count):
            windows.add(panel_piece(j))
        steps = count + line - 2
        def rows_here(number, i, rows, pieces):
            other = number[C] if i == 0 else 1 - number[C]
            at = jnp.full(rows.shape, number[Z] * cores + other, jnp.int32)
            for k in range(line * cores):
                j, start = divmod(k * own_rows, piece)
                for number_j, array in pieces:
                    if number_j == j:
                        rows = jnp.where(at == k, array[start : start + own_rows], rows)
            return rows

        def early_products():
            while len(mixed_wholes) < last or "partner_left" not in state:
                yield 1, ()

            def body(number, sums, inputs, outputs):
                pieces = [(j, inputs[2 + j]) for j in range(last)]
                pair = halves(jnp.concatenate([array[...] for _, array in pieces], axis=0))
                for i in range(2):
                    left = halves(inputs[i][:, : last * piece])
                    outputs[i][...] = product(left, pair, 1, 0)
                    outputs[2 + i][...] = rows_here(
                        number, i, jnp.zeros((own_rows, panel), f32), pieces
                    )

            state["early"] = yield 1, fetching(
                body,
                [((own_rows, panel), f32)] * 4,
                numbers,
                [],
                shape,
                [state["left"], state["partner_left"], *mixed_wholes],
            )

        mixed_wholes = []
        for process in (left_side, powers, right_factor, early_products):
            windows.add(process())

        for t in range(2 * steps):
            windows.open()
            current = gradient if t < steps else mixed
            choices = current.next_sums(t % steps) + gradient.finished(t)
            choices += mixed.finished(t - steps)
            names = [name for name, _ in wishes]
            choices += [choice for _, choice in wishes]
            wishes.clear()
            longer = 24 if steps < t < steps + 3 else 8
            extra = [longer] * 2 + [0] * (len(choices) - 2)
            if ("held", last) in names:
                extra[-1] = longer
            results = list(chosen_sums(numbers, choices, shape, extra))
            if t == 0:
                results[0], results[1], activations, grad_output, left_old, right_old = tie(
                    (*results, activations, grad_output, left_old, right_old)
                )
                windows.add(old_factors())
                windows.add(old_left())
                kept, *away = local(1, count)
                kept_rest.append(kept)
                arrived += [to_partner(a) for a in away]
            current.send(*results[:2])
            for name in reversed(names):
                state[name] = results.pop()
            (own if len(own) < count else mixed_wholes).extend(results[2:])
            windows.open()
            current.out[-1], current.home[-1] = windows.close(current.out[-1], current.home[-1])
        while windows.processes:
            windows.open()
            if windows.processes:
                windows.close()

        def body(number, sums, inputs, outputs):
            top_left, top_right, scale = scales(inputs[0][...] + inputs[1][...])
            pair = halves(sums[0][...])
            for i in range(2):
                rows = rows_here(number, i, inputs[6 + i][...], [(last, sums[0])])
                left = halves(inputs[2 + i][:, last * piece :])
                left = inputs[4 + i][...] + product(left, pair, 1, 0)
                outputs[i][...] = (left / top_left - 5.0 * rows) * (scale / top_right)

        mine, theirs = fetching(
            body,
            [((own_rows, panel), f32)] * 2,
            numbers,
            mixed.finished(steps),
            shape,
            [*state["squares"], state["left"], state["partner_left"], *state["early"]],
        )
        theirs = to_partner(theirs)

        def body(number, inputs, outputs):
            zeroth = jnp.full((own_rows, panel), number[C], jnp.int32) == 0
            mine, theirs = inputs[1][...], inputs[2][...]
            parts = jnp.where(zeroth, mine, theirs), jnp.where(zeroth, theirs, mine)
            for i, part in enumerate(parts):
                span = pl.ds(i * panel, panel)
                outputs[0][:, span] = inputs[0][:, span] + part

        (update,) = call(
            body, [((own_rows, block), f32)], numbers, [state["first_part"], mine, theirs]
        )
        return state["left_new"], state["right_new"], update

    return shards


def solution(mesh):
    dp, mp, pre = (mesh.shape[name] for name in ("dp", "mp", "pre"))
    cores = dp // (mp * pre)
    assert cores == 2
    split = Mesh(mesh.devices.reshape(dp // cores, cores, mp, pre), AXES)
    factor = P((MP, PRE), (LINE, CORE))
    in_specs = (
        P((LINE, CORE), None),
        P((LINE, CORE), (MP, PRE)),
        factor,
        factor,
        P(),
        P(),
    )
    out_specs = (factor, factor, P((LINE, CORE), (MP, PRE)))
    return jax.shard_map(
        make_step(dict(split.shape)),
        mesh=split,
        in_specs=in_specs,
        out_specs=out_specs,
        check_vma=False,
    )
```

```python
import jax
import jax.numpy as jnp
from jax import lax
from jax.experimental import pallas as pl
from jax.experimental.pallas import tpu as pltpu
from jax.sharding import Mesh, PartitionSpec as P

beta_decay = 0.9
norm_floor = 1e-06
count = 4

LINE, CORE, MP, PRE = "line", "core", "mp", "pre"
AXES = (LINE, CORE, MP, PRE)
f32, bf16 = jnp.float32, jnp.bfloat16


def halves(x):
    high = x.astype(bf16)
    return high, (x - high.astype(f32)).astype(bf16)


def whole_of(high, low):
    return high.astype(f32) + low.astype(f32)


def product(a, b, a_dim, b_dim):
    def one(x, y):
        return lax.dot_general(
            x, y, (((a_dim,), (b_dim,)), ((), ())), preferred_element_type=f32
        )

    return one(a[0], b[0]) + (one(a[0], b[1]) + one(a[1], b[0]))


def select_by(index, options):
    result = None
    for value, array in options.items():
        result = array if result is None else jnp.where(index == value, array, result)
    return result


def tie(values):
    return lax.optimization_barrier(tuple(values))


def call(body, outputs, numbers, arrays, space=pltpu.VMEM, scratch=(), mebibytes=32):
    inputs, results = len(arrays), len(outputs)

    def kernel(*refs):
        body(
            refs[0],
            refs[1 : 1 + inputs],
            refs[1 + inputs : 1 + inputs + results],
            *refs[1 + inputs + results :],
        )

    return pl.pallas_call(
        kernel,
        out_shape=[jax.ShapeDtypeStruct(shape, dtype) for shape, dtype in outputs],
        in_specs=[pl.BlockSpec(memory_space=pltpu.SMEM)]
        + [pl.BlockSpec(memory_space=space)] * inputs,
        out_specs=[pl.BlockSpec(memory_space=pltpu.VMEM)] * results,
        scratch_shapes=scratch,
        compiler_params=pltpu.CompilerParams(vmem_limit_bytes=mebibytes << 20),
        cost_estimate=pl.CostEstimate(flops=1, bytes_accessed=1, transcendentals=0),
    )(numbers, *arrays)


def added(numbers, arrays):
    def body(number, inputs, outputs):
        total = inputs[0][...]
        for array in inputs[1:]:
            total = total + array[...]
        outputs[0][...] = total

    return call(body, [(arrays[0].shape, f32)], numbers, arrays)[0]


def fetching(body, outputs, numbers, choices, shape, arrays=(), mebibytes=24):
    sources = []

    def place(array):
        for i, known in enumerate(sources):
            if known is array:
                return i
        sources.append(array)
        return len(sources) - 1

    shapes = [choice[2] if len(choice) > 2 else shape for choice in choices]
    choices = [
        (choice[0], {k: [(place(a), r) for a, r in terms] for k, terms in choice[1].items()})
        for choice in choices
    ]
    wholes = [place(array) for array in arrays]
    most = [max(1, *(len(t) for t in options.values())) for _, options in choices]
    many = len(choices)

    def inner(number, inputs, results, *scratch):
        held, kept = scratch[:many], scratch[many:-2]
        sems, kept_sems = scratch[-2:]

        def copies(o, terms):
            return [
                pltpu.make_async_copy(
                    inputs[a].at[pl.ds(r, shapes[o][0])], held[o].at[i], sems.at[o, i]
                )
                for i, (a, r) in enumerate(terms)
            ]

        loads = [
            pltpu.make_async_copy(inputs[a], kept[i], kept_sems.at[i])
            for i, a in enumerate(wholes)
        ]
        for o, (which, options) in enumerate(choices):
            for k, terms in options.items():

                @pl.when(number[which] == k)
                def _():
                    for copy in copies(o, terms):
                        copy.start()

        for copy in loads:
            copy.start()
        for o, (which, options) in enumerate(choices):
            for k, terms in options.items():

                @pl.when(number[which] == k)
                def _():
                    for copy in copies(o, terms):
                        copy.wait()
                    if not terms:
                        held[o][0] = jnp.zeros(shapes[o], f32)
                    if len(terms) > 1:
                        total = held[o][0]
                        for i in range(1, len(terms)):
                            total = total + held[o][i]
                        held[o][0] = total

        for copy in loads:
            copy.wait()
        body(number, [held[o].at[0] for o in range(many)], kept, results)

    return call(
        inner,
        outputs,
        numbers,
        sources,
        pl.ANY,
        [
            *[pltpu.VMEM((m,) + tuple(s), f32) for m, s in zip(most, shapes)],
            *[pltpu.VMEM(array.shape, array.dtype) for array in arrays],
            pltpu.SemaphoreType.DMA((max(many, 1), max(most + [1]))),
            pltpu.SemaphoreType.DMA((max(len(arrays), 1),)),
        ],
        mebibytes,
    )


def chosen_sums(numbers, choices, shape, more, tails):
    many = len(choices)
    sizes = [tail[2][0] for tail in tails] + [0] * (many - len(tails))

    def body(number, sums, inputs, outputs):
        for i, (result, rows, size) in enumerate(zip(outputs, more, sizes)):
            at = shape[0]
            result[:at] = sums[i][...]
            if size:
                result[at : at + size] = sums[many + i][...]
            if rows > size:
                result[at + size :] = jnp.zeros((rows - size,) + shape[1:], f32)

    out = [((shape[0] + rows,) + shape[1:], f32) for rows in more]
    return fetching(body, out, numbers, choices + tails, shape)


class Windows:
    def __init__(self):
        self.now = 0
        self.processes = []

    def add(self, process):
        self.processes.append([process, None, None])

    def open(self):
        ended = []
        for entry in self.processes:
            process, due, values = entry
            if values and due >= self.now:
                continue
            try:
                windows, entry[2] = process.send(values)
                entry[1] = self.now + windows - 1
            except StopIteration:
                ended.append(entry)
        for entry in ended:
            self.processes.remove(entry)

    def close(self, *others):
        due = [entry for entry in self.processes if entry[1] == self.now and entry[2]]
        flat = list(others)
        for entry in due:
            flat.extend(entry[2])
        if flat:
            flat = list(tie(flat))
        at = len(others)
        for entry in due:
            size = len(entry[2])
            entry[2] = flat[at : at + size]
            at += size
        self.now += 1
        return flat[: len(others)]


def make_step(sizes):
    line, cores, mp, pre = (sizes[name] for name in AXES)
    models = mp * pre
    last = count - 1

    def swap(array, axis, bit):
        return lax.ppermute(array, axis, [(i, i ^ bit) for i in range(sizes[axis])])

    def bits(axis):
        return [1 << i for i in range(sizes[axis].bit_length() - 1)]

    def total(numbers, array, axes):
        for axis in axes:
            for bit in bits(axis):
                pair = yield 1, (array, swap(array, axis, bit))
                array = added(numbers, pair)
        return array

    def snake(array, outward):
        pairs = []
        for z in range(line):
            for c in range(cores):
                goal = z + (1 if (c == 0) == outward else -1)
                if 0 <= goal < line:
                    pairs.append((z * cores + c, goal * cores + c))
                else:
                    pairs.append((z * cores + c, z * cores + 1 - c))
        return lax.ppermute(array, (LINE, CORE), pairs)

    def shards(activations, grad_output, left_old, right_old, probe_left, probe_right):
        z, core = lax.axis_index(LINE), lax.axis_index(CORE)
        x, y = lax.axis_index(MP), lax.axis_index(PRE)
        model = x * pre + y
        width = activations.shape[1]
        block = grad_output.shape[1]
        hidden = block * models
        panel = block // cores
        own_rows = width // (line * cores)
        model_rows = width // models
        piece = width // count
        owner_x, owner_y = z // pre, z % pre
        there = jnp.where(core == 0, z, line - 1 - z)
        numbers = jnp.stack(
            [z, core, there, line - 1 - there, x == owner_x, y == owner_y, model]
        ).astype(jnp.int32)
        Z, C, THERE, BACK, IN_X, IN_Y, MODEL = range(7)
        shape = (piece, panel)
        windows = Windows()
        state = {}

        def to_partner(array):
            return swap(array, CORE, 1)

        def device(number):
            return number[Z] * cores + number[C]

        def local(first, end):
            rows = (end - first) * piece
            tokens = activations.shape[0]

            parts = 4
            span = tokens // parts

            def body(number, inputs, outputs, left, right, sems):
                copies = []
                for i in range(parts):
                    at = pl.ds(i * span, span)
                    copies.append(
                        (
                            pltpu.make_async_copy(
                                inputs[0].at[at, pl.ds(first * piece, rows)],
                                left.at[at],
                                sems.at[0, i],
                            ),
                            pltpu.make_async_copy(
                                inputs[1].at[at], right.at[at], sems.at[1, i]
                            ),
                        )
                    )
                for i in range(min(2, parts)):
                    for copy in copies[i]:
                        copy.start()
                sums = [None] * (end - first)
                for i in range(parts):
                    for copy in copies[i]:
                        copy.wait()
                    if i + 2 < parts:
                        for copy in copies[i + 2]:
                            copy.start()
                    at = slice(i * span, (i + 1) * span)
                    for j in range(end - first):
                        term = lax.dot_general(
                            left[at, j * piece : (j + 1) * piece],
                            right[at],
                            (((0,), (0,)), ((), ())),
                            preferred_element_type=f32,
                        )
                        sums[j] = term if i == 0 else sums[j] + term
                zeroth = jnp.full(shape, number[C], jnp.int32) == 0
                for j, both in enumerate(sums):
                    low, high = both[:, :panel], both[:, panel:]
                    outputs[0][j * piece : (j + 1) * piece] = jnp.where(zeroth, low, high)
                    outputs[1 + j][...] = jnp.where(zeroth, high, low)

            return call(
                body,
                [((rows, panel), f32)] + [(shape, f32)] * (end - first),
                numbers,
                [activations, grad_output],
                pl.ANY,
                [
                    pltpu.VMEM((tokens, rows), bf16),
                    pltpu.VMEM(grad_output.shape, bf16),
                    pltpu.SemaphoreType.DMA((2, parts)),
                ],
                60,
            )

        kept_first, away = local(0, 1)
        arrived = [to_partner(away)]

        class Chain:
            def __init__(self, terms):
                self.terms = terms
                self.sent, self.out, self.home, self.options = [], [], [], []

            def next_sums(self, t):
                choices = []
                for which, got in ((THERE, self.out), (BACK, self.home)):
                    options = {}
                    for k in range(line):
                        options[k] = []
                        if 0 <= t - k < count:
                            options[k] = self.terms(t - k)
                            if k:
                                options[k] = options[k] + [(got[t - 1], 0)]
                    choices.append((which, options))
                return choices

            def next_tails(self, t, piece_number, array):
                choices = []
                if not 0 <= t - piece_number < line:
                    return choices
                for which, got in ((THERE, self.out), (BACK, self.home)):
                    options = {k: [] for k in range(line)}
                    k = t - piece_number
                    options[k] = [(array, 0)] + ([(got[t - 1], piece)] if k else [])
                    choices.append((which, options, array.shape))
                return choices

            def finished_tail(self, piece_number, array):
                j = piece_number
                options = {
                    k: [(self.sent[j + k], piece), (self.home[j + line - 2 - k], piece)]
                    for k in range(line - 1)
                }
                options[line - 1] = [(array, 0), (self.out[j + line - 2], piece)]
                return THERE, options, array.shape

            def send(self, going_out, going_home):
                self.sent.append(going_out)
                self.out.append(snake(going_out, True))
                self.home.append(snake(going_home, False))

            def finished(self, t):
                j = t - (line - 1)
                if not 0 <= j < count:
                    return []
                options = {
                    k: [(self.sent[j + k], 0), (self.home[j + line - 2 - k], 0)]
                    for k in range(line - 1)
                }
                options[line - 1] = self.terms(j) + [(self.out[j + line - 2], 0)]
                self.options.append((THERE, options))
                return self.options[-1:]

        gradient = Chain(
            lambda j: [
                (kept_rest[0], (j - 1) * piece) if j else (kept_first, 0),
                (arrived[j], 0),
            ]
        )
        mixed = Chain(lambda j: [(state["kept", j], 0), (state["swapped", j], 0)])
        own, wishes, kept_rest = [], [], []

        def row(array):
            return array.reshape(1, -1)

        def exchange(array, axis):
            return total(numbers, array, (axis,))

        def placed(number, column):
            wide = (own_rows, width)
            at = lax.broadcasted_iota(jnp.int32, wide, 0) + device(number) * own_rows
            here = lax.broadcasted_iota(jnp.int32, wide, 1) == at
            return jnp.sum(jnp.where(here, column, 0.0), axis=0, keepdims=True)

        def panel_of(which):
            return row(lax.dynamic_slice_in_dim(probe_right, which * panel, panel, 0))

        def beside(first, second):
            def body(number, inputs, outputs):
                size = inputs[0].shape[1]
                outputs[0][:, :size] = inputs[0][...]
                outputs[0][:, size:] = inputs[1][...]

            shape = first.shape[0], first.shape[1] + second.shape[1]
            return call(body, [(shape, f32)], numbers, [first, second])[0]

        def left_turned():
            return (beta_decay * left_old).T

        block_rows, image_rows = block // panel, width // panel
        tail_rows = -(-(block_rows + image_rows) // 8) * 8
        tail_piece = 2

        def old_factors():
            while windows.now < 1:
                yield 1, ()

            def body(number, inputs, outputs):
                old = beta_decay * inputs[0][...]
                outputs[0][...], outputs[1][...] = halves(old)
                image = jnp.sum(old * inputs[1][...], axis=1, keepdims=True).T
                outputs[2][...] = jnp.zeros((tail_rows, panel), f32)
                for r in range(block_rows):
                    outputs[2][r : r + 1] = image[:, r * panel : (r + 1) * panel]
                image = jnp.sum(inputs[2][...] * inputs[3][...], axis=1, keepdims=True)
                image = placed(number, image)
                for r in range(image_rows):
                    at = block_rows + r
                    outputs[2][at : at + 1] = image[:, r * panel : (r + 1) * panel]

            own_probe = lax.dynamic_slice_in_dim(probe_left, model * model_rows, model_rows, 0)
            high, low, images = call(
                body,
                [((block, panel), bf16), ((block, panel), bf16), ((tail_rows, panel), f32)],
                numbers,
                [right_old, panel_of(z * cores + core), left_turned(), row(own_probe)],
            )
            *state["old"], state["tail"] = yield 1, (high, low, images)

        def old_left():
            while windows.now < 1:
                yield 1, ()
            rows = left_turned()
            for axis in (PRE, MP):
                for bit in bits(axis):
                    rows, got = yield 1, (rows, swap(rows, axis, bit))
                    rows = beside(rows, got)
            state["old_left"] = rows

        def spread(array, axis, place, owner):
            result = None
            size = sizes[axis]
            for s in range(1, size):
                got = lax.ppermute(array, axis, [(i, (i + s) % size) for i in range(size)])
                if result is None:
                    result = got
                else:
                    result = jnp.where((place - s) % size == owner, got, result)
            return result

        def panel_piece(j):
            while len(own) <= j:
                yield 1, ()
            if j < depth:
                other, got = yield 1, (to_partner(own[j]), spread(own[j], PRE, y, owner_y))
                state["other", j] = other, 0
            else:
                (got,) = yield 1, (spread(own[j], PRE, y, owner_y),)
            wishes.append((("held", j), (IN_Y, {1: [(own[j], 0)], 0: [(got, 0)]})))
            while ("held", j) not in state:
                yield 1, ()
            held = state["held", j]
            held, got = yield 1, (held, spread(held, MP, x, owner_x))
            riders = []
            if j + depth == last:
                while len(own) < count:
                    yield 1, ()
                riders = [*own[depth:], first_images()]

            def body(number, inputs, outputs):
                here = jnp.full(shape, number[IN_X], jnp.int32) == 1
                pair = halves(jnp.where(here, inputs[0][:piece], inputs[1][:piece]))
                outputs[0][...], outputs[1][...] = pair
                both = product(pair, (inputs[2][...], inputs[3][...]), 1, 1)
                low, high = both[:, :panel], both[:, panel:]
                zeroth = jnp.full(shape, number[C], jnp.int32) == 0
                outputs[2][...] = jnp.where(zeroth, low, high)
                outputs[3][:piece] = jnp.where(zeroth, high, low)
                at = piece
                for rider in inputs[4:]:
                    outputs[3][at : at + rider.shape[0]] = rider[...]
                    at += rider.shape[0]

            away_rows = piece + sum(rider.shape[0] for rider in riders)
            high, low, state["kept", j], away = call(
                body,
                [(shape, bf16), (shape, bf16), (shape, f32), ((away_rows, panel), f32)],
                numbers,
                [held, got, *state["old"], *riders],
            )
            state["panel", j] = high, low
            _, _, got = yield 1, (high, low, to_partner(away))
            state["swapped", j] = got
            if riders:
                for i in range(depth, count):
                    state["other", i] = got, (i - depth + 1) * piece
                state["images"] = riders[-1], got, (count - depth + 1) * piece

        depth = 2
        rider_rows = -(-(2 * image_rows + block_rows) // 8) * 8

        def first_images():
            def body(number, inputs, outputs):
                right, left = inputs[count][...], inputs[count + 1][...].T
                across = jnp.zeros((1, panel), f32)
                for j in range(count):
                    rows = slice(j * piece, (j + 1) * piece)
                    across += jnp.sum(inputs[j][...] * left[rows], axis=0, keepdims=True)
                old = inputs[count + 2][...]
                outputs[0][...] = jnp.zeros((rider_rows, panel), f32)
                outputs[0][2 * image_rows : 2 * image_rows + block_rows] = old[:block_rows]
                for i, vector in enumerate((right, across)):
                    image = jnp.concatenate(
                        [
                            jnp.sum(inputs[j][...] * vector, axis=1, keepdims=True).T
                            for j in range(count)
                        ],
                        axis=1,
                    )
                    for r in range(image_rows):
                        at = i * image_rows + r
                        part = image[:, r * panel : (r + 1) * panel]
                        if i:
                            part = part + hidden * old[block_rows + r : block_rows + r + 1]
                        outputs[0][at : at + 1] = part

            return call(
                body,
                [((rider_rows, panel), f32)],
                numbers,
                [
                    *own,
                    panel_of(model * cores + core),
                    row(probe_left),
                    state["old_images"],
                ],
            )[0]

        def over_models(array):
            steps = [(axis, bit) for axis in (PRE, MP) for bit in bits(axis)]
            for i, (axis, bit) in enumerate(steps):
                terms = yield 1, (array, swap(array, axis, bit))
                if i < len(steps) - 1:
                    array = added(numbers, terms)
            return terms

        def first_part(crossed):
            (crossed,) = yield 1, (crossed,)
            crossed = yield from over_models(crossed)
            while "squares" not in state:
                yield 1, ()

            def body(number, sums, inputs, outputs):
                top_left, top_right, scale = scales(inputs[6][...] + inputs[7][...])
                grad = inputs[4][...], inputs[5][...]
                rows = pl.ds(pl.multiple_of(device(number) * own_rows, own_rows), own_rows)
                own = whole_of(inputs[4][rows, :], inputs[5][rows, :])
                crossed = product(halves(inputs[0][...] + inputs[1][...]), grad, 1, 0)
                outputs[0][...] = scale * (
                    25.0 * own
                    - inputs[2][...] * (5.0 / top_left)
                    - (5.0 * inputs[3][...] - crossed / top_left) / top_right
                )

            (state["first_part"],) = fetching(
                body,
                [((own_rows, block), f32)],
                numbers,
                [],
                shape,
                [*crossed, *state["left_parts"], *state["block"], *state["squares"]],
            )

        def left_side():
            while ("other", last) not in state or "images" not in state:
                yield 1, ()
            other = [state["other", j] for j in range(count)]
            images, got, start = state["images"]

            def body(number, inputs, outputs):
                zeroth = jnp.full(shape, number[C], jnp.int32) == 0
                for j in range(count):
                    at = other[j][1]
                    mine, theirs = inputs[j][...], inputs[count + j][at : at + piece]
                    rows = pl.ds(j * piece, piece)
                    for i, part in enumerate(
                        (jnp.where(zeroth, mine, theirs), jnp.where(zeroth, theirs, mine))
                    ):
                        columns = pl.ds(i * panel, panel)
                        outputs[0][rows, columns], outputs[1][rows, columns] = halves(part)
                rows = pl.ds(pl.multiple_of(device(number) * own_rows, own_rows), own_rows)
                gram = product(
                    (outputs[0][rows, :], outputs[1][rows, :]),
                    (outputs[0][...], outputs[1][...]),
                    1,
                    1,
                )
                outputs[2][:own_rows] = gram / hidden
                outputs[2][own_rows:] = jnp.zeros((8, width), f32)
                images = inputs[2 * count][...] + inputs[2 * count + 1][start:]
                for i in range(2):
                    for r in range(image_rows):
                        at = i * image_rows + r
                        outputs[2][own_rows + i : own_rows + i + 1, pl.ds(r * panel, panel)] = (
                            images[at : at + 1]
                        )
                for r in range(block_rows):
                    at = 2 * image_rows + r
                    outputs[3][:, pl.ds(r * panel, panel)] = images[at : at + 1]

            rows = (own_rows, width)
            high, low, gram, state["old_image"] = call(
                body,
                [((width, block), bf16)] * 2
                + [((own_rows + 8, width), f32), ((1, block), f32)],
                numbers,
                [*own, *(array for array, _ in other), images, got],
            )
            state["block"] = high, low
            gram = yield from over_models(gram)
            state["left_terms"] = gram

            def body(number, sums, inputs, outputs):
                gram = inputs[0][:own_rows] + inputs[1][:own_rows]
                old = []
                for m in range(models):
                    part = jnp.zeros((own_rows, model_rows), f32)
                    for k in range(models):
                        at = jnp.full(part.shape, number[MODEL], jnp.int32)
                        block_k = inputs[2][:, k * model_rows : (k + 1) * model_rows]
                        part = jnp.where(at == m ^ k, block_k, part)
                    old.append(part)
                left = jnp.concatenate(old, axis=1) + gram
                outputs[0][...] = left
                new = left[:, :model_rows]
                for m in range(1, models):
                    at = jnp.full(new.shape, number[MODEL], jnp.int32)
                    new = jnp.where(at == m, left[:, m * model_rows : (m + 1) * model_rows], new)
                outputs[4][...] = new.T
                grad = inputs[3][...], inputs[4][...]
                left_grad = product(halves(left), grad, 1, 0)
                outputs[1][...] = left_grad
                outputs[2][...] = product(halves(gram), grad, 1, 0) * (hidden / width)
                outputs[3][...] = product(halves(left_grad), grad, 1, 1) / width

            left, left_grad, gram_grad, crossed, new = fetching(
                body,
                [(rows, f32), ((own_rows, block), f32), ((own_rows, block), f32), (rows, f32)]
                + [((model_rows, own_rows), f32)],
                numbers,
                [],
                shape,
                [*gram, state["old_left"], *state["block"]],
            )
            state["left_parts"] = left_grad, gram_grad
            state["left"] = left
            windows.add(first_part(crossed))
            (state["partner_left"],) = yield 1, (to_partner(left),)
            state["left_new"] = new

        def powers():
            while "left_terms" not in state:
                yield 1, ()

            def body(number, inputs, outputs):
                images = inputs[5][own_rows:] + inputs[6][own_rows:]
                outputs[1][...] = images[1:2] / hidden
                grad = whole_of(inputs[1][...], inputs[2][...])
                first = inputs[0][...] + (
                    jnp.sum(grad * images[0:1].T, axis=0, keepdims=True) / width
                )
                outputs[0][:, :width] = jnp.sum(grad * first, axis=1, keepdims=True).T
                old = whole_of(inputs[3][...], inputs[4][...])
                outputs[0][:, width : width + panel] = jnp.sum(
                    old * first.T, axis=0, keepdims=True
                )
                square = jnp.sum(first * first, axis=1, keepdims=True)
                outputs[0][:, width + panel :] = jnp.broadcast_to(square, (1, 128))

            joined, first = call(
                body,
                [((1, width + panel + 128), f32), ((1, width), f32)],
                numbers,
                [
                    state["old_image"],
                    *state["block"],
                    *state["old"],
                    *state["left_terms"],
                ],
            )
            for axis in (PRE, MP):
                for bit in bits(axis):
                    joined = added(numbers, [joined, swap(joined, axis, bit)])
            first, joined = yield 1, (first, joined)
            while "left" not in state or ("panel", last) not in state:
                yield 1, ()

            def body(number, inputs, outputs):
                joined = inputs[2 + 2 * count][...]
                for array in inputs[3 + 2 * count :]:
                    joined = joined + array[...]
                vector = joined[:, :width].T
                second = joined[:, width : width + panel]
                for j in range(count):
                    part = whole_of(inputs[2 + 2 * j][...], inputs[3 + 2 * j][...])
                    rows = vector[j * piece : (j + 1) * piece]
                    second = second + jnp.sum(part * rows, axis=0, keepdims=True) / width
                square = joined[:, width + panel : width + panel + 1]
                second = second / jnp.sqrt(square + norm_floor)
                right = jnp.sum(second * second, axis=1, keepdims=True)
                first = inputs[0][...]
                unit = first / jnp.sqrt(
                    jnp.sum(first * first, axis=1, keepdims=True) + norm_floor
                )
                second = jnp.sum(inputs[1][...] * unit, axis=1, keepdims=True)
                left = jnp.sum(second * second, axis=0, keepdims=True)
                spot = lax.broadcasted_iota(jnp.int32, (1, 128), 1)
                outputs[0][...] = jnp.where(spot == 0, left, right)

            panels = [half for j in range(count) for half in state["panel", j]]
            (squares,) = call(
                body,
                [((1, 128), f32)],
                numbers,
                [first, state["left"], *panels, joined],
            )
            squares = added(numbers, [squares, to_partner(squares)])
            for bit in bits(LINE)[:-2]:
                squares = added(numbers, [squares, swap(squares, LINE, bit)])
            squares = added(numbers, (yield 1, (squares, swap(squares, LINE, bits(LINE)[-2]))))
            state["squares"] = yield 1, (squares, swap(squares, LINE, bits(LINE)[-1]))

        def scales(squares):
            top = jnp.sqrt(squares + norm_floor)
            top_left, top_right = top[:, 0:1], top[:, 1:2]
            return top_left, top_right, 1.0 / (16.0 * jnp.sqrt(jnp.sqrt(top_left * top_right)))

        def right_factor():
            while ("panel", last) not in state or "block" not in state or windows.now < steps + 2:
                yield 1, ()

            def body(number, sums, inputs, outputs):
                pair = [
                    jnp.concatenate([inputs[3 + 2 * j + i][...] for j in range(count)], axis=0)
                    for i in range(2)
                ]
                gram = product((inputs[1][...], inputs[2][...]), pair, 0, 0)
                outputs[0][...] = beta_decay * inputs[0][...] + gram / width

            panels = [half for j in range(count) for half in state["panel", j]]
            (state["right_new"],) = yield 1, fetching(
                body,
                [((block, panel), f32)],
                numbers,
                [],
                shape,
                [right_old, *state["block"], *panels],
                44,
            )

        for j in range(count):
            windows.add(panel_piece(j))
        steps = count + line - 2
        def rows_here(number, i, rows, pieces):
            other = number[C] if i == 0 else 1 - number[C]
            at = jnp.full(rows.shape, number[Z] * cores + other, jnp.int32)
            for k in range(line * cores):
                j, start = divmod(k * own_rows, piece)
                for number_j, array in pieces:
                    if number_j == j:
                        rows = jnp.where(at == k, array[start : start + own_rows], rows)
            return rows

        def early_products():
            while len(mixed_wholes) < last or "partner_left" not in state:
                yield 1, ()

            def body(number, sums, inputs, outputs):
                pieces = [(j, inputs[2 + j]) for j in range(last)]
                pair = halves(jnp.concatenate([array[...] for _, array in pieces], axis=0))
                for i in range(2):
                    left = halves(inputs[i][:, : last * piece])
                    outputs[i][...] = product(left, pair, 1, 0)
                    outputs[2 + i][...] = rows_here(
                        number, i, jnp.zeros((own_rows, panel), f32), pieces
                    )

            state["early"] = yield 1, fetching(
                body,
                [((own_rows, panel), f32)] * 4,
                numbers,
                [],
                shape,
                [state["left"], state["partner_left"], *mixed_wholes],
            )

        mixed_wholes = []
        for process in (left_side, powers, right_factor, early_products):
            windows.add(process())

        for t in range(2 * steps):
            windows.open()
            current = gradient if t < steps else mixed
            choices = current.next_sums(t % steps) + gradient.finished(t)
            choices += mixed.finished(t - steps)
            names = [name for name, _ in wishes]
            choices += [choice for _, choice in wishes]
            wishes.clear()
            longer = 24 if steps < t < steps + 3 else tail_rows
            extra = [longer] * 2 + [0] * (len(choices) - 2)
            if ("held", last) in names:
                extra[-1] = longer
            tails = []
            if t < steps and "tail" in state:
                tails = gradient.next_tails(t, tail_piece, state["tail"])
            results = list(chosen_sums(numbers, choices, shape, extra, tails))
            if t == 0:
                results[0], results[1], activations, grad_output, left_old, right_old = tie(
                    (*results, activations, grad_output, left_old, right_old)
                )
                windows.add(old_factors())
                windows.add(old_left())
                kept, *away = local(1, count)
                kept_rest.append(kept)
                arrived += [to_partner(a) for a in away]
            current.send(*results[:2])
            for name in reversed(names):
                state[name] = results.pop()
            (own if len(own) < count else mixed_wholes).extend(results[2:])
            if t == tail_piece + line - 1:
                tail = gradient.finished_tail(tail_piece, state["tail"])

                def copy_body(number, sums, inputs, outputs):
                    outputs[0][...] = sums[0][...]

                (state["old_images"],) = fetching(
                    copy_body, [(tail[2], f32)], numbers, [tail], shape
                )
            windows.open()
            current.out[-1], current.home[-1] = windows.close(current.out[-1], current.home[-1])
        while windows.processes:
            windows.open()
            if windows.processes:
                windows.close()

        def body(number, sums, inputs, outputs):
            top_left, top_right, scale = scales(inputs[0][...] + inputs[1][...])
            pair = halves(sums[0][...])
            for i in range(2):
                rows = rows_here(number, i, inputs[6 + i][...], [(last, sums[0])])
                left = halves(inputs[2 + i][:, last * piece :])
                left = inputs[4 + i][...] + product(left, pair, 1, 0)
                outputs[i][...] = (left / top_left - 5.0 * rows) * (scale / top_right)

        mine, theirs = fetching(
            body,
            [((own_rows, panel), f32)] * 2,
            numbers,
            mixed.finished(steps),
            shape,
            [*state["squares"], state["left"], state["partner_left"], *state["early"]],
        )
        theirs = to_partner(theirs)

        def body(number, inputs, outputs):
            zeroth = jnp.full((own_rows, panel), number[C], jnp.int32) == 0
            mine, theirs = inputs[1][...], inputs[2][...]
            parts = jnp.where(zeroth, mine, theirs), jnp.where(zeroth, theirs, mine)
            for i, part in enumerate(parts):
                span = pl.ds(i * panel, panel)
                outputs[0][:, span] = inputs[0][:, span] + part

        (update,) = call(
            body, [((own_rows, block), f32)], numbers, [state["first_part"], mine, theirs]
        )
        return state["left_new"], state["right_new"], update

    return shards


def solution(mesh):
    dp, mp, pre = (mesh.shape[name] for name in ("dp", "mp", "pre"))
    cores = dp // (mp * pre)
    assert cores == 2
    split = Mesh(mesh.devices.reshape(dp // cores, cores, mp, pre), AXES)
    factor = P((MP, PRE), (LINE, CORE))
    in_specs = (
        P((LINE, CORE), None),
        P((LINE, CORE), (MP, PRE)),
        factor,
        factor,
        P(),
        P(),
    )
    out_specs = (factor, factor, P((LINE, CORE), (MP, PRE)))
    return jax.shard_map(
        make_step(dict(split.shape)),
        mesh=split,
        in_specs=in_specs,
        out_specs=out_specs,
        check_vma=False,
    )
```

```python
import jax
import jax.numpy as jnp
from jax import lax
from jax.experimental import pallas as pl
from jax.experimental.pallas import tpu as pltpu
from jax.sharding import Mesh, PartitionSpec as P

beta_decay = 0.9
norm_floor = 1e-06
count = 4

LINE, CORE, MP, PRE = "line", "core", "mp", "pre"
AXES = (LINE, CORE, MP, PRE)
f32, bf16 = jnp.float32, jnp.bfloat16


def halves(x):
    high = x.astype(bf16)
    return high, (x - high.astype(f32)).astype(bf16)


def whole_of(high, low):
    return high.astype(f32) + low.astype(f32)


def product(a, b, a_dim, b_dim):
    def one(x, y):
        return lax.dot_general(
            x, y, (((a_dim,), (b_dim,)), ((), ())), preferred_element_type=f32
        )

    return one(a[0], b[0]) + (one(a[0], b[1]) + one(a[1], b[0]))


def select_by(index, options):
    result = None
    for value, array in options.items():
        result = array if result is None else jnp.where(index == value, array, result)
    return result


def tie(values):
    return lax.optimization_barrier(tuple(values))


def call(body, outputs, numbers, arrays, space=pltpu.VMEM, scratch=(), mebibytes=32):
    inputs, results = len(arrays), len(outputs)

    def kernel(*refs):
        body(
            refs[0],
            refs[1 : 1 + inputs],
            refs[1 + inputs : 1 + inputs + results],
            *refs[1 + inputs + results :],
        )

    return pl.pallas_call(
        kernel,
        out_shape=[jax.ShapeDtypeStruct(shape, dtype) for shape, dtype in outputs],
        in_specs=[pl.BlockSpec(memory_space=pltpu.SMEM)]
        + [pl.BlockSpec(memory_space=space)] * inputs,
        out_specs=[pl.BlockSpec(memory_space=pltpu.VMEM)] * results,
        scratch_shapes=scratch,
        compiler_params=pltpu.CompilerParams(vmem_limit_bytes=mebibytes << 20),
        cost_estimate=pl.CostEstimate(flops=1, bytes_accessed=1, transcendentals=0),
    )(numbers, *arrays)


def added(numbers, arrays):
    def body(number, inputs, outputs):
        total = inputs[0][...]
        for array in inputs[1:]:
            total = total + array[...]
        outputs[0][...] = total

    return call(body, [(arrays[0].shape, f32)], numbers, arrays)[0]


def fetching(body, outputs, numbers, choices, shape, arrays=(), mebibytes=24):
    sources = []

    def place(array):
        for i, known in enumerate(sources):
            if known is array:
                return i
        sources.append(array)
        return len(sources) - 1

    shapes = [choice[2] if len(choice) > 2 else shape for choice in choices]
    choices = [
        (choice[0], {k: [(place(a), r) for a, r in terms] for k, terms in choice[1].items()})
        for choice in choices
    ]
    wholes = [place(array) for array in arrays]
    most = [max(1, *(len(t) for t in options.values())) for _, options in choices]
    many = len(choices)

    def inner(number, inputs, results, *scratch):
        held, kept = scratch[:many], scratch[many:-2]
        sems, kept_sems = scratch[-2:]

        def copies(o, terms):
            return [
                pltpu.make_async_copy(
                    inputs[a].at[pl.ds(r, shapes[o][0])], held[o].at[i], sems.at[o, i]
                )
                for i, (a, r) in enumerate(terms)
            ]

        loads = [
            pltpu.make_async_copy(inputs[a], kept[i], kept_sems.at[i])
            for i, a in enumerate(wholes)
        ]
        for o, (which, options) in enumerate(choices):
            for k, terms in options.items():

                @pl.when(number[which] == k)
                def _():
                    for copy in copies(o, terms):
                        copy.start()

        for copy in loads:
            copy.start()
        for o, (which, options) in enumerate(choices):
            for k, terms in options.items():

                @pl.when(number[which] == k)
                def _():
                    for copy in copies(o, terms):
                        copy.wait()
                    if not terms:
                        held[o][0] = jnp.zeros(shapes[o], f32)
                    if len(terms) > 1:
                        total = held[o][0]
                        for i in range(1, len(terms)):
                            total = total + held[o][i]
                        held[o][0] = total

        for copy in loads:
            copy.wait()
        body(number, [held[o].at[0] for o in range(many)], kept, results)

    return call(
        inner,
        outputs,
        numbers,
        sources,
        pl.ANY,
        [
            *[pltpu.VMEM((m,) + tuple(s), f32) for m, s in zip(most, shapes)],
            *[pltpu.VMEM(array.shape, array.dtype) for array in arrays],
            pltpu.SemaphoreType.DMA((max(many, 1), max(most + [1]))),
            pltpu.SemaphoreType.DMA((max(len(arrays), 1),)),
        ],
        mebibytes,
    )


def chosen_sums(numbers, choices, shape, more, tails):
    many = len(choices)
    sizes = [tail[2][0] for tail in tails] + [0] * (many - len(tails))

    def body(number, sums, inputs, outputs):
        for i, (result, rows, size) in enumerate(zip(outputs, more, sizes)):
            at = shape[0]
            result[:at] = sums[i][...]
            if size:
                result[at : at + size] = sums[many + i][...]
            if rows > size:
                result[at + size :] = jnp.zeros((rows - size,) + shape[1:], f32)

    out = [((shape[0] + rows,) + shape[1:], f32) for rows in more]
    return fetching(body, out, numbers, choices + tails, shape)


class Windows:
    def __init__(self):
        self.now = 0
        self.processes = []

    def add(self, process):
        self.processes.append([process, None, None])

    def open(self):
        ended = []
        for entry in self.processes:
            process, due, values = entry
            if values and due >= self.now:
                continue
            try:
                windows, entry[2] = process.send(values)
                entry[1] = self.now + windows - 1
            except StopIteration:
                ended.append(entry)
        for entry in ended:
            self.processes.remove(entry)

    def close(self, *others):
        due = [entry for entry in self.processes if entry[1] == self.now and entry[2]]
        flat = list(others)
        for entry in due:
            flat.extend(entry[2])
        if flat:
            flat = list(tie(flat))
        at = len(others)
        for entry in due:
            size = len(entry[2])
            entry[2] = flat[at : at + size]
            at += size
        self.now += 1
        return flat[: len(others)]


def make_step(sizes):
    line, cores, mp, pre = (sizes[name] for name in AXES)
    models = mp * pre
    last = count - 1

    def swap(array, axis, bit):
        return lax.ppermute(array, axis, [(i, i ^ bit) for i in range(sizes[axis])])

    def bits(axis):
        return [1 << i for i in range(sizes[axis].bit_length() - 1)]

    def total(numbers, array, axes):
        for axis in axes:
            for bit in bits(axis):
                pair = yield 1, (array, swap(array, axis, bit))
                array = added(numbers, pair)
        return array

    def snake(array, outward):
        pairs = []
        for z in range(line):
            for c in range(cores):
                goal = z + (1 if (c == 0) == outward else -1)
                if 0 <= goal < line:
                    pairs.append((z * cores + c, goal * cores + c))
                else:
                    pairs.append((z * cores + c, z * cores + 1 - c))
        return lax.ppermute(array, (LINE, CORE), pairs)

    def shards(activations, grad_output, left_old, right_old, probe_left, probe_right):
        z, core = lax.axis_index(LINE), lax.axis_index(CORE)
        x, y = lax.axis_index(MP), lax.axis_index(PRE)
        model = x * pre + y
        width = activations.shape[1]
        block = grad_output.shape[1]
        hidden = block * models
        panel = block // cores
        own_rows = width // (line * cores)
        model_rows = width // models
        piece = width // count
        owner_x, owner_y = z // pre, z % pre
        there = jnp.where(core == 0, z, line - 1 - z)
        numbers = jnp.stack(
            [z, core, there, line - 1 - there, x == owner_x, y == owner_y, model]
        ).astype(jnp.int32)
        Z, C, THERE, BACK, IN_X, IN_Y, MODEL = range(7)
        shape = (piece, panel)
        windows = Windows()
        state = {}

        def to_partner(array):
            return swap(array, CORE, 1)

        def device(number):
            return number[Z] * cores + number[C]

        def local(first, end, mebibytes):
            pieces = end - first
            rows = pieces * piece
            parts = 4
            span = activations.shape[0] // parts

            def body(number, *refs):
                left, right = refs[:pieces], refs[pieces]
                outputs, sums = refs[pieces + 1 : -1], refs[-1]
                step = pl.program_id(0)
                for j in range(pieces):
                    at = slice(j * piece, (j + 1) * piece)
                    term = lax.dot_general(
                        left[j][...],
                        right[...],
                        (((0,), (0,)), ((), ())),
                        preferred_element_type=f32,
                    )

                    @pl.when(step == 0)
                    def _():
                        sums[at] = term

                    @pl.when(step > 0)
                    def _():
                        sums[at] += term

                @pl.when(step == parts - 1)
                def _():
                    zeroth = jnp.full(shape, number[C], jnp.int32) == 0
                    for j in range(pieces):
                        at = slice(j * piece, (j + 1) * piece)
                        low, high = sums[at, :panel], sums[at, panel:]
                        outputs[0][at] = jnp.where(zeroth, low, high)
                        outputs[1 + j][...] = jnp.where(zeroth, high, low)

            outs = [(rows, panel)] + [shape] * pieces
            return pl.pallas_call(
                body,
                grid=(parts,),
                out_shape=[jax.ShapeDtypeStruct(out, f32) for out in outs],
                in_specs=[pl.BlockSpec(memory_space=pltpu.SMEM)]
                + [
                    pl.BlockSpec((span, piece), lambda i, j=j: (i, j))
                    for j in range(first, end)
                ]
                + [pl.BlockSpec((span, block), lambda i: (i, 0))],
                out_specs=[pl.BlockSpec(out, lambda i: (0, 0)) for out in outs],
                scratch_shapes=[pltpu.VMEM((rows, block), f32)],
                compiler_params=pltpu.CompilerParams(vmem_limit_bytes=mebibytes << 20),
                cost_estimate=pl.CostEstimate(flops=1, bytes_accessed=1, transcendentals=0),
            )(numbers, *[activations] * pieces, grad_output)

        kept_first, away = local(0, 1, 60)
        arrived = [to_partner(away)]

        class Chain:
            def __init__(self, terms):
                self.terms = terms
                self.sent, self.out, self.home, self.options = [], [], [], []

            def next_sums(self, t):
                choices = []
                for which, got in ((THERE, self.out), (BACK, self.home)):
                    options = {}
                    for k in range(line):
                        options[k] = []
                        if 0 <= t - k < count:
                            options[k] = self.terms(t - k)
                            if k:
                                options[k] = options[k] + [(got[t - 1], 0)]
                    choices.append((which, options))
                return choices

            def next_tails(self, t, piece_number, array):
                choices = []
                if not 0 <= t - piece_number < line:
                    return choices
                for which, got in ((THERE, self.out), (BACK, self.home)):
                    options = {k: [] for k in range(line)}
                    k = t - piece_number
                    options[k] = [(array, 0)] + ([(got[t - 1], piece)] if k else [])
                    choices.append((which, options, array.shape))
                return choices

            def finished_tail(self, piece_number, array):
                j = piece_number
                options = {
                    k: [(self.sent[j + k], piece), (self.home[j + line - 2 - k], piece)]
                    for k in range(line - 1)
                }
                options[line - 1] = [(array, 0), (self.out[j + line - 2], piece)]
                return THERE, options, array.shape

            def send(self, going_out, going_home):
                self.sent.append(going_out)
                self.out.append(snake(going_out, True))
                self.home.append(snake(going_home, False))

            def finished(self, t):
                j = t - (line - 1)
                if not 0 <= j < count:
                    return []
                options = {
                    k: [(self.sent[j + k], 0), (self.home[j + line - 2 - k], 0)]
                    for k in range(line - 1)
                }
                options[line - 1] = self.terms(j) + [(self.out[j + line - 2], 0)]
                self.options.append((THERE, options))
                return self.options[-1:]

        gradient = Chain(
            lambda j: [
                (kept_rest[0], (j - 1) * piece) if j else (kept_first, 0),
                (arrived[j], 0),
            ]
        )
        mixed = Chain(lambda j: [(state["kept", j], 0), (state["swapped", j], 0)])
        own, wishes, kept_rest = [], [], []

        def row(array):
            return array.reshape(1, -1)

        def exchange(array, axis):
            return total(numbers, array, (axis,))

        def placed(number, column):
            wide = (own_rows, width)
            at = lax.broadcasted_iota(jnp.int32, wide, 0) + device(number) * own_rows
            here = lax.broadcasted_iota(jnp.int32, wide, 1) == at
            return jnp.sum(jnp.where(here, column, 0.0), axis=0, keepdims=True)

        def panel_of(which):
            return row(lax.dynamic_slice_in_dim(probe_right, which * panel, panel, 0))

        def beside(first, second):
            def body(number, inputs, outputs):
                size = inputs[0].shape[1]
                outputs[0][:, :size] = inputs[0][...]
                outputs[0][:, size:] = inputs[1][...]

            shape = first.shape[0], first.shape[1] + second.shape[1]
            return call(body, [(shape, f32)], numbers, [first, second])[0]

        def left_turned():
            return (beta_decay * left_old).T

        block_rows, image_rows = block // panel, width // panel
        tail_rows = -(-(block_rows + image_rows) // 8) * 8
        tail_piece = 2

        def old_factors():
            while windows.now < 1:
                yield 1, ()

            def body(number, inputs, outputs):
                old = beta_decay * inputs[0][...]
                outputs[0][...], outputs[1][...] = halves(old)
                image = jnp.sum(old * inputs[1][...], axis=1, keepdims=True).T
                outputs[2][...] = jnp.zeros((tail_rows, panel), f32)
                for r in range(block_rows):
                    outputs[2][r : r + 1] = image[:, r * panel : (r + 1) * panel]
                image = jnp.sum(inputs[2][...] * inputs[3][...], axis=1, keepdims=True)
                image = placed(number, image)
                for r in range(image_rows):
                    at = block_rows + r
                    outputs[2][at : at + 1] = image[:, r * panel : (r + 1) * panel]

            own_probe = lax.dynamic_slice_in_dim(probe_left, model * model_rows, model_rows, 0)
            high, low, images = call(
                body,
                [((block, panel), bf16), ((block, panel), bf16), ((tail_rows, panel), f32)],
                numbers,
                [right_old, panel_of(z * cores + core), left_turned(), row(own_probe)],
            )
            *state["old"], state["tail"] = yield 1, (high, low, images)

        def old_left():
            while windows.now < 1:
                yield 1, ()
            rows = left_turned()
            for axis in (PRE, MP):
                for bit in bits(axis):
                    rows, got = yield 1, (rows, swap(rows, axis, bit))
                    rows = beside(rows, got)
            state["old_left"] = rows

        def spread(array, axis, place, owner):
            result = None
            size = sizes[axis]
            for s in range(1, size):
                got = lax.ppermute(array, axis, [(i, (i + s) % size) for i in range(size)])
                if result is None:
                    result = got
                else:
                    result = jnp.where((place - s) % size == owner, got, result)
            return result

        def panel_piece(j):
            while len(own) <= j:
                yield 1, ()
            if j < depth:
                other, got = yield 1, (to_partner(own[j]), spread(own[j], PRE, y, owner_y))
                state["other", j] = other, 0
            else:
                (got,) = yield 1, (spread(own[j], PRE, y, owner_y),)
            wishes.append((("held", j), (IN_Y, {1: [(own[j], 0)], 0: [(got, 0)]})))
            while ("held", j) not in state:
                yield 1, ()
            held = state["held", j]
            held, got = yield 1, (held, spread(held, MP, x, owner_x))
            riders = []
            if j + depth == last:
                while len(own) < count:
                    yield 1, ()
                riders = [*own[depth:], first_images()]

            def body(number, inputs, outputs):
                here = jnp.full(shape, number[IN_X], jnp.int32) == 1
                pair = halves(jnp.where(here, inputs[0][:piece], inputs[1][:piece]))
                outputs[0][...], outputs[1][...] = pair
                both = product(pair, (inputs[2][...], inputs[3][...]), 1, 1)
                low, high = both[:, :panel], both[:, panel:]
                zeroth = jnp.full(shape, number[C], jnp.int32) == 0
                outputs[2][...] = jnp.where(zeroth, low, high)
                outputs[3][:piece] = jnp.where(zeroth, high, low)
                at = piece
                for rider in inputs[4:]:
                    size = min(rider.shape[0], piece)
                    outputs[3][at : at + size] = rider[:size]
                    at += size

            away_rows = piece + sum(min(rider.shape[0], piece) for rider in riders)
            high, low, state["kept", j], away = call(
                body,
                [(shape, bf16), (shape, bf16), (shape, f32), ((away_rows, panel), f32)],
                numbers,
                [held, got, *state["old"], *riders],
            )
            state["panel", j] = high, low
            _, _, got = yield 1, (high, low, to_partner(away))
            state["swapped", j] = got
            if riders:
                for i in range(depth, count):
                    state["other", i] = got, (i - depth + 1) * piece
                state["images"] = riders[-1], got, (count - depth + 1) * piece

        depth = 2
        rider_rows = -(-(2 * image_rows + block_rows) // 8) * 8

        def first_images():
            def body(number, inputs, outputs):
                right, left = inputs[count][...], inputs[count + 1][...].T
                across = jnp.zeros((1, panel), f32)
                for j in range(count):
                    rows = slice(j * piece, (j + 1) * piece)
                    across += jnp.sum(inputs[j][:piece] * left[rows], axis=0, keepdims=True)
                old = inputs[count + 2][...]
                outputs[0][...] = jnp.zeros((rider_rows, panel), f32)
                outputs[0][2 * image_rows : 2 * image_rows + block_rows] = old[:block_rows]
                for i, vector in enumerate((right, across)):
                    image = jnp.concatenate(
                        [
                            jnp.sum(inputs[j][:piece] * vector, axis=1, keepdims=True).T
                            for j in range(count)
                        ],
                        axis=1,
                    )
                    for r in range(image_rows):
                        at = i * image_rows + r
                        part = image[:, r * panel : (r + 1) * panel]
                        if i:
                            part = part + hidden * old[block_rows + r : block_rows + r + 1]
                        outputs[0][at : at + 1] = part

            return call(
                body,
                [((rider_rows, panel), f32)],
                numbers,
                [
                    *own,
                    panel_of(model * cores + core),
                    row(probe_left),
                    state["old_images"],
                ],
            )[0]

        def over_models(array):
            steps = [(axis, bit) for axis in (PRE, MP) for bit in bits(axis)]
            for i, (axis, bit) in enumerate(steps):
                terms = yield 1, (array, swap(array, axis, bit))
                if i < len(steps) - 1:
                    array = added(numbers, terms)
            return terms

        def first_part(crossed):
            (crossed,) = yield 1, (crossed,)
            crossed = yield from over_models(crossed)
            while "squares" not in state:
                yield 1, ()

            def body(number, sums, inputs, outputs):
                top_left, top_right, scale = scales(inputs[6][...] + inputs[7][...])
                grad = inputs[4][...], inputs[5][...]
                rows = pl.ds(pl.multiple_of(device(number) * own_rows, own_rows), own_rows)
                own = whole_of(inputs[4][rows, :], inputs[5][rows, :])
                crossed = product(halves(inputs[0][...] + inputs[1][...]), grad, 1, 0)
                outputs[0][...] = scale * (
                    25.0 * own
                    - inputs[2][...] * (5.0 / top_left)
                    - (5.0 * inputs[3][...] - crossed / top_left) / top_right
                )

            (state["first_part"],) = fetching(
                body,
                [((own_rows, block), f32)],
                numbers,
                [],
                shape,
                [*crossed, *state["left_parts"], *state["block"], *state["squares"]],
            )

        def left_side():
            while ("other", last) not in state or "images" not in state:
                yield 1, ()
            other = [state["other", j] for j in range(count)]
            images, got, start = state["images"]

            def body(number, inputs, outputs):
                zeroth = jnp.full(shape, number[C], jnp.int32) == 0
                for j in range(count):
                    at = other[j][1]
                    mine, theirs = inputs[j][:piece], inputs[count + j][at : at + piece]
                    rows = pl.ds(j * piece, piece)
                    for i, part in enumerate(
                        (jnp.where(zeroth, mine, theirs), jnp.where(zeroth, theirs, mine))
                    ):
                        columns = pl.ds(i * panel, panel)
                        outputs[0][rows, columns], outputs[1][rows, columns] = halves(part)
                rows = pl.ds(pl.multiple_of(device(number) * own_rows, own_rows), own_rows)
                gram = product(
                    (outputs[0][rows, :], outputs[1][rows, :]),
                    (outputs[0][...], outputs[1][...]),
                    1,
                    1,
                )
                outputs[2][:own_rows] = gram / hidden
                outputs[2][own_rows:] = jnp.zeros((8, width), f32)
                images = inputs[2 * count][...] + inputs[2 * count + 1][start:]
                for i in range(2):
                    for r in range(image_rows):
                        at = i * image_rows + r
                        outputs[2][own_rows + i : own_rows + i + 1, pl.ds(r * panel, panel)] = (
                            images[at : at + 1]
                        )
                for r in range(block_rows):
                    at = 2 * image_rows + r
                    outputs[3][:, pl.ds(r * panel, panel)] = images[at : at + 1]

            rows = (own_rows, width)
            high, low, gram, state["old_image"] = call(
                body,
                [((width, block), bf16)] * 2
                + [((own_rows + 8, width), f32), ((1, block), f32)],
                numbers,
                [*own, *(array for array, _ in other), images, got],
            )
            state["block"] = high, low
            gram = yield from over_models(gram)
            state["left_terms"] = gram

            def body(number, sums, inputs, outputs):
                gram = inputs[0][:own_rows] + inputs[1][:own_rows]
                old = []
                for m in range(models):
                    part = jnp.zeros((own_rows, model_rows), f32)
                    for k in range(models):
                        at = jnp.full(part.shape, number[MODEL], jnp.int32)
                        block_k = inputs[2][:, k * model_rows : (k + 1) * model_rows]
                        part = jnp.where(at == m ^ k, block_k, part)
                    old.append(part)
                left = jnp.concatenate(old, axis=1) + gram
                outputs[0][...] = left
                new = left[:, :model_rows]
                for m in range(1, models):
                    at = jnp.full(new.shape, number[MODEL], jnp.int32)
                    new = jnp.where(at == m, left[:, m * model_rows : (m + 1) * model_rows], new)
                outputs[4][...] = new.T
                grad = inputs[3][...], inputs[4][...]
                left_grad = product(halves(left), grad, 1, 0)
                outputs[1][...] = left_grad
                outputs[2][...] = gram
                outputs[3][...] = product(halves(left_grad), grad, 1, 1) / width

            left, left_grad, gram, crossed, new = fetching(
                body,
                [(rows, f32), ((own_rows, block), f32), (rows, f32), (rows, f32)]
                + [((model_rows, own_rows), f32)],
                numbers,
                [],
                shape,
                [*gram, state["old_left"], *state["block"]],
            )
            state["left"] = left
            windows.add(first_part(crossed))
            state["partner_left"], left_grad, gram = yield 1, (to_partner(left), left_grad, gram)

            def body(number, inputs, outputs):
                grad = inputs[1][...], inputs[2][...]
                outputs[0][...] = product(halves(inputs[0][...]), grad, 1, 0) * (hidden / width)

            (gram_grad,) = call(
                body, [((own_rows, block), f32)], numbers, [gram, *state["block"]]
            )
            state["left_parts"] = yield 1, (left_grad, gram_grad)
            state["left_new"] = new

        def powers():
            while "left_terms" not in state:
                yield 1, ()

            def body(number, inputs, outputs):
                images = inputs[5][own_rows:] + inputs[6][own_rows:]
                outputs[1][...] = images[1:2] / hidden
                grad = whole_of(inputs[1][...], inputs[2][...])
                first = inputs[0][...] + (
                    jnp.sum(grad * images[0:1].T, axis=0, keepdims=True) / width
                )
                outputs[0][:, :width] = jnp.sum(grad * first, axis=1, keepdims=True).T
                old = whole_of(inputs[3][...], inputs[4][...])
                outputs[0][:, width : width + panel] = jnp.sum(
                    old * first.T, axis=0, keepdims=True
                )
                square = jnp.sum(first * first, axis=1, keepdims=True)
                outputs[0][:, width + panel :] = jnp.broadcast_to(square, (1, 128))

            joined, first = call(
                body,
                [((1, width + panel + 128), f32), ((1, width), f32)],
                numbers,
                [
                    state["old_image"],
                    *state["block"],
                    *state["old"],
                    *state["left_terms"],
                ],
            )
            for axis in (PRE, MP):
                for bit in bits(axis):
                    joined = added(numbers, [joined, swap(joined, axis, bit)])
            first, joined = yield 1, (first, joined)
            while "left" not in state or ("panel", last) not in state:
                yield 1, ()

            def body(number, inputs, outputs):
                joined = inputs[2 + 2 * count][...]
                for array in inputs[3 + 2 * count :]:
                    joined = joined + array[...]
                vector = joined[:, :width].T
                second = joined[:, width : width + panel]
                for j in range(count):
                    part = whole_of(inputs[2 + 2 * j][...], inputs[3 + 2 * j][...])
                    rows = vector[j * piece : (j + 1) * piece]
                    second = second + jnp.sum(part * rows, axis=0, keepdims=True) / width
                square = joined[:, width + panel : width + panel + 1]
                second = second / jnp.sqrt(square + norm_floor)
                right = jnp.sum(second * second, axis=1, keepdims=True)
                first = inputs[0][...]
                unit = first / jnp.sqrt(
                    jnp.sum(first * first, axis=1, keepdims=True) + norm_floor
                )
                second = jnp.sum(inputs[1][...] * unit, axis=1, keepdims=True)
                left = jnp.sum(second * second, axis=0, keepdims=True)
                spot = lax.broadcasted_iota(jnp.int32, (1, 128), 1)
                outputs[0][...] = jnp.where(spot == 0, left, right)

            panels = [half for j in range(count) for half in state["panel", j]]
            (squares,) = call(
                body,
                [((1, 128), f32)],
                numbers,
                [first, state["left"], *panels, joined],
            )
            squares = added(numbers, [squares, to_partner(squares)])
            for bit in bits(LINE)[:-2]:
                squares = added(numbers, [squares, swap(squares, LINE, bit)])
            squares = added(numbers, (yield 1, (squares, swap(squares, LINE, bits(LINE)[-2]))))
            state["squares"] = yield 1, (squares, swap(squares, LINE, bits(LINE)[-1]))

        def scales(squares):
            top = jnp.sqrt(squares + norm_floor)
            top_left, top_right = top[:, 0:1], top[:, 1:2]
            return top_left, top_right, 1.0 / (16.0 * jnp.sqrt(jnp.sqrt(top_left * top_right)))

        def right_factor():
            while ("panel", last) not in state or "block" not in state or windows.now < steps + 2:
                yield 1, ()

            def body(number, sums, inputs, outputs):
                pair = [
                    jnp.concatenate([inputs[3 + 2 * j + i][...] for j in range(count)], axis=0)
                    for i in range(2)
                ]
                gram = product((inputs[1][...], inputs[2][...]), pair, 0, 0)
                outputs[0][...] = beta_decay * inputs[0][...] + gram / width

            panels = [half for j in range(count) for half in state["panel", j]]
            (state["right_new"],) = yield 1, fetching(
                body,
                [((block, panel), f32)],
                numbers,
                [],
                shape,
                [right_old, *state["block"], *panels],
                44,
            )

        for j in range(count):
            windows.add(panel_piece(j))
        steps = count + line - 2
        def rows_here(number, i, rows, pieces):
            other = number[C] if i == 0 else 1 - number[C]
            at = jnp.full(rows.shape, number[Z] * cores + other, jnp.int32)
            for k in range(line * cores):
                j, start = divmod(k * own_rows, piece)
                for number_j, array in pieces:
                    if number_j == j:
                        rows = jnp.where(at == k, array[start : start + own_rows], rows)
            return rows

        def early_products():
            while len(mixed_wholes) < last or "partner_left" not in state:
                yield 1, ()

            def body(number, sums, inputs, outputs):
                pieces = [(j, inputs[2 + j]) for j in range(last)]
                pair = halves(jnp.concatenate([array[:piece] for _, array in pieces], axis=0))
                for i in range(2):
                    left = halves(inputs[i][:, : last * piece])
                    outputs[i][...] = product(left, pair, 1, 0)
                    outputs[2 + i][...] = rows_here(
                        number, i, jnp.zeros((own_rows, panel), f32), pieces
                    )

            state["early"] = yield 1, fetching(
                body,
                [((own_rows, panel), f32)] * 4,
                numbers,
                [],
                shape,
                [state["left"], state["partner_left"], *mixed_wholes],
            )

        mixed_wholes = []
        for process in (left_side, powers, right_factor, early_products):
            windows.add(process())

        for t in range(2 * steps):
            windows.open()
            current = gradient if t < steps else mixed
            choices = current.next_sums(t % steps) + gradient.finished(t)
            choices += mixed.finished(t - steps)
            names = [name for name, _ in wishes]
            choices += [choice for _, choice in wishes]
            wishes.clear()
            longer = tail_rows + (16 if steps < t < steps + 3 else 8)
            extra = [longer] * 2 + [8] * (len(choices) - 2)
            if ("held", last) in names:
                extra[-1] = longer
            tails = []
            if t < steps and "tail" in state:
                tails = gradient.next_tails(t, tail_piece, state["tail"])
            results = list(chosen_sums(numbers, choices, shape, extra, tails))
            if t == 0:
                results[0], results[1], activations, grad_output, left_old, right_old = tie(
                    (*results, activations, grad_output, left_old, right_old)
                )
                windows.add(old_factors())
                windows.add(old_left())
                kept, *away = local(1, count, 40)
                kept_rest.append(kept)
                arrived += [to_partner(a) for a in away]
            current.send(*results[:2])
            for name in reversed(names):
                state[name] = results.pop()
            (own if len(own) < count else mixed_wholes).extend(results[2:])
            if t == tail_piece + line - 1:
                tail = gradient.finished_tail(tail_piece, state["tail"])

                def copy_body(number, sums, inputs, outputs):
                    outputs[0][...] = sums[0][...]

                (state["old_images"],) = fetching(
                    copy_body, [(tail[2], f32)], numbers, [tail], shape
                )
            windows.open()
            current.out[-1], current.home[-1] = windows.close(current.out[-1], current.home[-1])
        while windows.processes:
            windows.open()
            if windows.processes:
                windows.close()

        def body(number, sums, inputs, outputs):
            top_left, top_right, scale = scales(inputs[0][...] + inputs[1][...])
            pair = halves(sums[0][...])
            for i in range(2):
                rows = rows_here(number, i, inputs[6 + i][...], [(last, sums[0])])
                left = halves(inputs[2 + i][:, last * piece :])
                left = inputs[4 + i][...] + product(left, pair, 1, 0)
                outputs[i][...] = (left / top_left - 5.0 * rows) * (scale / top_right)

        mine, theirs = fetching(
            body,
            [((own_rows, panel), f32)] * 2,
            numbers,
            mixed.finished(steps),
            shape,
            [*state["squares"], state["left"], state["partner_left"], *state["early"]],
        )
        theirs = to_partner(theirs)

        def body(number, inputs, outputs):
            zeroth = jnp.full((own_rows, panel), number[C], jnp.int32) == 0
            mine, theirs = inputs[1][...], inputs[2][...]
            parts = jnp.where(zeroth, mine, theirs), jnp.where(zeroth, theirs, mine)
            for i, part in enumerate(parts):
                span = pl.ds(i * panel, panel)
                outputs[0][:, span] = inputs[0][:, span] + part

        (update,) = call(
            body, [((own_rows, block), f32)], numbers, [state["first_part"], mine, theirs]
        )
        return state["left_new"], state["right_new"], update

    return shards


def solution(mesh):
    dp, mp, pre = (mesh.shape[name] for name in ("dp", "mp", "pre"))
    cores = dp // (mp * pre)
    assert cores == 2
    split = Mesh(mesh.devices.reshape(dp // cores, cores, mp, pre), AXES)
    factor = P((MP, PRE), (LINE, CORE))
    in_specs = (
        P((LINE, CORE), None),
        P((LINE, CORE), (MP, PRE)),
        factor,
        factor,
        P(),
        P(),
    )
    out_specs = (factor, factor, P((LINE, CORE), (MP, PRE)))
    return jax.shard_map(
        make_step(dict(split.shape)),
        mesh=split,
        in_specs=in_specs,
        out_specs=out_specs,
        check_vma=False,
    )
```

```python
import jax
import jax.numpy as jnp
from jax import lax
from jax.experimental import pallas as pl
from jax.experimental.pallas import tpu as pltpu
from jax.sharding import Mesh, PartitionSpec as P

beta_decay = 0.9
norm_floor = 1e-06
count = 4

LINE, CORE, MP, PRE = "line", "core", "mp", "pre"
AXES = (LINE, CORE, MP, PRE)
f32, bf16 = jnp.float32, jnp.bfloat16


def halves(x):
    high = x.astype(bf16)
    return high, (x - high.astype(f32)).astype(bf16)


def whole_of(high, low):
    return high.astype(f32) + low.astype(f32)


def product(a, b, a_dim, b_dim):
    def one(x, y):
        return lax.dot_general(
            x, y, (((a_dim,), (b_dim,)), ((), ())), preferred_element_type=f32
        )

    return one(a[0], b[0]) + (one(a[0], b[1]) + one(a[1], b[0]))


def select_by(index, options):
    result = None
    for value, array in options.items():
        result = array if result is None else jnp.where(index == value, array, result)
    return result


def tie(values):
    return lax.optimization_barrier(tuple(values))


def call(body, outputs, numbers, arrays, space=pltpu.VMEM, scratch=(), mebibytes=32):
    inputs, results = len(arrays), len(outputs)

    def kernel(*refs):
        body(
            refs[0],
            refs[1 : 1 + inputs],
            refs[1 + inputs : 1 + inputs + results],
            *refs[1 + inputs + results :],
        )

    return pl.pallas_call(
        kernel,
        out_shape=[jax.ShapeDtypeStruct(shape, dtype) for shape, dtype in outputs],
        in_specs=[pl.BlockSpec(memory_space=pltpu.SMEM)]
        + [pl.BlockSpec(memory_space=space)] * inputs,
        out_specs=[pl.BlockSpec(memory_space=pltpu.VMEM)] * results,
        scratch_shapes=scratch,
        compiler_params=pltpu.CompilerParams(vmem_limit_bytes=mebibytes << 20),
        cost_estimate=pl.CostEstimate(flops=1, bytes_accessed=1, transcendentals=0),
    )(numbers, *arrays)


def added(numbers, arrays):
    def body(number, inputs, outputs):
        total = inputs[0][...]
        for array in inputs[1:]:
            total = total + array[...]
        outputs[0][...] = total

    return call(body, [(arrays[0].shape, f32)], numbers, arrays)[0]


def fetching(body, outputs, numbers, choices, shape, arrays=(), mebibytes=24):
    sources = []

    def place(array):
        for i, known in enumerate(sources):
            if known is array:
                return i
        sources.append(array)
        return len(sources) - 1

    shapes = [choice[2] if len(choice) > 2 else shape for choice in choices]
    choices = [
        (choice[0], {k: [(place(a), r) for a, r in terms] for k, terms in choice[1].items()})
        for choice in choices
    ]
    wholes = [place(array) for array in arrays]
    most = [max(1, *(len(t) for t in options.values())) for _, options in choices]
    many = len(choices)

    def inner(number, inputs, results, *scratch):
        held, kept = scratch[:many], scratch[many:-2]
        sems, kept_sems = scratch[-2:]

        def copies(o, terms):
            return [
                pltpu.make_async_copy(
                    inputs[a].at[pl.ds(r, shapes[o][0])], held[o].at[i], sems.at[o, i]
                )
                for i, (a, r) in enumerate(terms)
            ]

        loads = [
            pltpu.make_async_copy(inputs[a], kept[i], kept_sems.at[i])
            for i, a in enumerate(wholes)
        ]
        for o, (which, options) in enumerate(choices):
            for k, terms in options.items():

                @pl.when(number[which] == k)
                def _():
                    for copy in copies(o, terms):
                        copy.start()

        for copy in loads:
            copy.start()
        for o, (which, options) in enumerate(choices):
            for k, terms in options.items():

                @pl.when(number[which] == k)
                def _():
                    for copy in copies(o, terms):
                        copy.wait()
                    if not terms:
                        held[o][0] = jnp.zeros(shapes[o], f32)
                    if len(terms) > 1:
                        total = held[o][0]
                        for i in range(1, len(terms)):
                            total = total + held[o][i]
                        held[o][0] = total

        for copy in loads:
            copy.wait()
        body(number, [held[o].at[0] for o in range(many)], kept, results)

    return call(
        inner,
        outputs,
        numbers,
        sources,
        pl.ANY,
        [
            *[pltpu.VMEM((m,) + tuple(s), f32) for m, s in zip(most, shapes)],
            *[pltpu.VMEM(array.shape, array.dtype) for array in arrays],
            pltpu.SemaphoreType.DMA((max(many, 1), max(most + [1]))),
            pltpu.SemaphoreType.DMA((max(len(arrays), 1),)),
        ],
        mebibytes,
    )


def chosen_sums(numbers, choices, shape, more, tails):
    many = len(choices)
    sizes = [tail[2][0] for tail in tails] + [0] * (many - len(tails))

    def body(number, sums, inputs, outputs):
        for i, (result, rows, size) in enumerate(zip(outputs, more, sizes)):
            at = shape[0]
            result[:at] = sums[i][...]
            if size:
                result[at : at + size] = sums[many + i][...]
            if rows > size:
                result[at + size :] = jnp.zeros((rows - size,) + shape[1:], f32)

    out = [((shape[0] + rows,) + shape[1:], f32) for rows in more]
    return fetching(body, out, numbers, choices + tails, shape)


class Windows:
    def __init__(self):
        self.now = 0
        self.processes = []

    def add(self, process):
        self.processes.append([process, None, None])

    def open(self):
        ended = []
        for entry in self.processes:
            process, due, values = entry
            if values and due >= self.now:
                continue
            try:
                windows, entry[2] = process.send(values)
                entry[1] = self.now + windows - 1
            except StopIteration:
                ended.append(entry)
        for entry in ended:
            self.processes.remove(entry)

    def close(self, *others):
        due = [entry for entry in self.processes if entry[1] == self.now and entry[2]]
        flat = list(others)
        for entry in due:
            flat.extend(entry[2])
        if flat:
            flat = list(tie(flat))
        at = len(others)
        for entry in due:
            size = len(entry[2])
            entry[2] = flat[at : at + size]
            at += size
        self.now += 1
        return flat[: len(others)]


def make_step(sizes):
    line, cores, mp, pre = (sizes[name] for name in AXES)
    models = mp * pre
    last = count - 1

    def swap(array, axis, bit):
        return lax.ppermute(array, axis, [(i, i ^ bit) for i in range(sizes[axis])])

    def bits(axis):
        return [1 << i for i in range(sizes[axis].bit_length() - 1)]

    def total(numbers, array, axes):
        for axis in axes:
            for bit in bits(axis):
                pair = yield 1, (array, swap(array, axis, bit))
                array = added(numbers, pair)
        return array

    def snake(array, outward):
        pairs = []
        for z in range(line):
            for c in range(cores):
                goal = z + (1 if (c == 0) == outward else -1)
                if 0 <= goal < line:
                    pairs.append((z * cores + c, goal * cores + c))
                else:
                    pairs.append((z * cores + c, z * cores + 1 - c))
        return lax.ppermute(array, (LINE, CORE), pairs)

    def shards(activations, grad_output, left_old, right_old, probe_left, probe_right):
        z, core = lax.axis_index(LINE), lax.axis_index(CORE)
        x, y = lax.axis_index(MP), lax.axis_index(PRE)
        model = x * pre + y
        width = activations.shape[1]
        block = grad_output.shape[1]
        hidden = block * models
        panel = block // cores
        own_rows = width // (line * cores)
        model_rows = width // models
        piece = width // count
        owner_x, owner_y = z // pre, z % pre
        there = jnp.where(core == 0, z, line - 1 - z)
        numbers = jnp.stack(
            [z, core, there, line - 1 - there, x == owner_x, y == owner_y, model]
        ).astype(jnp.int32)
        Z, C, THERE, BACK, IN_X, IN_Y, MODEL = range(7)
        shape = (piece, panel)
        windows = Windows()
        state = {}

        def to_partner(array):
            return swap(array, CORE, 1)

        def device(number):
            return number[Z] * cores + number[C]

        def local(first, end):
            pieces = end - first
            rows = pieces * piece
            parts = max(1, panel // 256)
            span = panel // parts

            def column(i, number):
                which = jnp.where(i < parts, 1 - number[C], number[C])
                return 0, which * parts + i % parts

            def body(number, *refs):
                left, right, outputs = refs[:pieces], refs[pieces], refs[pieces + 1 :]
                step = pl.program_id(0)
                for j in range(pieces):
                    term = lax.dot_general(
                        left[j][...],
                        right[...],
                        (((0,), (0,)), ((), ())),
                        preferred_element_type=f32,
                    )
                    for i in range(2 * parts):

                        @pl.when(step == i)
                        def _():
                            columns = slice(i % parts * span, (i % parts + 1) * span)
                            if i < parts:
                                outputs[1 + j][:, columns] = term
                            else:
                                outputs[0][j * piece : (j + 1) * piece, columns] = term

            tokens = activations.shape[0]
            outs = [(rows, panel)] + [shape] * pieces
            return pl.pallas_call(
                body,
                out_shape=[jax.ShapeDtypeStruct(out, f32) for out in outs],
                grid_spec=pltpu.PrefetchScalarGridSpec(
                    num_scalar_prefetch=1,
                    grid=(2 * parts,),
                    in_specs=[
                        pl.BlockSpec((tokens, piece), lambda i, number, j=j: (0, j))
                        for j in range(first, end)
                    ]
                    + [pl.BlockSpec((tokens, span), column)],
                    out_specs=[pl.BlockSpec(out, lambda i, number: (0, 0)) for out in outs],
                ),
                compiler_params=pltpu.CompilerParams(vmem_limit_bytes=60 << 20),
                cost_estimate=pl.CostEstimate(flops=1, bytes_accessed=1, transcendentals=0),
            )(numbers, *[activations] * pieces, grad_output)

        kept_first, away = local(0, 1)
        arrived = [to_partner(away)]

        class Chain:
            def __init__(self, terms):
                self.terms = terms
                self.sent, self.out, self.home, self.options = [], [], [], []

            def next_sums(self, t):
                choices = []
                for which, got in ((THERE, self.out), (BACK, self.home)):
                    options = {}
                    for k in range(line):
                        options[k] = []
                        if 0 <= t - k < count:
                            options[k] = self.terms(t - k)
                            if k:
                                options[k] = options[k] + [(got[t - 1], 0)]
                    choices.append((which, options))
                return choices

            def next_tails(self, t, piece_number, array):
                choices = []
                if not 0 <= t - piece_number < line:
                    return choices
                for which, got in ((THERE, self.out), (BACK, self.home)):
                    options = {k: [] for k in range(line)}
                    k = t - piece_number
                    options[k] = [(array, 0)] + ([(got[t - 1], piece)] if k else [])
                    choices.append((which, options, array.shape))
                return choices

            def finished_tail(self, piece_number, array):
                j = piece_number
                options = {
                    k: [(self.sent[j + k], piece), (self.home[j + line - 2 - k], piece)]
                    for k in range(line - 1)
                }
                options[line - 1] = [(array, 0), (self.out[j + line - 2], piece)]
                return THERE, options, array.shape

            def send(self, going_out, going_home):
                self.sent.append(going_out)
                self.out.append(snake(going_out, True))
                self.home.append(snake(going_home, False))

            def finished(self, t):
                j = t - (line - 1)
                if not 0 <= j < count:
                    return []
                options = {
                    k: [(self.sent[j + k], 0), (self.home[j + line - 2 - k], 0)]
                    for k in range(line - 1)
                }
                options[line - 1] = self.terms(j) + [(self.out[j + line - 2], 0)]
                self.options.append((THERE, options))
                return self.options[-1:]

        gradient = Chain(
            lambda j: [
                (kept_rest[0], (j - 1) * piece) if j else (kept_first, 0),
                (arrived[j], 0),
            ]
        )
        mixed = Chain(lambda j: [(state["kept", j], 0), (state["swapped", j], 0)])
        own, wishes, kept_rest = [], [], []

        def row(array):
            return array.reshape(1, -1)

        def exchange(array, axis):
            return total(numbers, array, (axis,))

        def placed(number, column):
            wide = (own_rows, width)
            at = lax.broadcasted_iota(jnp.int32, wide, 0) + device(number) * own_rows
            here = lax.broadcasted_iota(jnp.int32, wide, 1) == at
            return jnp.sum(jnp.where(here, column, 0.0), axis=0, keepdims=True)

        def panel_of(which):
            return row(lax.dynamic_slice_in_dim(probe_right, which * panel, panel, 0))

        def beside(first, second):
            def body(number, inputs, outputs):
                size = inputs[0].shape[1]
                outputs[0][:, :size] = inputs[0][...]
                outputs[0][:, size:] = inputs[1][...]

            shape = first.shape[0], first.shape[1] + second.shape[1]
            return call(body, [(shape, f32)], numbers, [first, second])[0]

        def left_turned():
            return (beta_decay * left_old).T

        block_rows, image_rows = block // panel, width // panel
        tail_rows = -(-(block_rows + image_rows) // 8) * 8
        tail_piece = 2

        def old_factors():
            while windows.now < 1:
                yield 1, ()

            def body(number, inputs, outputs):
                old = beta_decay * inputs[0][...]
                outputs[0][...], outputs[1][...] = halves(old)
                image = jnp.sum(old * inputs[1][...], axis=1, keepdims=True).T
                outputs[2][...] = jnp.zeros((tail_rows, panel), f32)
                for r in range(block_rows):
                    outputs[2][r : r + 1] = image[:, r * panel : (r + 1) * panel]
                image = jnp.sum(inputs[2][...] * inputs[3][...], axis=1, keepdims=True)
                image = placed(number, image)
                for r in range(image_rows):
                    at = block_rows + r
                    outputs[2][at : at + 1] = image[:, r * panel : (r + 1) * panel]

            own_probe = lax.dynamic_slice_in_dim(probe_left, model * model_rows, model_rows, 0)
            high, low, images = call(
                body,
                [((block, panel), bf16), ((block, panel), bf16), ((tail_rows, panel), f32)],
                numbers,
                [right_old, panel_of(z * cores + core), left_turned(), row(own_probe)],
            )
            *state["old"], state["tail"] = yield 1, (high, low, images)

        def old_left():
            while windows.now < 1:
                yield 1, ()
            rows = left_turned()
            for axis in (PRE, MP):
                for bit in bits(axis):
                    rows, got = yield 1, (rows, swap(rows, axis, bit))
                    rows = beside(rows, got)
            state["old_left"] = rows

        def spread(array, axis, place, owner):
            result = None
            size = sizes[axis]
            for s in range(1, size):
                got = lax.ppermute(array, axis, [(i, (i + s) % size) for i in range(size)])
                if result is None:
                    result = got
                else:
                    result = jnp.where((place - s) % size == owner, got, result)
            return result

        def panel_piece(j):
            while len(own) <= j:
                yield 1, ()
            if j < depth:
                other, got = yield 1, (to_partner(own[j]), spread(own[j], PRE, y, owner_y))
                state["other", j] = other, 0
            else:
                (got,) = yield 1, (spread(own[j], PRE, y, owner_y),)
            wishes.append((("held", j), (IN_Y, {1: [(own[j], 0)], 0: [(got, 0)]})))
            while ("held", j) not in state:
                yield 1, ()
            held = state["held", j]
            held, got = yield 1, (held, spread(held, MP, x, owner_x))
            riders = []
            if j + depth == last:
                while len(own) < count:
                    yield 1, ()
                riders = [*own[depth:], first_images()]

            def body(number, inputs, outputs):
                here = jnp.full(shape, number[IN_X], jnp.int32) == 1
                pair = halves(jnp.where(here, inputs[0][:piece], inputs[1][:piece]))
                outputs[0][...], outputs[1][...] = pair
                both = product(pair, (inputs[2][...], inputs[3][...]), 1, 1)
                low, high = both[:, :panel], both[:, panel:]
                zeroth = jnp.full(shape, number[C], jnp.int32) == 0
                outputs[2][...] = jnp.where(zeroth, low, high)
                outputs[3][:piece] = jnp.where(zeroth, high, low)
                at = piece
                for rider in inputs[4:]:
                    size = min(rider.shape[0], piece)
                    outputs[3][at : at + size] = rider[:size]
                    at += size

            away_rows = piece + sum(min(rider.shape[0], piece) for rider in riders)
            high, low, state["kept", j], away = call(
                body,
                [(shape, bf16), (shape, bf16), (shape, f32), ((away_rows, panel), f32)],
                numbers,
                [held, got, *state["old"], *riders],
            )
            state["panel", j] = high, low
            _, _, got = yield 1, (high, low, to_partner(away))
            state["swapped", j] = got
            if riders:
                for i in range(depth, count):
                    state["other", i] = got, (i - depth + 1) * piece
                state["images"] = riders[-1], got, (count - depth + 1) * piece

        depth = 2
        rider_rows = -(-(2 * image_rows + block_rows) // 8) * 8

        def first_images():
            def body(number, inputs, outputs):
                right, left = inputs[count][...], inputs[count + 1][...].T
                across = jnp.zeros((1, panel), f32)
                for j in range(count):
                    rows = slice(j * piece, (j + 1) * piece)
                    across += jnp.sum(inputs[j][:piece] * left[rows], axis=0, keepdims=True)
                old = inputs[count + 2][...]
                outputs[0][...] = jnp.zeros((rider_rows, panel), f32)
                outputs[0][2 * image_rows : 2 * image_rows + block_rows] = old[:block_rows]
                for i, vector in enumerate((right, across)):
                    image = jnp.concatenate(
                        [
                            jnp.sum(inputs[j][:piece] * vector, axis=1, keepdims=True).T
                            for j in range(count)
                        ],
                        axis=1,
                    )
                    for r in range(image_rows):
                        at = i * image_rows + r
                        part = image[:, r * panel : (r + 1) * panel]
                        if i:
                            part = part + hidden * old[block_rows + r : block_rows + r + 1]
                        outputs[0][at : at + 1] = part

            return call(
                body,
                [((rider_rows, panel), f32)],
                numbers,
                [
                    *own,
                    panel_of(model * cores + core),
                    row(probe_left),
                    state["old_images"],
                ],
            )[0]

        def over_models(array):
            steps = [(axis, bit) for axis in (PRE, MP) for bit in bits(axis)]
            for i, (axis, bit) in enumerate(steps):
                terms = yield 1, (array, swap(array, axis, bit))
                if i < len(steps) - 1:
                    array = added(numbers, terms)
            return terms

        def first_part(crossed):
            (crossed,) = yield 1, (crossed,)
            crossed = yield from over_models(crossed)
            while "squares" not in state:
                yield 1, ()

            def body(number, sums, inputs, outputs):
                top_left, top_right, scale = scales(inputs[6][...] + inputs[7][...])
                grad = inputs[4][...], inputs[5][...]
                rows = pl.ds(pl.multiple_of(device(number) * own_rows, own_rows), own_rows)
                own = whole_of(inputs[4][rows, :], inputs[5][rows, :])
                crossed = product(halves(inputs[0][...] + inputs[1][...]), grad, 1, 0)
                outputs[0][...] = scale * (
                    25.0 * own
                    - inputs[2][...] * (5.0 / top_left)
                    - (5.0 * inputs[3][...] - crossed / top_left) / top_right
                )

            (state["first_part"],) = fetching(
                body,
                [((own_rows, block), f32)],
                numbers,
                [],
                shape,
                [*crossed, *state["left_parts"], *state["block"], *state["squares"]],
            )

        def left_side():
            while ("other", last) not in state or "images" not in state:
                yield 1, ()
            other = [state["other", j] for j in range(count)]
            images, got, start = state["images"]

            def body(number, inputs, outputs):
                zeroth = jnp.full(shape, number[C], jnp.int32) == 0
                for j in range(count):
                    at = other[j][1]
                    mine, theirs = inputs[j][:piece], inputs[count + j][at : at + piece]
                    rows = pl.ds(j * piece, piece)
                    for i, part in enumerate(
                        (jnp.where(zeroth, mine, theirs), jnp.where(zeroth, theirs, mine))
                    ):
                        columns = pl.ds(i * panel, panel)
                        outputs[0][rows, columns], outputs[1][rows, columns] = halves(part)
                rows = pl.ds(pl.multiple_of(device(number) * own_rows, own_rows), own_rows)
                gram = product(
                    (outputs[0][rows, :], outputs[1][rows, :]),
                    (outputs[0][...], outputs[1][...]),
                    1,
                    1,
                )
                outputs[2][:own_rows] = gram / hidden
                outputs[2][own_rows:] = jnp.zeros((8, width), f32)
                images = inputs[2 * count][...] + inputs[2 * count + 1][start:]
                for i in range(2):
                    for r in range(image_rows):
                        at = i * image_rows + r
                        outputs[2][own_rows + i : own_rows + i + 1, pl.ds(r * panel, panel)] = (
                            images[at : at + 1]
                        )
                for r in range(block_rows):
                    at = 2 * image_rows + r
                    outputs[3][:, pl.ds(r * panel, panel)] = images[at : at + 1]

            rows = (own_rows, width)
            high, low, gram, state["old_image"] = call(
                body,
                [((width, block), bf16)] * 2
                + [((own_rows + 8, width), f32), ((1, block), f32)],
                numbers,
                [*own, *(array for array, _ in other), images, got],
            )
            state["block"] = high, low
            gram = yield from over_models(gram)
            state["left_terms"] = gram

            def body(number, sums, inputs, outputs):
                gram = inputs[0][:own_rows] + inputs[1][:own_rows]
                old = []
                for m in range(models):
                    part = jnp.zeros((own_rows, model_rows), f32)
                    for k in range(models):
                        at = jnp.full(part.shape, number[MODEL], jnp.int32)
                        block_k = inputs[2][:, k * model_rows : (k + 1) * model_rows]
                        part = jnp.where(at == m ^ k, block_k, part)
                    old.append(part)
                left = jnp.concatenate(old, axis=1) + gram
                outputs[0][...] = left
                new = left[:, :model_rows]
                for m in range(1, models):
                    at = jnp.full(new.shape, number[MODEL], jnp.int32)
                    new = jnp.where(at == m, left[:, m * model_rows : (m + 1) * model_rows], new)
                outputs[4][...] = new.T
                grad = inputs[3][...], inputs[4][...]
                left_grad = product(halves(left), grad, 1, 0)
                outputs[1][...] = left_grad
                outputs[2][...] = gram
                outputs[3][...] = product(halves(left_grad), grad, 1, 1) / width

            left, left_grad, gram, crossed, new = fetching(
                body,
                [(rows, f32), ((own_rows, block), f32), (rows, f32), (rows, f32)]
                + [((model_rows, own_rows), f32)],
                numbers,
                [],
                shape,
                [*gram, state["old_left"], *state["block"]],
            )
            state["left"] = left
            windows.add(first_part(crossed))
            state["partner_left"], left_grad, gram = yield 1, (to_partner(left), left_grad, gram)

            def body(number, inputs, outputs):
                grad = inputs[1][...], inputs[2][...]
                outputs[0][...] = product(halves(inputs[0][...]), grad, 1, 0) * (hidden / width)

            (gram_grad,) = call(
                body, [((own_rows, block), f32)], numbers, [gram, *state["block"]]
            )
            state["left_parts"] = yield 1, (left_grad, gram_grad)
            state["left_new"] = new

        def powers():
            while "left_terms" not in state:
                yield 1, ()

            def body(number, inputs, outputs):
                images = inputs[5][own_rows:] + inputs[6][own_rows:]
                outputs[1][...] = images[1:2] / hidden
                grad = whole_of(inputs[1][...], inputs[2][...])
                first = inputs[0][...] + (
                    jnp.sum(grad * images[0:1].T, axis=0, keepdims=True) / width
                )
                outputs[0][:, :width] = jnp.sum(grad * first, axis=1, keepdims=True).T
                old = whole_of(inputs[3][...], inputs[4][...])
                outputs[0][:, width : width + panel] = jnp.sum(
                    old * first.T, axis=0, keepdims=True
                )
                square = jnp.sum(first * first, axis=1, keepdims=True)
                outputs[0][:, width + panel :] = jnp.broadcast_to(square, (1, 128))

            joined, first = call(
                body,
                [((1, width + panel + 128), f32), ((1, width), f32)],
                numbers,
                [
                    state["old_image"],
                    *state["block"],
                    *state["old"],
                    *state["left_terms"],
                ],
            )
            for axis in (PRE, MP):
                for bit in bits(axis):
                    joined = added(numbers, [joined, swap(joined, axis, bit)])
            first, joined = yield 1, (first, joined)
            while "left" not in state or ("panel", last) not in state:
                yield 1, ()

            def body(number, inputs, outputs):
                joined = inputs[2 + 2 * count][...]
                for array in inputs[3 + 2 * count :]:
                    joined = joined + array[...]
                vector = joined[:, :width].T
                second = joined[:, width : width + panel]
                for j in range(count):
                    part = whole_of(inputs[2 + 2 * j][...], inputs[3 + 2 * j][...])
                    rows = vector[j * piece : (j + 1) * piece]
                    second = second + jnp.sum(part * rows, axis=0, keepdims=True) / width
                square = joined[:, width + panel : width + panel + 1]
                second = second / jnp.sqrt(square + norm_floor)
                right = jnp.sum(second * second, axis=1, keepdims=True)
                first = inputs[0][...]
                unit = first / jnp.sqrt(
                    jnp.sum(first * first, axis=1, keepdims=True) + norm_floor
                )
                second = jnp.sum(inputs[1][...] * unit, axis=1, keepdims=True)
                left = jnp.sum(second * second, axis=0, keepdims=True)
                spot = lax.broadcasted_iota(jnp.int32, (1, 128), 1)
                outputs[0][...] = jnp.where(spot == 0, left, right)

            panels = [half for j in range(count) for half in state["panel", j]]
            (squares,) = call(
                body,
                [((1, 128), f32)],
                numbers,
                [first, state["left"], *panels, joined],
            )
            squares = added(numbers, [squares, to_partner(squares)])
            for bit in bits(LINE)[:-2]:
                squares = added(numbers, [squares, swap(squares, LINE, bit)])
            squares = added(numbers, (yield 1, (squares, swap(squares, LINE, bits(LINE)[-2]))))
            state["squares"] = yield 1, (squares, swap(squares, LINE, bits(LINE)[-1]))

        def scales(squares):
            top = jnp.sqrt(squares + norm_floor)
            top_left, top_right = top[:, 0:1], top[:, 1:2]
            return top_left, top_right, 1.0 / (16.0 * jnp.sqrt(jnp.sqrt(top_left * top_right)))

        def right_factor():
            while ("panel", last) not in state or "block" not in state or windows.now < steps + 2:
                yield 1, ()

            def body(number, sums, inputs, outputs):
                pair = [
                    jnp.concatenate([inputs[3 + 2 * j + i][...] for j in range(count)], axis=0)
                    for i in range(2)
                ]
                gram = product((inputs[1][...], inputs[2][...]), pair, 0, 0)
                outputs[0][...] = beta_decay * inputs[0][...] + gram / width

            panels = [half for j in range(count) for half in state["panel", j]]
            (state["right_new"],) = yield 1, fetching(
                body,
                [((block, panel), f32)],
                numbers,
                [],
                shape,
                [right_old, *state["block"], *panels],
                44,
            )

        for j in range(count):
            windows.add(panel_piece(j))
        steps = count + line - 2
        def rows_here(number, i, rows, pieces):
            other = number[C] if i == 0 else 1 - number[C]
            at = jnp.full(rows.shape, number[Z] * cores + other, jnp.int32)
            for k in range(line * cores):
                j, start = divmod(k * own_rows, piece)
                for number_j, array in pieces:
                    if number_j == j:
                        rows = jnp.where(at == k, array[start : start + own_rows], rows)
            return rows

        def early_products():
            while len(mixed_wholes) < last or "partner_left" not in state:
                yield 1, ()

            def body(number, sums, inputs, outputs):
                pieces = [(j, inputs[2 + j]) for j in range(last)]
                pair = halves(jnp.concatenate([array[:piece] for _, array in pieces], axis=0))
                for i in range(2):
                    left = halves(inputs[i][:, : last * piece])
                    outputs[i][...] = product(left, pair, 1, 0)
                    outputs[2 + i][...] = rows_here(
                        number, i, jnp.zeros((own_rows, panel), f32), pieces
                    )

            state["early"] = yield 1, fetching(
                body,
                [((own_rows, panel), f32)] * 4,
                numbers,
                [],
                shape,
                [state["left"], state["partner_left"], *mixed_wholes],
            )

        mixed_wholes = []
        for process in (left_side, powers, right_factor, early_products):
            windows.add(process())

        for t in range(2 * steps):
            windows.open()
            current = gradient if t < steps else mixed
            choices = current.next_sums(t % steps) + gradient.finished(t)
            choices += mixed.finished(t - steps)
            names = [name for name, _ in wishes]
            choices += [choice for _, choice in wishes]
            wishes.clear()
            crowded = t == line + depth - 1
            longer = tail_rows + (16 if steps < t < steps + 3 else 8 if crowded else 0)
            extra = [longer] * 2 + [0] * (len(choices) - 2)
            for i, name in enumerate(names):
                extra[len(extra) - len(names) + i] = 8 if crowded else 0
            if crowded:
                extra[2] = 8
            if ("held", last) in names:
                extra[-1] = longer
            tails = []
            if t < steps and "tail" in state:
                tails = gradient.next_tails(t, tail_piece, state["tail"])
            results = list(chosen_sums(numbers, choices, shape, extra, tails))
            if t == 0:
                results[0], results[1], activations, grad_output, left_old, right_old = tie(
                    (*results, activations, grad_output, left_old, right_old)
                )
                windows.add(old_factors())
                windows.add(old_left())
                kept, *away = local(1, count)
                kept_rest.append(kept)
                arrived += [to_partner(a) for a in away]
            current.send(*results[:2])
            for name in reversed(names):
                state[name] = results.pop()
            (own if len(own) < count else mixed_wholes).extend(results[2:])
            if t == tail_piece + line - 1:
                tail = gradient.finished_tail(tail_piece, state["tail"])

                def copy_body(number, sums, inputs, outputs):
                    outputs[0][...] = sums[0][...]

                (state["old_images"],) = fetching(
                    copy_body, [(tail[2], f32)], numbers, [tail], shape
                )
            windows.open()
            current.out[-1], current.home[-1] = windows.close(current.out[-1], current.home[-1])
        while windows.processes:
            windows.open()
            if windows.processes:
                windows.close()

        def body(number, sums, inputs, outputs):
            top_left, top_right, scale = scales(inputs[0][...] + inputs[1][...])
            pair = halves(sums[0][...])
            for i in range(2):
                rows = rows_here(number, i, inputs[6 + i][...], [(last, sums[0])])
                left = halves(inputs[2 + i][:, last * piece :])
                left = inputs[4 + i][...] + product(left, pair, 1, 0)
                outputs[i][...] = (left / top_left - 5.0 * rows) * (scale / top_right)

        mine, theirs = fetching(
            body,
            [((own_rows, panel), f32)] * 2,
            numbers,
            mixed.finished(steps),
            shape,
            [*state["squares"], state["left"], state["partner_left"], *state["early"]],
        )
        theirs = to_partner(theirs)

        def body(number, inputs, outputs):
            zeroth = jnp.full((own_rows, panel), number[C], jnp.int32) == 0
            mine, theirs = inputs[1][...], inputs[2][...]
            parts = jnp.where(zeroth, mine, theirs), jnp.where(zeroth, theirs, mine)
            for i, part in enumerate(parts):
                span = pl.ds(i * panel, panel)
                outputs[0][:, span] = inputs[0][:, span] + part

        (update,) = call(
            body, [((own_rows, block), f32)], numbers, [state["first_part"], mine, theirs]
        )
        return state["left_new"], state["right_new"], update

    return shards


def solution(mesh):
    dp, mp, pre = (mesh.shape[name] for name in ("dp", "mp", "pre"))
    cores = dp // (mp * pre)
    assert cores == 2
    split = Mesh(mesh.devices.reshape(dp // cores, cores, mp, pre), AXES)
    factor = P((MP, PRE), (LINE, CORE))
    in_specs = (
        P((LINE, CORE), None),
        P((LINE, CORE), (MP, PRE)),
        factor,
        factor,
        P(),
        P(),
    )
    out_specs = (factor, factor, P((LINE, CORE), (MP, PRE)))
    return jax.shard_map(
        make_step(dict(split.shape)),
        mesh=split,
        in_specs=in_specs,
        out_specs=out_specs,
        check_vma=False,
    )
```

```python
import jax
import jax.numpy as jnp
from jax import lax
from jax.experimental import pallas as pl
from jax.experimental.pallas import tpu as pltpu
from jax.sharding import Mesh, PartitionSpec as P

beta_decay = 0.9
norm_floor = 1e-06
count = 4

LINE, CORE, MP, PRE = "line", "core", "mp", "pre"
AXES = (LINE, CORE, MP, PRE)
f32, bf16 = jnp.float32, jnp.bfloat16


def halves(x):
    high = x.astype(bf16)
    return high, (x - high.astype(f32)).astype(bf16)


def whole_of(high, low):
    return high.astype(f32) + low.astype(f32)


def product(a, b, a_dim, b_dim):
    def one(x, y):
        return lax.dot_general(
            x, y, (((a_dim,), (b_dim,)), ((), ())), preferred_element_type=f32
        )

    return one(a[0], b[0]) + (one(a[0], b[1]) + one(a[1], b[0]))


def select_by(index, options):
    result = None
    for value, array in options.items():
        result = array if result is None else jnp.where(index == value, array, result)
    return result


def tie(values):
    return lax.optimization_barrier(tuple(values))


def call(body, outputs, numbers, arrays, space=pltpu.VMEM, scratch=(), mebibytes=32):
    inputs, results = len(arrays), len(outputs)
    spaces = space if isinstance(space, list) else [space] * inputs

    def kernel(*refs):
        body(
            refs[0],
            refs[1 : 1 + inputs],
            refs[1 + inputs : 1 + inputs + results],
            *refs[1 + inputs + results :],
        )

    return pl.pallas_call(
        kernel,
        out_shape=[jax.ShapeDtypeStruct(shape, dtype) for shape, dtype in outputs],
        in_specs=[pl.BlockSpec(memory_space=pltpu.SMEM)]
        + [pl.BlockSpec(memory_space=s) for s in spaces],
        out_specs=[pl.BlockSpec(memory_space=pltpu.VMEM)] * results,
        scratch_shapes=scratch,
        compiler_params=pltpu.CompilerParams(vmem_limit_bytes=mebibytes << 20),
        cost_estimate=pl.CostEstimate(flops=1, bytes_accessed=1, transcendentals=0),
    )(numbers, *arrays)


def added(numbers, arrays):
    def body(number, inputs, outputs):
        total = inputs[0][...]
        for array in inputs[1:]:
            total = total + array[...]
        outputs[0][...] = total

    return call(body, [(arrays[0].shape, f32)], numbers, arrays)[0]


def fetching(body, outputs, numbers, choices, shape, arrays=(), mebibytes=24, pinned=()):
    sources = []

    def place(array):
        for i, known in enumerate(sources):
            if known is array:
                return i
        sources.append(array)
        return len(sources) - 1

    shapes = [choice[2] if len(choice) > 2 else shape for choice in choices]
    choices = [
        (choice[0], {k: [(place(a), r) for a, r in terms] for k, terms in choice[1].items()})
        for choice in choices
    ]
    wholes = [place(array) for array in arrays]
    most = [max(1, *(len(t) for t in options.values())) for _, options in choices]
    many = len(choices)

    def inner(number, inputs, results, *scratch):
        held, kept = scratch[:many], scratch[many:-2]
        sems, kept_sems = scratch[-2:]

        def copies(o, terms):
            return [
                pltpu.make_async_copy(
                    inputs[a].at[pl.ds(r, shapes[o][0])], held[o].at[i], sems.at[o, i]
                )
                for i, (a, r) in enumerate(terms)
            ]

        loads = [
            pltpu.make_async_copy(inputs[a], kept[i], kept_sems.at[i])
            for i, a in enumerate(wholes)
        ]
        for o, (which, options) in enumerate(choices):
            for k, terms in options.items():

                @pl.when(number[which] == k)
                def _():
                    for copy in copies(o, terms):
                        copy.start()

        for copy in loads:
            copy.start()
        for o, (which, options) in enumerate(choices):
            for k, terms in options.items():

                @pl.when(number[which] == k)
                def _():
                    for copy in copies(o, terms):
                        copy.wait()
                    if not terms:
                        held[o][0] = jnp.zeros(shapes[o], f32)
                    if len(terms) > 1:
                        total = held[o][0]
                        for i in range(1, len(terms)):
                            total = total + held[o][i]
                        held[o][0] = total

        for copy in loads:
            copy.wait()
        body(number, [held[o].at[0] for o in range(many)], kept, results)

    return call(
        inner,
        outputs,
        numbers,
        sources,
        [pltpu.HBM if any(a is p for p in pinned) else pl.ANY for a in sources],
        [
            *[pltpu.VMEM((m,) + tuple(s), f32) for m, s in zip(most, shapes)],
            *[pltpu.VMEM(array.shape, array.dtype) for array in arrays],
            pltpu.SemaphoreType.DMA((max(many, 1), max(most + [1]))),
            pltpu.SemaphoreType.DMA((max(len(arrays), 1),)),
        ],
        mebibytes,
    )


def chosen_sums(numbers, choices, shape, more, tails, pinned):
    many = len(choices)
    sizes = [tail[2][0] for tail in tails] + [0] * (many - len(tails))

    def body(number, sums, inputs, outputs):
        for i, (result, rows, size) in enumerate(zip(outputs, more, sizes)):
            at = shape[0]
            result[:at] = sums[i][...]
            if size:
                result[at : at + size] = sums[many + i][...]
            if rows > size:
                result[at + size :] = jnp.zeros((rows - size,) + shape[1:], f32)

    out = [((shape[0] + rows,) + shape[1:], f32) for rows in more]
    return fetching(body, out, numbers, choices + tails, shape, pinned=pinned)


class Windows:
    def __init__(self):
        self.now = 0
        self.processes = []

    def add(self, process):
        self.processes.append([process, None, None])

    def open(self):
        ended = []
        for entry in self.processes:
            process, due, values = entry
            if values and due >= self.now:
                continue
            try:
                windows, entry[2] = process.send(values)
                entry[1] = self.now + windows - 1
            except StopIteration:
                ended.append(entry)
        for entry in ended:
            self.processes.remove(entry)

    def close(self, *others):
        due = [entry for entry in self.processes if entry[1] == self.now and entry[2]]
        flat = list(others)
        for entry in due:
            flat.extend(entry[2])
        if flat:
            flat = list(tie(flat))
        at = len(others)
        for entry in due:
            size = len(entry[2])
            entry[2] = flat[at : at + size]
            at += size
        self.now += 1
        return flat[: len(others)]


def make_step(sizes):
    line, cores, mp, pre = (sizes[name] for name in AXES)
    models = mp * pre
    last = count - 1

    def swap(array, axis, bit):
        return lax.ppermute(array, axis, [(i, i ^ bit) for i in range(sizes[axis])])

    def bits(axis):
        return [1 << i for i in range(sizes[axis].bit_length() - 1)]

    def total(numbers, array, axes):
        for axis in axes:
            for bit in bits(axis):
                pair = yield 1, (array, swap(array, axis, bit))
                array = added(numbers, pair)
        return array

    def snake(array, outward):
        pairs = []
        for z in range(line):
            for c in range(cores):
                goal = z + (1 if (c == 0) == outward else -1)
                if 0 <= goal < line:
                    pairs.append((z * cores + c, goal * cores + c))
                else:
                    pairs.append((z * cores + c, z * cores + 1 - c))
        return lax.ppermute(array, (LINE, CORE), pairs)

    def shards(activations, grad_output, left_old, right_old, probe_left, probe_right):
        z, core = lax.axis_index(LINE), lax.axis_index(CORE)
        x, y = lax.axis_index(MP), lax.axis_index(PRE)
        model = x * pre + y
        width = activations.shape[1]
        block = grad_output.shape[1]
        hidden = block * models
        panel = block // cores
        own_rows = width // (line * cores)
        model_rows = width // models
        piece = width // count
        owner_x, owner_y = z // pre, z % pre
        there = jnp.where(core == 0, z, line - 1 - z)
        numbers = jnp.stack(
            [z, core, there, line - 1 - there, x == owner_x, y == owner_y, model]
        ).astype(jnp.int32)
        Z, C, THERE, BACK, IN_X, IN_Y, MODEL = range(7)
        shape = (piece, panel)
        windows = Windows()
        state = {}

        def to_partner(array):
            return swap(array, CORE, 1)

        def device(number):
            return number[Z] * cores + number[C]

        def local(first, end):
            rows = (end - first) * piece
            tokens = activations.shape[0]
            parts, slices = 4, 3
            span = tokens // parts
            thin = span // slices

            def body(number, inputs, outputs, left, right, sems):
                copies = []
                for i in range(parts):
                    for k in range(slices):
                        at = pl.ds(i * span + k * thin, thin)
                        copies.append(
                            pltpu.make_async_copy(
                                inputs[0].at[at, pl.ds(first * piece, rows)],
                                left.at[at],
                                sems.at[0, i, k],
                            )
                        )
                        copies.append(
                            pltpu.make_async_copy(
                                inputs[1].at[at], right.at[at], sems.at[1, i, k]
                            )
                        )
                for copy in copies:
                    copy.start()
                sums = [None] * (end - first)
                for i in range(parts):
                    for copy in copies[2 * slices * i : 2 * slices * (i + 1)]:
                        copy.wait()
                    at = slice(i * span, (i + 1) * span)
                    for j in range(end - first):
                        term = lax.dot_general(
                            left[at, j * piece : (j + 1) * piece],
                            right[at],
                            (((0,), (0,)), ((), ())),
                            preferred_element_type=f32,
                        )
                        sums[j] = term if i == 0 else sums[j] + term
                zeroth = jnp.full(shape, number[C], jnp.int32) == 0
                for j, both in enumerate(sums):
                    low, high = both[:, :panel], both[:, panel:]
                    outputs[0][j * piece : (j + 1) * piece] = jnp.where(zeroth, low, high)
                    outputs[1 + j][...] = jnp.where(zeroth, high, low)

            return call(
                body,
                [((rows, panel), f32)] + [(shape, f32)] * (end - first),
                numbers,
                [activations, grad_output],
                pl.ANY,
                [
                    pltpu.VMEM((tokens, rows), bf16),
                    pltpu.VMEM(grad_output.shape, bf16),
                    pltpu.SemaphoreType.DMA((2, parts, slices)),
                ],
                60,
            )

        kept_first, away = local(0, 1)
        arrived = [to_partner(away)]

        class Chain:
            def __init__(self, terms):
                self.terms = terms
                self.sent, self.out, self.home, self.options = [], [], [], []

            def next_sums(self, t):
                choices = []
                for which, got in ((THERE, self.out), (BACK, self.home)):
                    options = {}
                    for k in range(line):
                        options[k] = []
                        if 0 <= t - k < count:
                            options[k] = self.terms(t - k)
                            if k:
                                options[k] = options[k] + [(got[t - 1], 0)]
                    choices.append((which, options))
                return choices

            def next_tails(self, t, piece_number, array):
                choices = []
                if not 0 <= t - piece_number < line:
                    return choices
                for which, got in ((THERE, self.out), (BACK, self.home)):
                    options = {k: [] for k in range(line)}
                    k = t - piece_number
                    options[k] = [(array, 0)] + ([(got[t - 1], piece)] if k else [])
                    choices.append((which, options, array.shape))
                return choices

            def finished_tail(self, piece_number, array):
                j = piece_number
                options = {
                    k: [(self.sent[j + k], piece), (self.home[j + line - 2 - k], piece)]
                    for k in range(line - 1)
                }
                options[line - 1] = [(array, 0), (self.out[j + line - 2], piece)]
                return THERE, options, array.shape

            def send(self, going_out, going_home):
                self.sent.append(going_out)
                self.out.append(snake(going_out, True))
                self.home.append(snake(going_home, False))

            def finished(self, t):
                j = t - (line - 1)
                if not 0 <= j < count:
                    return []
                options = {
                    k: [(self.sent[j + k], 0), (self.home[j + line - 2 - k], 0)]
                    for k in range(line - 1)
                }
                options[line - 1] = self.terms(j) + [(self.out[j + line - 2], 0)]
                self.options.append((THERE, options))
                return self.options[-1:]

        gradient = Chain(
            lambda j: [
                (kept_rest[0], (j - 1) * piece) if j else (kept_first, 0),
                (arrived[j], 0),
            ]
        )
        mixed = Chain(lambda j: [(state["kept", j], 0), (state["swapped", j], 0)])
        own, wishes, kept_rest = [], [], []

        def row(array):
            return array.reshape(1, -1)

        def exchange(array, axis):
            return total(numbers, array, (axis,))

        def placed(number, column):
            wide = (own_rows, width)
            at = lax.broadcasted_iota(jnp.int32, wide, 0) + device(number) * own_rows
            here = lax.broadcasted_iota(jnp.int32, wide, 1) == at
            return jnp.sum(jnp.where(here, column, 0.0), axis=0, keepdims=True)

        def panel_of(which):
            return row(lax.dynamic_slice_in_dim(probe_right, which * panel, panel, 0))

        def beside(first, second):
            def body(number, inputs, outputs):
                size = inputs[0].shape[1]
                outputs[0][:, :size] = inputs[0][...]
                outputs[0][:, size:] = inputs[1][...]

            shape = first.shape[0], first.shape[1] + second.shape[1]
            return call(body, [(shape, f32)], numbers, [first, second])[0]

        def left_turned():
            return (beta_decay * left_old).T

        block_rows, image_rows = block // panel, width // panel
        tail_rows = -(-(block_rows + image_rows) // 8) * 8
        tail_piece = 2

        def old_factors():
            while windows.now < 1:
                yield 1, ()

            def body(number, inputs, outputs):
                old = beta_decay * inputs[0][...]
                outputs[0][...], outputs[1][...] = halves(old)
                image = jnp.sum(old * inputs[1][...], axis=1, keepdims=True).T
                outputs[2][...] = jnp.zeros((tail_rows, panel), f32)
                for r in range(block_rows):
                    outputs[2][r : r + 1] = image[:, r * panel : (r + 1) * panel]
                image = jnp.sum(inputs[2][...] * inputs[3][...], axis=1, keepdims=True)
                image = placed(number, image)
                for r in range(image_rows):
                    at = block_rows + r
                    outputs[2][at : at + 1] = image[:, r * panel : (r + 1) * panel]

            own_probe = lax.dynamic_slice_in_dim(probe_left, model * model_rows, model_rows, 0)
            high, low, images = call(
                body,
                [((block, panel), bf16), ((block, panel), bf16), ((tail_rows, panel), f32)],
                numbers,
                [right_old, panel_of(z * cores + core), left_turned(), row(own_probe)],
            )
            *state["old"], state["tail"] = yield 1, (high, low, images)

        def old_left():
            while windows.now < 1:
                yield 1, ()
            rows = left_turned()
            for axis in (PRE, MP):
                for bit in bits(axis):
                    rows, got = yield 1, (rows, swap(rows, axis, bit))
                    rows = beside(rows, got)
            state["old_left"] = rows

        def spread(array, axis, place, owner):
            result = None
            size = sizes[axis]
            for s in range(1, size):
                got = lax.ppermute(array, axis, [(i, (i + s) % size) for i in range(size)])
                if result is None:
                    result = got
                else:
                    result = jnp.where((place - s) % size == owner, got, result)
            return result

        def panel_piece(j):
            while len(own) <= j:
                yield 1, ()
            if j < depth:
                other, got = yield 1, (to_partner(own[j]), spread(own[j], PRE, y, owner_y))
                state["other", j] = other, 0
            else:
                (got,) = yield 1, (spread(own[j], PRE, y, owner_y),)
            wishes.append((("held", j), (IN_Y, {1: [(own[j], 0)], 0: [(got, 0)]})))
            while ("held", j) not in state:
                yield 1, ()
            held = state["held", j]
            held, got = yield 1, (held, spread(held, MP, x, owner_x))
            riders = []
            if j + depth == last:
                while len(own) < count:
                    yield 1, ()
                riders = [*own[depth:], first_images()]

            def body(number, inputs, outputs):
                here = jnp.full(shape, number[IN_X], jnp.int32) == 1
                pair = halves(jnp.where(here, inputs[0][:piece], inputs[1][:piece]))
                outputs[0][...], outputs[1][...] = pair
                both = product(pair, (inputs[2][...], inputs[3][...]), 1, 1)
                low, high = both[:, :panel], both[:, panel:]
                zeroth = jnp.full(shape, number[C], jnp.int32) == 0
                outputs[2][...] = jnp.where(zeroth, low, high)
                outputs[3][:piece] = jnp.where(zeroth, high, low)
                at = piece
                for rider in inputs[4:]:
                    size = min(rider.shape[0], piece)
                    outputs[3][at : at + size] = rider[:size]
                    at += size

            away_rows = piece + sum(min(rider.shape[0], piece) for rider in riders)
            high, low, state["kept", j], away = call(
                body,
                [(shape, bf16), (shape, bf16), (shape, f32), ((away_rows, panel), f32)],
                numbers,
                [held, got, *state["old"], *riders],
            )
            state["panel", j] = high, low
            _, _, got = yield 1, (high, low, to_partner(away))
            state["swapped", j] = got
            if riders:
                for i in range(depth, count):
                    state["other", i] = got, (i - depth + 1) * piece
                state["images"] = riders[-1], got, (count - depth + 1) * piece

        depth = 2
        rider_rows = -(-(2 * image_rows + block_rows) // 8) * 8

        def first_images():
            def body(number, inputs, outputs):
                right, left = inputs[count][...], inputs[count + 1][...].T
                across = jnp.zeros((1, panel), f32)
                for j in range(count):
                    rows = slice(j * piece, (j + 1) * piece)
                    across += jnp.sum(inputs[j][:piece] * left[rows], axis=0, keepdims=True)
                old = inputs[count + 2][...]
                outputs[0][...] = jnp.zeros((rider_rows, panel), f32)
                outputs[0][2 * image_rows : 2 * image_rows + block_rows] = old[:block_rows]
                for i, vector in enumerate((right, across)):
                    image = jnp.concatenate(
                        [
                            jnp.sum(inputs[j][:piece] * vector, axis=1, keepdims=True).T
                            for j in range(count)
                        ],
                        axis=1,
                    )
                    for r in range(image_rows):
                        at = i * image_rows + r
                        part = image[:, r * panel : (r + 1) * panel]
                        if i:
                            part = part + hidden * old[block_rows + r : block_rows + r + 1]
                        outputs[0][at : at + 1] = part

            return call(
                body,
                [((rider_rows, panel), f32)],
                numbers,
                [
                    *own,
                    panel_of(model * cores + core),
                    row(probe_left),
                    state["old_images"],
                ],
            )[0]

        def over_models(array):
            steps = [(axis, bit) for axis in (PRE, MP) for bit in bits(axis)]
            for i, (axis, bit) in enumerate(steps):
                terms = yield 1, (array, swap(array, axis, bit))
                if i < len(steps) - 1:
                    array = added(numbers, terms)
            return terms

        def first_part(crossed):
            (crossed,) = yield 1, (crossed,)
            crossed = yield from over_models(crossed)
            while "squares" not in state:
                yield 1, ()

            def body(number, sums, inputs, outputs):
                top_left, top_right, scale = scales(inputs[6][...] + inputs[7][...])
                grad = inputs[4][...], inputs[5][...]
                rows = pl.ds(pl.multiple_of(device(number) * own_rows, own_rows), own_rows)
                own = whole_of(inputs[4][rows, :], inputs[5][rows, :])
                crossed = product(halves(inputs[0][...] + inputs[1][...]), grad, 1, 0)
                outputs[0][...] = scale * (
                    25.0 * own
                    - inputs[2][...] * (5.0 / top_left)
                    - (5.0 * inputs[3][...] - crossed / top_left) / top_right
                )

            (state["first_part"],) = fetching(
                body,
                [((own_rows, block), f32)],
                numbers,
                [],
                shape,
                [*crossed, *state["left_parts"], *state["block"], *state["squares"]],
            )

        def hold_block():
            state["block"] = yield 1, state["block"]

        def left_side():
            while ("other", last) not in state or "images" not in state:
                yield 1, ()
            other = [state["other", j] for j in range(count)]
            images, got, start = state["images"]

            def split_block(number, inputs, high, low):
                zeroth = jnp.full(shape, number[C], jnp.int32) == 0
                for j in range(count):
                    at = other[j][1]
                    mine, theirs = inputs[j][:piece], inputs[count + j][at : at + piece]
                    rows = pl.ds(j * piece, piece)
                    for i, part in enumerate(
                        (jnp.where(zeroth, mine, theirs), jnp.where(zeroth, theirs, mine))
                    ):
                        columns = pl.ds(i * panel, panel)
                        high[rows, columns], low[rows, columns] = halves(part)

            def body(number, inputs, outputs, high, low):
                split_block(number, inputs, high, low)
                rows = pl.ds(pl.multiple_of(device(number) * own_rows, own_rows), own_rows)
                gram = product((high[rows, :], low[rows, :]), (high[...], low[...]), 1, 1)
                outputs[0][:own_rows] = gram / hidden
                outputs[0][own_rows:] = jnp.zeros((8, width), f32)
                images = inputs[2 * count][...] + inputs[2 * count + 1][start:]
                for i in range(2):
                    for r in range(image_rows):
                        at = i * image_rows + r
                        outputs[0][own_rows + i : own_rows + i + 1, pl.ds(r * panel, panel)] = (
                            images[at : at + 1]
                        )
                for r in range(block_rows):
                    at = 2 * image_rows + r
                    outputs[1][:, pl.ds(r * panel, panel)] = images[at : at + 1]

            rows = (own_rows, width)
            sources = [*own, *(array for array, _ in other)]
            gram, state["old_image"] = call(
                body,
                [((own_rows + 8, width), f32), ((1, block), f32)],
                numbers,
                [*sources, images, got],
                scratch=[pltpu.VMEM((width, block), bf16)] * 2,
            )

            def body(number, inputs, outputs):
                split_block(number, inputs, *outputs)

            high, low = call(body, [((width, block), bf16)] * 2, numbers, sources)
            state["block"] = high, low
            windows.add(hold_block())
            gram = yield from over_models(gram)
            state["left_terms"] = gram

            def body(number, sums, inputs, outputs):
                gram = inputs[0][:own_rows] + inputs[1][:own_rows]
                old = []
                for m in range(models):
                    part = jnp.zeros((own_rows, model_rows), f32)
                    for k in range(models):
                        at = jnp.full(part.shape, number[MODEL], jnp.int32)
                        block_k = inputs[2][:, k * model_rows : (k + 1) * model_rows]
                        part = jnp.where(at == m ^ k, block_k, part)
                    old.append(part)
                left = jnp.concatenate(old, axis=1) + gram
                outputs[0][...] = left
                new = left[:, :model_rows]
                for m in range(1, models):
                    at = jnp.full(new.shape, number[MODEL], jnp.int32)
                    new = jnp.where(at == m, left[:, m * model_rows : (m + 1) * model_rows], new)
                outputs[4][...] = new.T
                grad = inputs[3][...], inputs[4][...]
                left_grad = product(halves(left), grad, 1, 0)
                outputs[1][...] = left_grad
                outputs[2][...] = gram
                outputs[3][...] = product(halves(left_grad), grad, 1, 1) / width

            left, left_grad, gram, crossed, new = fetching(
                body,
                [(rows, f32), ((own_rows, block), f32), (rows, f32), (rows, f32)]
                + [((model_rows, own_rows), f32)],
                numbers,
                [],
                shape,
                [*gram, state["old_left"], *state["block"]],
            )
            state["left"] = left
            windows.add(first_part(crossed))
            state["partner_left"], left_grad, gram = yield 1, (to_partner(left), left_grad, gram)

            def body(number, inputs, outputs):
                grad = inputs[1][...], inputs[2][...]
                outputs[0][...] = product(halves(inputs[0][...]), grad, 1, 0) * (hidden / width)

            (gram_grad,) = call(
                body, [((own_rows, block), f32)], numbers, [gram, *state["block"]]
            )
            state["left_parts"] = yield 1, (left_grad, gram_grad)
            state["left_new"] = new

        def powers():
            while "left_terms" not in state:
                yield 1, ()

            def body(number, inputs, outputs):
                images = inputs[5][own_rows:] + inputs[6][own_rows:]
                outputs[1][...] = images[1:2] / hidden
                grad = whole_of(inputs[1][...], inputs[2][...])
                first = inputs[0][...] + (
                    jnp.sum(grad * images[0:1].T, axis=0, keepdims=True) / width
                )
                outputs[0][:, :width] = jnp.sum(grad * first, axis=1, keepdims=True).T
                old = whole_of(inputs[3][...], inputs[4][...])
                outputs[0][:, width : width + panel] = jnp.sum(
                    old * first.T, axis=0, keepdims=True
                )
                square = jnp.sum(first * first, axis=1, keepdims=True)
                outputs[0][:, width + panel :] = jnp.broadcast_to(square, (1, 128))

            joined, first = call(
                body,
                [((1, width + panel + 128), f32), ((1, width), f32)],
                numbers,
                [
                    state["old_image"],
                    *state["block"],
                    *state["old"],
                    *state["left_terms"],
                ],
            )
            for axis in (PRE, MP):
                for bit in bits(axis):
                    joined = added(numbers, [joined, swap(joined, axis, bit)])
            first, joined = yield 1, (first, joined)
            while "left" not in state or ("panel", last) not in state:
                yield 1, ()

            def body(number, inputs, outputs):
                joined = inputs[2 + 2 * count][...]
                for array in inputs[3 + 2 * count :]:
                    joined = joined + array[...]
                vector = joined[:, :width].T
                second = joined[:, width : width + panel]
                for j in range(count):
                    part = whole_of(inputs[2 + 2 * j][...], inputs[3 + 2 * j][...])
                    rows = vector[j * piece : (j + 1) * piece]
                    second = second + jnp.sum(part * rows, axis=0, keepdims=True) / width
                square = joined[:, width + panel : width + panel + 1]
                second = second / jnp.sqrt(square + norm_floor)
                right = jnp.sum(second * second, axis=1, keepdims=True)
                first = inputs[0][...]
                unit = first / jnp.sqrt(
                    jnp.sum(first * first, axis=1, keepdims=True) + norm_floor
                )
                second = jnp.sum(inputs[1][...] * unit, axis=1, keepdims=True)
                left = jnp.sum(second * second, axis=0, keepdims=True)
                spot = lax.broadcasted_iota(jnp.int32, (1, 128), 1)
                outputs[0][...] = jnp.where(spot == 0, left, right)

            panels = [half for j in range(count) for half in state["panel", j]]
            (squares,) = call(
                body,
                [((1, 128), f32)],
                numbers,
                [first, state["left"], *panels, joined],
            )
            squares = added(numbers, [squares, to_partner(squares)])
            for bit in bits(LINE)[:-2]:
                squares = added(numbers, [squares, swap(squares, LINE, bit)])
            squares = added(numbers, (yield 1, (squares, swap(squares, LINE, bits(LINE)[-2]))))
            state["squares"] = yield 1, (squares, swap(squares, LINE, bits(LINE)[-1]))

        def scales(squares):
            top = jnp.sqrt(squares + norm_floor)
            top_left, top_right = top[:, 0:1], top[:, 1:2]
            return top_left, top_right, 1.0 / (16.0 * jnp.sqrt(jnp.sqrt(top_left * top_right)))

        def right_factor():
            while ("panel", last) not in state or "block" not in state or windows.now < steps + 2:
                yield 1, ()

            def body(number, sums, inputs, outputs):
                pair = [
                    jnp.concatenate([inputs[3 + 2 * j + i][...] for j in range(count)], axis=0)
                    for i in range(2)
                ]
                gram = product((inputs[1][...], inputs[2][...]), pair, 0, 0)
                outputs[0][...] = beta_decay * inputs[0][...] + gram / width

            panels = [half for j in range(count) for half in state["panel", j]]
            (state["right_new"],) = yield 1, fetching(
                body,
                [((block, panel), f32)],
                numbers,
                [],
                shape,
                [right_old, *state["block"], *panels],
                44,
            )

        for j in range(count):
            windows.add(panel_piece(j))
        steps = count + line - 2
        def rows_here(number, i, rows, pieces):
            other = number[C] if i == 0 else 1 - number[C]
            at = jnp.full(rows.shape, number[Z] * cores + other, jnp.int32)
            for k in range(line * cores):
                j, start = divmod(k * own_rows, piece)
                for number_j, array in pieces:
                    if number_j == j:
                        rows = jnp.where(at == k, array[start : start + own_rows], rows)
            return rows

        def early_products():
            while len(mixed_wholes) < last or "partner_left" not in state:
                yield 1, ()

            def body(number, sums, inputs, outputs):
                pieces = [(j, inputs[2 + j]) for j in range(last)]
                pair = halves(jnp.concatenate([array[:piece] for _, array in pieces], axis=0))
                for i in range(2):
                    left = halves(inputs[i][:, : last * piece])
                    outputs[i][...] = product(left, pair, 1, 0)
                    outputs[2 + i][...] = rows_here(
                        number, i, jnp.zeros((own_rows, panel), f32), pieces
                    )

            state["early"] = yield 1, fetching(
                body,
                [((own_rows, panel), f32)] * 4,
                numbers,
                [],
                shape,
                [state["left"], state["partner_left"], *mixed_wholes],
            )

        mixed_wholes = []
        for process in (left_side, powers, right_factor, early_products):
            windows.add(process())

        for t in range(2 * steps):
            windows.open()
            current = gradient if t < steps else mixed
            choices = current.next_sums(t % steps) + gradient.finished(t)
            choices += mixed.finished(t - steps)
            names = [name for name, _ in wishes]
            choices += [choice for _, choice in wishes]
            wishes.clear()
            crowded = t == line + depth - 1
            longer = tail_rows + (16 if steps < t < steps + 3 else 8 if crowded else 0)
            extra = [longer] * 2 + [0] * (len(choices) - 2)
            for i, name in enumerate(names):
                extra[len(extra) - len(names) + i] = 8 if crowded else 0
            if crowded:
                extra[2] = 8
            if ("held", last) in names:
                extra[-1] = longer
            tails = []
            if t < steps and "tail" in state:
                tails = gradient.next_tails(t, tail_piece, state["tail"])
            pinned = [kept_first, *kept_rest]
            results = list(chosen_sums(numbers, choices, shape, extra, tails, pinned))
            if t == 0:
                results[0], results[1], activations, grad_output, left_old, right_old = tie(
                    (*results, activations, grad_output, left_old, right_old)
                )
                windows.add(old_factors())
                windows.add(old_left())
                kept, *away = local(1, count)
                kept_rest.append(kept)
                arrived += [to_partner(a) for a in away]
            current.send(*results[:2])
            for name in reversed(names):
                state[name] = results.pop()
            (own if len(own) < count else mixed_wholes).extend(results[2:])
            if t == tail_piece + line - 1:
                tail = gradient.finished_tail(tail_piece, state["tail"])

                def copy_body(number, sums, inputs, outputs):
                    outputs[0][...] = sums[0][...]

                (state["old_images"],) = fetching(
                    copy_body, [(tail[2], f32)], numbers, [tail], shape
                )
            windows.open()
            current.out[-1], current.home[-1] = windows.close(current.out[-1], current.home[-1])
        while windows.processes:
            windows.open()
            if windows.processes:
                windows.close()

        def body(number, sums, inputs, outputs):
            top_left, top_right, scale = scales(inputs[0][...] + inputs[1][...])
            pair = halves(sums[0][...])
            for i in range(2):
                rows = rows_here(number, i, inputs[6 + i][...], [(last, sums[0])])
                left = halves(inputs[2 + i][:, last * piece :])
                left = inputs[4 + i][...] + product(left, pair, 1, 0)
                outputs[i][...] = (left / top_left - 5.0 * rows) * (scale / top_right)

        mine, theirs = fetching(
            body,
            [((own_rows, panel), f32)] * 2,
            numbers,
            mixed.finished(steps),
            shape,
            [*state["squares"], state["left"], state["partner_left"], *state["early"]],
        )
        theirs = to_partner(theirs)

        def body(number, inputs, outputs):
            zeroth = jnp.full((own_rows, panel), number[C], jnp.int32) == 0
            mine, theirs = inputs[1][...], inputs[2][...]
            parts = jnp.where(zeroth, mine, theirs), jnp.where(zeroth, theirs, mine)
            for i, part in enumerate(parts):
                span = pl.ds(i * panel, panel)
                outputs[0][:, span] = inputs[0][:, span] + part

        (update,) = call(
            body, [((own_rows, block), f32)], numbers, [state["first_part"], mine, theirs]
        )
        return state["left_new"], state["right_new"], update

    return shards


def solution(mesh):
    dp, mp, pre = (mesh.shape[name] for name in ("dp", "mp", "pre"))
    cores = dp // (mp * pre)
    assert cores == 2
    split = Mesh(mesh.devices.reshape(dp // cores, cores, mp, pre), AXES)
    factor = P((MP, PRE), (LINE, CORE))
    in_specs = (
        P((LINE, CORE), None),
        P((LINE, CORE), (MP, PRE)),
        factor,
        factor,
        P(),
        P(),
    )
    out_specs = (factor, factor, P((LINE, CORE), (MP, PRE)))
    return jax.shard_map(
        make_step(dict(split.shape)),
        mesh=split,
        in_specs=in_specs,
        out_specs=out_specs,
        check_vma=False,
    )
```

```python
import jax
import jax.numpy as jnp
from jax import lax
from jax.experimental import pallas as pl
from jax.experimental.pallas import tpu as pltpu
from jax.sharding import Mesh, PartitionSpec as P

beta_decay = 0.9
norm_floor = 1e-06
count = 4

LINE, CORE, MP, PRE = "line", "core", "mp", "pre"
AXES = (LINE, CORE, MP, PRE)
f32, bf16 = jnp.float32, jnp.bfloat16


def halves(x):
    high = x.astype(bf16)
    return high, (x - high.astype(f32)).astype(bf16)


def whole_of(high, low):
    return high.astype(f32) + low.astype(f32)


def product(a, b, a_dim, b_dim):
    def one(x, y):
        return lax.dot_general(
            x, y, (((a_dim,), (b_dim,)), ((), ())), preferred_element_type=f32
        )

    return one(a[0], b[0]) + (one(a[0], b[1]) + one(a[1], b[0]))


def select_by(index, options):
    result = None
    for value, array in options.items():
        result = array if result is None else jnp.where(index == value, array, result)
    return result


def tie(values):
    return lax.optimization_barrier(tuple(values))


def call(body, outputs, numbers, arrays, space=pltpu.VMEM, scratch=(), mebibytes=32):
    inputs, results = len(arrays), len(outputs)

    def kernel(*refs):
        body(
            refs[0],
            refs[1 : 1 + inputs],
            refs[1 + inputs : 1 + inputs + results],
            *refs[1 + inputs + results :],
        )

    return pl.pallas_call(
        kernel,
        out_shape=[jax.ShapeDtypeStruct(shape, dtype) for shape, dtype in outputs],
        in_specs=[pl.BlockSpec(memory_space=pltpu.SMEM)]
        + [pl.BlockSpec(memory_space=space)] * inputs,
        out_specs=[pl.BlockSpec(memory_space=pltpu.VMEM)] * results,
        scratch_shapes=scratch,
        compiler_params=pltpu.CompilerParams(vmem_limit_bytes=mebibytes << 20),
        cost_estimate=pl.CostEstimate(flops=1, bytes_accessed=1, transcendentals=0),
    )(numbers, *arrays)


def added(numbers, arrays):
    def body(number, inputs, outputs):
        total = inputs[0][...]
        for array in inputs[1:]:
            total = total + array[...]
        outputs[0][...] = total

    return call(body, [(arrays[0].shape, f32)], numbers, arrays)[0]


def fetching(body, outputs, numbers, choices, shape, arrays=(), mebibytes=24):
    sources = []

    def place(array):
        for i, known in enumerate(sources):
            if known is array:
                return i
        sources.append(array)
        return len(sources) - 1

    shapes = [choice[2] if len(choice) > 2 else shape for choice in choices]
    choices = [
        (choice[0], {k: [(place(a), r) for a, r in terms] for k, terms in choice[1].items()})
        for choice in choices
    ]
    wholes = [place(array) for array in arrays]
    most = [max(1, *(len(t) for t in options.values())) for _, options in choices]
    many = len(choices)

    def inner(number, inputs, results, *scratch):
        held, kept = scratch[:many], scratch[many:-2]
        sems, kept_sems = scratch[-2:]

        def copies(o, terms):
            return [
                pltpu.make_async_copy(
                    inputs[a].at[pl.ds(r, shapes[o][0])], held[o].at[i], sems.at[o, i]
                )
                for i, (a, r) in enumerate(terms)
            ]

        loads = [
            pltpu.make_async_copy(inputs[a], kept[i], kept_sems.at[i])
            for i, a in enumerate(wholes)
        ]
        for o, (which, options) in enumerate(choices):
            for k, terms in options.items():

                @pl.when(number[which] == k)
                def _():
                    for copy in copies(o, terms):
                        copy.start()

        for copy in loads:
            copy.start()
        for o, (which, options) in enumerate(choices):
            for k, terms in options.items():

                @pl.when(number[which] == k)
                def _():
                    for copy in copies(o, terms):
                        copy.wait()
                    if not terms:
                        held[o][0] = jnp.zeros(shapes[o], f32)
                    if len(terms) > 1:
                        total = held[o][0]
                        for i in range(1, len(terms)):
                            total = total + held[o][i]
                        held[o][0] = total

        for copy in loads:
            copy.wait()
        body(number, [held[o].at[0] for o in range(many)], kept, results)

    return call(
        inner,
        outputs,
        numbers,
        sources,
        pl.ANY,
        [
            *[pltpu.VMEM((m,) + tuple(s), f32) for m, s in zip(most, shapes)],
            *[pltpu.VMEM(array.shape, array.dtype) for array in arrays],
            pltpu.SemaphoreType.DMA((max(many, 1), max(most + [1]))),
            pltpu.SemaphoreType.DMA((max(len(arrays), 1),)),
        ],
        mebibytes,
    )


def chosen_sums(numbers, choices, shape, more, tails):
    many = len(choices)
    sizes = [tail[2][0] for tail in tails] + [0] * (many - len(tails))

    def body(number, sums, inputs, outputs):
        for i, (result, rows, size) in enumerate(zip(outputs, more, sizes)):
            at = shape[0]
            result[:at] = sums[i][...]
            if size:
                result[at : at + size] = sums[many + i][...]
            if rows > size:
                result[at + size :] = jnp.zeros((rows - size,) + shape[1:], f32)

    out = [((shape[0] + rows,) + shape[1:], f32) for rows in more]
    return fetching(body, out, numbers, choices + tails, shape)


class Windows:
    def __init__(self):
        self.now = 0
        self.processes = []

    def add(self, process):
        self.processes.append([process, None, None])

    def open(self):
        ended = []
        for entry in self.processes:
            process, due, values = entry
            if values and due >= self.now:
                continue
            try:
                windows, entry[2] = process.send(values)
                entry[1] = self.now + windows - 1
            except StopIteration:
                ended.append(entry)
        for entry in ended:
            self.processes.remove(entry)

    def close(self, *others):
        due = [entry for entry in self.processes if entry[1] == self.now and entry[2]]
        flat = list(others)
        for entry in due:
            flat.extend(entry[2])
        if flat:
            flat = list(tie(flat))
        at = len(others)
        for entry in due:
            size = len(entry[2])
            entry[2] = flat[at : at + size]
            at += size
        self.now += 1
        return flat[: len(others)]


def make_step(sizes):
    line, cores, mp, pre = (sizes[name] for name in AXES)
    models = mp * pre
    last = count - 1

    def swap(array, axis, bit):
        return lax.ppermute(array, axis, [(i, i ^ bit) for i in range(sizes[axis])])

    def bits(axis):
        return [1 << i for i in range(sizes[axis].bit_length() - 1)]

    def total(numbers, array, axes):
        for axis in axes:
            for bit in bits(axis):
                pair = yield 1, (array, swap(array, axis, bit))
                array = added(numbers, pair)
        return array

    def snake(array, outward):
        pairs = []
        for z in range(line):
            for c in range(cores):
                goal = z + (1 if (c == 0) == outward else -1)
                if 0 <= goal < line:
                    pairs.append((z * cores + c, goal * cores + c))
                else:
                    pairs.append((z * cores + c, z * cores + 1 - c))
        return lax.ppermute(array, (LINE, CORE), pairs)

    def shards(activations, grad_output, left_old, right_old, probe_left, probe_right):
        z, core = lax.axis_index(LINE), lax.axis_index(CORE)
        x, y = lax.axis_index(MP), lax.axis_index(PRE)
        model = x * pre + y
        width = activations.shape[1]
        block = grad_output.shape[1]
        hidden = block * models
        panel = block // cores
        own_rows = width // (line * cores)
        model_rows = width // models
        piece = width // count
        owner_x, owner_y = z // pre, z % pre
        there = jnp.where(core == 0, z, line - 1 - z)
        numbers = jnp.stack(
            [z, core, there, line - 1 - there, x == owner_x, y == owner_y, model]
        ).astype(jnp.int32)
        Z, C, THERE, BACK, IN_X, IN_Y, MODEL = range(7)
        shape = (piece, panel)
        windows = Windows()
        state = {}

        def to_partner(array):
            return swap(array, CORE, 1)

        def device(number):
            return number[Z] * cores + number[C]

        def local(first, end, mebibytes):
            rows = (end - first) * piece
            tokens = activations.shape[0]
            parts, slices = 4, 3
            span = tokens // parts
            thin = span // slices

            def body(number, inputs, outputs, left, right, sems):
                copies = []
                for i in range(parts):
                    for k in range(slices):
                        at = pl.ds(i * span + k * thin, thin)
                        copies.append(
                            pltpu.make_async_copy(
                                inputs[0].at[at, pl.ds(first * piece, rows)],
                                left.at[at],
                                sems.at[0, i, k],
                            )
                        )
                        copies.append(
                            pltpu.make_async_copy(
                                inputs[1].at[at], right.at[at], sems.at[1, i, k]
                            )
                        )
                for copy in copies:
                    copy.start()
                sums = [None] * (end - first)
                for i in range(parts):
                    for copy in copies[2 * slices * i : 2 * slices * (i + 1)]:
                        copy.wait()
                    at = slice(i * span, (i + 1) * span)
                    for j in range(end - first):
                        term = lax.dot_general(
                            left[at, j * piece : (j + 1) * piece],
                            right[at],
                            (((0,), (0,)), ((), ())),
                            preferred_element_type=f32,
                        )
                        sums[j] = term if i == 0 else sums[j] + term
                zeroth = jnp.full(shape, number[C], jnp.int32) == 0
                for j, both in enumerate(sums):
                    low, high = both[:, :panel], both[:, panel:]
                    outputs[0][j * piece : (j + 1) * piece] = jnp.where(zeroth, low, high)
                    outputs[1 + j][...] = jnp.where(zeroth, high, low)

            return call(
                body,
                [((rows, panel), f32)] + [(shape, f32)] * (end - first),
                numbers,
                [activations, grad_output],
                pl.ANY,
                [
                    pltpu.VMEM((tokens, rows), bf16),
                    pltpu.VMEM(grad_output.shape, bf16),
                    pltpu.SemaphoreType.DMA((2, parts, slices)),
                ],
                mebibytes,
            )

        kept_first, away = local(0, 1, 60)
        arrived = [to_partner(away)]

        class Chain:
            def __init__(self, terms):
                self.terms = terms
                self.sent, self.out, self.home, self.options = [], [], [], []

            def next_sums(self, t):
                choices = []
                for which, got in ((THERE, self.out), (BACK, self.home)):
                    options = {}
                    for k in range(line):
                        options[k] = []
                        if 0 <= t - k < count:
                            options[k] = self.terms(t - k)
                            if k:
                                options[k] = options[k] + [(got[t - 1], 0)]
                    choices.append((which, options))
                return choices

            def next_tails(self, t, piece_number, array):
                choices = []
                if not 0 <= t - piece_number < line:
                    return choices
                for which, got in ((THERE, self.out), (BACK, self.home)):
                    options = {k: [] for k in range(line)}
                    k = t - piece_number
                    options[k] = [(array, 0)] + ([(got[t - 1], piece)] if k else [])
                    choices.append((which, options, array.shape))
                return choices

            def finished_tail(self, piece_number, array):
                j = piece_number
                options = {
                    k: [(self.sent[j + k], piece), (self.home[j + line - 2 - k], piece)]
                    for k in range(line - 1)
                }
                options[line - 1] = [(array, 0), (self.out[j + line - 2], piece)]
                return THERE, options, array.shape

            def send(self, going_out, going_home):
                self.sent.append(going_out)
                self.out.append(snake(going_out, True))
                self.home.append(snake(going_home, False))

            def finished(self, t):
                j = t - (line - 1)
                if not 0 <= j < count:
                    return []
                options = {
                    k: [(self.sent[j + k], 0), (self.home[j + line - 2 - k], 0)]
                    for k in range(line - 1)
                }
                options[line - 1] = self.terms(j) + [(self.out[j + line - 2], 0)]
                self.options.append((THERE, options))
                return self.options[-1:]

        gradient = Chain(
            lambda j: [
                (kept_rest[0], (j - 1) * piece) if j else (kept_first, 0),
                (arrived[j], 0),
            ]
        )
        mixed = Chain(lambda j: [(state["kept", j], 0), (state["swapped", j], 0)])
        own, wishes, kept_rest = [], [], []

        def row(array):
            return array.reshape(1, -1)

        def exchange(array, axis):
            return total(numbers, array, (axis,))

        def placed(number, column):
            wide = (own_rows, width)
            at = lax.broadcasted_iota(jnp.int32, wide, 0) + device(number) * own_rows
            here = lax.broadcasted_iota(jnp.int32, wide, 1) == at
            return jnp.sum(jnp.where(here, column, 0.0), axis=0, keepdims=True)

        def panel_of(which):
            return row(lax.dynamic_slice_in_dim(probe_right, which * panel, panel, 0))

        def beside(first, second):
            def body(number, inputs, outputs):
                size = inputs[0].shape[1]
                outputs[0][:, :size] = inputs[0][...]
                outputs[0][:, size:] = inputs[1][...]

            shape = first.shape[0], first.shape[1] + second.shape[1]
            return call(body, [(shape, f32)], numbers, [first, second])[0]

        def left_turned():
            return (beta_decay * left_old).T

        block_rows, image_rows = block // panel, width // panel
        tail_rows = -(-(block_rows + image_rows) // 8) * 8
        tail_piece = 2

        def old_factors():
            while windows.now < 1:
                yield 1, ()

            def body(number, inputs, outputs):
                old = beta_decay * inputs[0][...]
                outputs[0][...], outputs[1][...] = halves(old)
                image = jnp.sum(old * inputs[1][...], axis=1, keepdims=True).T
                outputs[2][...] = jnp.zeros((tail_rows, panel), f32)
                for r in range(block_rows):
                    outputs[2][r : r + 1] = image[:, r * panel : (r + 1) * panel]
                image = jnp.sum(inputs[2][...] * inputs[3][...], axis=1, keepdims=True)
                image = placed(number, image)
                for r in range(image_rows):
                    at = block_rows + r
                    outputs[2][at : at + 1] = image[:, r * panel : (r + 1) * panel]

            own_probe = lax.dynamic_slice_in_dim(probe_left, model * model_rows, model_rows, 0)
            high, low, images = call(
                body,
                [((block, panel), bf16), ((block, panel), bf16), ((tail_rows, panel), f32)],
                numbers,
                [right_old, panel_of(z * cores + core), left_turned(), row(own_probe)],
            )
            *state["old"], state["tail"] = yield 1, (high, low, images)

        def old_left():
            while windows.now < 1:
                yield 1, ()
            rows = left_turned()
            for axis in (PRE, MP):
                for bit in bits(axis):
                    rows, got = yield 1, (rows, swap(rows, axis, bit))
                    rows = beside(rows, got)
            state["old_left"] = rows

        def spread(array, axis, place, owner):
            result = None
            size = sizes[axis]
            for s in range(1, size):
                got = lax.ppermute(array, axis, [(i, (i + s) % size) for i in range(size)])
                if result is None:
                    result = got
                else:
                    result = jnp.where((place - s) % size == owner, got, result)
            return result

        def panel_piece(j):
            while len(own) <= j:
                yield 1, ()
            if j < depth:
                other, got = yield 1, (to_partner(own[j]), spread(own[j], PRE, y, owner_y))
                state["other", j] = other, 0
            else:
                (got,) = yield 1, (spread(own[j], PRE, y, owner_y),)
            wishes.append((("held", j), (IN_Y, {1: [(own[j], 0)], 0: [(got, 0)]})))
            while ("held", j) not in state:
                yield 1, ()
            held = state["held", j]
            held, got = yield 1, (held, spread(held, MP, x, owner_x))
            riders = []
            if j + depth == last:
                while len(own) < count:
                    yield 1, ()
                riders = [*own[depth:], first_images()]

            def body(number, inputs, outputs):
                here = jnp.full(shape, number[IN_X], jnp.int32) == 1
                pair = halves(jnp.where(here, inputs[0][:piece], inputs[1][:piece]))
                outputs[0][...], outputs[1][...] = pair
                both = product(pair, (inputs[2][...], inputs[3][...]), 1, 1)
                low, high = both[:, :panel], both[:, panel:]
                zeroth = jnp.full(shape, number[C], jnp.int32) == 0
                outputs[2][...] = jnp.where(zeroth, low, high)
                outputs[3][:piece] = jnp.where(zeroth, high, low)
                at = piece
                for rider in inputs[4:]:
                    size = min(rider.shape[0], piece)
                    outputs[3][at : at + size] = rider[:size]
                    at += size

            away_rows = piece + sum(min(rider.shape[0], piece) for rider in riders)
            high, low, state["kept", j], away = call(
                body,
                [(shape, bf16), (shape, bf16), (shape, f32), ((away_rows, panel), f32)],
                numbers,
                [held, got, *state["old"], *riders],
            )
            state["panel", j] = high, low
            _, _, got = yield 1, (high, low, to_partner(away))
            state["swapped", j] = got
            if riders:
                for i in range(depth, count):
                    state["other", i] = got, (i - depth + 1) * piece
                state["images"] = riders[-1], got, (count - depth + 1) * piece

        depth = 2
        rider_rows = -(-(2 * image_rows + block_rows) // 8) * 8

        def first_images():
            def body(number, inputs, outputs):
                right, left = inputs[count][...], inputs[count + 1][...].T
                across = jnp.zeros((1, panel), f32)
                for j in range(count):
                    rows = slice(j * piece, (j + 1) * piece)
                    across += jnp.sum(inputs[j][:piece] * left[rows], axis=0, keepdims=True)
                old = inputs[count + 2][...]
                outputs[0][...] = jnp.zeros((rider_rows, panel), f32)
                outputs[0][2 * image_rows : 2 * image_rows + block_rows] = old[:block_rows]
                for i, vector in enumerate((right, across)):
                    image = jnp.concatenate(
                        [
                            jnp.sum(inputs[j][:piece] * vector, axis=1, keepdims=True).T
                            for j in range(count)
                        ],
                        axis=1,
                    )
                    for r in range(image_rows):
                        at = i * image_rows + r
                        part = image[:, r * panel : (r + 1) * panel]
                        if i:
                            part = part + hidden * old[block_rows + r : block_rows + r + 1]
                        outputs[0][at : at + 1] = part

            return call(
                body,
                [((rider_rows, panel), f32)],
                numbers,
                [
                    *own,
                    panel_of(model * cores + core),
                    row(probe_left),
                    state["old_images"],
                ],
            )[0]

        def over_models(array):
            steps = [(axis, bit) for axis in (PRE, MP) for bit in bits(axis)]
            for i, (axis, bit) in enumerate(steps):
                terms = yield 1, (array, swap(array, axis, bit))
                if i < len(steps) - 1:
                    array = added(numbers, terms)
            return terms

        def first_part(crossed):
            (crossed,) = yield 1, (crossed,)
            crossed = yield from over_models(crossed)
            while "squares" not in state:
                yield 1, ()

            def body(number, sums, inputs, outputs):
                top_left, top_right, scale = scales(inputs[6][...] + inputs[7][...])
                grad = inputs[4][...], inputs[5][...]
                rows = pl.ds(pl.multiple_of(device(number) * own_rows, own_rows), own_rows)
                own = whole_of(inputs[4][rows, :], inputs[5][rows, :])
                crossed = product(halves(inputs[0][...] + inputs[1][...]), grad, 1, 0)
                outputs[0][...] = scale * (
                    25.0 * own
                    - inputs[2][...] * (5.0 / top_left)
                    - (5.0 * inputs[3][...] - crossed / top_left) / top_right
                )

            (state["first_part"],) = fetching(
                body,
                [((own_rows, block), f32)],
                numbers,
                [],
                shape,
                [*crossed, *state["left_parts"], *state["block"], *state["squares"]],
            )

        def hold_block():
            state["block"] = yield 1, state["block"]

        def left_side():
            while ("other", last) not in state or "images" not in state:
                yield 1, ()
            other = [state["other", j] for j in range(count)]
            images, got, start = state["images"]

            def split_block(number, inputs, high, low):
                zeroth = jnp.full(shape, number[C], jnp.int32) == 0
                for j in range(count):
                    at = other[j][1]
                    mine, theirs = inputs[j][:piece], inputs[count + j][at : at + piece]
                    rows = pl.ds(j * piece, piece)
                    for i, part in enumerate(
                        (jnp.where(zeroth, mine, theirs), jnp.where(zeroth, theirs, mine))
                    ):
                        columns = pl.ds(i * panel, panel)
                        high[rows, columns], low[rows, columns] = halves(part)

            def body(number, inputs, outputs, high, low):
                split_block(number, inputs, high, low)
                rows = pl.ds(pl.multiple_of(device(number) * own_rows, own_rows), own_rows)
                gram = product((high[...], low[...]), (high[rows, :], low[rows, :]), 1, 1)
                outputs[0][:own_rows] = gram.T / hidden
                outputs[0][own_rows:] = jnp.zeros((8, width), f32)
                images = inputs[2 * count][...] + inputs[2 * count + 1][start:]
                for i in range(2):
                    for r in range(image_rows):
                        at = i * image_rows + r
                        outputs[0][own_rows + i : own_rows + i + 1, pl.ds(r * panel, panel)] = (
                            images[at : at + 1]
                        )
                for r in range(block_rows):
                    at = 2 * image_rows + r
                    outputs[1][:, pl.ds(r * panel, panel)] = images[at : at + 1]

            rows = (own_rows, width)
            sources = [*own, *(array for array, _ in other)]
            gram, state["old_image"] = call(
                body,
                [((own_rows + 8, width), f32), ((1, block), f32)],
                numbers,
                [*sources, images, got],
                scratch=[pltpu.VMEM((width, block), bf16)] * 2,
            )

            def body(number, inputs, outputs):
                split_block(number, inputs, *outputs)

            high, low = call(body, [((width, block), bf16)] * 2, numbers, sources)
            state["block"] = high, low
            windows.add(hold_block())
            gram = yield from over_models(gram)
            state["left_terms"] = gram

            def body(number, sums, inputs, outputs):
                gram = inputs[0][:own_rows] + inputs[1][:own_rows]
                old = []
                for m in range(models):
                    part = jnp.zeros((own_rows, model_rows), f32)
                    for k in range(models):
                        at = jnp.full(part.shape, number[MODEL], jnp.int32)
                        block_k = inputs[2][:, k * model_rows : (k + 1) * model_rows]
                        part = jnp.where(at == m ^ k, block_k, part)
                    old.append(part)
                left = jnp.concatenate(old, axis=1) + gram
                outputs[0][...] = left
                new = left[:, :model_rows]
                for m in range(1, models):
                    at = jnp.full(new.shape, number[MODEL], jnp.int32)
                    new = jnp.where(at == m, left[:, m * model_rows : (m + 1) * model_rows], new)
                outputs[4][...] = new.T
                grad = inputs[3][...], inputs[4][...]
                left_grad = product(halves(left), grad, 1, 0)
                outputs[1][...] = left_grad
                outputs[2][...] = gram
                outputs[3][...] = product(grad, halves(left_grad), 1, 1).T / width

            left, left_grad, gram, crossed, new = fetching(
                body,
                [(rows, f32), ((own_rows, block), f32), (rows, f32), (rows, f32)]
                + [((model_rows, own_rows), f32)],
                numbers,
                [],
                shape,
                [*gram, state["old_left"], *state["block"]],
            )
            state["left"] = left
            windows.add(first_part(crossed))
            left_grad, gram, left = yield 1, (left_grad, gram, left)
            partner_left = to_partner(left)

            def body(number, inputs, outputs):
                grad = inputs[1][...], inputs[2][...]
                outputs[0][...] = product(halves(inputs[0][...]), grad, 1, 0) * (hidden / width)

            (gram_grad,) = call(
                body, [((own_rows, block), f32)], numbers, [gram, *state["block"]]
            )
            state["partner_left"], *state["left_parts"] = yield 1, (
                partner_left,
                left_grad,
                gram_grad,
            )
            state["left_new"] = new

        def powers():
            while "left_terms" not in state:
                yield 1, ()

            def body(number, inputs, outputs):
                images = inputs[5][own_rows:] + inputs[6][own_rows:]
                outputs[1][...] = images[1:2] / hidden
                grad = whole_of(inputs[1][...], inputs[2][...])
                first = inputs[0][...] + (
                    jnp.sum(grad * images[0:1].T, axis=0, keepdims=True) / width
                )
                outputs[0][:, :width] = jnp.sum(grad * first, axis=1, keepdims=True).T
                old = whole_of(inputs[3][...], inputs[4][...])
                outputs[0][:, width : width + panel] = jnp.sum(
                    old * first.T, axis=0, keepdims=True
                )
                square = jnp.sum(first * first, axis=1, keepdims=True)
                outputs[0][:, width + panel :] = jnp.broadcast_to(square, (1, 128))

            joined, first = call(
                body,
                [((1, width + panel + 128), f32), ((1, width), f32)],
                numbers,
                [
                    state["old_image"],
                    *state["block"],
                    *state["old"],
                    *state["left_terms"],
                ],
            )
            for axis in (PRE, MP):
                for bit in bits(axis):
                    joined = added(numbers, [joined, swap(joined, axis, bit)])
            first, joined = yield 1, (first, joined)
            while "left" not in state or ("panel", last) not in state:
                yield 1, ()

            def body(number, inputs, outputs):
                joined = inputs[2 + 2 * count][...]
                for array in inputs[3 + 2 * count :]:
                    joined = joined + array[...]
                vector = joined[:, :width].T
                second = joined[:, width : width + panel]
                for j in range(count):
                    part = whole_of(inputs[2 + 2 * j][...], inputs[3 + 2 * j][...])
                    rows = vector[j * piece : (j + 1) * piece]
                    second = second + jnp.sum(part * rows, axis=0, keepdims=True) / width
                square = joined[:, width + panel : width + panel + 1]
                second = second / jnp.sqrt(square + norm_floor)
                right = jnp.sum(second * second, axis=1, keepdims=True)
                first = inputs[0][...]
                unit = first / jnp.sqrt(
                    jnp.sum(first * first, axis=1, keepdims=True) + norm_floor
                )
                second = jnp.sum(inputs[1][...] * unit, axis=1, keepdims=True)
                left = jnp.sum(second * second, axis=0, keepdims=True)
                spot = lax.broadcasted_iota(jnp.int32, (1, 128), 1)
                outputs[0][...] = jnp.where(spot == 0, left, right)

            panels = [half for j in range(count) for half in state["panel", j]]
            (squares,) = call(
                body,
                [((1, 128), f32)],
                numbers,
                [first, state["left"], *panels, joined],
            )
            squares = added(numbers, [squares, to_partner(squares)])
            for bit in bits(LINE)[:-2]:
                squares = added(numbers, [squares, swap(squares, LINE, bit)])
            squares = added(numbers, (yield 1, (squares, swap(squares, LINE, bits(LINE)[-2]))))
            state["squares"] = yield 1, (squares, swap(squares, LINE, bits(LINE)[-1]))

        def scales(squares):
            top = jnp.sqrt(squares + norm_floor)
            top_left, top_right = top[:, 0:1], top[:, 1:2]
            return top_left, top_right, 1.0 / (16.0 * jnp.sqrt(jnp.sqrt(top_left * top_right)))

        def right_factor():
            while ("panel", last) not in state or "block" not in state or windows.now < steps + 2:
                yield 1, ()

            def body(number, sums, inputs, outputs):
                pair = [
                    jnp.concatenate([inputs[3 + 2 * j + i][...] for j in range(count)], axis=0)
                    for i in range(2)
                ]
                gram = product((inputs[1][...], inputs[2][...]), pair, 0, 0)
                outputs[0][...] = beta_decay * inputs[0][...] + gram / width

            panels = [half for j in range(count) for half in state["panel", j]]
            (state["right_new"],) = yield 1, fetching(
                body,
                [((block, panel), f32)],
                numbers,
                [],
                shape,
                [right_old, *state["block"], *panels],
                44,
            )

        for j in range(count):
            windows.add(panel_piece(j))
        steps = count + line - 2
        def rows_here(number, i, rows, pieces):
            other = number[C] if i == 0 else 1 - number[C]
            at = jnp.full(rows.shape, number[Z] * cores + other, jnp.int32)
            for k in range(line * cores):
                j, start = divmod(k * own_rows, piece)
                for number_j, array in pieces:
                    if number_j == j:
                        rows = jnp.where(at == k, array[start : start + own_rows], rows)
            return rows

        def early_products():
            while len(mixed_wholes) < last or "partner_left" not in state:
                yield 1, ()

            def body(number, sums, inputs, outputs):
                pieces = [(j, inputs[2 + j]) for j in range(last)]
                pair = halves(jnp.concatenate([array[:piece] for _, array in pieces], axis=0))
                for i in range(2):
                    left = halves(inputs[i][:, : last * piece])
                    outputs[i][...] = product(left, pair, 1, 0)
                    outputs[2 + i][...] = rows_here(
                        number, i, jnp.zeros((own_rows, panel), f32), pieces
                    )

            state["early"] = yield 1, fetching(
                body,
                [((own_rows, panel), f32)] * 4,
                numbers,
                [],
                shape,
                [state["left"], state["partner_left"], *mixed_wholes],
            )

        mixed_wholes = []
        for process in (left_side, powers, right_factor, early_products):
            windows.add(process())

        for t in range(2 * steps):
            windows.open()
            current = gradient if t < steps else mixed
            choices = current.next_sums(t % steps) + gradient.finished(t)
            choices += mixed.finished(t - steps)
            names = [name for name, _ in wishes]
            choices += [choice for _, choice in wishes]
            wishes.clear()
            crowded = t == line + depth - 1
            longer = tail_rows + (16 if steps < t < steps + 3 else 8 if crowded else 0)
            extra = [longer] * 2 + [0] * (len(choices) - 2)
            for i, name in enumerate(names):
                extra[len(extra) - len(names) + i] = 8 if crowded else 0
            if crowded:
                extra[2] = 8
            if ("held", last) in names:
                extra[-1] = longer
            tails = []
            if t < steps and "tail" in state:
                tails = gradient.next_tails(t, tail_piece, state["tail"])
            results = list(chosen_sums(numbers, choices, shape, extra, tails))
            if t == 0:
                results[0], results[1], activations, grad_output, left_old, right_old = tie(
                    (*results, activations, grad_output, left_old, right_old)
                )
                windows.add(old_factors())
                windows.add(old_left())
                kept, *away = local(1, count, 40)
                kept_rest.append(kept)
                arrived += [to_partner(a) for a in away]
            current.send(*results[:2])
            for name in reversed(names):
                state[name] = results.pop()
            (own if len(own) < count else mixed_wholes).extend(results[2:])
            if t == tail_piece + line - 1:
                tail = gradient.finished_tail(tail_piece, state["tail"])

                def copy_body(number, sums, inputs, outputs):
                    outputs[0][...] = sums[0][...]

                (state["old_images"],) = fetching(
                    copy_body, [(tail[2], f32)], numbers, [tail], shape
                )
            windows.open()
            current.out[-1], current.home[-1] = windows.close(current.out[-1], current.home[-1])
        while windows.processes:
            windows.open()
            if windows.processes:
                windows.close()

        def body(number, sums, inputs, outputs):
            top_left, top_right, scale = scales(inputs[0][...] + inputs[1][...])
            pair = halves(sums[0][...])
            for i in range(2):
                rows = rows_here(number, i, inputs[6 + i][...], [(last, sums[0])])
                left = halves(inputs[2 + i][:, last * piece :])
                left = inputs[4 + i][...] + product(left, pair, 1, 0)
                outputs[i][...] = (left / top_left - 5.0 * rows) * (scale / top_right)

        mine, theirs = fetching(
            body,
            [((own_rows, panel), f32)] * 2,
            numbers,
            mixed.finished(steps),
            shape,
            [*state["squares"], state["left"], state["partner_left"], *state["early"]],
        )
        theirs = to_partner(theirs)

        def body(number, inputs, outputs):
            zeroth = jnp.full((own_rows, panel), number[C], jnp.int32) == 0
            mine, theirs = inputs[1][...], inputs[2][...]
            parts = jnp.where(zeroth, mine, theirs), jnp.where(zeroth, theirs, mine)
            for i, part in enumerate(parts):
                span = pl.ds(i * panel, panel)
                outputs[0][:, span] = inputs[0][:, span] + part

        (update,) = call(
            body, [((own_rows, block), f32)], numbers, [state["first_part"], mine, theirs]
        )
        return state["left_new"], state["right_new"], update

    return shards


def solution(mesh):
    dp, mp, pre = (mesh.shape[name] for name in ("dp", "mp", "pre"))
    cores = dp // (mp * pre)
    assert cores == 2
    split = Mesh(mesh.devices.reshape(dp // cores, cores, mp, pre), AXES)
    factor = P((MP, PRE), (LINE, CORE))
    in_specs = (
        P((LINE, CORE), None),
        P((LINE, CORE), (MP, PRE)),
        factor,
        factor,
        P(),
        P(),
    )
    out_specs = (factor, factor, P((LINE, CORE), (MP, PRE)))
    return jax.shard_map(
        make_step(dict(split.shape)),
        mesh=split,
        in_specs=in_specs,
        out_specs=out_specs,
        check_vma=False,
    )
```

```python
import jax
import jax.numpy as jnp
from jax import lax
from jax.experimental import pallas as pl
from jax.experimental.pallas import tpu as pltpu
from jax.sharding import Mesh, PartitionSpec as P

beta_decay = 0.9
norm_floor = 1e-06
count = 4

LINE, CORE, MP, PRE = "line", "core", "mp", "pre"
AXES = (LINE, CORE, MP, PRE)
f32, bf16 = jnp.float32, jnp.bfloat16


def halves(x):
    high = x.astype(bf16)
    return high, (x - high.astype(f32)).astype(bf16)


def whole_of(high, low):
    return high.astype(f32) + low.astype(f32)


def product(a, b, a_dim, b_dim):
    def one(x, y):
        return lax.dot_general(
            x, y, (((a_dim,), (b_dim,)), ((), ())), preferred_element_type=f32
        )

    return one(a[0], b[0]) + (one(a[0], b[1]) + one(a[1], b[0]))


def select_by(index, options):
    result = None
    for value, array in options.items():
        result = array if result is None else jnp.where(index == value, array, result)
    return result


def tie(values):
    return lax.optimization_barrier(tuple(values))


def call(body, outputs, numbers, arrays, space=pltpu.VMEM, scratch=(), mebibytes=24):
    inputs, results = len(arrays), len(outputs)

    def kernel(*refs):
        body(
            refs[0],
            refs[1 : 1 + inputs],
            refs[1 + inputs : 1 + inputs + results],
            *refs[1 + inputs + results :],
        )

    return pl.pallas_call(
        kernel,
        out_shape=[jax.ShapeDtypeStruct(shape, dtype) for shape, dtype in outputs],
        in_specs=[pl.BlockSpec(memory_space=pltpu.SMEM)]
        + [pl.BlockSpec(memory_space=space)] * inputs,
        out_specs=[pl.BlockSpec(memory_space=pltpu.VMEM)] * results,
        scratch_shapes=scratch,
        compiler_params=pltpu.CompilerParams(vmem_limit_bytes=mebibytes << 20),
        cost_estimate=pl.CostEstimate(flops=1, bytes_accessed=1, transcendentals=0),
    )(numbers, *arrays)


def added(numbers, arrays):
    def body(number, inputs, outputs):
        total = inputs[0][...]
        for array in inputs[1:]:
            total = total + array[...]
        outputs[0][...] = total

    return call(body, [(arrays[0].shape, f32)], numbers, arrays)[0]


def fetching(body, outputs, numbers, choices, shape, arrays=(), mebibytes=18):
    sources = []

    def place(array):
        for i, known in enumerate(sources):
            if known is array:
                return i
        sources.append(array)
        return len(sources) - 1

    shapes = [choice[2] if len(choice) > 2 else shape for choice in choices]
    choices = [
        (choice[0], {k: [(place(a), r) for a, r in terms] for k, terms in choice[1].items()})
        for choice in choices
    ]
    wholes = [place(array) for array in arrays]
    most = [max(1, *(len(t) for t in options.values())) for _, options in choices]
    many = len(choices)

    def inner(number, inputs, results, *scratch):
        held, kept = scratch[:many], scratch[many:-2]
        sems, kept_sems = scratch[-2:]

        def copies(o, terms):
            return [
                pltpu.make_async_copy(
                    inputs[a].at[pl.ds(r, shapes[o][0])], held[o].at[i], sems.at[o, i]
                )
                for i, (a, r) in enumerate(terms)
            ]

        loads = [
            pltpu.make_async_copy(inputs[a], kept[i], kept_sems.at[i])
            for i, a in enumerate(wholes)
        ]
        for o, (which, options) in enumerate(choices):
            for k, terms in options.items():

                @pl.when(number[which] == k)
                def _():
                    for copy in copies(o, terms):
                        copy.start()

        for copy in loads:
            copy.start()
        for o, (which, options) in enumerate(choices):
            for k, terms in options.items():

                @pl.when(number[which] == k)
                def _():
                    for copy in copies(o, terms):
                        copy.wait()
                    if not terms:
                        held[o][0] = jnp.zeros(shapes[o], f32)
                    if len(terms) > 1:
                        total = held[o][0]
                        for i in range(1, len(terms)):
                            total = total + held[o][i]
                        held[o][0] = total

        for copy in loads:
            copy.wait()
        body(number, [held[o].at[0] for o in range(many)], kept, results)

    return call(
        inner,
        outputs,
        numbers,
        sources,
        pl.ANY,
        [
            *[pltpu.VMEM((m,) + tuple(s), f32) for m, s in zip(most, shapes)],
            *[pltpu.VMEM(array.shape, array.dtype) for array in arrays],
            pltpu.SemaphoreType.DMA((max(many, 1), max(most + [1]))),
            pltpu.SemaphoreType.DMA((max(len(arrays), 1),)),
        ],
        mebibytes,
    )


def chosen_sums(numbers, choices, shape, more, tails):
    many = len(choices)
    sizes = [tail[2][0] for tail in tails] + [0] * (many - len(tails))

    def body(number, sums, inputs, outputs):
        for i, (result, rows, size) in enumerate(zip(outputs, more, sizes)):
            at = shape[0]
            result[:at] = sums[i][...]
            if size:
                result[at : at + size] = sums[many + i][...]
            if rows > size:
                result[at + size :] = jnp.zeros((rows - size,) + shape[1:], f32)

    out = [((shape[0] + rows,) + shape[1:], f32) for rows in more]
    return fetching(body, out, numbers, choices + tails, shape, mebibytes=12)


class Windows:
    def __init__(self):
        self.now = 0
        self.processes = []

    def add(self, process):
        self.processes.append([process, None, None])

    def open(self):
        ended = []
        for entry in self.processes:
            process, due, values = entry
            if values and due >= self.now:
                continue
            try:
                windows, entry[2] = process.send(values)
                entry[1] = self.now + windows - 1
            except StopIteration:
                ended.append(entry)
        for entry in ended:
            self.processes.remove(entry)

    def close(self, *others):
        due = [entry for entry in self.processes if entry[1] == self.now and entry[2]]
        flat = list(others)
        for entry in due:
            flat.extend(entry[2])
        if flat:
            flat = list(tie(flat))
        at = len(others)
        for entry in due:
            size = len(entry[2])
            entry[2] = flat[at : at + size]
            at += size
        self.now += 1
        return flat[: len(others)]


def make_step(sizes):
    line, cores, mp, pre = (sizes[name] for name in AXES)
    models = mp * pre
    last = count - 1

    def swap(array, axis, bit):
        return lax.ppermute(array, axis, [(i, i ^ bit) for i in range(sizes[axis])])

    def bits(axis):
        return [1 << i for i in range(sizes[axis].bit_length() - 1)]

    def total(numbers, array, axes):
        for axis in axes:
            for bit in bits(axis):
                pair = yield 1, (array, swap(array, axis, bit))
                array = added(numbers, pair)
        return array

    def snake(array, outward):
        pairs = []
        for z in range(line):
            for c in range(cores):
                goal = z + (1 if (c == 0) == outward else -1)
                if 0 <= goal < line:
                    pairs.append((z * cores + c, goal * cores + c))
                else:
                    pairs.append((z * cores + c, z * cores + 1 - c))
        return lax.ppermute(array, (LINE, CORE), pairs)

    def shards(activations, grad_output, left_old, right_old, probe_left, probe_right):
        z, core = lax.axis_index(LINE), lax.axis_index(CORE)
        x, y = lax.axis_index(MP), lax.axis_index(PRE)
        model = x * pre + y
        width = activations.shape[1]
        block = grad_output.shape[1]
        hidden = block * models
        panel = block // cores
        own_rows = width // (line * cores)
        model_rows = width // models
        piece = width // count
        owner_x, owner_y = z // pre, z % pre
        there = jnp.where(core == 0, z, line - 1 - z)
        numbers = jnp.stack(
            [z, core, there, line - 1 - there, x == owner_x, y == owner_y, model]
        ).astype(jnp.int32)
        Z, C, THERE, BACK, IN_X, IN_Y, MODEL = range(7)
        shape = (piece, panel)
        windows = Windows()
        state = {}

        def to_partner(array):
            return swap(array, CORE, 1)

        def device(number):
            return number[Z] * cores + number[C]

        def local(first, end, mebibytes):
            rows = (end - first) * piece
            tokens = activations.shape[0]
            parts, slices = 4, 3
            span = tokens // parts
            thin = span // slices

            def body(number, inputs, outputs, left, right, sems):
                copies = []
                for i in range(parts):
                    for k in range(slices):
                        at = pl.ds(i * span + k * thin, thin)
                        copies.append(
                            pltpu.make_async_copy(
                                inputs[0].at[at, pl.ds(first * piece, rows)],
                                left.at[at],
                                sems.at[0, i, k],
                            )
                        )
                        copies.append(
                            pltpu.make_async_copy(
                                inputs[1].at[at], right.at[at], sems.at[1, i, k]
                            )
                        )
                for copy in copies:
                    copy.start()
                sums = [None] * (end - first)
                for i in range(parts):
                    for copy in copies[2 * slices * i : 2 * slices * (i + 1)]:
                        copy.wait()
                    at = slice(i * span, (i + 1) * span)
                    for j in range(end - first):
                        term = lax.dot_general(
                            left[at, j * piece : (j + 1) * piece],
                            right[at],
                            (((0,), (0,)), ((), ())),
                            preferred_element_type=f32,
                        )
                        sums[j] = term if i == 0 else sums[j] + term
                zeroth = jnp.full(shape, number[C], jnp.int32) == 0
                for j, both in enumerate(sums):
                    low, high = both[:, :panel], both[:, panel:]
                    outputs[0][j * piece : (j + 1) * piece] = jnp.where(zeroth, low, high)
                    outputs[1 + j][...] = jnp.where(zeroth, high, low)

            return call(
                body,
                [((rows, panel), f32)] + [(shape, f32)] * (end - first),
                numbers,
                [activations, grad_output],
                pl.ANY,
                [
                    pltpu.VMEM((tokens, rows), bf16),
                    pltpu.VMEM(grad_output.shape, bf16),
                    pltpu.SemaphoreType.DMA((2, parts, slices)),
                ],
                mebibytes,
            )

        kept_first, away = local(0, 1, 60)
        arrived = [to_partner(away)]

        class Chain:
            def __init__(self, terms):
                self.terms = terms
                self.sent, self.out, self.home, self.options = [], [], [], []

            def next_sums(self, t):
                choices = []
                for which, got in ((THERE, self.out), (BACK, self.home)):
                    options = {}
                    for k in range(line):
                        options[k] = []
                        if 0 <= t - k < count:
                            options[k] = self.terms(t - k)
                            if k:
                                options[k] = options[k] + [(got[t - 1], 0)]
                    choices.append((which, options))
                return choices

            def next_tails(self, t, piece_number, array):
                choices = []
                if not 0 <= t - piece_number < line:
                    return choices
                for which, got in ((THERE, self.out), (BACK, self.home)):
                    options = {k: [] for k in range(line)}
                    k = t - piece_number
                    options[k] = [(array, 0)] + ([(got[t - 1], piece)] if k else [])
                    choices.append((which, options, array.shape))
                return choices

            def finished_tail(self, piece_number, array):
                j = piece_number
                options = {
                    k: [(self.sent[j + k], piece), (self.home[j + line - 2 - k], piece)]
                    for k in range(line - 1)
                }
                options[line - 1] = [(array, 0), (self.out[j + line - 2], piece)]
                return THERE, options, array.shape

            def send(self, going_out, going_home):
                self.sent.append(going_out)
                self.out.append(snake(going_out, True))
                self.home.append(snake(going_home, False))

            def finished(self, t):
                j = t - (line - 1)
                if not 0 <= j < count:
                    return []
                options = {
                    k: [(self.sent[j + k], 0), (self.home[j + line - 2 - k], 0)]
                    for k in range(line - 1)
                }
                options[line - 1] = self.terms(j) + [(self.out[j + line - 2], 0)]
                self.options.append((THERE, options))
                return self.options[-1:]

        gradient = Chain(
            lambda j: [
                (kept_rest[0], (j - 1) * piece) if j else (kept_first, 0),
                (arrived[j], 0),
            ]
        )
        mixed = Chain(lambda j: [(state["kept", j], 0), (state["swapped", j], 0)])
        own, wishes, kept_rest = [], [], []

        def row(array):
            return array.reshape(1, -1)

        def exchange(array, axis):
            return total(numbers, array, (axis,))

        def placed(number, column):
            wide = (own_rows, width)
            at = lax.broadcasted_iota(jnp.int32, wide, 0) + device(number) * own_rows
            here = lax.broadcasted_iota(jnp.int32, wide, 1) == at
            return jnp.sum(jnp.where(here, column, 0.0), axis=0, keepdims=True)

        def panel_of(which):
            return row(lax.dynamic_slice_in_dim(probe_right, which * panel, panel, 0))

        def beside(first, second):
            def body(number, inputs, outputs):
                size = inputs[0].shape[1]
                outputs[0][:, :size] = inputs[0][...]
                outputs[0][:, size:] = inputs[1][...]

            shape = first.shape[0], first.shape[1] + second.shape[1]
            return call(body, [(shape, f32)], numbers, [first, second])[0]

        def left_turned():
            return (beta_decay * left_old).T

        block_rows, image_rows = block // panel, width // panel
        tail_rows = -(-(block_rows + image_rows) // 8) * 8
        tail_piece = 2

        def old_factors():
            while windows.now < 1:
                yield 1, ()

            def body(number, inputs, outputs):
                old = beta_decay * inputs[0][...]
                outputs[0][...], outputs[1][...] = halves(old)
                image = jnp.sum(old * inputs[1][...], axis=1, keepdims=True).T
                outputs[2][...] = jnp.zeros((tail_rows, panel), f32)
                for r in range(block_rows):
                    outputs[2][r : r + 1] = image[:, r * panel : (r + 1) * panel]
                image = jnp.sum(inputs[2][...] * inputs[3][...], axis=1, keepdims=True)
                image = placed(number, image)
                for r in range(image_rows):
                    at = block_rows + r
                    outputs[2][at : at + 1] = image[:, r * panel : (r + 1) * panel]

            own_probe = lax.dynamic_slice_in_dim(probe_left, model * model_rows, model_rows, 0)
            high, low, images = call(
                body,
                [((block, panel), bf16), ((block, panel), bf16), ((tail_rows, panel), f32)],
                numbers,
                [right_old, panel_of(z * cores + core), left_turned(), row(own_probe)],
            )
            *state["old"], state["tail"] = yield 1, (high, low, images)

        def old_left():
            while windows.now < 1:
                yield 1, ()
            rows = left_turned()
            for axis in (PRE, MP):
                for bit in bits(axis):
                    rows, got = yield 1, (rows, swap(rows, axis, bit))
                    rows = beside(rows, got)
            state["old_left"] = rows

        def spread(array, axis, place, owner):
            result = None
            size = sizes[axis]
            for s in range(1, size):
                got = lax.ppermute(array, axis, [(i, (i + s) % size) for i in range(size)])
                if result is None:
                    result = got
                else:
                    result = jnp.where((place - s) % size == owner, got, result)
            return result

        def panel_piece(j):
            while len(own) <= j:
                yield 1, ()
            if j < depth:
                other, got = yield 1, (to_partner(own[j]), spread(own[j], PRE, y, owner_y))
                state["other", j] = other, 0
            else:
                (got,) = yield 1, (spread(own[j], PRE, y, owner_y),)
            wishes.append((("held", j), (IN_Y, {1: [(own[j], 0)], 0: [(got, 0)]})))
            while ("held", j) not in state:
                yield 1, ()
            held = state["held", j]
            held, got = yield 1, (held, spread(held, MP, x, owner_x))
            riders = []
            if j + depth == last:
                while len(own) < count:
                    yield 1, ()
                riders = [*own[depth:], first_images()]

            def body(number, inputs, outputs):
                here = jnp.full(shape, number[IN_X], jnp.int32) == 1
                pair = halves(jnp.where(here, inputs[0][:piece], inputs[1][:piece]))
                outputs[0][...], outputs[1][...] = pair
                both = product(pair, (inputs[2][...], inputs[3][...]), 1, 1)
                low, high = both[:, :panel], both[:, panel:]
                zeroth = jnp.full(shape, number[C], jnp.int32) == 0
                outputs[2][...] = jnp.where(zeroth, low, high)
                outputs[3][:piece] = jnp.where(zeroth, high, low)
                at = piece
                for rider in inputs[4:]:
                    size = min(rider.shape[0], piece)
                    outputs[3][at : at + size] = rider[:size]
                    at += size

            away_rows = piece + sum(min(rider.shape[0], piece) for rider in riders)
            high, low, state["kept", j], away = call(
                body,
                [(shape, bf16), (shape, bf16), (shape, f32), ((away_rows, panel), f32)],
                numbers,
                [held, got, *state["old"], *riders],
            )
            state["panel", j] = high, low
            _, _, got = yield 1, (high, low, to_partner(away))
            state["swapped", j] = got
            if riders:
                for i in range(depth, count):
                    state["other", i] = got, (i - depth + 1) * piece
                state["images"] = riders[-1], got, (count - depth + 1) * piece

        depth = 2
        rider_rows = -(-(2 * image_rows + block_rows) // 8) * 8

        def first_images():
            def body(number, inputs, outputs):
                right, left = inputs[count][...], inputs[count + 1][...].T
                across = jnp.zeros((1, panel), f32)
                for j in range(count):
                    rows = slice(j * piece, (j + 1) * piece)
                    across += jnp.sum(inputs[j][:piece] * left[rows], axis=0, keepdims=True)
                old = inputs[count + 2][...]
                outputs[0][...] = jnp.zeros((rider_rows, panel), f32)
                outputs[0][2 * image_rows : 2 * image_rows + block_rows] = old[:block_rows]
                for i, vector in enumerate((right, across)):
                    image = jnp.concatenate(
                        [
                            jnp.sum(inputs[j][:piece] * vector, axis=1, keepdims=True).T
                            for j in range(count)
                        ],
                        axis=1,
                    )
                    for r in range(image_rows):
                        at = i * image_rows + r
                        part = image[:, r * panel : (r + 1) * panel]
                        if i:
                            part = part + hidden * old[block_rows + r : block_rows + r + 1]
                        outputs[0][at : at + 1] = part

            return call(
                body,
                [((rider_rows, panel), f32)],
                numbers,
                [
                    *own,
                    panel_of(model * cores + core),
                    row(probe_left),
                    state["old_images"],
                ],
            )[0]

        def over_models(array):
            steps = [(axis, bit) for axis in (PRE, MP) for bit in bits(axis)]
            for i, (axis, bit) in enumerate(steps):
                terms = yield 1, (array, swap(array, axis, bit))
                if i < len(steps) - 1:
                    array = added(numbers, terms)
            return terms

        def first_part(crossed):
            (crossed,) = yield 1, (crossed,)
            crossed = yield from over_models(crossed)
            while "squares" not in state:
                yield 1, ()

            def body(number, sums, inputs, outputs):
                top_left, top_right, scale = scales(inputs[6][...] + inputs[7][...])
                grad = inputs[4][...], inputs[5][...]
                rows = pl.ds(pl.multiple_of(device(number) * own_rows, own_rows), own_rows)
                own = whole_of(inputs[4][rows, :], inputs[5][rows, :])
                crossed = product(halves(inputs[0][...] + inputs[1][...]), grad, 1, 0)
                outputs[0][...] = scale * (
                    25.0 * own
                    - inputs[2][...] * (5.0 / top_left)
                    - (5.0 * inputs[3][...] - crossed / top_left) / top_right
                )

            (state["first_part"],) = fetching(
                body,
                [((own_rows, block), f32)],
                numbers,
                [],
                shape,
                [*crossed, *state["left_parts"], *state["block"], *state["squares"]],
            )

        def hold_block():
            state["block"] = yield 1, state["block"]

        def left_side():
            while ("other", last) not in state or "images" not in state:
                yield 1, ()
            other = [state["other", j] for j in range(count)]
            images, got, start = state["images"]

            def split_block(number, inputs, high, low):
                zeroth = jnp.full(shape, number[C], jnp.int32) == 0
                for j in range(count):
                    at = other[j][1]
                    mine, theirs = inputs[j][:piece], inputs[count + j][at : at + piece]
                    rows = pl.ds(j * piece, piece)
                    for i, part in enumerate(
                        (jnp.where(zeroth, mine, theirs), jnp.where(zeroth, theirs, mine))
                    ):
                        columns = pl.ds(i * panel, panel)
                        high[rows, columns], low[rows, columns] = halves(part)

            def body(number, inputs, outputs, high, low):
                split_block(number, inputs, high, low)
                rows = pl.ds(pl.multiple_of(device(number) * own_rows, own_rows), own_rows)
                gram = product((high[...], low[...]), (high[rows, :], low[rows, :]), 1, 1)
                outputs[0][:own_rows] = gram.T / hidden
                outputs[0][own_rows:] = jnp.zeros((8, width), f32)
                images = inputs[2 * count][...] + inputs[2 * count + 1][start:]
                for i in range(2):
                    for r in range(image_rows):
                        at = i * image_rows + r
                        outputs[0][own_rows + i : own_rows + i + 1, pl.ds(r * panel, panel)] = (
                            images[at : at + 1]
                        )
                for r in range(block_rows):
                    at = 2 * image_rows + r
                    outputs[1][:, pl.ds(r * panel, panel)] = images[at : at + 1]

            rows = (own_rows, width)
            sources = [*own, *(array for array, _ in other)]
            gram, state["old_image"] = call(
                body,
                [((own_rows + 8, width), f32), ((1, block), f32)],
                numbers,
                [*sources, images, got],
                scratch=[pltpu.VMEM((width, block), bf16)] * 2,
            )

            def body(number, inputs, outputs):
                split_block(number, inputs, *outputs)

            high, low = call(body, [((width, block), bf16)] * 2, numbers, sources)
            state["block"] = high, low
            windows.add(hold_block())
            gram = yield from over_models(gram)
            state["left_terms"] = gram

            def body(number, sums, inputs, outputs):
                gram = inputs[0][:own_rows] + inputs[1][:own_rows]
                old = []
                for m in range(models):
                    part = jnp.zeros((own_rows, model_rows), f32)
                    for k in range(models):
                        at = jnp.full(part.shape, number[MODEL], jnp.int32)
                        block_k = inputs[2][:, k * model_rows : (k + 1) * model_rows]
                        part = jnp.where(at == m ^ k, block_k, part)
                    old.append(part)
                left = jnp.concatenate(old, axis=1) + gram
                outputs[0][...] = left
                new = left[:, :model_rows]
                for m in range(1, models):
                    at = jnp.full(new.shape, number[MODEL], jnp.int32)
                    new = jnp.where(at == m, left[:, m * model_rows : (m + 1) * model_rows], new)
                outputs[4][...] = new.T
                grad = inputs[3][...], inputs[4][...]
                left_grad = product(halves(left), grad, 1, 0)
                outputs[1][...] = left_grad
                outputs[2][...] = gram
                outputs[3][...] = product(grad, halves(left_grad), 1, 1).T / width

            left, left_grad, gram, crossed, new = fetching(
                body,
                [(rows, f32), ((own_rows, block), f32), (rows, f32), (rows, f32)]
                + [((model_rows, own_rows), f32)],
                numbers,
                [],
                shape,
                [*gram, state["old_left"], *state["block"]],
            )
            state["left"] = left
            windows.add(first_part(crossed))
            left_grad, gram, left = yield 1, (left_grad, gram, left)
            partner_left = to_partner(left)

            def body(number, inputs, outputs):
                grad = inputs[1][...], inputs[2][...]
                outputs[0][...] = product(halves(inputs[0][...]), grad, 1, 0) * (hidden / width)

            (gram_grad,) = call(
                body, [((own_rows, block), f32)], numbers, [gram, *state["block"]]
            )
            state["partner_left"], *state["left_parts"] = yield 1, (
                partner_left,
                left_grad,
                gram_grad,
            )
            state["left_new"] = new

        def powers():
            while "left_terms" not in state:
                yield 1, ()

            def body(number, inputs, outputs):
                images = inputs[5][own_rows:] + inputs[6][own_rows:]
                outputs[1][...] = images[1:2] / hidden
                grad = whole_of(inputs[1][...], inputs[2][...])
                first = inputs[0][...] + (
                    jnp.sum(grad * images[0:1].T, axis=0, keepdims=True) / width
                )
                outputs[0][:, :width] = jnp.sum(grad * first, axis=1, keepdims=True).T
                old = whole_of(inputs[3][...], inputs[4][...])
                outputs[0][:, width : width + panel] = jnp.sum(
                    old * first.T, axis=0, keepdims=True
                )
                square = jnp.sum(first * first, axis=1, keepdims=True)
                outputs[0][:, width + panel :] = jnp.broadcast_to(square, (1, 128))

            joined, first = call(
                body,
                [((1, width + panel + 128), f32), ((1, width), f32)],
                numbers,
                [
                    state["old_image"],
                    *state["block"],
                    *state["old"],
                    *state["left_terms"],
                ],
            )
            for axis in (PRE, MP):
                for bit in bits(axis):
                    joined = added(numbers, [joined, swap(joined, axis, bit)])
            first, joined = yield 1, (first, joined)
            while "left" not in state or ("panel", last) not in state:
                yield 1, ()

            def body(number, inputs, outputs):
                joined = inputs[2 + 2 * count][...]
                for array in inputs[3 + 2 * count :]:
                    joined = joined + array[...]
                vector = joined[:, :width].T
                second = joined[:, width : width + panel]
                for j in range(count):
                    part = whole_of(inputs[2 + 2 * j][...], inputs[3 + 2 * j][...])
                    rows = vector[j * piece : (j + 1) * piece]
                    second = second + jnp.sum(part * rows, axis=0, keepdims=True) / width
                square = joined[:, width + panel : width + panel + 1]
                second = second / jnp.sqrt(square + norm_floor)
                right = jnp.sum(second * second, axis=1, keepdims=True)
                first = inputs[0][...]
                unit = first / jnp.sqrt(
                    jnp.sum(first * first, axis=1, keepdims=True) + norm_floor
                )
                second = jnp.sum(inputs[1][...] * unit, axis=1, keepdims=True)
                left = jnp.sum(second * second, axis=0, keepdims=True)
                spot = lax.broadcasted_iota(jnp.int32, (1, 128), 1)
                outputs[0][...] = jnp.where(spot == 0, left, right)

            panels = [half for j in range(count) for half in state["panel", j]]
            (squares,) = call(
                body,
                [((1, 128), f32)],
                numbers,
                [first, state["left"], *panels, joined],
            )
            squares = added(numbers, [squares, to_partner(squares)])
            for bit in bits(LINE)[:-2]:
                squares = added(numbers, [squares, swap(squares, LINE, bit)])
            squares = added(numbers, (yield 1, (squares, swap(squares, LINE, bits(LINE)[-2]))))
            state["squares"] = yield 1, (squares, swap(squares, LINE, bits(LINE)[-1]))

        def scales(squares):
            top = jnp.sqrt(squares + norm_floor)
            top_left, top_right = top[:, 0:1], top[:, 1:2]
            return top_left, top_right, 1.0 / (16.0 * jnp.sqrt(jnp.sqrt(top_left * top_right)))

        def right_factor():
            while ("panel", last) not in state or "block" not in state or windows.now < steps + 2:
                yield 1, ()

            def body(number, sums, inputs, outputs):
                pair = [
                    jnp.concatenate([inputs[3 + 2 * j + i][...] for j in range(count)], axis=0)
                    for i in range(2)
                ]
                gram = product((inputs[1][...], inputs[2][...]), pair, 0, 0)
                outputs[0][...] = beta_decay * inputs[0][...] + gram / width

            panels = [half for j in range(count) for half in state["panel", j]]
            (state["right_new"],) = yield 1, fetching(
                body,
                [((block, panel), f32)],
                numbers,
                [],
                shape,
                [right_old, *state["block"], *panels],
                32,
            )

        for j in range(count):
            windows.add(panel_piece(j))
        steps = count + line - 2
        def rows_here(number, i, rows, pieces):
            other = number[C] if i == 0 else 1 - number[C]
            at = jnp.full(rows.shape, number[Z] * cores + other, jnp.int32)
            for k in range(line * cores):
                j, start = divmod(k * own_rows, piece)
                for number_j, array in pieces:
                    if number_j == j:
                        rows = jnp.where(at == k, array[start : start + own_rows], rows)
            return rows

        def early_products():
            while len(mixed_wholes) < last or "partner_left" not in state:
                yield 1, ()

            def body(number, sums, inputs, outputs):
                pieces = [(j, inputs[2 + j]) for j in range(last)]
                pair = halves(jnp.concatenate([array[:piece] for _, array in pieces], axis=0))
                for i in range(2):
                    left = halves(inputs[i][:, : last * piece])
                    outputs[i][...] = product(left, pair, 1, 0)
                    outputs[2 + i][...] = rows_here(
                        number, i, jnp.zeros((own_rows, panel), f32), pieces
                    )

            state["early"] = yield 1, fetching(
                body,
                [((own_rows, panel), f32)] * 4,
                numbers,
                [],
                shape,
                [state["left"], state["partner_left"], *mixed_wholes],
            )

        mixed_wholes = []
        for process in (left_side, powers, right_factor, early_products):
            windows.add(process())

        for t in range(2 * steps):
            windows.open()
            current = gradient if t < steps else mixed
            choices = current.next_sums(t % steps) + gradient.finished(t)
            choices += mixed.finished(t - steps)
            names = [name for name, _ in wishes]
            choices += [choice for _, choice in wishes]
            wishes.clear()
            crowded = t == line + depth - 1
            longer = tail_rows + (16 if steps < t < steps + 3 else 8 if crowded else 0)
            extra = [longer] * 2 + [0] * (len(choices) - 2)
            for i, name in enumerate(names):
                extra[len(extra) - len(names) + i] = 8 if crowded else 0
            if crowded:
                extra[2] = 8
            if ("held", last) in names:
                extra[-1] = longer
            tails = []
            if t < steps and "tail" in state:
                tails = gradient.next_tails(t, tail_piece, state["tail"])
            results = list(chosen_sums(numbers, choices, shape, extra, tails))
            if t == 0:
                results[0], results[1], activations, grad_output, left_old, right_old = tie(
                    (*results, activations, grad_output, left_old, right_old)
                )
                windows.add(old_factors())
                windows.add(old_left())
                kept, *away = local(1, count, 40)
                kept_rest.append(kept)
                arrived += [to_partner(a) for a in away]
            current.send(*results[:2])
            for name in reversed(names):
                state[name] = results.pop()
            (own if len(own) < count else mixed_wholes).extend(results[2:])
            if t == tail_piece + line - 1:
                tail = gradient.finished_tail(tail_piece, state["tail"])

                def copy_body(number, sums, inputs, outputs):
                    outputs[0][...] = sums[0][...]

                (state["old_images"],) = fetching(
                    copy_body, [(tail[2], f32)], numbers, [tail], shape
                )
            windows.open()
            current.out[-1], current.home[-1] = windows.close(current.out[-1], current.home[-1])
        while windows.processes:
            windows.open()
            if windows.processes:
                windows.close()

        def body(number, sums, inputs, outputs):
            top_left, top_right, scale = scales(inputs[0][...] + inputs[1][...])
            pair = halves(sums[0][...])
            for i in range(2):
                rows = rows_here(number, i, inputs[6 + i][...], [(last, sums[0])])
                left = halves(inputs[2 + i][:, last * piece :])
                left = inputs[4 + i][...] + product(left, pair, 1, 0)
                outputs[i][...] = (left / top_left - 5.0 * rows) * (scale / top_right)

        mine, theirs = fetching(
            body,
            [((own_rows, panel), f32)] * 2,
            numbers,
            mixed.finished(steps),
            shape,
            [*state["squares"], state["left"], state["partner_left"], *state["early"]],
        )
        theirs = to_partner(theirs)

        def body(number, inputs, outputs):
            zeroth = jnp.full((own_rows, panel), number[C], jnp.int32) == 0
            mine, theirs = inputs[1][...], inputs[2][...]
            parts = jnp.where(zeroth, mine, theirs), jnp.where(zeroth, theirs, mine)
            for i, part in enumerate(parts):
                span = pl.ds(i * panel, panel)
                outputs[0][:, span] = inputs[0][:, span] + part

        (update,) = call(
            body, [((own_rows, block), f32)], numbers, [state["first_part"], mine, theirs]
        )
        return state["left_new"], state["right_new"], update

    return shards


def solution(mesh):
    dp, mp, pre = (mesh.shape[name] for name in ("dp", "mp", "pre"))
    cores = dp // (mp * pre)
    assert cores == 2
    split = Mesh(mesh.devices.reshape(dp // cores, cores, mp, pre), AXES)
    factor = P((MP, PRE), (LINE, CORE))
    in_specs = (
        P((LINE, CORE), None),
        P((LINE, CORE), (MP, PRE)),
        factor,
        factor,
        P(),
        P(),
    )
    out_specs = (factor, factor, P((LINE, CORE), (MP, PRE)))
    return jax.shard_map(
        make_step(dict(split.shape)),
        mesh=split,
        in_specs=in_specs,
        out_specs=out_specs,
        check_vma=False,
    )
```

```python
import jax
import jax.numpy as jnp
from jax import lax
from jax.experimental import pallas as pl
from jax.experimental.pallas import tpu as pltpu
from jax.sharding import Mesh, PartitionSpec as P

beta_decay = 0.9
norm_floor = 1e-06
count = 4

LINE, CORE, MP, PRE = "line", "core", "mp", "pre"
AXES = (LINE, CORE, MP, PRE)
f32, bf16 = jnp.float32, jnp.bfloat16


def halves(x):
    high = x.astype(bf16)
    return high, (x - high.astype(f32)).astype(bf16)


def whole_of(high, low):
    return high.astype(f32) + low.astype(f32)


def product(a, b, a_dim, b_dim):
    def one(x, y):
        return lax.dot_general(
            x, y, (((a_dim,), (b_dim,)), ((), ())), preferred_element_type=f32
        )

    return one(a[0], b[0]) + (one(a[0], b[1]) + one(a[1], b[0]))


def select_by(index, options):
    result = None
    for value, array in options.items():
        result = array if result is None else jnp.where(index == value, array, result)
    return result


def tie(values):
    return lax.optimization_barrier(tuple(values))


def call(body, outputs, numbers, arrays, space=pltpu.VMEM, scratch=(), mebibytes=24):
    inputs, results = len(arrays), len(outputs)

    def kernel(*refs):
        body(
            refs[0],
            refs[1 : 1 + inputs],
            refs[1 + inputs : 1 + inputs + results],
            *refs[1 + inputs + results :],
        )

    return pl.pallas_call(
        kernel,
        out_shape=[jax.ShapeDtypeStruct(shape, dtype) for shape, dtype in outputs],
        in_specs=[pl.BlockSpec(memory_space=pltpu.SMEM)]
        + [pl.BlockSpec(memory_space=space)] * inputs,
        out_specs=[pl.BlockSpec(memory_space=pltpu.VMEM)] * results,
        scratch_shapes=scratch,
        compiler_params=pltpu.CompilerParams(vmem_limit_bytes=mebibytes << 20),
        cost_estimate=pl.CostEstimate(flops=1, bytes_accessed=1, transcendentals=0),
    )(numbers, *arrays)


def added(numbers, arrays):
    def body(number, inputs, outputs):
        total = inputs[0][...]
        for array in inputs[1:]:
            total = total + array[...]
        outputs[0][...] = total

    return call(body, [(arrays[0].shape, f32)], numbers, arrays)[0]


def fetching(body, outputs, numbers, choices, shape, arrays=(), mebibytes=18):
    sources = []

    def place(array):
        for i, known in enumerate(sources):
            if known is array:
                return i
        sources.append(array)
        return len(sources) - 1

    shapes = [choice[2] if len(choice) > 2 else shape for choice in choices]
    choices = [
        (choice[0], {k: [(place(a), r) for a, r in terms] for k, terms in choice[1].items()})
        for choice in choices
    ]
    wholes = [place(array) for array in arrays]
    most = [max(1, *(len(t) for t in options.values())) for _, options in choices]
    many = len(choices)

    def inner(number, inputs, results, *scratch):
        held, kept = scratch[:many], scratch[many:-2]
        sems, kept_sems = scratch[-2:]

        def copies(o, terms):
            return [
                pltpu.make_async_copy(
                    inputs[a].at[pl.ds(r, shapes[o][0])], held[o].at[i], sems.at[o, i]
                )
                for i, (a, r) in enumerate(terms)
            ]

        loads = [
            pltpu.make_async_copy(inputs[a], kept[i], kept_sems.at[i])
            for i, a in enumerate(wholes)
        ]
        for o, (which, options) in enumerate(choices):
            for k, terms in options.items():

                @pl.when(number[which] == k)
                def _():
                    for copy in copies(o, terms):
                        copy.start()

        for copy in loads:
            copy.start()
        for o, (which, options) in enumerate(choices):
            for k, terms in options.items():

                @pl.when(number[which] == k)
                def _():
                    for copy in copies(o, terms):
                        copy.wait()
                    if not terms:
                        held[o][0] = jnp.zeros(shapes[o], f32)
                    if len(terms) > 1:
                        total = held[o][0]
                        for i in range(1, len(terms)):
                            total = total + held[o][i]
                        held[o][0] = total

        for copy in loads:
            copy.wait()
        body(number, [held[o].at[0] for o in range(many)], kept, results)

    return call(
        inner,
        outputs,
        numbers,
        sources,
        pl.ANY,
        [
            *[pltpu.VMEM((m,) + tuple(s), f32) for m, s in zip(most, shapes)],
            *[pltpu.VMEM(array.shape, array.dtype) for array in arrays],
            pltpu.SemaphoreType.DMA((max(many, 1), max(most + [1]))),
            pltpu.SemaphoreType.DMA((max(len(arrays), 1),)),
        ],
        mebibytes,
    )


def chosen_sums(numbers, choices, shape, more, tails):
    many = len(choices)
    sizes = [tail[2][0] for tail in tails] + [0] * (many - len(tails))
    arrays = []

    def place(array):
        for i, known in enumerate(arrays):
            if known is array:
                return i
        arrays.append(array)
        return len(arrays) - 1

    plans = [
        (choice[0], {k: [(place(a), r) for a, r in terms] for k, terms in choice[1].items()})
        for choice in choices + tails
    ]

    def body(number, inputs, outputs):
        def write(plan, result, at, rows):
            which, options = plan
            for k, terms in options.items():

                @pl.when(number[which] == k)
                def _():
                    total = jnp.zeros((rows,) + shape[1:], f32)
                    for i, (a, r) in enumerate(terms):
                        part = inputs[a][r : r + rows]
                        total = part if i == 0 else total + part
                    result[at : at + rows] = total

        for i, (result, rows, size) in enumerate(zip(outputs, more, sizes)):
            at = shape[0]
            write(plans[i], result, 0, at)
            if size:
                write(plans[many + i], result, at, size)
            if rows > size:
                result[at + size :] = jnp.zeros((rows - size,) + shape[1:], f32)

    out = [((shape[0] + rows,) + shape[1:], f32) for rows in more]
    return call(body, out, numbers, arrays, mebibytes=12)


class Windows:
    def __init__(self):
        self.now = 0
        self.processes = []

    def add(self, process):
        self.processes.append([process, None, None])

    def open(self):
        ended = []
        for entry in self.processes:
            process, due, values = entry
            if values and due >= self.now:
                continue
            try:
                windows, entry[2] = process.send(values)
                entry[1] = self.now + windows - 1
            except StopIteration:
                ended.append(entry)
        for entry in ended:
            self.processes.remove(entry)

    def close(self, *others):
        due = [entry for entry in self.processes if entry[1] == self.now and entry[2]]
        flat = list(others)
        for entry in due:
            flat.extend(entry[2])
        if flat:
            flat = list(tie(flat))
        at = len(others)
        for entry in due:
            size = len(entry[2])
            entry[2] = flat[at : at + size]
            at += size
        self.now += 1
        return flat[: len(others)]


def make_step(sizes):
    line, cores, mp, pre = (sizes[name] for name in AXES)
    models = mp * pre
    last = count - 1

    def swap(array, axis, bit):
        return lax.ppermute(array, axis, [(i, i ^ bit) for i in range(sizes[axis])])

    def bits(axis):
        return [1 << i for i in range(sizes[axis].bit_length() - 1)]

    def total(numbers, array, axes):
        for axis in axes:
            for bit in bits(axis):
                pair = yield 1, (array, swap(array, axis, bit))
                array = added(numbers, pair)
        return array

    def snake(array, outward):
        pairs = []
        for z in range(line):
            for c in range(cores):
                goal = z + (1 if (c == 0) == outward else -1)
                if 0 <= goal < line:
                    pairs.append((z * cores + c, goal * cores + c))
                else:
                    pairs.append((z * cores + c, z * cores + 1 - c))
        return lax.ppermute(array, (LINE, CORE), pairs)

    def shards(activations, grad_output, left_old, right_old, probe_left, probe_right):
        z, core = lax.axis_index(LINE), lax.axis_index(CORE)
        x, y = lax.axis_index(MP), lax.axis_index(PRE)
        model = x * pre + y
        width = activations.shape[1]
        block = grad_output.shape[1]
        hidden = block * models
        panel = block // cores
        own_rows = width // (line * cores)
        model_rows = width // models
        piece = width // count
        owner_x, owner_y = z // pre, z % pre
        there = jnp.where(core == 0, z, line - 1 - z)
        numbers = jnp.stack(
            [z, core, there, line - 1 - there, x == owner_x, y == owner_y, model]
        ).astype(jnp.int32)
        Z, C, THERE, BACK, IN_X, IN_Y, MODEL = range(7)
        shape = (piece, panel)
        windows = Windows()
        state = {}

        def to_partner(array):
            return swap(array, CORE, 1)

        def device(number):
            return number[Z] * cores + number[C]

        def local(first, end, mebibytes):
            rows = (end - first) * piece
            tokens = activations.shape[0]
            parts, slices = 4, 3
            span = tokens // parts
            thin = span // slices

            def body(number, inputs, outputs, left, right, sems):
                copies = []
                for i in range(parts):
                    for k in range(slices):
                        at = pl.ds(i * span + k * thin, thin)
                        copies.append(
                            pltpu.make_async_copy(
                                inputs[0].at[at, pl.ds(first * piece, rows)],
                                left.at[at],
                                sems.at[0, i, k],
                            )
                        )
                        copies.append(
                            pltpu.make_async_copy(
                                inputs[1].at[at], right.at[at], sems.at[1, i, k]
                            )
                        )
                for copy in copies:
                    copy.start()
                sums = [None] * (end - first)
                for i in range(parts):
                    for copy in copies[2 * slices * i : 2 * slices * (i + 1)]:
                        copy.wait()
                    at = slice(i * span, (i + 1) * span)
                    for j in range(end - first):
                        term = lax.dot_general(
                            left[at, j * piece : (j + 1) * piece],
                            right[at],
                            (((0,), (0,)), ((), ())),
                            preferred_element_type=f32,
                        )
                        sums[j] = term if i == 0 else sums[j] + term
                zeroth = jnp.full(shape, number[C], jnp.int32) == 0
                for j, both in enumerate(sums):
                    low, high = both[:, :panel], both[:, panel:]
                    outputs[0][j * piece : (j + 1) * piece] = jnp.where(zeroth, low, high)
                    outputs[1 + j][...] = jnp.where(zeroth, high, low)

            return call(
                body,
                [((rows, panel), f32)] + [(shape, f32)] * (end - first),
                numbers,
                [activations, grad_output],
                pl.ANY,
                [
                    pltpu.VMEM((tokens, rows), bf16),
                    pltpu.VMEM(grad_output.shape, bf16),
                    pltpu.SemaphoreType.DMA((2, parts, slices)),
                ],
                mebibytes,
            )

        kept_first, away = local(0, 1, 60)
        arrived = [to_partner(away)]

        class Chain:
            def __init__(self, terms):
                self.terms = terms
                self.sent, self.out, self.home, self.options = [], [], [], []

            def next_sums(self, t):
                choices = []
                for which, got in ((THERE, self.out), (BACK, self.home)):
                    options = {}
                    for k in range(line):
                        options[k] = []
                        if 0 <= t - k < count:
                            options[k] = self.terms(t - k)
                            if k:
                                options[k] = options[k] + [(got[t - 1], 0)]
                    choices.append((which, options))
                return choices

            def next_tails(self, t, piece_number, array):
                choices = []
                if not 0 <= t - piece_number < line:
                    return choices
                for which, got in ((THERE, self.out), (BACK, self.home)):
                    options = {k: [] for k in range(line)}
                    k = t - piece_number
                    options[k] = [(array, 0)] + ([(got[t - 1], piece)] if k else [])
                    choices.append((which, options, array.shape))
                return choices

            def finished_tail(self, piece_number, array):
                j = piece_number
                options = {
                    k: [(self.sent[j + k], piece), (self.home[j + line - 2 - k], piece)]
                    for k in range(line - 1)
                }
                options[line - 1] = [(array, 0), (self.out[j + line - 2], piece)]
                return THERE, options, array.shape

            def send(self, going_out, going_home):
                self.sent.append(going_out)
                self.out.append(snake(going_out, True))
                self.home.append(snake(going_home, False))

            def finished(self, t):
                j = t - (line - 1)
                if not 0 <= j < count:
                    return []
                options = {
                    k: [(self.sent[j + k], 0), (self.home[j + line - 2 - k], 0)]
                    for k in range(line - 1)
                }
                options[line - 1] = self.terms(j) + [(self.out[j + line - 2], 0)]
                self.options.append((THERE, options))
                return self.options[-1:]

        gradient = Chain(
            lambda j: [
                (kept_rest[0], (j - 1) * piece) if j else (kept_first, 0),
                (arrived[j], 0),
            ]
        )
        mixed = Chain(lambda j: [(state["kept", j], 0), (state["swapped", j], 0)])
        own, wishes, kept_rest = [], [], []

        def row(array):
            return array.reshape(1, -1)

        def exchange(array, axis):
            return total(numbers, array, (axis,))

        def placed(number, column):
            wide = (own_rows, width)
            at = lax.broadcasted_iota(jnp.int32, wide, 0) + device(number) * own_rows
            here = lax.broadcasted_iota(jnp.int32, wide, 1) == at
            return jnp.sum(jnp.where(here, column, 0.0), axis=0, keepdims=True)

        def panel_of(which):
            return row(lax.dynamic_slice_in_dim(probe_right, which * panel, panel, 0))

        def beside(first, second):
            def body(number, inputs, outputs):
                size = inputs[0].shape[1]
                outputs[0][:, :size] = inputs[0][...]
                outputs[0][:, size:] = inputs[1][...]

            shape = first.shape[0], first.shape[1] + second.shape[1]
            return call(body, [(shape, f32)], numbers, [first, second])[0]

        def left_turned():
            return (beta_decay * left_old).T

        block_rows, image_rows = block // panel, width // panel
        tail_rows = -(-(block_rows + image_rows) // 8) * 8
        tail_piece = 2

        def old_factors():
            while windows.now < 1:
                yield 1, ()

            def body(number, inputs, outputs):
                old = beta_decay * inputs[0][...]
                outputs[0][...], outputs[1][...] = halves(old)
                image = jnp.sum(old * inputs[1][...], axis=1, keepdims=True).T
                outputs[2][...] = jnp.zeros((tail_rows, panel), f32)
                for r in range(block_rows):
                    outputs[2][r : r + 1] = image[:, r * panel : (r + 1) * panel]
                image = jnp.sum(inputs[2][...] * inputs[3][...], axis=1, keepdims=True)
                image = placed(number, image)
                for r in range(image_rows):
                    at = block_rows + r
                    outputs[2][at : at + 1] = image[:, r * panel : (r + 1) * panel]

            own_probe = lax.dynamic_slice_in_dim(probe_left, model * model_rows, model_rows, 0)
            high, low, images = call(
                body,
                [((block, panel), bf16), ((block, panel), bf16), ((tail_rows, panel), f32)],
                numbers,
                [right_old, panel_of(z * cores + core), left_turned(), row(own_probe)],
            )
            *state["old"], state["tail"] = yield 1, (high, low, images)

        def old_left():
            while windows.now < 1:
                yield 1, ()
            rows = left_turned()
            for axis in (PRE, MP):
                for bit in bits(axis):
                    rows, got = yield 1, (rows, swap(rows, axis, bit))
                    rows = beside(rows, got)
            state["old_left"] = rows

        def spread(array, axis, place, owner):
            result = None
            size = sizes[axis]
            for s in range(1, size):
                got = lax.ppermute(array, axis, [(i, (i + s) % size) for i in range(size)])
                if result is None:
                    result = got
                else:
                    result = jnp.where((place - s) % size == owner, got, result)
            return result

        def panel_piece(j):
            while len(own) <= j:
                yield 1, ()
            if j < depth:
                other, got = yield 1, (to_partner(own[j]), spread(own[j], PRE, y, owner_y))
                state["other", j] = other, 0
            else:
                (got,) = yield 1, (spread(own[j], PRE, y, owner_y),)
            wishes.append((("held", j), (IN_Y, {1: [(own[j], 0)], 0: [(got, 0)]})))
            while ("held", j) not in state:
                yield 1, ()
            held = state["held", j]
            held, got = yield 1, (held, spread(held, MP, x, owner_x))
            riders = []
            if j + depth == last:
                while len(own) < count:
                    yield 1, ()
                riders = [*own[depth:], first_images()]

            def body(number, inputs, outputs):
                here = jnp.full(shape, number[IN_X], jnp.int32) == 1
                pair = halves(jnp.where(here, inputs[0][:piece], inputs[1][:piece]))
                outputs[0][...], outputs[1][...] = pair
                both = product(pair, (inputs[2][...], inputs[3][...]), 1, 1)
                low, high = both[:, :panel], both[:, panel:]
                zeroth = jnp.full(shape, number[C], jnp.int32) == 0
                outputs[2][...] = jnp.where(zeroth, low, high)
                outputs[3][:piece] = jnp.where(zeroth, high, low)
                at = piece
                for rider in inputs[4:]:
                    size = min(rider.shape[0], piece)
                    outputs[3][at : at + size] = rider[:size]
                    at += size

            away_rows = piece + sum(min(rider.shape[0], piece) for rider in riders)
            high, low, state["kept", j], away = call(
                body,
                [(shape, bf16), (shape, bf16), (shape, f32), ((away_rows, panel), f32)],
                numbers,
                [held, got, *state["old"], *riders],
            )
            state["panel", j] = high, low
            _, _, got = yield 1, (high, low, to_partner(away))
            state["swapped", j] = got
            if riders:
                for i in range(depth, count):
                    state["other", i] = got, (i - depth + 1) * piece
                state["images"] = riders[-1], got, (count - depth + 1) * piece

        depth = 2
        rider_rows = -(-(2 * image_rows + block_rows) // 8) * 8

        def first_images():
            def body(number, inputs, outputs):
                right, left = inputs[count][...], inputs[count + 1][...].T
                across = jnp.zeros((1, panel), f32)
                for j in range(count):
                    rows = slice(j * piece, (j + 1) * piece)
                    across += jnp.sum(inputs[j][:piece] * left[rows], axis=0, keepdims=True)
                old = inputs[count + 2][...]
                outputs[0][...] = jnp.zeros((rider_rows, panel), f32)
                outputs[0][2 * image_rows : 2 * image_rows + block_rows] = old[:block_rows]
                for i, vector in enumerate((right, across)):
                    image = jnp.concatenate(
                        [
                            jnp.sum(inputs[j][:piece] * vector, axis=1, keepdims=True).T
                            for j in range(count)
                        ],
                        axis=1,
                    )
                    for r in range(image_rows):
                        at = i * image_rows + r
                        part = image[:, r * panel : (r + 1) * panel]
                        if i:
                            part = part + hidden * old[block_rows + r : block_rows + r + 1]
                        outputs[0][at : at + 1] = part

            return call(
                body,
                [((rider_rows, panel), f32)],
                numbers,
                [
                    *own,
                    panel_of(model * cores + core),
                    row(probe_left),
                    state["old_images"],
                ],
            )[0]

        def over_models(array):
            steps = [(axis, bit) for axis in (PRE, MP) for bit in bits(axis)]
            for i, (axis, bit) in enumerate(steps):
                terms = yield 1, (array, swap(array, axis, bit))
                if i < len(steps) - 1:
                    array = added(numbers, terms)
            return terms

        def first_part(crossed):
            (crossed,) = yield 1, (crossed,)
            crossed = yield from over_models(crossed)
            while "squares" not in state:
                yield 1, ()

            def body(number, sums, inputs, outputs):
                top_left, top_right, scale = scales(inputs[6][...] + inputs[7][...])
                grad = inputs[4][...], inputs[5][...]
                rows = pl.ds(pl.multiple_of(device(number) * own_rows, own_rows), own_rows)
                own = whole_of(inputs[4][rows, :], inputs[5][rows, :])
                crossed = product(halves(inputs[0][...] + inputs[1][...]), grad, 1, 0)
                outputs[0][...] = scale * (
                    25.0 * own
                    - inputs[2][...] * (5.0 / top_left)
                    - (5.0 * inputs[3][...] - crossed / top_left) / top_right
                )

            (state["first_part"],) = fetching(
                body,
                [((own_rows, block), f32)],
                numbers,
                [],
                shape,
                [*crossed, *state["left_parts"], *state["block"], *state["squares"]],
            )

        def hold_block():
            state["block"] = yield 1, state["block"]

        def left_side():
            while ("other", last) not in state or "images" not in state:
                yield 1, ()
            other = [state["other", j] for j in range(count)]
            images, got, start = state["images"]

            def split_block(number, inputs, high, low):
                zeroth = jnp.full(shape, number[C], jnp.int32) == 0
                for j in range(count):
                    at = other[j][1]
                    mine, theirs = inputs[j][:piece], inputs[count + j][at : at + piece]
                    rows = pl.ds(j * piece, piece)
                    for i, part in enumerate(
                        (jnp.where(zeroth, mine, theirs), jnp.where(zeroth, theirs, mine))
                    ):
                        columns = pl.ds(i * panel, panel)
                        high[rows, columns], low[rows, columns] = halves(part)

            def body(number, inputs, outputs, high, low):
                split_block(number, inputs, high, low)
                rows = pl.ds(pl.multiple_of(device(number) * own_rows, own_rows), own_rows)
                gram = product((high[...], low[...]), (high[rows, :], low[rows, :]), 1, 1)
                outputs[0][:own_rows] = gram.T / hidden
                outputs[0][own_rows:] = jnp.zeros((8, width), f32)
                images = inputs[2 * count][...] + inputs[2 * count + 1][start:]
                for i in range(2):
                    for r in range(image_rows):
                        at = i * image_rows + r
                        outputs[0][own_rows + i : own_rows + i + 1, pl.ds(r * panel, panel)] = (
                            images[at : at + 1]
                        )
                for r in range(block_rows):
                    at = 2 * image_rows + r
                    outputs[1][:, pl.ds(r * panel, panel)] = images[at : at + 1]

            rows = (own_rows, width)
            sources = [*own, *(array for array, _ in other)]
            gram, state["old_image"] = call(
                body,
                [((own_rows + 8, width), f32), ((1, block), f32)],
                numbers,
                [*sources, images, got],
                scratch=[pltpu.VMEM((width, block), bf16)] * 2,
            )

            def body(number, inputs, outputs):
                split_block(number, inputs, *outputs)

            high, low = call(body, [((width, block), bf16)] * 2, numbers, sources)
            state["block"] = high, low
            windows.add(hold_block())
            gram = yield from over_models(gram)
            state["left_terms"] = gram

            def body(number, sums, inputs, outputs):
                gram = inputs[0][:own_rows] + inputs[1][:own_rows]
                old = []
                for m in range(models):
                    part = jnp.zeros((own_rows, model_rows), f32)
                    for k in range(models):
                        at = jnp.full(part.shape, number[MODEL], jnp.int32)
                        block_k = inputs[2][:, k * model_rows : (k + 1) * model_rows]
                        part = jnp.where(at == m ^ k, block_k, part)
                    old.append(part)
                left = jnp.concatenate(old, axis=1) + gram
                outputs[0][...] = left
                new = left[:, :model_rows]
                for m in range(1, models):
                    at = jnp.full(new.shape, number[MODEL], jnp.int32)
                    new = jnp.where(at == m, left[:, m * model_rows : (m + 1) * model_rows], new)
                outputs[4][...] = new.T
                grad = inputs[3][...], inputs[4][...]
                left_grad = product(halves(left), grad, 1, 0)
                outputs[1][...] = left_grad
                outputs[2][...] = gram
                outputs[3][...] = product(grad, halves(left_grad), 1, 1).T / width

            left, left_grad, gram, crossed, new = fetching(
                body,
                [(rows, f32), ((own_rows, block), f32), (rows, f32), (rows, f32)]
                + [((model_rows, own_rows), f32)],
                numbers,
                [],
                shape,
                [*gram, state["old_left"], *state["block"]],
            )
            state["left"] = left
            windows.add(first_part(crossed))
            left_grad, gram, left = yield 1, (left_grad, gram, left)
            partner_left = to_partner(left)

            def body(number, inputs, outputs):
                grad = inputs[1][...], inputs[2][...]
                outputs[0][...] = product(halves(inputs[0][...]), grad, 1, 0) * (hidden / width)

            (gram_grad,) = call(
                body, [((own_rows, block), f32)], numbers, [gram, *state["block"]]
            )
            state["partner_left"], *state["left_parts"] = yield 1, (
                partner_left,
                left_grad,
                gram_grad,
            )
            state["left_new"] = new

        def powers():
            while "left_terms" not in state:
                yield 1, ()

            def body(number, inputs, outputs):
                images = inputs[5][own_rows:] + inputs[6][own_rows:]
                outputs[1][...] = images[1:2] / hidden
                grad = whole_of(inputs[1][...], inputs[2][...])
                first = inputs[0][...] + (
                    jnp.sum(grad * images[0:1].T, axis=0, keepdims=True) / width
                )
                outputs[0][:, :width] = jnp.sum(grad * first, axis=1, keepdims=True).T
                old = whole_of(inputs[3][...], inputs[4][...])
                outputs[0][:, width : width + panel] = jnp.sum(
                    old * first.T, axis=0, keepdims=True
                )
                square = jnp.sum(first * first, axis=1, keepdims=True)
                outputs[0][:, width + panel :] = jnp.broadcast_to(square, (1, 128))

            joined, first = call(
                body,
                [((1, width + panel + 128), f32), ((1, width), f32)],
                numbers,
                [
                    state["old_image"],
                    *state["block"],
                    *state["old"],
                    *state["left_terms"],
                ],
            )
            for axis in (PRE, MP):
                for bit in bits(axis):
                    joined = added(numbers, [joined, swap(joined, axis, bit)])
            first, joined = yield 1, (first, joined)
            while "left" not in state or ("panel", last) not in state:
                yield 1, ()

            def body(number, inputs, outputs):
                joined = inputs[2 + 2 * count][...]
                for array in inputs[3 + 2 * count :]:
                    joined = joined + array[...]
                vector = joined[:, :width].T
                second = joined[:, width : width + panel]
                for j in range(count):
                    part = whole_of(inputs[2 + 2 * j][...], inputs[3 + 2 * j][...])
                    rows = vector[j * piece : (j + 1) * piece]
                    second = second + jnp.sum(part * rows, axis=0, keepdims=True) / width
                square = joined[:, width + panel : width + panel + 1]
                second = second / jnp.sqrt(square + norm_floor)
                right = jnp.sum(second * second, axis=1, keepdims=True)
                first = inputs[0][...]
                unit = first / jnp.sqrt(
                    jnp.sum(first * first, axis=1, keepdims=True) + norm_floor
                )
                second = jnp.sum(inputs[1][...] * unit, axis=1, keepdims=True)
                left = jnp.sum(second * second, axis=0, keepdims=True)
                spot = lax.broadcasted_iota(jnp.int32, (1, 128), 1)
                outputs[0][...] = jnp.where(spot == 0, left, right)

            panels = [half for j in range(count) for half in state["panel", j]]
            (squares,) = call(
                body,
                [((1, 128), f32)],
                numbers,
                [first, state["left"], *panels, joined],
            )
            squares = added(numbers, [squares, to_partner(squares)])
            for bit in bits(LINE)[:-2]:
                squares = added(numbers, [squares, swap(squares, LINE, bit)])
            squares = added(numbers, (yield 1, (squares, swap(squares, LINE, bits(LINE)[-2]))))
            state["squares"] = yield 1, (squares, swap(squares, LINE, bits(LINE)[-1]))

        def scales(squares):
            top = jnp.sqrt(squares + norm_floor)
            top_left, top_right = top[:, 0:1], top[:, 1:2]
            return top_left, top_right, 1.0 / (16.0 * jnp.sqrt(jnp.sqrt(top_left * top_right)))

        def right_factor():
            while ("panel", last) not in state or "block" not in state or windows.now < steps + 2:
                yield 1, ()

            def body(number, sums, inputs, outputs):
                pair = [
                    jnp.concatenate([inputs[3 + 2 * j + i][...] for j in range(count)], axis=0)
                    for i in range(2)
                ]
                gram = product((inputs[1][...], inputs[2][...]), pair, 0, 0)
                outputs[0][...] = beta_decay * inputs[0][...] + gram / width

            panels = [half for j in range(count) for half in state["panel", j]]
            (state["right_new"],) = yield 1, fetching(
                body,
                [((block, panel), f32)],
                numbers,
                [],
                shape,
                [right_old, *state["block"], *panels],
                32,
            )

        for j in range(count):
            windows.add(panel_piece(j))
        steps = count + line - 2
        def rows_here(number, i, rows, pieces):
            other = number[C] if i == 0 else 1 - number[C]
            at = jnp.full(rows.shape, number[Z] * cores + other, jnp.int32)
            for k in range(line * cores):
                j, start = divmod(k * own_rows, piece)
                for number_j, array in pieces:
                    if number_j == j:
                        rows = jnp.where(at == k, array[start : start + own_rows], rows)
            return rows

        def early_products():
            while len(mixed_wholes) < last or "partner_left" not in state:
                yield 1, ()

            def body(number, sums, inputs, outputs):
                pieces = [(j, inputs[2 + j]) for j in range(last)]
                pair = halves(jnp.concatenate([array[:piece] for _, array in pieces], axis=0))
                for i in range(2):
                    left = halves(inputs[i][:, : last * piece])
                    outputs[i][...] = product(left, pair, 1, 0)
                    outputs[2 + i][...] = rows_here(
                        number, i, jnp.zeros((own_rows, panel), f32), pieces
                    )

            state["early"] = yield 1, fetching(
                body,
                [((own_rows, panel), f32)] * 4,
                numbers,
                [],
                shape,
                [state["left"], state["partner_left"], *mixed_wholes],
            )

        mixed_wholes = []
        for process in (left_side, powers, right_factor, early_products):
            windows.add(process())

        for t in range(2 * steps):
            windows.open()
            current = gradient if t < steps else mixed
            choices = current.next_sums(t % steps) + gradient.finished(t)
            choices += mixed.finished(t - steps)
            names = [name for name, _ in wishes]
            choices += [choice for _, choice in wishes]
            wishes.clear()
            crowded = t == line + depth - 1
            longer = tail_rows + (16 if steps < t < steps + 3 else 8 if crowded else 0)
            extra = [longer] * 2 + [0] * (len(choices) - 2)
            for i, name in enumerate(names):
                extra[len(extra) - len(names) + i] = 8 if crowded else 0
            if crowded:
                extra[2] = 8
            if ("held", last) in names:
                extra[-1] = longer
            tails = []
            if t < steps and "tail" in state:
                tails = gradient.next_tails(t, tail_piece, state["tail"])
            results = list(chosen_sums(numbers, choices, shape, extra, tails))
            if t == 0:
                results[0], results[1], activations, grad_output, left_old, right_old = tie(
                    (*results, activations, grad_output, left_old, right_old)
                )
                windows.add(old_factors())
                windows.add(old_left())
                kept, *away = local(1, count, 40)
                kept_rest.append(kept)
                arrived += [to_partner(a) for a in away]
            current.send(*results[:2])
            for name in reversed(names):
                state[name] = results.pop()
            (own if len(own) < count else mixed_wholes).extend(results[2:])
            if t == tail_piece + line - 1:
                tail = gradient.finished_tail(tail_piece, state["tail"])

                def copy_body(number, sums, inputs, outputs):
                    outputs[0][...] = sums[0][...]

                (state["old_images"],) = fetching(
                    copy_body, [(tail[2], f32)], numbers, [tail], shape
                )
            windows.open()
            current.out[-1], current.home[-1] = windows.close(current.out[-1], current.home[-1])
        while windows.processes:
            windows.open()
            if windows.processes:
                windows.close()

        def body(number, sums, inputs, outputs):
            top_left, top_right, scale = scales(inputs[0][...] + inputs[1][...])
            pair = halves(sums[0][...])
            for i in range(2):
                rows = rows_here(number, i, inputs[6 + i][...], [(last, sums[0])])
                left = halves(inputs[2 + i][:, last * piece :])
                left = inputs[4 + i][...] + product(left, pair, 1, 0)
                outputs[i][...] = (left / top_left - 5.0 * rows) * (scale / top_right)

        mine, theirs = fetching(
            body,
            [((own_rows, panel), f32)] * 2,
            numbers,
            mixed.finished(steps),
            shape,
            [*state["squares"], state["left"], state["partner_left"], *state["early"]],
        )
        theirs = to_partner(theirs)

        def body(number, inputs, outputs):
            zeroth = jnp.full((own_rows, panel), number[C], jnp.int32) == 0
            mine, theirs = inputs[1][...], inputs[2][...]
            parts = jnp.where(zeroth, mine, theirs), jnp.where(zeroth, theirs, mine)
            for i, part in enumerate(parts):
                span = pl.ds(i * panel, panel)
                outputs[0][:, span] = inputs[0][:, span] + part

        (update,) = call(
            body, [((own_rows, block), f32)], numbers, [state["first_part"], mine, theirs]
        )
        return state["left_new"], state["right_new"], update

    return shards


def solution(mesh):
    dp, mp, pre = (mesh.shape[name] for name in ("dp", "mp", "pre"))
    cores = dp // (mp * pre)
    assert cores == 2
    split = Mesh(mesh.devices.reshape(dp // cores, cores, mp, pre), AXES)
    factor = P((MP, PRE), (LINE, CORE))
    in_specs = (
        P((LINE, CORE), None),
        P((LINE, CORE), (MP, PRE)),
        factor,
        factor,
        P(),
        P(),
    )
    out_specs = (factor, factor, P((LINE, CORE), (MP, PRE)))
    return jax.shard_map(
        make_step(dict(split.shape)),
        mesh=split,
        in_specs=in_specs,
        out_specs=out_specs,
        check_vma=False,
    )
```

```python
import jax
import jax.numpy as jnp
from jax import lax
from jax.experimental import pallas as pl
from jax.experimental.pallas import tpu as pltpu
from jax.sharding import Mesh, PartitionSpec as P

beta_decay = 0.9
norm_floor = 1e-06
count = 4

LINE, CORE, MP, PRE = "line", "core", "mp", "pre"
AXES = (LINE, CORE, MP, PRE)
f32, bf16 = jnp.float32, jnp.bfloat16


def halves(x):
    high = x.astype(bf16)
    return high, (x - high.astype(f32)).astype(bf16)


def whole_of(high, low):
    return high.astype(f32) + low.astype(f32)


def product(a, b, a_dim, b_dim):
    def one(x, y):
        return lax.dot_general(
            x, y, (((a_dim,), (b_dim,)), ((), ())), preferred_element_type=f32
        )

    return one(a[0], b[0]) + (one(a[0], b[1]) + one(a[1], b[0]))


def select_by(index, options):
    result = None
    for value, array in options.items():
        result = array if result is None else jnp.where(index == value, array, result)
    return result


def tie(values):
    return lax.optimization_barrier(tuple(values))


def call(body, outputs, numbers, arrays, space=pltpu.VMEM, scratch=(), mebibytes=24):
    inputs, results = len(arrays), len(outputs)

    def kernel(*refs):
        body(
            refs[0],
            refs[1 : 1 + inputs],
            refs[1 + inputs : 1 + inputs + results],
            *refs[1 + inputs + results :],
        )

    return pl.pallas_call(
        kernel,
        out_shape=[jax.ShapeDtypeStruct(shape, dtype) for shape, dtype in outputs],
        in_specs=[pl.BlockSpec(memory_space=pltpu.SMEM)]
        + [pl.BlockSpec(memory_space=space)] * inputs,
        out_specs=[pl.BlockSpec(memory_space=pltpu.VMEM)] * results,
        scratch_shapes=scratch,
        compiler_params=pltpu.CompilerParams(vmem_limit_bytes=mebibytes << 20),
        cost_estimate=pl.CostEstimate(flops=1, bytes_accessed=1, transcendentals=0),
    )(numbers, *arrays)


def added(numbers, arrays):
    def body(number, inputs, outputs):
        total = inputs[0][...]
        for array in inputs[1:]:
            total = total + array[...]
        outputs[0][...] = total

    return call(body, [(arrays[0].shape, f32)], numbers, arrays)[0]


def fetching(body, outputs, numbers, choices, shape, arrays=(), mebibytes=18):
    sources = []

    def place(array):
        for i, known in enumerate(sources):
            if known is array:
                return i
        sources.append(array)
        return len(sources) - 1

    shapes = [choice[2] if len(choice) > 2 else shape for choice in choices]
    choices = [
        (choice[0], {k: [(place(a), r) for a, r in terms] for k, terms in choice[1].items()})
        for choice in choices
    ]
    wholes = [place(array) for array in arrays]
    most = [max(1, *(len(t) for t in options.values())) for _, options in choices]
    many = len(choices)

    def inner(number, inputs, results, *scratch):
        held, kept = scratch[:many], scratch[many:-2]
        sems, kept_sems = scratch[-2:]

        def copies(o, terms):
            return [
                pltpu.make_async_copy(
                    inputs[a].at[pl.ds(r, shapes[o][0])], held[o].at[i], sems.at[o, i]
                )
                for i, (a, r) in enumerate(terms)
            ]

        loads = [
            pltpu.make_async_copy(inputs[a], kept[i], kept_sems.at[i])
            for i, a in enumerate(wholes)
        ]
        for o, (which, options) in enumerate(choices):
            for k, terms in options.items():

                @pl.when(number[which] == k)
                def _():
                    for copy in copies(o, terms):
                        copy.start()

        for copy in loads:
            copy.start()
        for o, (which, options) in enumerate(choices):
            for k, terms in options.items():

                @pl.when(number[which] == k)
                def _():
                    for copy in copies(o, terms):
                        copy.wait()
                    if not terms:
                        held[o][0] = jnp.zeros(shapes[o], f32)
                    if len(terms) > 1:
                        total = held[o][0]
                        for i in range(1, len(terms)):
                            total = total + held[o][i]
                        held[o][0] = total

        for copy in loads:
            copy.wait()
        body(number, [held[o].at[0] for o in range(many)], kept, results)

    return call(
        inner,
        outputs,
        numbers,
        sources,
        pl.ANY,
        [
            *[pltpu.VMEM((m,) + tuple(s), f32) for m, s in zip(most, shapes)],
            *[pltpu.VMEM(array.shape, array.dtype) for array in arrays],
            pltpu.SemaphoreType.DMA((max(many, 1), max(most + [1]))),
            pltpu.SemaphoreType.DMA((max(len(arrays), 1),)),
        ],
        mebibytes,
    )


def chosen_sums(numbers, choices, shape, more, tails):
    many = len(choices)
    sizes = [tail[2][0] for tail in tails] + [0] * (many - len(tails))
    arrays = []

    def place(array):
        for i, known in enumerate(arrays):
            if known is array:
                return i
        arrays.append(array)
        return len(arrays) - 1

    plans = [
        (choice[0], {k: [(place(a), r) for a, r in terms] for k, terms in choice[1].items()})
        for choice in choices + tails
    ]

    def body(number, inputs, outputs):
        def write(plan, result, at, rows):
            which, options = plan
            for k, terms in options.items():

                @pl.when(number[which] == k)
                def _():
                    total = jnp.zeros((rows,) + shape[1:], f32)
                    for i, (a, r) in enumerate(terms):
                        part = inputs[a][r : r + rows]
                        total = part if i == 0 else total + part
                    result[at : at + rows] = total

        for i, (result, rows, size) in enumerate(zip(outputs, more, sizes)):
            at = shape[0]
            write(plans[i], result, 0, at)
            if size:
                write(plans[many + i], result, at, size)
            if rows > size:
                result[at + size :] = jnp.zeros((rows - size,) + shape[1:], f32)

    out = [((shape[0] + rows,) + shape[1:], f32) for rows in more]
    return call(body, out, numbers, arrays, mebibytes=12)


class Windows:
    def __init__(self):
        self.now = 0
        self.processes = []

    def add(self, process):
        self.processes.append([process, None, None])

    def open(self):
        ended = []
        for entry in self.processes:
            process, due, values = entry
            if values and due >= self.now:
                continue
            try:
                windows, entry[2] = process.send(values)
                entry[1] = self.now + windows - 1
            except StopIteration:
                ended.append(entry)
        for entry in ended:
            self.processes.remove(entry)

    def close(self, *others):
        due = [entry for entry in self.processes if entry[1] == self.now and entry[2]]
        flat = list(others)
        for entry in due:
            flat.extend(entry[2])
        if flat:
            flat = list(tie(flat))
        at = len(others)
        for entry in due:
            size = len(entry[2])
            entry[2] = flat[at : at + size]
            at += size
        self.now += 1
        return flat[: len(others)]


def make_step(sizes):
    line, cores, mp, pre = (sizes[name] for name in AXES)
    models = mp * pre
    last = count - 1

    def swap(array, axis, bit):
        return lax.ppermute(array, axis, [(i, i ^ bit) for i in range(sizes[axis])])

    def bits(axis):
        return [1 << i for i in range(sizes[axis].bit_length() - 1)]

    def total(numbers, array, axes):
        for axis in axes:
            for bit in bits(axis):
                pair = yield 1, (array, swap(array, axis, bit))
                array = added(numbers, pair)
        return array

    def snake(array, outward):
        pairs = []
        for z in range(line):
            for c in range(cores):
                goal = z + (1 if (c == 0) == outward else -1)
                if 0 <= goal < line:
                    pairs.append((z * cores + c, goal * cores + c))
                else:
                    pairs.append((z * cores + c, z * cores + 1 - c))
        return lax.ppermute(array, (LINE, CORE), pairs)

    def shards(activations, grad_output, left_old, right_old, probe_left, probe_right):
        z, core = lax.axis_index(LINE), lax.axis_index(CORE)
        x, y = lax.axis_index(MP), lax.axis_index(PRE)
        model = x * pre + y
        width = activations.shape[1]
        block = grad_output.shape[1]
        hidden = block * models
        panel = block // cores
        own_rows = width // (line * cores)
        model_rows = width // models
        piece = width // count
        owner_x, owner_y = z // pre, z % pre
        there = jnp.where(core == 0, z, line - 1 - z)
        numbers = jnp.stack(
            [z, core, there, line - 1 - there, x == owner_x, y == owner_y, model]
        ).astype(jnp.int32)
        Z, C, THERE, BACK, IN_X, IN_Y, MODEL = range(7)
        shape = (piece, panel)
        windows = Windows()
        state = {}

        def to_partner(array):
            return swap(array, CORE, 1)

        def device(number):
            return number[Z] * cores + number[C]

        def local(first, end, mebibytes):
            rows = (end - first) * piece
            tokens = activations.shape[0]
            parts, slices = 4, 3
            span = tokens // parts
            thin = span // slices

            def body(number, inputs, outputs, left, right, sems):
                copies = []
                for i in range(parts):
                    for k in range(slices):
                        at = pl.ds(i * span + k * thin, thin)
                        copies.append(
                            pltpu.make_async_copy(
                                inputs[0].at[at, pl.ds(first * piece, rows)],
                                left.at[at],
                                sems.at[0, i, k],
                            )
                        )
                        copies.append(
                            pltpu.make_async_copy(
                                inputs[1].at[at], right.at[at], sems.at[1, i, k]
                            )
                        )
                for copy in copies:
                    copy.start()
                sums = [None] * (end - first)
                for i in range(parts):
                    for copy in copies[2 * slices * i : 2 * slices * (i + 1)]:
                        copy.wait()
                    at = slice(i * span, (i + 1) * span)
                    for j in range(end - first):
                        term = lax.dot_general(
                            left[at, j * piece : (j + 1) * piece],
                            right[at],
                            (((0,), (0,)), ((), ())),
                            preferred_element_type=f32,
                        )
                        sums[j] = term if i == 0 else sums[j] + term
                zeroth = jnp.full(shape, number[C], jnp.int32) == 0
                for j, both in enumerate(sums):
                    low, high = both[:, :panel], both[:, panel:]
                    outputs[0][j * piece : (j + 1) * piece] = jnp.where(zeroth, low, high)
                    outputs[1 + j][...] = jnp.where(zeroth, high, low)

            return call(
                body,
                [((rows, panel), f32)] + [(shape, f32)] * (end - first),
                numbers,
                [activations, grad_output],
                pl.ANY,
                [
                    pltpu.VMEM((tokens, rows), bf16),
                    pltpu.VMEM(grad_output.shape, bf16),
                    pltpu.SemaphoreType.DMA((2, parts, slices)),
                ],
                mebibytes,
            )

        kept_first, away = local(0, 1, 52)
        arrived = [to_partner(away)]

        class Chain:
            def __init__(self, terms):
                self.terms = terms
                self.sent, self.out, self.home, self.options = [], [], [], []

            def next_sums(self, t):
                choices = []
                for which, got in ((THERE, self.out), (BACK, self.home)):
                    options = {}
                    for k in range(line):
                        options[k] = []
                        if 0 <= t - k < count:
                            options[k] = self.terms(t - k)
                            if k:
                                options[k] = options[k] + [(got[t - 1], 0)]
                    choices.append((which, options))
                return choices

            def next_tails(self, t, piece_number, array):
                choices = []
                if not 0 <= t - piece_number < line:
                    return choices
                for which, got in ((THERE, self.out), (BACK, self.home)):
                    options = {k: [] for k in range(line)}
                    k = t - piece_number
                    options[k] = [(array, 0)] + ([(got[t - 1], piece)] if k else [])
                    choices.append((which, options, array.shape))
                return choices

            def finished_tail(self, piece_number, array):
                j = piece_number
                options = {
                    k: [(self.sent[j + k], piece), (self.home[j + line - 2 - k], piece)]
                    for k in range(line - 1)
                }
                options[line - 1] = [(array, 0), (self.out[j + line - 2], piece)]
                return THERE, options, array.shape

            def send(self, going_out, going_home):
                self.sent.append(going_out)
                self.out.append(snake(going_out, True))
                self.home.append(snake(going_home, False))

            def finished(self, t):
                j = t - (line - 1)
                if not 0 <= j < count:
                    return []
                options = {
                    k: [(self.sent[j + k], 0), (self.home[j + line - 2 - k], 0)]
                    for k in range(line - 1)
                }
                options[line - 1] = self.terms(j) + [(self.out[j + line - 2], 0)]
                self.options.append((THERE, options))
                return self.options[-1:]

        gradient = Chain(
            lambda j: [
                (kept_rest[0], (j - 1) * piece) if j else (kept_first, 0),
                (arrived[j], 0),
            ]
        )
        mixed = Chain(lambda j: [(state["kept", j], 0), (state["swapped", j], 0)])
        own, wishes, kept_rest = [], [], []

        def row(array):
            return array.reshape(1, -1)

        def exchange(array, axis):
            return total(numbers, array, (axis,))

        def placed(number, column):
            wide = (own_rows, width)
            at = lax.broadcasted_iota(jnp.int32, wide, 0) + device(number) * own_rows
            here = lax.broadcasted_iota(jnp.int32, wide, 1) == at
            return jnp.sum(jnp.where(here, column, 0.0), axis=0, keepdims=True)

        def panel_of(which):
            return row(lax.dynamic_slice_in_dim(probe_right, which * panel, panel, 0))

        def beside(first, second):
            def body(number, inputs, outputs):
                size = inputs[0].shape[1]
                outputs[0][:, :size] = inputs[0][...]
                outputs[0][:, size:] = inputs[1][...]

            shape = first.shape[0], first.shape[1] + second.shape[1]
            return call(body, [(shape, f32)], numbers, [first, second])[0]

        def left_turned():
            return (beta_decay * left_old).T

        block_rows, image_rows = block // panel, width // panel
        tail_rows = -(-(block_rows + image_rows) // 8) * 8
        tail_piece = 2

        def old_factors():
            while windows.now < 1:
                yield 1, ()

            def body(number, inputs, outputs):
                old = beta_decay * inputs[0][...]
                outputs[0][...], outputs[1][...] = halves(old)
                image = jnp.sum(old * inputs[1][...], axis=1, keepdims=True).T
                outputs[2][...] = jnp.zeros((tail_rows, panel), f32)
                for r in range(block_rows):
                    outputs[2][r : r + 1] = image[:, r * panel : (r + 1) * panel]
                image = jnp.sum(inputs[2][...] * inputs[3][...], axis=1, keepdims=True)
                image = placed(number, image)
                for r in range(image_rows):
                    at = block_rows + r
                    outputs[2][at : at + 1] = image[:, r * panel : (r + 1) * panel]

            own_probe = lax.dynamic_slice_in_dim(probe_left, model * model_rows, model_rows, 0)
            high, low, images = call(
                body,
                [((block, panel), bf16), ((block, panel), bf16), ((tail_rows, panel), f32)],
                numbers,
                [right_old, panel_of(z * cores + core), left_turned(), row(own_probe)],
            )
            *state["old"], state["tail"] = yield 1, (high, low, images)

        def old_left():
            while windows.now < 1:
                yield 1, ()
            rows = left_turned()
            for axis in (PRE, MP):
                for bit in bits(axis):
                    rows, got = yield 1, (rows, swap(rows, axis, bit))
                    rows = beside(rows, got)
            state["old_left"] = rows

        def spread(array, axis, place, owner):
            result = None
            size = sizes[axis]
            for s in range(1, size):
                got = lax.ppermute(array, axis, [(i, (i + s) % size) for i in range(size)])
                if result is None:
                    result = got
                else:
                    result = jnp.where((place - s) % size == owner, got, result)
            return result

        def panel_piece(j):
            while len(own) <= j:
                yield 1, ()
            if j < depth:
                other, got = yield 1, (to_partner(own[j]), spread(own[j], PRE, y, owner_y))
                state["other", j] = other, 0
            else:
                (got,) = yield 1, (spread(own[j], PRE, y, owner_y),)
            wishes.append((("held", j), (IN_Y, {1: [(own[j], 0)], 0: [(got, 0)]})))
            while ("held", j) not in state:
                yield 1, ()
            held = state["held", j]
            held, got = yield 1, (held, spread(held, MP, x, owner_x))
            riders = []
            if j + depth == last:
                while len(own) < count:
                    yield 1, ()
                riders = [*own[depth:], first_images()]

            def body(number, inputs, outputs):
                here = jnp.full(shape, number[IN_X], jnp.int32) == 1
                pair = halves(jnp.where(here, inputs[0][:piece], inputs[1][:piece]))
                outputs[0][...], outputs[1][...] = pair
                both = product(pair, (inputs[2][...], inputs[3][...]), 1, 1)
                low, high = both[:, :panel], both[:, panel:]
                zeroth = jnp.full(shape, number[C], jnp.int32) == 0
                outputs[2][...] = jnp.where(zeroth, low, high)
                outputs[3][:piece] = jnp.where(zeroth, high, low)
                at = piece
                for rider in inputs[4:]:
                    size = min(rider.shape[0], piece)
                    outputs[3][at : at + size] = rider[:size]
                    at += size

            away_rows = piece + sum(min(rider.shape[0], piece) for rider in riders)
            high, low, state["kept", j], away = call(
                body,
                [(shape, bf16), (shape, bf16), (shape, f32), ((away_rows, panel), f32)],
                numbers,
                [held, got, *state["old"], *riders],
            )
            state["panel", j] = high, low
            _, _, got = yield 1, (high, low, to_partner(away))
            state["swapped", j] = got
            if riders:
                for i in range(depth, count):
                    state["other", i] = got, (i - depth + 1) * piece
                state["images"] = riders[-1], got, (count - depth + 1) * piece

        depth = 2
        rider_rows = -(-(2 * image_rows + block_rows) // 8) * 8

        def first_images():
            def body(number, inputs, outputs):
                right, left = inputs[count][...], inputs[count + 1][...].T
                across = jnp.zeros((1, panel), f32)
                for j in range(count):
                    rows = slice(j * piece, (j + 1) * piece)
                    across += jnp.sum(inputs[j][:piece] * left[rows], axis=0, keepdims=True)
                old = inputs[count + 2][...]
                outputs[0][...] = jnp.zeros((rider_rows, panel), f32)
                outputs[0][2 * image_rows : 2 * image_rows + block_rows] = old[:block_rows]
                for i, vector in enumerate((right, across)):
                    image = jnp.concatenate(
                        [
                            jnp.sum(inputs[j][:piece] * vector, axis=1, keepdims=True).T
                            for j in range(count)
                        ],
                        axis=1,
                    )
                    for r in range(image_rows):
                        at = i * image_rows + r
                        part = image[:, r * panel : (r + 1) * panel]
                        if i:
                            part = part + hidden * old[block_rows + r : block_rows + r + 1]
                        outputs[0][at : at + 1] = part

            return call(
                body,
                [((rider_rows, panel), f32)],
                numbers,
                [
                    *own,
                    panel_of(model * cores + core),
                    row(probe_left),
                    state["old_images"],
                ],
            )[0]

        def over_models(array):
            steps = [(axis, bit) for axis in (PRE, MP) for bit in bits(axis)]
            for i, (axis, bit) in enumerate(steps):
                terms = yield 1, (array, swap(array, axis, bit))
                if i < len(steps) - 1:
                    array = added(numbers, terms)
            return terms

        def first_part(crossed):
            (crossed,) = yield 1, (crossed,)
            crossed = yield from over_models(crossed)
            while "squares" not in state:
                yield 1, ()

            def body(number, inputs, outputs):
                top_left, top_right, scale = scales(inputs[6][...] + inputs[7][...])
                grad = inputs[4][...], inputs[5][...]
                rows = pl.ds(pl.multiple_of(device(number) * own_rows, own_rows), own_rows)
                own = whole_of(inputs[4][rows, :], inputs[5][rows, :])
                crossed = product(halves(inputs[0][...] + inputs[1][...]), grad, 1, 0)
                outputs[0][...] = scale * (
                    25.0 * own
                    - inputs[2][...] * (5.0 / top_left)
                    - (5.0 * inputs[3][...] - crossed / top_left) / top_right
                )

            (state["first_part"],) = call(
                body,
                [((own_rows, block), f32)],
                numbers,
                [*crossed, *state["left_parts"], *state["block"], *state["squares"]],
            )

        def hold_block():
            state["block"] = yield 1, state["block"]

        def left_side():
            while ("other", last) not in state or "images" not in state:
                yield 1, ()
            other = [state["other", j] for j in range(count)]
            images, got, start = state["images"]

            def split_block(number, inputs, high, low):
                zeroth = jnp.full(shape, number[C], jnp.int32) == 0
                for j in range(count):
                    at = other[j][1]
                    mine, theirs = inputs[j][:piece], inputs[count + j][at : at + piece]
                    rows = pl.ds(j * piece, piece)
                    for i, part in enumerate(
                        (jnp.where(zeroth, mine, theirs), jnp.where(zeroth, theirs, mine))
                    ):
                        columns = pl.ds(i * panel, panel)
                        high[rows, columns], low[rows, columns] = halves(part)

            def body(number, inputs, outputs, high, low):
                split_block(number, inputs, high, low)
                rows = pl.ds(pl.multiple_of(device(number) * own_rows, own_rows), own_rows)
                gram = product((high[...], low[...]), (high[rows, :], low[rows, :]), 1, 1)
                outputs[0][:own_rows] = gram.T / hidden
                outputs[0][own_rows:] = jnp.zeros((8, width), f32)
                images = inputs[2 * count][...] + inputs[2 * count + 1][start:]
                for i in range(2):
                    for r in range(image_rows):
                        at = i * image_rows + r
                        outputs[0][own_rows + i : own_rows + i + 1, pl.ds(r * panel, panel)] = (
                            images[at : at + 1]
                        )
                for r in range(block_rows):
                    at = 2 * image_rows + r
                    outputs[1][:, pl.ds(r * panel, panel)] = images[at : at + 1]

            rows = (own_rows, width)
            sources = [*own, *(array for array, _ in other)]
            gram, state["old_image"] = call(
                body,
                [((own_rows + 8, width), f32), ((1, block), f32)],
                numbers,
                [*sources, images, got],
                scratch=[pltpu.VMEM((width, block), bf16)] * 2,
            )

            def body(number, inputs, outputs):
                split_block(number, inputs, *outputs)

            high, low = call(body, [((width, block), bf16)] * 2, numbers, sources)
            state["block"] = high, low
            windows.add(hold_block())
            gram = yield from over_models(gram)
            state["left_terms"] = gram

            def body(number, inputs, outputs):
                gram = inputs[0][:own_rows] + inputs[1][:own_rows]
                old = []
                for m in range(models):
                    part = jnp.zeros((own_rows, model_rows), f32)
                    for k in range(models):
                        at = jnp.full(part.shape, number[MODEL], jnp.int32)
                        block_k = inputs[2][:, k * model_rows : (k + 1) * model_rows]
                        part = jnp.where(at == m ^ k, block_k, part)
                    old.append(part)
                left = jnp.concatenate(old, axis=1) + gram
                outputs[0][...] = left
                new = left[:, :model_rows]
                for m in range(1, models):
                    at = jnp.full(new.shape, number[MODEL], jnp.int32)
                    new = jnp.where(at == m, left[:, m * model_rows : (m + 1) * model_rows], new)
                outputs[4][...] = new.T
                grad = inputs[3][...], inputs[4][...]
                left_grad = product(halves(left), grad, 1, 0)
                outputs[1][...] = left_grad
                outputs[2][...] = gram
                outputs[3][...] = product(grad, halves(left_grad), 1, 1).T / width

            left, left_grad, gram, crossed, new = call(
                body,
                [(rows, f32), ((own_rows, block), f32), (rows, f32), (rows, f32)]
                + [((model_rows, own_rows), f32)],
                numbers,
                [*gram, state["old_left"], *state["block"]],
            )
            state["left"] = left
            windows.add(first_part(crossed))
            left_grad, gram, left = yield 1, (left_grad, gram, left)
            partner_left = to_partner(left)

            def body(number, inputs, outputs):
                grad = inputs[1][...], inputs[2][...]
                outputs[0][...] = product(halves(inputs[0][...]), grad, 1, 0) * (hidden / width)

            (gram_grad,) = call(
                body, [((own_rows, block), f32)], numbers, [gram, *state["block"]]
            )
            state["partner_left"], *state["left_parts"] = yield 1, (
                partner_left,
                left_grad,
                gram_grad,
            )
            state["left_new"] = new

        def powers():
            while "left_terms" not in state:
                yield 1, ()

            def body(number, inputs, outputs):
                images = inputs[5][own_rows:] + inputs[6][own_rows:]
                outputs[1][...] = images[1:2] / hidden
                grad = whole_of(inputs[1][...], inputs[2][...])
                first = inputs[0][...] + (
                    jnp.sum(grad * images[0:1].T, axis=0, keepdims=True) / width
                )
                outputs[0][:, :width] = jnp.sum(grad * first, axis=1, keepdims=True).T
                old = whole_of(inputs[3][...], inputs[4][...])
                outputs[0][:, width : width + panel] = jnp.sum(
                    old * first.T, axis=0, keepdims=True
                )
                square = jnp.sum(first * first, axis=1, keepdims=True)
                outputs[0][:, width + panel :] = jnp.broadcast_to(square, (1, 128))

            joined, first = call(
                body,
                [((1, width + panel + 128), f32), ((1, width), f32)],
                numbers,
                [
                    state["old_image"],
                    *state["block"],
                    *state["old"],
                    *state["left_terms"],
                ],
            )
            for axis in (PRE, MP):
                for bit in bits(axis):
                    joined = added(numbers, [joined, swap(joined, axis, bit)])
            first, joined = yield 1, (first, joined)
            while "left" not in state or ("panel", last) not in state:
                yield 1, ()

            def body(number, inputs, outputs):
                joined = inputs[2 + 2 * count][...]
                for array in inputs[3 + 2 * count :]:
                    joined = joined + array[...]
                vector = joined[:, :width].T
                second = joined[:, width : width + panel]
                for j in range(count):
                    part = whole_of(inputs[2 + 2 * j][...], inputs[3 + 2 * j][...])
                    rows = vector[j * piece : (j + 1) * piece]
                    second = second + jnp.sum(part * rows, axis=0, keepdims=True) / width
                square = joined[:, width + panel : width + panel + 1]
                second = second / jnp.sqrt(square + norm_floor)
                right = jnp.sum(second * second, axis=1, keepdims=True)
                first = inputs[0][...]
                unit = first / jnp.sqrt(
                    jnp.sum(first * first, axis=1, keepdims=True) + norm_floor
                )
                second = jnp.sum(inputs[1][...] * unit, axis=1, keepdims=True)
                left = jnp.sum(second * second, axis=0, keepdims=True)
                spot = lax.broadcasted_iota(jnp.int32, (1, 128), 1)
                outputs[0][...] = jnp.where(spot == 0, left, right)

            panels = [half for j in range(count) for half in state["panel", j]]
            (squares,) = call(
                body,
                [((1, 128), f32)],
                numbers,
                [first, state["left"], *panels, joined],
            )
            squares = added(numbers, [squares, to_partner(squares)])
            for bit in bits(LINE)[:-2]:
                squares = added(numbers, [squares, swap(squares, LINE, bit)])
            squares = added(numbers, (yield 1, (squares, swap(squares, LINE, bits(LINE)[-2]))))
            state["squares"] = yield 1, (squares, swap(squares, LINE, bits(LINE)[-1]))

        def scales(squares):
            top = jnp.sqrt(squares + norm_floor)
            top_left, top_right = top[:, 0:1], top[:, 1:2]
            return top_left, top_right, 1.0 / (16.0 * jnp.sqrt(jnp.sqrt(top_left * top_right)))

        def right_factor():
            while ("panel", last) not in state or "block" not in state or windows.now < steps + 2:
                yield 1, ()

            def body(number, sums, inputs, outputs):
                pair = [
                    jnp.concatenate([inputs[3 + 2 * j + i][...] for j in range(count)], axis=0)
                    for i in range(2)
                ]
                gram = product((inputs[1][...], inputs[2][...]), pair, 0, 0)
                outputs[0][...] = beta_decay * inputs[0][...] + gram / width

            panels = [half for j in range(count) for half in state["panel", j]]
            (state["right_new"],) = yield 1, fetching(
                body,
                [((block, panel), f32)],
                numbers,
                [],
                shape,
                [right_old, *state["block"], *panels],
                32,
            )

        for j in range(count):
            windows.add(panel_piece(j))
        steps = count + line - 2
        def rows_here(number, i, rows, pieces):
            other = number[C] if i == 0 else 1 - number[C]
            at = jnp.full(rows.shape, number[Z] * cores + other, jnp.int32)
            for k in range(line * cores):
                j, start = divmod(k * own_rows, piece)
                for number_j, array in pieces:
                    if number_j == j:
                        rows = jnp.where(at == k, array[start : start + own_rows], rows)
            return rows

        def early_products():
            while len(mixed_wholes) < last or "partner_left" not in state:
                yield 1, ()

            def body(number, inputs, outputs):
                pieces = [(j, inputs[2 + j]) for j in range(last)]
                pair = halves(jnp.concatenate([array[:piece] for _, array in pieces], axis=0))
                for i in range(2):
                    left = halves(inputs[i][:, : last * piece])
                    outputs[i][...] = product(left, pair, 1, 0)
                    outputs[2 + i][...] = rows_here(
                        number, i, jnp.zeros((own_rows, panel), f32), pieces
                    )

            state["early"] = yield 1, call(
                body,
                [((own_rows, panel), f32)] * 4,
                numbers,
                [state["left"], state["partner_left"], *mixed_wholes],
            )

        mixed_wholes = []
        for process in (left_side, powers, right_factor, early_products):
            windows.add(process())

        for t in range(2 * steps):
            windows.open()
            current = gradient if t < steps else mixed
            choices = current.next_sums(t % steps) + gradient.finished(t)
            choices += mixed.finished(t - steps)
            names = [name for name, _ in wishes]
            choices += [choice for _, choice in wishes]
            wishes.clear()
            crowded = t == line + depth - 1
            longer = tail_rows + (16 if steps < t < steps + 3 else 8 if crowded else 0)
            extra = [longer] * 2 + [0] * (len(choices) - 2)
            for i, name in enumerate(names):
                extra[len(extra) - len(names) + i] = 8 if crowded else 0
            if crowded:
                extra[2] = 8
            if ("held", last) in names:
                extra[-1] = longer
            tails = []
            if t < steps and "tail" in state:
                tails = gradient.next_tails(t, tail_piece, state["tail"])
            results = list(chosen_sums(numbers, choices, shape, extra, tails))
            if t == 0:
                results[0], results[1], activations, grad_output, left_old, right_old = tie(
                    (*results, activations, grad_output, left_old, right_old)
                )
                windows.add(old_factors())
                windows.add(old_left())
                kept, *away = local(1, count, 40)
                kept_rest.append(kept)
                arrived += [to_partner(a) for a in away]
            current.send(*results[:2])
            for name in reversed(names):
                state[name] = results.pop()
            (own if len(own) < count else mixed_wholes).extend(results[2:])
            if t == tail_piece + line - 1:
                tail = gradient.finished_tail(tail_piece, state["tail"])

                def copy_body(number, sums, inputs, outputs):
                    outputs[0][...] = sums[0][...]

                (state["old_images"],) = fetching(
                    copy_body, [(tail[2], f32)], numbers, [tail], shape
                )
            windows.open()
            current.out[-1], current.home[-1] = windows.close(current.out[-1], current.home[-1])
        while windows.processes:
            windows.open()
            if windows.processes:
                windows.close()

        def body(number, sums, inputs, outputs):
            top_left, top_right, scale = scales(inputs[0][...] + inputs[1][...])
            pair = halves(sums[0][...])
            for i in range(2):
                rows = rows_here(number, i, inputs[6 + i][...], [(last, sums[0])])
                left = halves(inputs[2 + i][:, last * piece :])
                left = inputs[4 + i][...] + product(left, pair, 1, 0)
                outputs[i][...] = (left / top_left - 5.0 * rows) * (scale / top_right)

        mine, theirs = fetching(
            body,
            [((own_rows, panel), f32)] * 2,
            numbers,
            mixed.finished(steps),
            shape,
            [*state["squares"], state["left"], state["partner_left"], *state["early"]],
        )
        theirs = to_partner(theirs)

        def body(number, inputs, outputs):
            zeroth = jnp.full((own_rows, panel), number[C], jnp.int32) == 0
            mine, theirs = inputs[1][...], inputs[2][...]
            parts = jnp.where(zeroth, mine, theirs), jnp.where(zeroth, theirs, mine)
            for i, part in enumerate(parts):
                span = pl.ds(i * panel, panel)
                outputs[0][:, span] = inputs[0][:, span] + part

        (update,) = call(
            body, [((own_rows, block), f32)], numbers, [state["first_part"], mine, theirs]
        )
        return state["left_new"], state["right_new"], update

    return shards


def solution(mesh):
    dp, mp, pre = (mesh.shape[name] for name in ("dp", "mp", "pre"))
    cores = dp // (mp * pre)
    assert cores == 2
    split = Mesh(mesh.devices.reshape(dp // cores, cores, mp, pre), AXES)
    factor = P((MP, PRE), (LINE, CORE))
    in_specs = (
        P((LINE, CORE), None),
        P((LINE, CORE), (MP, PRE)),
        factor,
        factor,
        P(),
        P(),
    )
    out_specs = (factor, factor, P((LINE, CORE), (MP, PRE)))
    return jax.shard_map(
        make_step(dict(split.shape)),
        mesh=split,
        in_specs=in_specs,
        out_specs=out_specs,
        check_vma=False,
    )
```

```python
import jax
import jax.numpy as jnp
from jax import lax
from jax.experimental import pallas as pl
from jax.experimental.pallas import tpu as pltpu
from jax.sharding import Mesh, PartitionSpec as P

beta_decay = 0.9
norm_floor = 1e-06
count = 4

LINE, CORE, MP, PRE = "line", "core", "mp", "pre"
AXES = (LINE, CORE, MP, PRE)
f32, bf16 = jnp.float32, jnp.bfloat16


def halves(x):
    high = x.astype(bf16)
    return high, (x - high.astype(f32)).astype(bf16)


def whole_of(high, low):
    return high.astype(f32) + low.astype(f32)


def product(a, b, a_dim, b_dim):
    def one(x, y):
        return lax.dot_general(
            x, y, (((a_dim,), (b_dim,)), ((), ())), preferred_element_type=f32
        )

    return one(a[0], b[0]) + (one(a[0], b[1]) + one(a[1], b[0]))


def select_by(index, options):
    result = None
    for value, array in options.items():
        result = array if result is None else jnp.where(index == value, array, result)
    return result


def tie(values):
    return lax.optimization_barrier(tuple(values))


def call(body, outputs, numbers, arrays, space=pltpu.VMEM, scratch=(), mebibytes=24):
    inputs, results = len(arrays), len(outputs)

    def kernel(*refs):
        body(
            refs[0],
            refs[1 : 1 + inputs],
            refs[1 + inputs : 1 + inputs + results],
            *refs[1 + inputs + results :],
        )

    return pl.pallas_call(
        kernel,
        out_shape=[jax.ShapeDtypeStruct(shape, dtype) for shape, dtype in outputs],
        in_specs=[pl.BlockSpec(memory_space=pltpu.SMEM)]
        + [pl.BlockSpec(memory_space=space)] * inputs,
        out_specs=[pl.BlockSpec(memory_space=pltpu.VMEM)] * results,
        scratch_shapes=scratch,
        compiler_params=pltpu.CompilerParams(vmem_limit_bytes=mebibytes << 20),
        cost_estimate=pl.CostEstimate(flops=1, bytes_accessed=1, transcendentals=0),
    )(numbers, *arrays)


def added(numbers, arrays):
    def body(number, inputs, outputs):
        total = inputs[0][...]
        for array in inputs[1:]:
            total = total + array[...]
        outputs[0][...] = total

    return call(body, [(arrays[0].shape, f32)], numbers, arrays)[0]


def fetching(body, outputs, numbers, choices, shape, arrays=(), mebibytes=18):
    sources = []

    def place(array):
        for i, known in enumerate(sources):
            if known is array:
                return i
        sources.append(array)
        return len(sources) - 1

    shapes = [choice[2] if len(choice) > 2 else shape for choice in choices]
    choices = [
        (choice[0], {k: [(place(a), r) for a, r in terms] for k, terms in choice[1].items()})
        for choice in choices
    ]
    wholes = [place(array) for array in arrays]
    most = [max(1, *(len(t) for t in options.values())) for _, options in choices]
    many = len(choices)

    def inner(number, inputs, results, *scratch):
        held, kept = scratch[:many], scratch[many:-2]
        sems, kept_sems = scratch[-2:]

        def copies(o, terms):
            return [
                pltpu.make_async_copy(
                    inputs[a].at[pl.ds(r, shapes[o][0])], held[o].at[i], sems.at[o, i]
                )
                for i, (a, r) in enumerate(terms)
            ]

        loads = [
            pltpu.make_async_copy(inputs[a], kept[i], kept_sems.at[i])
            for i, a in enumerate(wholes)
        ]
        for o, (which, options) in enumerate(choices):
            for k, terms in options.items():

                @pl.when(number[which] == k)
                def _():
                    for copy in copies(o, terms):
                        copy.start()

        for copy in loads:
            copy.start()
        for o, (which, options) in enumerate(choices):
            for k, terms in options.items():

                @pl.when(number[which] == k)
                def _():
                    for copy in copies(o, terms):
                        copy.wait()
                    if not terms:
                        held[o][0] = jnp.zeros(shapes[o], f32)
                    if len(terms) > 1:
                        total = held[o][0]
                        for i in range(1, len(terms)):
                            total = total + held[o][i]
                        held[o][0] = total

        for copy in loads:
            copy.wait()
        body(number, [held[o].at[0] for o in range(many)], kept, results)

    return call(
        inner,
        outputs,
        numbers,
        sources,
        pl.ANY,
        [
            *[pltpu.VMEM((m,) + tuple(s), f32) for m, s in zip(most, shapes)],
            *[pltpu.VMEM(array.shape, array.dtype) for array in arrays],
            pltpu.SemaphoreType.DMA((max(many, 1), max(most + [1]))),
            pltpu.SemaphoreType.DMA((max(len(arrays), 1),)),
        ],
        mebibytes,
    )


def chosen_sums(numbers, choices, shape, more, tails):
    many = len(choices)
    sizes = [tail[2][0] for tail in tails] + [0] * (many - len(tails))
    arrays = []

    def place(array):
        for i, known in enumerate(arrays):
            if known is array:
                return i
        arrays.append(array)
        return len(arrays) - 1

    plans = [
        (choice[0], {k: [(place(a), r) for a, r in terms] for k, terms in choice[1].items()})
        for choice in choices + tails
    ]

    def body(number, inputs, outputs):
        def write(plan, result, at, rows):
            which, options = plan
            for k, terms in options.items():

                @pl.when(number[which] == k)
                def _():
                    thick = min(rows, 32)

                    def add(step, _):
                        start = pl.multiple_of(step * thick, thick)
                        total = jnp.zeros((thick,) + shape[1:], f32)
                        for i, (a, r) in enumerate(terms):
                            part = inputs[a][pl.ds(r + start, thick)]
                            total = part if i == 0 else total + part
                        result[pl.ds(at + start, thick)] = total
                        return 0

                    lax.fori_loop(0, rows // thick, add, 0)

        for i, (result, rows, size) in enumerate(zip(outputs, more, sizes)):
            at = shape[0]
            write(plans[i], result, 0, at)
            if size:
                write(plans[many + i], result, at, size)
            if rows > size:
                result[at + size :] = jnp.zeros((rows - size,) + shape[1:], f32)

    out = [((shape[0] + rows,) + shape[1:], f32) for rows in more]
    return call(body, out, numbers, arrays, mebibytes=12)


class Windows:
    def __init__(self):
        self.now = 0
        self.processes = []

    def add(self, process):
        self.processes.append([process, None, None])

    def open(self):
        ended = []
        for entry in self.processes:
            process, due, values = entry
            if values and due >= self.now:
                continue
            try:
                windows, entry[2] = process.send(values)
                entry[1] = self.now + windows - 1
            except StopIteration:
                ended.append(entry)
        for entry in ended:
            self.processes.remove(entry)

    def close(self, *others):
        due = [entry for entry in self.processes if entry[1] == self.now and entry[2]]
        flat = list(others)
        for entry in due:
            flat.extend(entry[2])
        if flat:
            flat = list(tie(flat))
        at = len(others)
        for entry in due:
            size = len(entry[2])
            entry[2] = flat[at : at + size]
            at += size
        self.now += 1
        return flat[: len(others)]


def make_step(sizes):
    line, cores, mp, pre = (sizes[name] for name in AXES)
    models = mp * pre
    last = count - 1

    def swap(array, axis, bit):
        return lax.ppermute(array, axis, [(i, i ^ bit) for i in range(sizes[axis])])

    def bits(axis):
        return [1 << i for i in range(sizes[axis].bit_length() - 1)]

    def total(numbers, array, axes):
        for axis in axes:
            for bit in bits(axis):
                pair = yield 1, (array, swap(array, axis, bit))
                array = added(numbers, pair)
        return array

    def snake(array, outward):
        pairs = []
        for z in range(line):
            for c in range(cores):
                goal = z + (1 if (c == 0) == outward else -1)
                if 0 <= goal < line:
                    pairs.append((z * cores + c, goal * cores + c))
                else:
                    pairs.append((z * cores + c, z * cores + 1 - c))
        return lax.ppermute(array, (LINE, CORE), pairs)

    def shards(activations, grad_output, left_old, right_old, probe_left, probe_right):
        z, core = lax.axis_index(LINE), lax.axis_index(CORE)
        x, y = lax.axis_index(MP), lax.axis_index(PRE)
        model = x * pre + y
        width = activations.shape[1]
        block = grad_output.shape[1]
        hidden = block * models
        panel = block // cores
        own_rows = width // (line * cores)
        model_rows = width // models
        piece = width // count
        owner_x, owner_y = z // pre, z % pre
        there = jnp.where(core == 0, z, line - 1 - z)
        numbers = jnp.stack(
            [z, core, there, line - 1 - there, x == owner_x, y == owner_y, model]
        ).astype(jnp.int32)
        Z, C, THERE, BACK, IN_X, IN_Y, MODEL = range(7)
        shape = (piece, panel)
        windows = Windows()
        state = {}

        def to_partner(array):
            return swap(array, CORE, 1)

        def device(number):
            return number[Z] * cores + number[C]

        def local(first, end, mebibytes):
            rows = (end - first) * piece
            tokens = activations.shape[0]
            parts, slices = 4, 3
            span = tokens // parts
            thin = span // slices

            def body(number, inputs, outputs, left, right, sems):
                copies = []
                for i in range(parts):
                    for k in range(slices):
                        at = pl.ds(i * span + k * thin, thin)
                        copies.append(
                            pltpu.make_async_copy(
                                inputs[0].at[at, pl.ds(first * piece, rows)],
                                left.at[at],
                                sems.at[0, i, k],
                            )
                        )
                        copies.append(
                            pltpu.make_async_copy(
                                inputs[1].at[at], right.at[at], sems.at[1, i, k]
                            )
                        )
                for copy in copies:
                    copy.start()
                sums = [None] * (end - first)
                for i in range(parts):
                    for copy in copies[2 * slices * i : 2 * slices * (i + 1)]:
                        copy.wait()
                    at = slice(i * span, (i + 1) * span)
                    for j in range(end - first):
                        term = lax.dot_general(
                            left[at, j * piece : (j + 1) * piece],
                            right[at],
                            (((0,), (0,)), ((), ())),
                            preferred_element_type=f32,
                        )
                        sums[j] = term if i == 0 else sums[j] + term
                zeroth = jnp.full(shape, number[C], jnp.int32) == 0
                for j, both in enumerate(sums):
                    low, high = both[:, :panel], both[:, panel:]
                    outputs[0][j * piece : (j + 1) * piece] = jnp.where(zeroth, low, high)
                    outputs[1 + j][...] = jnp.where(zeroth, high, low)

            return call(
                body,
                [((rows, panel), f32)] + [(shape, f32)] * (end - first),
                numbers,
                [activations, grad_output],
                pl.ANY,
                [
                    pltpu.VMEM((tokens, rows), bf16),
                    pltpu.VMEM(grad_output.shape, bf16),
                    pltpu.SemaphoreType.DMA((2, parts, slices)),
                ],
                mebibytes,
            )

        kept_first, away = local(0, 1, 52)
        arrived = [to_partner(away)]

        class Chain:
            def __init__(self, terms):
                self.terms = terms
                self.sent, self.out, self.home, self.options = [], [], [], []

            def next_sums(self, t):
                choices = []
                for which, got in ((THERE, self.out), (BACK, self.home)):
                    options = {}
                    for k in range(line):
                        options[k] = []
                        if 0 <= t - k < count:
                            options[k] = self.terms(t - k)
                            if k:
                                options[k] = options[k] + [(got[t - 1], 0)]
                    choices.append((which, options))
                return choices

            def next_tails(self, t, piece_number, array):
                choices = []
                if not 0 <= t - piece_number < line:
                    return choices
                for which, got in ((THERE, self.out), (BACK, self.home)):
                    options = {k: [] for k in range(line)}
                    k = t - piece_number
                    options[k] = [(array, 0)] + ([(got[t - 1], piece)] if k else [])
                    choices.append((which, options, array.shape))
                return choices

            def finished_tail(self, piece_number, array):
                j = piece_number
                options = {
                    k: [(self.sent[j + k], piece), (self.home[j + line - 2 - k], piece)]
                    for k in range(line - 1)
                }
                options[line - 1] = [(array, 0), (self.out[j + line - 2], piece)]
                return THERE, options, array.shape

            def send(self, going_out, going_home):
                self.sent.append(going_out)
                self.out.append(snake(going_out, True))
                self.home.append(snake(going_home, False))

            def finished(self, t):
                j = t - (line - 1)
                if not 0 <= j < count:
                    return []
                options = {
                    k: [(self.sent[j + k], 0), (self.home[j + line - 2 - k], 0)]
                    for k in range(line - 1)
                }
                options[line - 1] = self.terms(j) + [(self.out[j + line - 2], 0)]
                self.options.append((THERE, options))
                return self.options[-1:]

        gradient = Chain(
            lambda j: [
                (kept_rest[0], (j - 1) * piece) if j else (kept_first, 0),
                (arrived[j], 0),
            ]
        )
        mixed = Chain(lambda j: [(state["kept", j], 0), (state["swapped", j], 0)])
        own, wishes, kept_rest = [], [], []

        def row(array):
            return array.reshape(1, -1)

        def exchange(array, axis):
            return total(numbers, array, (axis,))

        def placed(number, column):
            wide = (own_rows, width)
            at = lax.broadcasted_iota(jnp.int32, wide, 0) + device(number) * own_rows
            here = lax.broadcasted_iota(jnp.int32, wide, 1) == at
            return jnp.sum(jnp.where(here, column, 0.0), axis=0, keepdims=True)

        def panel_of(which):
            return row(lax.dynamic_slice_in_dim(probe_right, which * panel, panel, 0))

        def beside(first, second):
            def body(number, inputs, outputs):
                size = inputs[0].shape[1]
                outputs[0][:, :size] = inputs[0][...]
                outputs[0][:, size:] = inputs[1][...]

            shape = first.shape[0], first.shape[1] + second.shape[1]
            return call(body, [(shape, f32)], numbers, [first, second])[0]

        def left_turned():
            return (beta_decay * left_old).T

        block_rows, image_rows = block // panel, width // panel
        tail_rows = -(-(block_rows + image_rows) // 8) * 8
        tail_piece = 2

        def old_factors():
            while windows.now < 1:
                yield 1, ()

            def body(number, inputs, outputs):
                old = beta_decay * inputs[0][...]
                outputs[0][...], outputs[1][...] = halves(old)
                image = jnp.sum(old * inputs[1][...], axis=1, keepdims=True).T
                outputs[2][...] = jnp.zeros((tail_rows, panel), f32)
                for r in range(block_rows):
                    outputs[2][r : r + 1] = image[:, r * panel : (r + 1) * panel]
                image = jnp.sum(inputs[2][...] * inputs[3][...], axis=1, keepdims=True)
                image = placed(number, image)
                for r in range(image_rows):
                    at = block_rows + r
                    outputs[2][at : at + 1] = image[:, r * panel : (r + 1) * panel]

            own_probe = lax.dynamic_slice_in_dim(probe_left, model * model_rows, model_rows, 0)
            high, low, images = call(
                body,
                [((block, panel), bf16), ((block, panel), bf16), ((tail_rows, panel), f32)],
                numbers,
                [right_old, panel_of(z * cores + core), left_turned(), row(own_probe)],
            )
            *state["old"], state["tail"] = yield 1, (high, low, images)

        def old_left():
            while windows.now < 1:
                yield 1, ()
            rows = left_turned()
            for axis in (PRE, MP):
                for bit in bits(axis):
                    rows, got = yield 1, (rows, swap(rows, axis, bit))
                    rows = beside(rows, got)
            state["old_left"] = rows

        def spread(array, axis, place, owner):
            result = None
            size = sizes[axis]
            for s in range(1, size):
                got = lax.ppermute(array, axis, [(i, (i + s) % size) for i in range(size)])
                if result is None:
                    result = got
                else:
                    result = jnp.where((place - s) % size == owner, got, result)
            return result

        def panel_piece(j):
            while len(own) <= j:
                yield 1, ()
            if j < depth:
                other, got = yield 1, (to_partner(own[j]), spread(own[j], PRE, y, owner_y))
                state["other", j] = other, 0
            else:
                (got,) = yield 1, (spread(own[j], PRE, y, owner_y),)
            wishes.append((("held", j), (IN_Y, {1: [(own[j], 0)], 0: [(got, 0)]})))
            while ("held", j) not in state:
                yield 1, ()
            held = state["held", j]
            held, got = yield 1, (held, spread(held, MP, x, owner_x))
            riders = []
            if j + depth == last:
                while len(own) < count:
                    yield 1, ()
                riders = [*own[depth:], first_images()]

            def body(number, inputs, outputs):
                here = jnp.full(shape, number[IN_X], jnp.int32) == 1
                pair = halves(jnp.where(here, inputs[0][:piece], inputs[1][:piece]))
                outputs[0][...], outputs[1][...] = pair
                both = product(pair, (inputs[2][...], inputs[3][...]), 1, 1)
                low, high = both[:, :panel], both[:, panel:]
                zeroth = jnp.full(shape, number[C], jnp.int32) == 0
                outputs[2][...] = jnp.where(zeroth, low, high)
                outputs[3][:piece] = jnp.where(zeroth, high, low)
                at = piece
                for rider in inputs[4:]:
                    size = min(rider.shape[0], piece)
                    outputs[3][at : at + size] = rider[:size]
                    at += size

            away_rows = piece + sum(min(rider.shape[0], piece) for rider in riders)
            high, low, state["kept", j], away = call(
                body,
                [(shape, bf16), (shape, bf16), (shape, f32), ((away_rows, panel), f32)],
                numbers,
                [held, got, *state["old"], *riders],
            )
            state["panel", j] = high, low
            _, _, got = yield 1, (high, low, to_partner(away))
            state["swapped", j] = got
            if riders:
                for i in range(depth, count):
                    state["other", i] = got, (i - depth + 1) * piece
                state["images"] = riders[-1], got, (count - depth + 1) * piece

        depth = 2
        rider_rows = -(-(2 * image_rows + block_rows) // 8) * 8

        def first_images():
            def body(number, inputs, outputs):
                right, left = inputs[count][...], inputs[count + 1][...].T
                across = jnp.zeros((1, panel), f32)
                for j in range(count):
                    rows = slice(j * piece, (j + 1) * piece)
                    across += jnp.sum(inputs[j][:piece] * left[rows], axis=0, keepdims=True)
                old = inputs[count + 2][...]
                outputs[0][...] = jnp.zeros((rider_rows, panel), f32)
                outputs[0][2 * image_rows : 2 * image_rows + block_rows] = old[:block_rows]
                for i, vector in enumerate((right, across)):
                    image = jnp.concatenate(
                        [
                            jnp.sum(inputs[j][:piece] * vector, axis=1, keepdims=True).T
                            for j in range(count)
                        ],
                        axis=1,
                    )
                    for r in range(image_rows):
                        at = i * image_rows + r
                        part = image[:, r * panel : (r + 1) * panel]
                        if i:
                            part = part + hidden * old[block_rows + r : block_rows + r + 1]
                        outputs[0][at : at + 1] = part

            return call(
                body,
                [((rider_rows, panel), f32)],
                numbers,
                [
                    *own,
                    panel_of(model * cores + core),
                    row(probe_left),
                    state["old_images"],
                ],
            )[0]

        def over_models(array):
            steps = [(axis, bit) for axis in (PRE, MP) for bit in bits(axis)]
            for i, (axis, bit) in enumerate(steps):
                terms = yield 1, (array, swap(array, axis, bit))
                if i < len(steps) - 1:
                    array = added(numbers, terms)
            return terms

        def first_part(crossed):
            (crossed,) = yield 1, (crossed,)
            crossed = yield from over_models(crossed)
            while "squares" not in state:
                yield 1, ()

            def body(number, inputs, outputs):
                top_left, top_right, scale = scales(inputs[6][...] + inputs[7][...])
                grad = inputs[4][...], inputs[5][...]
                rows = pl.ds(pl.multiple_of(device(number) * own_rows, own_rows), own_rows)
                own = whole_of(inputs[4][rows, :], inputs[5][rows, :])
                crossed = product(halves(inputs[0][...] + inputs[1][...]), grad, 1, 0)
                outputs[0][...] = scale * (
                    25.0 * own
                    - inputs[2][...] * (5.0 / top_left)
                    - (5.0 * inputs[3][...] - crossed / top_left) / top_right
                )

            (state["first_part"],) = call(
                body,
                [((own_rows, block), f32)],
                numbers,
                [*crossed, *state["left_parts"], *state["block"], *state["squares"]],
            )

        def hold_block():
            state["block"] = yield 1, state["block"]

        def left_side():
            while ("other", last) not in state or "images" not in state:
                yield 1, ()
            other = [state["other", j] for j in range(count)]
            images, got, start = state["images"]

            def split_block(number, inputs, high, low):
                zeroth = jnp.full(shape, number[C], jnp.int32) == 0
                for j in range(count):
                    at = other[j][1]
                    mine, theirs = inputs[j][:piece], inputs[count + j][at : at + piece]
                    rows = pl.ds(j * piece, piece)
                    for i, part in enumerate(
                        (jnp.where(zeroth, mine, theirs), jnp.where(zeroth, theirs, mine))
                    ):
                        columns = pl.ds(i * panel, panel)
                        high[rows, columns], low[rows, columns] = halves(part)

            def body(number, inputs, outputs, high, low):
                split_block(number, inputs, high, low)
                rows = pl.ds(pl.multiple_of(device(number) * own_rows, own_rows), own_rows)
                gram = product((high[...], low[...]), (high[rows, :], low[rows, :]), 1, 1)
                outputs[0][:own_rows] = gram.T / hidden
                outputs[0][own_rows:] = jnp.zeros((8, width), f32)
                images = inputs[2 * count][...] + inputs[2 * count + 1][start:]
                for i in range(2):
                    for r in range(image_rows):
                        at = i * image_rows + r
                        outputs[0][own_rows + i : own_rows + i + 1, pl.ds(r * panel, panel)] = (
                            images[at : at + 1]
                        )
                for r in range(block_rows):
                    at = 2 * image_rows + r
                    outputs[1][:, pl.ds(r * panel, panel)] = images[at : at + 1]

            rows = (own_rows, width)
            sources = [*own, *(array for array, _ in other)]
            gram, state["old_image"] = call(
                body,
                [((own_rows + 8, width), f32), ((1, block), f32)],
                numbers,
                [*sources, images, got],
                scratch=[pltpu.VMEM((width, block), bf16)] * 2,
            )

            def body(number, inputs, outputs):
                split_block(number, inputs, *outputs)

            high, low = call(body, [((width, block), bf16)] * 2, numbers, sources)
            state["block"] = high, low
            windows.add(hold_block())
            gram = yield from over_models(gram)
            state["left_terms"] = gram

            def body(number, inputs, outputs):
                gram = inputs[0][:own_rows] + inputs[1][:own_rows]
                old = []
                for m in range(models):
                    part = jnp.zeros((own_rows, model_rows), f32)
                    for k in range(models):
                        at = jnp.full(part.shape, number[MODEL], jnp.int32)
                        block_k = inputs[2][:, k * model_rows : (k + 1) * model_rows]
                        part = jnp.where(at == m ^ k, block_k, part)
                    old.append(part)
                left = jnp.concatenate(old, axis=1) + gram
                outputs[0][...] = left
                new = left[:, :model_rows]
                for m in range(1, models):
                    at = jnp.full(new.shape, number[MODEL], jnp.int32)
                    new = jnp.where(at == m, left[:, m * model_rows : (m + 1) * model_rows], new)
                outputs[4][...] = new.T
                grad = inputs[3][...], inputs[4][...]
                left_grad = product(halves(left), grad, 1, 0)
                outputs[1][...] = left_grad
                outputs[2][...] = gram
                outputs[3][...] = product(grad, halves(left_grad), 1, 1).T / width

            left, left_grad, gram, crossed, new = call(
                body,
                [(rows, f32), ((own_rows, block), f32), (rows, f32), (rows, f32)]
                + [((model_rows, own_rows), f32)],
                numbers,
                [*gram, state["old_left"], *state["block"]],
            )
            state["left"] = left
            windows.add(first_part(crossed))
            left_grad, gram, left = yield 1, (left_grad, gram, left)
            partner_left = to_partner(left)

            def body(number, inputs, outputs):
                grad = inputs[1][...], inputs[2][...]
                outputs[0][...] = product(halves(inputs[0][...]), grad, 1, 0) * (hidden / width)

            (gram_grad,) = call(
                body, [((own_rows, block), f32)], numbers, [gram, *state["block"]]
            )
            state["partner_left"], *state["left_parts"] = yield 1, (
                partner_left,
                left_grad,
                gram_grad,
            )
            state["left_new"] = new

        def powers():
            while "left_terms" not in state:
                yield 1, ()

            def body(number, inputs, outputs):
                images = inputs[5][own_rows:] + inputs[6][own_rows:]
                outputs[1][...] = images[1:2] / hidden
                grad = whole_of(inputs[1][...], inputs[2][...])
                first = inputs[0][...] + (
                    jnp.sum(grad * images[0:1].T, axis=0, keepdims=True) / width
                )
                outputs[0][:, :width] = jnp.sum(grad * first, axis=1, keepdims=True).T
                old = whole_of(inputs[3][...], inputs[4][...])
                outputs[0][:, width : width + panel] = jnp.sum(
                    old * first.T, axis=0, keepdims=True
                )
                square = jnp.sum(first * first, axis=1, keepdims=True)
                outputs[0][:, width + panel :] = jnp.broadcast_to(square, (1, 128))

            joined, first = call(
                body,
                [((1, width + panel + 128), f32), ((1, width), f32)],
                numbers,
                [
                    state["old_image"],
                    *state["block"],
                    *state["old"],
                    *state["left_terms"],
                ],
            )
            for axis in (PRE, MP):
                for bit in bits(axis):
                    joined = added(numbers, [joined, swap(joined, axis, bit)])
            first, joined = yield 1, (first, joined)
            while "left" not in state or ("panel", last) not in state:
                yield 1, ()

            def body(number, inputs, outputs):
                joined = inputs[2 + 2 * count][...]
                for array in inputs[3 + 2 * count :]:
                    joined = joined + array[...]
                vector = joined[:, :width].T
                second = joined[:, width : width + panel]
                for j in range(count):
                    part = whole_of(inputs[2 + 2 * j][...], inputs[3 + 2 * j][...])
                    rows = vector[j * piece : (j + 1) * piece]
                    second = second + jnp.sum(part * rows, axis=0, keepdims=True) / width
                square = joined[:, width + panel : width + panel + 1]
                second = second / jnp.sqrt(square + norm_floor)
                right = jnp.sum(second * second, axis=1, keepdims=True)
                first = inputs[0][...]
                unit = first / jnp.sqrt(
                    jnp.sum(first * first, axis=1, keepdims=True) + norm_floor
                )
                second = jnp.sum(inputs[1][...] * unit, axis=1, keepdims=True)
                left = jnp.sum(second * second, axis=0, keepdims=True)
                spot = lax.broadcasted_iota(jnp.int32, (1, 128), 1)
                outputs[0][...] = jnp.where(spot == 0, left, right)

            panels = [half for j in range(count) for half in state["panel", j]]
            (squares,) = call(
                body,
                [((1, 128), f32)],
                numbers,
                [first, state["left"], *panels, joined],
            )
            squares = added(numbers, [squares, to_partner(squares)])
            for bit in bits(LINE)[:-2]:
                squares = added(numbers, [squares, swap(squares, LINE, bit)])
            squares = added(numbers, (yield 1, (squares, swap(squares, LINE, bits(LINE)[-2]))))
            state["squares"] = yield 1, (squares, swap(squares, LINE, bits(LINE)[-1]))

        def scales(squares):
            top = jnp.sqrt(squares + norm_floor)
            top_left, top_right = top[:, 0:1], top[:, 1:2]
            return top_left, top_right, 1.0 / (16.0 * jnp.sqrt(jnp.sqrt(top_left * top_right)))

        def right_factor():
            while ("panel", last) not in state or "block" not in state or windows.now < steps + 2:
                yield 1, ()

            def body(number, sums, inputs, outputs):
                pair = [
                    jnp.concatenate([inputs[3 + 2 * j + i][...] for j in range(count)], axis=0)
                    for i in range(2)
                ]
                gram = product((inputs[1][...], inputs[2][...]), pair, 0, 0)
                outputs[0][...] = beta_decay * inputs[0][...] + gram / width

            panels = [half for j in range(count) for half in state["panel", j]]
            (state["right_new"],) = yield 1, fetching(
                body,
                [((block, panel), f32)],
                numbers,
                [],
                shape,
                [right_old, *state["block"], *panels],
                32,
            )

        for j in range(count):
            windows.add(panel_piece(j))
        steps = count + line - 2
        def rows_here(number, i, rows, pieces):
            other = number[C] if i == 0 else 1 - number[C]
            at = jnp.full(rows.shape, number[Z] * cores + other, jnp.int32)
            for k in range(line * cores):
                j, start = divmod(k * own_rows, piece)
                for number_j, array in pieces:
                    if number_j == j:
                        rows = jnp.where(at == k, array[start : start + own_rows], rows)
            return rows

        def early_products():
            while len(mixed_wholes) < last or "partner_left" not in state:
                yield 1, ()

            def body(number, inputs, outputs):
                pieces = [(j, inputs[2 + j]) for j in range(last)]
                pair = halves(jnp.concatenate([array[:piece] for _, array in pieces], axis=0))
                for i in range(2):
                    left = halves(inputs[i][:, : last * piece])
                    outputs[i][...] = product(left, pair, 1, 0)
                    outputs[2 + i][...] = rows_here(
                        number, i, jnp.zeros((own_rows, panel), f32), pieces
                    )

            state["early"] = yield 1, call(
                body,
                [((own_rows, panel), f32)] * 4,
                numbers,
                [state["left"], state["partner_left"], *mixed_wholes],
            )

        mixed_wholes = []
        for process in (left_side, powers, right_factor, early_products):
            windows.add(process())

        for t in range(2 * steps):
            windows.open()
            current = gradient if t < steps else mixed
            choices = current.next_sums(t % steps) + gradient.finished(t)
            choices += mixed.finished(t - steps)
            names = [name for name, _ in wishes]
            choices += [choice for _, choice in wishes]
            wishes.clear()
            crowded = t == line + depth - 1
            longer = tail_rows + (16 if steps < t < steps + 3 else 8 if crowded else 0)
            extra = [longer] * 2 + [0] * (len(choices) - 2)
            for i, name in enumerate(names):
                extra[len(extra) - len(names) + i] = 8 if crowded else 0
            if crowded:
                extra[2] = 8
            if ("held", last) in names:
                extra[-1] = longer
            tails = []
            if t < steps and "tail" in state:
                tails = gradient.next_tails(t, tail_piece, state["tail"])
            results = list(chosen_sums(numbers, choices, shape, extra, tails))
            if t == 0:
                results[0], results[1], activations, grad_output, left_old, right_old = tie(
                    (*results, activations, grad_output, left_old, right_old)
                )
                windows.add(old_factors())
                windows.add(old_left())
                kept, *away = local(1, count, 40)
                kept_rest.append(kept)
                arrived += [to_partner(a) for a in away]
            current.send(*results[:2])
            for name in reversed(names):
                state[name] = results.pop()
            (own if len(own) < count else mixed_wholes).extend(results[2:])
            if t == tail_piece + line - 1:
                tail = gradient.finished_tail(tail_piece, state["tail"])

                def copy_body(number, sums, inputs, outputs):
                    outputs[0][...] = sums[0][...]

                (state["old_images"],) = fetching(
                    copy_body, [(tail[2], f32)], numbers, [tail], shape
                )
            windows.open()
            current.out[-1], current.home[-1] = windows.close(current.out[-1], current.home[-1])
        while windows.processes:
            windows.open()
            if windows.processes:
                windows.close()

        def body(number, sums, inputs, outputs):
            top_left, top_right, scale = scales(inputs[0][...] + inputs[1][...])
            pair = halves(sums[0][...])
            for i in range(2):
                rows = rows_here(number, i, inputs[6 + i][...], [(last, sums[0])])
                left = halves(inputs[2 + i][:, last * piece :])
                left = inputs[4 + i][...] + product(left, pair, 1, 0)
                outputs[i][...] = (left / top_left - 5.0 * rows) * (scale / top_right)

        mine, theirs = fetching(
            body,
            [((own_rows, panel), f32)] * 2,
            numbers,
            mixed.finished(steps),
            shape,
            [*state["squares"], state["left"], state["partner_left"], *state["early"]],
        )
        theirs = to_partner(theirs)

        def body(number, inputs, outputs):
            zeroth = jnp.full((own_rows, panel), number[C], jnp.int32) == 0
            mine, theirs = inputs[1][...], inputs[2][...]
            parts = jnp.where(zeroth, mine, theirs), jnp.where(zeroth, theirs, mine)
            for i, part in enumerate(parts):
                span = pl.ds(i * panel, panel)
                outputs[0][:, span] = inputs[0][:, span] + part

        (update,) = call(
            body, [((own_rows, block), f32)], numbers, [state["first_part"], mine, theirs]
        )
        return state["left_new"], state["right_new"], update

    return shards


def solution(mesh):
    dp, mp, pre = (mesh.shape[name] for name in ("dp", "mp", "pre"))
    cores = dp // (mp * pre)
    assert cores == 2
    split = Mesh(mesh.devices.reshape(dp // cores, cores, mp, pre), AXES)
    factor = P((MP, PRE), (LINE, CORE))
    in_specs = (
        P((LINE, CORE), None),
        P((LINE, CORE), (MP, PRE)),
        factor,
        factor,
        P(),
        P(),
    )
    out_specs = (factor, factor, P((LINE, CORE), (MP, PRE)))
    return jax.shard_map(
        make_step(dict(split.shape)),
        mesh=split,
        in_specs=in_specs,
        out_specs=out_specs,
        check_vma=False,
    )
```

```python
import jax
import jax.numpy as jnp
from jax import lax
from jax.experimental import pallas as pl
from jax.experimental.pallas import tpu as pltpu
from jax.sharding import Mesh, PartitionSpec as P

beta_decay = 0.9
norm_floor = 1e-06
count = 4

LINE, CORE, MP, PRE = "line", "core", "mp", "pre"
AXES = (LINE, CORE, MP, PRE)
f32, bf16 = jnp.float32, jnp.bfloat16


def halves(x):
    high = x.astype(bf16)
    return high, (x - high.astype(f32)).astype(bf16)


def whole_of(high, low):
    return high.astype(f32) + low.astype(f32)


def product(a, b, a_dim, b_dim):
    def one(x, y):
        return lax.dot_general(
            x, y, (((a_dim,), (b_dim,)), ((), ())), preferred_element_type=f32
        )

    return one(a[0], b[0]) + (one(a[0], b[1]) + one(a[1], b[0]))


def select_by(index, options):
    result = None
    for value, array in options.items():
        result = array if result is None else jnp.where(index == value, array, result)
    return result


def tie(values):
    return lax.optimization_barrier(tuple(values))


def call(body, outputs, numbers, arrays, space=pltpu.VMEM, scratch=(), mebibytes=20):
    inputs, results = len(arrays), len(outputs)

    def kernel(*refs):
        body(
            refs[0],
            refs[1 : 1 + inputs],
            refs[1 + inputs : 1 + inputs + results],
            *refs[1 + inputs + results :],
        )

    return pl.pallas_call(
        kernel,
        out_shape=[jax.ShapeDtypeStruct(shape, dtype) for shape, dtype in outputs],
        in_specs=[pl.BlockSpec(memory_space=pltpu.SMEM)]
        + [pl.BlockSpec(memory_space=space)] * inputs,
        out_specs=[pl.BlockSpec(memory_space=pltpu.VMEM)] * results,
        scratch_shapes=scratch,
        compiler_params=pltpu.CompilerParams(vmem_limit_bytes=mebibytes << 20),
        cost_estimate=pl.CostEstimate(flops=1, bytes_accessed=1, transcendentals=0),
    )(numbers, *arrays)


def added(numbers, arrays):
    def body(number, inputs, outputs):
        total = inputs[0][...]
        for array in inputs[1:]:
            total = total + array[...]
        outputs[0][...] = total

    return call(body, [(arrays[0].shape, f32)], numbers, arrays)[0]


def fetching(body, outputs, numbers, choices, shape, arrays=(), mebibytes=18):
    sources = []

    def place(array):
        for i, known in enumerate(sources):
            if known is array:
                return i
        sources.append(array)
        return len(sources) - 1

    shapes = [choice[2] if len(choice) > 2 else shape for choice in choices]
    choices = [
        (choice[0], {k: [(place(a), r) for a, r in terms] for k, terms in choice[1].items()})
        for choice in choices
    ]
    wholes = [place(array) for array in arrays]
    most = [max(1, *(len(t) for t in options.values())) for _, options in choices]
    many = len(choices)

    def inner(number, inputs, results, *scratch):
        held, kept = scratch[:many], scratch[many:-2]
        sems, kept_sems = scratch[-2:]

        def copies(o, terms):
            return [
                pltpu.make_async_copy(
                    inputs[a].at[pl.ds(r, shapes[o][0])], held[o].at[i], sems.at[o, i]
                )
                for i, (a, r) in enumerate(terms)
            ]

        loads = [
            pltpu.make_async_copy(inputs[a], kept[i], kept_sems.at[i])
            for i, a in enumerate(wholes)
        ]
        for o, (which, options) in enumerate(choices):
            for k, terms in options.items():

                @pl.when(number[which] == k)
                def _():
                    for copy in copies(o, terms):
                        copy.start()

        for copy in loads:
            copy.start()
        for o, (which, options) in enumerate(choices):
            for k, terms in options.items():

                @pl.when(number[which] == k)
                def _():
                    for copy in copies(o, terms):
                        copy.wait()
                    if not terms:
                        held[o][0] = jnp.zeros(shapes[o], f32)
                    if len(terms) > 1:
                        total = held[o][0]
                        for i in range(1, len(terms)):
                            total = total + held[o][i]
                        held[o][0] = total

        for copy in loads:
            copy.wait()
        body(number, [held[o].at[0] for o in range(many)], kept, results)

    return call(
        inner,
        outputs,
        numbers,
        sources,
        pl.ANY,
        [
            *[pltpu.VMEM((m,) + tuple(s), f32) for m, s in zip(most, shapes)],
            *[pltpu.VMEM(array.shape, array.dtype) for array in arrays],
            pltpu.SemaphoreType.DMA((max(many, 1), max(most + [1]))),
            pltpu.SemaphoreType.DMA((max(len(arrays), 1),)),
        ],
        mebibytes,
    )


def chosen_sums(numbers, choices, shape, more, tails):
    many = len(choices)
    sizes = [tail[2][0] for tail in tails] + [0] * (many - len(tails))
    arrays = []

    def place(array):
        for i, known in enumerate(arrays):
            if known is array:
                return i
        arrays.append(array)
        return len(arrays) - 1

    plans = [
        (choice[0], {k: [(place(a), r) for a, r in terms] for k, terms in choice[1].items()})
        for choice in choices + tails
    ]

    def body(number, inputs, outputs):
        def write(plan, result, at, rows):
            which, options = plan
            for k, terms in options.items():

                @pl.when(number[which] == k)
                def _():
                    total = jnp.zeros((rows,) + shape[1:], f32)
                    for i, (a, r) in enumerate(terms):
                        part = inputs[a][r : r + rows]
                        total = part if i == 0 else total + part
                    result[at : at + rows] = total

        for i, (result, rows, size) in enumerate(zip(outputs, more, sizes)):
            at = shape[0]
            write(plans[i], result, 0, at)
            if size:
                write(plans[many + i], result, at, size)
            if rows > size:
                result[at + size :] = jnp.zeros((rows - size,) + shape[1:], f32)

    out = [((shape[0] + rows,) + shape[1:], f32) for rows in more]
    return call(body, out, numbers, arrays, mebibytes=12)


class Windows:
    def __init__(self):
        self.now = 0
        self.processes = []

    def add(self, process):
        self.processes.append([process, None, None])

    def open(self):
        ended = []
        for entry in self.processes:
            process, due, values = entry
            if values and due >= self.now:
                continue
            try:
                windows, entry[2] = process.send(values)
                entry[1] = self.now + windows - 1
            except StopIteration:
                ended.append(entry)
        for entry in ended:
            self.processes.remove(entry)

    def close(self, *others):
        due = [entry for entry in self.processes if entry[1] == self.now and entry[2]]
        flat = list(others)
        for entry in due:
            flat.extend(entry[2])
        if flat:
            flat = list(tie(flat))
        at = len(others)
        for entry in due:
            size = len(entry[2])
            entry[2] = flat[at : at + size]
            at += size
        self.now += 1
        return flat[: len(others)]


def make_step(sizes):
    line, cores, mp, pre = (sizes[name] for name in AXES)
    models = mp * pre
    last = count - 1

    def swap(array, axis, bit):
        return lax.ppermute(array, axis, [(i, i ^ bit) for i in range(sizes[axis])])

    def bits(axis):
        return [1 << i for i in range(sizes[axis].bit_length() - 1)]

    def total(numbers, array, axes):
        for axis in axes:
            for bit in bits(axis):
                pair = yield 1, (array, swap(array, axis, bit))
                array = added(numbers, pair)
        return array

    def snake(array, outward):
        pairs = []
        for z in range(line):
            for c in range(cores):
                goal = z + (1 if (c == 0) == outward else -1)
                if 0 <= goal < line:
                    pairs.append((z * cores + c, goal * cores + c))
                else:
                    pairs.append((z * cores + c, z * cores + 1 - c))
        return lax.ppermute(array, (LINE, CORE), pairs)

    def shards(activations, grad_output, left_old, right_old, probe_left, probe_right):
        z, core = lax.axis_index(LINE), lax.axis_index(CORE)
        x, y = lax.axis_index(MP), lax.axis_index(PRE)
        model = x * pre + y
        width = activations.shape[1]
        block = grad_output.shape[1]
        hidden = block * models
        panel = block // cores
        own_rows = width // (line * cores)
        model_rows = width // models
        piece = width // count
        owner_x, owner_y = z // pre, z % pre
        there = jnp.where(core == 0, z, line - 1 - z)
        numbers = jnp.stack(
            [z, core, there, line - 1 - there, x == owner_x, y == owner_y, model]
        ).astype(jnp.int32)
        Z, C, THERE, BACK, IN_X, IN_Y, MODEL = range(7)
        shape = (piece, panel)
        windows = Windows()
        state = {}

        def to_partner(array):
            return swap(array, CORE, 1)

        def device(number):
            return number[Z] * cores + number[C]

        def local(first, end, mebibytes):
            rows = (end - first) * piece
            tokens = activations.shape[0]
            parts, slices = 4, 3
            span = tokens // parts
            thin = span // slices

            def body(number, inputs, outputs, left, right, sems):
                copies = []
                for i in range(parts):
                    for k in range(slices):
                        at = pl.ds(i * span + k * thin, thin)
                        copies.append(
                            pltpu.make_async_copy(
                                inputs[0].at[at, pl.ds(first * piece, rows)],
                                left.at[at],
                                sems.at[0, i, k],
                            )
                        )
                        copies.append(
                            pltpu.make_async_copy(
                                inputs[1].at[at], right.at[at], sems.at[1, i, k]
                            )
                        )
                for copy in copies:
                    copy.start()
                sums = [None] * (end - first)
                for i in range(parts):
                    for copy in copies[2 * slices * i : 2 * slices * (i + 1)]:
                        copy.wait()
                    at = slice(i * span, (i + 1) * span)
                    for j in range(end - first):
                        term = lax.dot_general(
                            left[at, j * piece : (j + 1) * piece],
                            right[at],
                            (((0,), (0,)), ((), ())),
                            preferred_element_type=f32,
                        )
                        sums[j] = term if i == 0 else sums[j] + term
                zeroth = jnp.full(shape, number[C], jnp.int32) == 0
                for j, both in enumerate(sums):
                    low, high = both[:, :panel], both[:, panel:]
                    outputs[0][j * piece : (j + 1) * piece] = jnp.where(zeroth, low, high)
                    outputs[1 + j][...] = jnp.where(zeroth, high, low)

            return call(
                body,
                [((rows, panel), f32)] + [(shape, f32)] * (end - first),
                numbers,
                [activations, grad_output],
                pl.ANY,
                [
                    pltpu.VMEM((tokens, rows), bf16),
                    pltpu.VMEM(grad_output.shape, bf16),
                    pltpu.SemaphoreType.DMA((2, parts, slices)),
                ],
                mebibytes,
            )

        kept_first, away = local(0, 1, 52)
        arrived = [to_partner(away)]

        class Chain:
            def __init__(self, terms):
                self.terms = terms
                self.sent, self.out, self.home, self.options = [], [], [], []

            def next_sums(self, t):
                choices = []
                for which, got in ((THERE, self.out), (BACK, self.home)):
                    options = {}
                    for k in range(line):
                        options[k] = []
                        if 0 <= t - k < count:
                            options[k] = self.terms(t - k)
                            if k:
                                options[k] = options[k] + [(got[t - 1], 0)]
                    choices.append((which, options))
                return choices

            def next_tails(self, t, piece_number, array):
                choices = []
                if not 0 <= t - piece_number < line:
                    return choices
                for which, got in ((THERE, self.out), (BACK, self.home)):
                    options = {k: [] for k in range(line)}
                    k = t - piece_number
                    options[k] = [(array, 0)] + ([(got[t - 1], piece)] if k else [])
                    choices.append((which, options, array.shape))
                return choices

            def finished_tail(self, piece_number, array):
                j = piece_number
                options = {
                    k: [(self.sent[j + k], piece), (self.home[j + line - 2 - k], piece)]
                    for k in range(line - 1)
                }
                options[line - 1] = [(array, 0), (self.out[j + line - 2], piece)]
                return THERE, options, array.shape

            def send(self, going_out, going_home):
                self.sent.append(going_out)
                self.out.append(snake(going_out, True))
                self.home.append(snake(going_home, False))

            def finished(self, t):
                j = t - (line - 1)
                if not 0 <= j < count:
                    return []
                options = {
                    k: [(self.sent[j + k], 0), (self.home[j + line - 2 - k], 0)]
                    for k in range(line - 1)
                }
                options[line - 1] = self.terms(j) + [(self.out[j + line - 2], 0)]
                self.options.append((THERE, options))
                return self.options[-1:]

        gradient = Chain(
            lambda j: [
                (kept_rest[0], (j - 1) * piece) if j else (kept_first, 0),
                (arrived[j], 0),
            ]
        )
        mixed = Chain(lambda j: [(state["kept", j], 0), (state["swapped", j], 0)])
        own, wishes, kept_rest = [], [], []

        def row(array):
            return array.reshape(1, -1)

        def exchange(array, axis):
            return total(numbers, array, (axis,))

        def placed(number, column):
            wide = (own_rows, width)
            at = lax.broadcasted_iota(jnp.int32, wide, 0) + device(number) * own_rows
            here = lax.broadcasted_iota(jnp.int32, wide, 1) == at
            return jnp.sum(jnp.where(here, column, 0.0), axis=0, keepdims=True)

        def panel_of(which):
            return row(lax.dynamic_slice_in_dim(probe_right, which * panel, panel, 0))

        def beside(first, second):
            def body(number, inputs, outputs):
                size = inputs[0].shape[1]
                outputs[0][:, :size] = inputs[0][...]
                outputs[0][:, size:] = inputs[1][...]

            shape = first.shape[0], first.shape[1] + second.shape[1]
            return call(body, [(shape, f32)], numbers, [first, second])[0]

        def left_turned():
            return (beta_decay * left_old).T

        block_rows, image_rows = block // panel, width // panel
        tail_rows = -(-(block_rows + image_rows) // 8) * 8
        tail_piece = 2

        def old_factors():
            while windows.now < 1:
                yield 1, ()

            def body(number, inputs, outputs):
                old = beta_decay * inputs[0][...]
                outputs[0][...], outputs[1][...] = halves(old)
                image = jnp.sum(old * inputs[1][...], axis=1, keepdims=True).T
                outputs[2][...] = jnp.zeros((tail_rows, panel), f32)
                for r in range(block_rows):
                    outputs[2][r : r + 1] = image[:, r * panel : (r + 1) * panel]
                image = jnp.sum(inputs[2][...] * inputs[3][...], axis=1, keepdims=True)
                image = placed(number, image)
                for r in range(image_rows):
                    at = block_rows + r
                    outputs[2][at : at + 1] = image[:, r * panel : (r + 1) * panel]

            own_probe = lax.dynamic_slice_in_dim(probe_left, model * model_rows, model_rows, 0)
            high, low, images = call(
                body,
                [((block, panel), bf16), ((block, panel), bf16), ((tail_rows, panel), f32)],
                numbers,
                [right_old, panel_of(z * cores + core), left_turned(), row(own_probe)],
            )
            *state["old"], state["tail"] = yield 1, (high, low, images)

        def old_left():
            while windows.now < 1:
                yield 1, ()
            rows = left_turned()
            for axis in (PRE, MP):
                for bit in bits(axis):
                    rows, got = yield 1, (rows, swap(rows, axis, bit))
                    rows = beside(rows, got)
            state["old_left"] = rows

        def spread(array, axis, place, owner):
            result = None
            size = sizes[axis]
            for s in range(1, size):
                got = lax.ppermute(array, axis, [(i, (i + s) % size) for i in range(size)])
                if result is None:
                    result = got
                else:
                    result = jnp.where((place - s) % size == owner, got, result)
            return result

        def panel_piece(j):
            while len(own) <= j:
                yield 1, ()
            if j < depth:
                other, got = yield 1, (to_partner(own[j]), spread(own[j], PRE, y, owner_y))
                state["other", j] = other, 0
            else:
                (got,) = yield 1, (spread(own[j], PRE, y, owner_y),)
            wishes.append((("held", j), (IN_Y, {1: [(own[j], 0)], 0: [(got, 0)]})))
            while ("held", j) not in state:
                yield 1, ()
            held = state["held", j]
            held, got = yield 1, (held, spread(held, MP, x, owner_x))
            riders = []
            if j + depth == last:
                while len(own) < count:
                    yield 1, ()
                riders = [*own[depth:], first_images()]

            def body(number, inputs, outputs):
                here = jnp.full(shape, number[IN_X], jnp.int32) == 1
                pair = halves(jnp.where(here, inputs[0][:piece], inputs[1][:piece]))
                outputs[0][...], outputs[1][...] = pair
                both = product(pair, (inputs[2][...], inputs[3][...]), 1, 1)
                low, high = both[:, :panel], both[:, panel:]
                zeroth = jnp.full(shape, number[C], jnp.int32) == 0
                outputs[2][...] = jnp.where(zeroth, low, high)
                outputs[3][:piece] = jnp.where(zeroth, high, low)
                at = piece
                for rider in inputs[4:]:
                    size = min(rider.shape[0], piece)
                    outputs[3][at : at + size] = rider[:size]
                    at += size

            away_rows = piece + sum(min(rider.shape[0], piece) for rider in riders)
            high, low, state["kept", j], away = call(
                body,
                [(shape, bf16), (shape, bf16), (shape, f32), ((away_rows, panel), f32)],
                numbers,
                [held, got, *state["old"], *riders],
            )
            state["panel", j] = high, low
            _, _, got = yield 1, (high, low, to_partner(away))
            state["swapped", j] = got
            if riders:
                for i in range(depth, count):
                    state["other", i] = got, (i - depth + 1) * piece
                state["images"] = riders[-1], got, (count - depth + 1) * piece

        depth = 2
        rider_rows = -(-(2 * image_rows + block_rows) // 8) * 8

        def first_images():
            def body(number, inputs, outputs):
                right, left = inputs[count][...], inputs[count + 1][...].T
                across = jnp.zeros((1, panel), f32)
                for j in range(count):
                    rows = slice(j * piece, (j + 1) * piece)
                    across += jnp.sum(inputs[j][:piece] * left[rows], axis=0, keepdims=True)
                old = inputs[count + 2][...]
                outputs[0][...] = jnp.zeros((rider_rows, panel), f32)
                outputs[0][2 * image_rows : 2 * image_rows + block_rows] = old[:block_rows]
                for i, vector in enumerate((right, across)):
                    image = jnp.concatenate(
                        [
                            jnp.sum(inputs[j][:piece] * vector, axis=1, keepdims=True).T
                            for j in range(count)
                        ],
                        axis=1,
                    )
                    for r in range(image_rows):
                        at = i * image_rows + r
                        part = image[:, r * panel : (r + 1) * panel]
                        if i:
                            part = part + hidden * old[block_rows + r : block_rows + r + 1]
                        outputs[0][at : at + 1] = part

            return call(
                body,
                [((rider_rows, panel), f32)],
                numbers,
                [
                    *own,
                    panel_of(model * cores + core),
                    row(probe_left),
                    state["old_images"],
                ],
            )[0]

        def over_models(array):
            steps = [(axis, bit) for axis in (PRE, MP) for bit in bits(axis)]
            for i, (axis, bit) in enumerate(steps):
                terms = yield 1, (array, swap(array, axis, bit))
                if i < len(steps) - 1:
                    array = added(numbers, terms)
            return terms

        def first_part(crossed):
            (crossed,) = yield 1, (crossed,)
            crossed = yield from over_models(crossed)
            while "squares" not in state:
                yield 1, ()

            def body(number, inputs, outputs):
                top_left, top_right, scale = scales(inputs[6][...] + inputs[7][...])
                grad = inputs[4][...], inputs[5][...]
                rows = pl.ds(pl.multiple_of(device(number) * own_rows, own_rows), own_rows)
                own = whole_of(inputs[4][rows, :], inputs[5][rows, :])
                crossed = product(halves(inputs[0][...] + inputs[1][...]), grad, 1, 0)
                outputs[0][...] = scale * (
                    25.0 * own
                    - inputs[2][...] * (5.0 / top_left)
                    - (5.0 * inputs[3][...] - crossed / top_left) / top_right
                )

            (state["first_part"],) = call(
                body,
                [((own_rows, block), f32)],
                numbers,
                [*crossed, *state["left_parts"], *state["block"], *state["squares"]],
            )

        def hold_block():
            state["block"] = yield 1, state["block"]

        def left_side():
            while ("other", last) not in state or "images" not in state:
                yield 1, ()
            other = [state["other", j] for j in range(count)]
            images, got, start = state["images"]

            def split_block(number, inputs, high, low):
                zeroth = jnp.full(shape, number[C], jnp.int32) == 0
                for j in range(count):
                    at = other[j][1]
                    mine, theirs = inputs[j][:piece], inputs[count + j][at : at + piece]
                    rows = pl.ds(j * piece, piece)
                    for i, part in enumerate(
                        (jnp.where(zeroth, mine, theirs), jnp.where(zeroth, theirs, mine))
                    ):
                        columns = pl.ds(i * panel, panel)
                        high[rows, columns], low[rows, columns] = halves(part)

            def body(number, inputs, outputs, high, low):
                split_block(number, inputs, high, low)
                rows = pl.ds(pl.multiple_of(device(number) * own_rows, own_rows), own_rows)
                gram = product((high[...], low[...]), (high[rows, :], low[rows, :]), 1, 1)
                outputs[0][:own_rows] = gram.T / hidden
                outputs[0][own_rows:] = jnp.zeros((8, width), f32)
                images = inputs[2 * count][...] + inputs[2 * count + 1][start:]
                for i in range(2):
                    for r in range(image_rows):
                        at = i * image_rows + r
                        outputs[0][own_rows + i : own_rows + i + 1, pl.ds(r * panel, panel)] = (
                            images[at : at + 1]
                        )
                for r in range(block_rows):
                    at = 2 * image_rows + r
                    outputs[1][:, pl.ds(r * panel, panel)] = images[at : at + 1]

            rows = (own_rows, width)
            sources = [*own, *(array for array, _ in other)]
            gram, state["old_image"] = call(
                body,
                [((own_rows + 8, width), f32), ((1, block), f32)],
                numbers,
                [*sources, images, got],
                scratch=[pltpu.VMEM((width, block), bf16)] * 2,
            )

            def body(number, inputs, outputs):
                split_block(number, inputs, *outputs)

            high, low = call(body, [((width, block), bf16)] * 2, numbers, sources)
            state["block"] = high, low
            windows.add(hold_block())
            gram = yield from over_models(gram)
            state["left_terms"] = gram

            def body(number, inputs, outputs):
                gram = inputs[0][:own_rows] + inputs[1][:own_rows]
                old = []
                for m in range(models):
                    part = jnp.zeros((own_rows, model_rows), f32)
                    for k in range(models):
                        at = jnp.full(part.shape, number[MODEL], jnp.int32)
                        block_k = inputs[2][:, k * model_rows : (k + 1) * model_rows]
                        part = jnp.where(at == m ^ k, block_k, part)
                    old.append(part)
                left = jnp.concatenate(old, axis=1) + gram
                outputs[0][...] = left
                new = left[:, :model_rows]
                for m in range(1, models):
                    at = jnp.full(new.shape, number[MODEL], jnp.int32)
                    new = jnp.where(at == m, left[:, m * model_rows : (m + 1) * model_rows], new)
                outputs[4][...] = new.T
                grad = inputs[3][...], inputs[4][...]
                left_grad = product(halves(left), grad, 1, 0)
                outputs[1][...] = left_grad
                outputs[2][...] = gram
                outputs[3][...] = product(grad, halves(left_grad), 1, 1).T / width

            left, left_grad, gram, crossed, new = call(
                body,
                [(rows, f32), ((own_rows, block), f32), (rows, f32), (rows, f32)]
                + [((model_rows, own_rows), f32)],
                numbers,
                [*gram, state["old_left"], *state["block"]],
            )
            state["left"] = left
            windows.add(first_part(crossed))
            left_grad, gram, left = yield 1, (left_grad, gram, left)
            partner_left = to_partner(left)

            def body(number, inputs, outputs):
                grad = inputs[1][...], inputs[2][...]
                outputs[0][...] = product(halves(inputs[0][...]), grad, 1, 0) * (hidden / width)

            (gram_grad,) = call(
                body, [((own_rows, block), f32)], numbers, [gram, *state["block"]]
            )
            state["partner_left"], *state["left_parts"] = yield 1, (
                partner_left,
                left_grad,
                gram_grad,
            )
            state["left_new"] = new

        def powers():
            while "left_terms" not in state:
                yield 1, ()

            def body(number, inputs, outputs):
                images = inputs[5][own_rows:] + inputs[6][own_rows:]
                outputs[1][...] = images[1:2] / hidden
                grad = whole_of(inputs[1][...], inputs[2][...])
                first = inputs[0][...] + (
                    jnp.sum(grad * images[0:1].T, axis=0, keepdims=True) / width
                )
                outputs[0][:, :width] = jnp.sum(grad * first, axis=1, keepdims=True).T
                old = whole_of(inputs[3][...], inputs[4][...])
                outputs[0][:, width : width + panel] = jnp.sum(
                    old * first.T, axis=0, keepdims=True
                )
                square = jnp.sum(first * first, axis=1, keepdims=True)
                outputs[0][:, width + panel :] = jnp.broadcast_to(square, (1, 128))

            joined, first = call(
                body,
                [((1, width + panel + 128), f32), ((1, width), f32)],
                numbers,
                [
                    state["old_image"],
                    *state["block"],
                    *state["old"],
                    *state["left_terms"],
                ],
            )
            for axis in (PRE, MP):
                for bit in bits(axis):
                    joined = added(numbers, [joined, swap(joined, axis, bit)])
            first, joined = yield 1, (first, joined)
            while "left" not in state or ("panel", last) not in state:
                yield 1, ()

            def body(number, inputs, outputs):
                joined = inputs[2 + 2 * count][...]
                for array in inputs[3 + 2 * count :]:
                    joined = joined + array[...]
                vector = joined[:, :width].T
                second = joined[:, width : width + panel]
                for j in range(count):
                    part = whole_of(inputs[2 + 2 * j][...], inputs[3 + 2 * j][...])
                    rows = vector[j * piece : (j + 1) * piece]
                    second = second + jnp.sum(part * rows, axis=0, keepdims=True) / width
                square = joined[:, width + panel : width + panel + 1]
                second = second / jnp.sqrt(square + norm_floor)
                right = jnp.sum(second * second, axis=1, keepdims=True)
                first = inputs[0][...]
                unit = first / jnp.sqrt(
                    jnp.sum(first * first, axis=1, keepdims=True) + norm_floor
                )
                second = jnp.sum(inputs[1][...] * unit, axis=1, keepdims=True)
                left = jnp.sum(second * second, axis=0, keepdims=True)
                spot = lax.broadcasted_iota(jnp.int32, (1, 128), 1)
                outputs[0][...] = jnp.where(spot == 0, left, right)

            panels = [half for j in range(count) for half in state["panel", j]]
            (squares,) = call(
                body,
                [((1, 128), f32)],
                numbers,
                [first, state["left"], *panels, joined],
            )
            squares = added(numbers, [squares, to_partner(squares)])
            for bit in bits(LINE)[:-2]:
                squares = added(numbers, [squares, swap(squares, LINE, bit)])
            squares = added(numbers, (yield 1, (squares, swap(squares, LINE, bits(LINE)[-2]))))
            state["squares"] = yield 1, (squares, swap(squares, LINE, bits(LINE)[-1]))

        def scales(squares):
            top = jnp.sqrt(squares + norm_floor)
            top_left, top_right = top[:, 0:1], top[:, 1:2]
            return top_left, top_right, 1.0 / (16.0 * jnp.sqrt(jnp.sqrt(top_left * top_right)))

        def right_factor():
            while ("panel", last) not in state or "block" not in state or windows.now < steps + 2:
                yield 1, ()

            def body(number, sums, inputs, outputs):
                pair = [
                    jnp.concatenate([inputs[3 + 2 * j + i][...] for j in range(count)], axis=0)
                    for i in range(2)
                ]
                gram = product((inputs[1][...], inputs[2][...]), pair, 0, 0)
                outputs[0][...] = beta_decay * inputs[0][...] + gram / width

            panels = [half for j in range(count) for half in state["panel", j]]
            (state["right_new"],) = yield 1, fetching(
                body,
                [((block, panel), f32)],
                numbers,
                [],
                shape,
                [right_old, *state["block"], *panels],
                32,
            )

        for j in range(count):
            windows.add(panel_piece(j))
        steps = count + line - 2
        def rows_here(number, i, rows, pieces):
            other = number[C] if i == 0 else 1 - number[C]
            at = jnp.full(rows.shape, number[Z] * cores + other, jnp.int32)
            for k in range(line * cores):
                j, start = divmod(k * own_rows, piece)
                for number_j, array in pieces:
                    if number_j == j:
                        rows = jnp.where(at == k, array[start : start + own_rows], rows)
            return rows

        def early_products():
            while len(mixed_wholes) < last or "partner_left" not in state:
                yield 1, ()

            def body(number, inputs, outputs):
                pieces = [(j, inputs[2 + j]) for j in range(last)]
                pair = halves(jnp.concatenate([array[:piece] for _, array in pieces], axis=0))
                for i in range(2):
                    left = halves(inputs[i][:, : last * piece])
                    outputs[i][...] = product(left, pair, 1, 0)
                    outputs[2 + i][...] = rows_here(
                        number, i, jnp.zeros((own_rows, panel), f32), pieces
                    )

            state["early"] = yield 1, call(
                body,
                [((own_rows, panel), f32)] * 4,
                numbers,
                [state["left"], state["partner_left"], *mixed_wholes],
            )

        mixed_wholes = []
        for process in (left_side, powers, right_factor, early_products):
            windows.add(process())

        for t in range(2 * steps):
            windows.open()
            current = gradient if t < steps else mixed
            choices = current.next_sums(t % steps) + gradient.finished(t)
            choices += mixed.finished(t - steps)
            names = [name for name, _ in wishes]
            choices += [choice for _, choice in wishes]
            wishes.clear()
            crowded = t == line + depth - 1
            longer = tail_rows + (16 if steps < t < steps + 3 else 8 if crowded else 0)
            extra = [longer] * 2 + [0] * (len(choices) - 2)
            for i, name in enumerate(names):
                extra[len(extra) - len(names) + i] = 8 if crowded else 0
            if crowded:
                extra[2] = 8
            if ("held", last) in names:
                extra[-1] = longer
            tails = []
            if t < steps and "tail" in state:
                tails = gradient.next_tails(t, tail_piece, state["tail"])
            results = list(chosen_sums(numbers, choices, shape, extra, tails))
            if t == 0:
                results[0], results[1], activations, grad_output, left_old, right_old = tie(
                    (*results, activations, grad_output, left_old, right_old)
                )
                windows.add(old_factors())
                windows.add(old_left())
                kept, *away = local(1, count, 28)
                kept_rest.append(kept)
                arrived += [to_partner(a) for a in away]
            current.send(*results[:2])
            for name in reversed(names):
                state[name] = results.pop()
            (own if len(own) < count else mixed_wholes).extend(results[2:])
            if t == tail_piece + line - 1:
                tail = gradient.finished_tail(tail_piece, state["tail"])

                def copy_body(number, sums, inputs, outputs):
                    outputs[0][...] = sums[0][...]

                (state["old_images"],) = fetching(
                    copy_body, [(tail[2], f32)], numbers, [tail], shape
                )
            windows.open()
            current.out[-1], current.home[-1] = windows.close(current.out[-1], current.home[-1])
        while windows.processes:
            windows.open()
            if windows.processes:
                windows.close()

        def body(number, sums, inputs, outputs):
            top_left, top_right, scale = scales(inputs[0][...] + inputs[1][...])
            pair = halves(sums[0][...])
            for i in range(2):
                rows = rows_here(number, i, inputs[6 + i][...], [(last, sums[0])])
                left = halves(inputs[2 + i][:, last * piece :])
                left = inputs[4 + i][...] + product(left, pair, 1, 0)
                outputs[i][...] = (left / top_left - 5.0 * rows) * (scale / top_right)

        mine, theirs = fetching(
            body,
            [((own_rows, panel), f32)] * 2,
            numbers,
            mixed.finished(steps),
            shape,
            [*state["squares"], state["left"], state["partner_left"], *state["early"]],
        )
        theirs = to_partner(theirs)

        def body(number, inputs, outputs):
            zeroth = jnp.full((own_rows, panel), number[C], jnp.int32) == 0
            mine, theirs = inputs[1][...], inputs[2][...]
            parts = jnp.where(zeroth, mine, theirs), jnp.where(zeroth, theirs, mine)
            for i, part in enumerate(parts):
                span = pl.ds(i * panel, panel)
                outputs[0][:, span] = inputs[0][:, span] + part

        (update,) = call(
            body, [((own_rows, block), f32)], numbers, [state["first_part"], mine, theirs]
        )
        return state["left_new"], state["right_new"], update

    return shards


def solution(mesh):
    dp, mp, pre = (mesh.shape[name] for name in ("dp", "mp", "pre"))
    cores = dp // (mp * pre)
    assert cores == 2
    split = Mesh(mesh.devices.reshape(dp // cores, cores, mp, pre), AXES)
    factor = P((MP, PRE), (LINE, CORE))
    in_specs = (
        P((LINE, CORE), None),
        P((LINE, CORE), (MP, PRE)),
        factor,
        factor,
        P(),
        P(),
    )
    out_specs = (factor, factor, P((LINE, CORE), (MP, PRE)))
    return jax.shard_map(
        make_step(dict(split.shape)),
        mesh=split,
        in_specs=in_specs,
        out_specs=out_specs,
        check_vma=False,
    )
```
